128 devices in a mesh: seq: 32 (over x, y, core), head: 4 (over z).
Axes of the slice: x: 4, y: 4, z: 4, core: 2. Of those that a mesh axis runs over, the one named last changes fastest.
Arguments:
- layer_in: bfloat16 [16384, 2048], P('seq', 'head'), may hold values from -6 to 6
- gain1: float32 [2048], replicated, may hold values from 0.25 to 1.75
- wq: bfloat16 [2048, 2048], P(None, 'head'), may hold values from -0.125 to 0.125
- wk: bfloat16 [2048, 2048], P(None, 'head'), may hold values from -0.125 to 0.125
- wv: bfloat16 [2048, 4096], P(None, 'head'), may hold values from -0.125 to 0.125
- wg: bfloat16 [2048, 4096], P(None, 'head'), may hold values from -0.125 to 0.125
- wo: bfloat16 [4096, 2048], P('head'), may hold values from -0.125 to 0.125
- gain2: float32 [2048], replicated, may hold values from 0.25 to 1.75
- w1: bfloat16 [2048, 4096], P(None, 'head'), may hold values from -0.125 to 0.125
- w2: bfloat16 [4096, 2048], P('head'), may hold values from -0.125 to 0.125
- starts: int32 [3], replicated, may hold values from 0 to 16383, as said below
- cotangent: bfloat16 [16384, 2048], P('seq', 'head'), may hold values from -6 to 6
Outputs:
- out: bfloat16 [16384, 2048], P('seq', 'head')
- grad_x: float32 [16384, 2048], P('seq', 'head')
- grad_gain1: float32 [2048], P('head')
- grad_wq: float32 [2048, 2048], P('seq', 'head')
- grad_wk: float32 [2048, 2048], P('seq', 'head')
- grad_wv: float32 [2048, 4096], P('seq', 'head')
- grad_wg: float32 [2048, 4096], P('seq', 'head')
- grad_wo: float32 [4096, 2048], P('head', 'seq')
- grad_gain2: float32 [2048], P('head')
- grad_w1: float32 [2048, 4096], P('seq', 'head')
- grad_w2: float32 [4096, 2048], P('head', 'seq')
The draws below stay inside these ranges and needn't reach their ends.
Inputs may be any that keep to these rules, and one draw needn't show every extreme that they name: starts[0] = 0 and the starts rise strictly; starts[1] and starts[2] each lie in the first 512 tokens or in the last 512 tokens, so that one document holds tokens of both.
All inputs are finite; a program needn't handle non-finite values.
Results may differ from the reference program's by a relative error of at most 0.023.
Values may be sent and summed in bfloat16 or wider, within the bound.
No kernel may reach another device: no remote copies, remote signals or barrier semaphores. Data moves between devices by JAX's collectives and lax.ppermute only.
A program may use at most 256 MiB of HBM per device.

```python
import math
import jax
import jax.numpy as jnp
from jax import lax

D = 2048
HEADS = 8
KEY_DIM = 256
VALUE_DIM = 512
FF = 4096
TOK_DEV = 512
QK = 2048
VV = 4096
TOKENS = 16384
BLOCK = 512


def draw_starts(key, part):
    key = jax.random.fold_in(key, 11)
    pick_key, first_key, second_key = jax.random.split(key, 3)
    pick = jax.random.randint(pick_key, (), 0, 3)
    first = jax.random.randint(first_key, (), 1, TOK_DEV - 1)
    second = first + 1 + jax.random.randint(second_key, (), 0, TOK_DEV - 1 - first)
    tail = TOKENS - TOK_DEV
    start_one = jnp.where(pick == 0, tail + first, first)
    start_two = jnp.where(pick == 2, second, tail + second)
    return jnp.stack([jnp.zeros((), jnp.int32), start_one.astype(jnp.int32), start_two.astype(jnp.int32)]).astype(jnp.int32)


def levels(rng, dims, pieces, least, top_value):
    gain, own = 1.0, jax.random.fold_in(rng, 6)
    for dim, blocks in pieces:
        steps = jnp.exp(jax.random.uniform(jax.random.fold_in(own, dim), (blocks,), jnp.float32, least / len(pieces), top_value / len(pieces)))
        gain = gain * jnp.repeat(steps, dims[dim] // blocks).reshape([-1 if axis == dim else 1 for axis in range(len(dims))])
    return gain


def noise(rng, shape, scale, reach, cuts=(), held_as=jnp.bfloat16):
    loudness = levels(rng, shape, cuts, -0.22, 0.18) if cuts else 1.0
    values = jax.random.normal(rng, shape, jnp.float32) * scale * loudness
    return jnp.minimum(jnp.maximum(values, -reach), reach).astype(held_as)


def setup_inputs(seed: int = 0) -> dict:
    key_of = jax.random.split(jax.random.key(seed), 13)
    return {
        "layer_in": noise(key_of[0], (TOKENS, D), 1.0, 6.0, ((0, 32), (1, 4))),
        "gain1": jnp.clip(1.0 + 0.15 * jax.random.normal(key_of[1], (D,), jnp.float32), 0.25, 1.75),
        "wq": noise(key_of[2], (D, QK), D ** -0.5, 0.125, ((1, 4),)),
        "wk": noise(key_of[3], (D, QK), D ** -0.5, 0.125, ((1, 4),)),
        "wv": noise(key_of[4], (D, VV), D ** -0.5, 0.125, ((1, 4),)),
        "wg": noise(key_of[5], (D, VV), D ** -0.5, 0.125, ((1, 4),)),
        "wo": noise(key_of[6], (VV, D), (VV // 2) ** -0.5, 0.125, ((0, 4),)),
        "gain2": jnp.clip(1.0 + 0.15 * jax.random.normal(key_of[7], (D,), jnp.float32), 0.25, 1.75),
        "w1": noise(key_of[8], (D, FF), D ** -0.5, 0.125, ((1, 4),)),
        "w2": noise(key_of[9], (FF, D), (FF // 2) ** -0.5, 0.125, ((0, 4),)),
        "starts": draw_starts(jax.random.fold_in(key_of[12], 71), 0),
        "cotangent": noise(key_of[11], (TOKENS, D), 1.0, 6.0, ((0, 32), (1, 4))),
    }


epsilon = 1e-05
highest_precision = lax.Precision.HIGHEST

@jax.custom_vjp
def low(v):
    return lax.optimization_barrier(v.astype(jnp.bfloat16)).astype(jnp.float32)

@jax.custom_vjp
def low_back(v):
    return v

def low_keep(v):
    return (low(v), None)

def low_pass(kept, grad):
    return (grad,)

def back_keep(v):
    return (v, None)

def back_low(kept, grad):
    return (low(grad),)
low.defvjp(low_keep, low_pass)
low_back.defvjp(back_keep, back_low)

def matmul(left, right):
    return jnp.dot(left, right, preferred_element_type=jnp.float32, precision=highest_precision)

def layer_norm(value_row_set, gain_vec):
    centered = value_row_set - lax.optimization_barrier(jnp.mean(value_row_set, axis=-1, keepdims=True))
    inverse = lax.rsqrt(lax.optimization_barrier(jnp.mean(centered * centered, axis=-1, keepdims=True)) + epsilon)
    return centered * inverse * gain_vec

def rotate_pairs(value_row_set, cosine, sine_table, direction):
    half_dim = value_row_set.shape[-1] // 2
    first_part = value_row_set[..., :half_dim]
    second = value_row_set[..., half_dim:]
    return jnp.concatenate([first_part * cosine - direction * second * sine_table, second * cosine + direction * first_part * sine_table], axis=-1)

def retain_block(carry, block):
    running_state, prior_doc = carry
    segment_queries, segment_keys, segment_values, doc_block = block
    log_decay = jnp.log1p(-jnp.exp2(-5.0 - jnp.arange(HEADS).astype(jnp.float32)))
    offsets = jnp.arange(BLOCK, dtype=jnp.int32)
    gap_grid = offsets[:, None] - offsets[None, :]
    causal = gap_grid >= 0
    keep_mask = causal & (doc_block[:, None] == doc_block[None, :])
    gap_float = jnp.where(causal, gap_grid, 0).astype(jnp.float32)
    decay_grid = jnp.where(keep_mask[None], jnp.exp(gap_float[None] * log_decay[:, None, None]), 0.0)
    step_float = offsets.astype(jnp.float32)
    arrival_decay = jnp.exp((step_float[None, :] + 1.0) * log_decay[:, None]) * (doc_block == prior_doc).astype(jnp.float32)[None, :]
    last_doc = doc_block[BLOCK - 1].astype(jnp.int32)
    departure_decay = jnp.exp((BLOCK - 1.0 - step_float)[None, :] * log_decay[:, None]) * (doc_block == last_doc).astype(jnp.float32)[None, :]
    segment_decay = jnp.exp(BLOCK * log_decay) * (last_doc == prior_doc).astype(jnp.float32)
    scores = jnp.einsum('thk,shk->hts', segment_queries, segment_keys, precision=highest_precision)
    within_segment_part = jnp.einsum('hts,shv->thv', scores * decay_grid, segment_values, precision=highest_precision)
    carried_over = arrival_decay.T[:, :, None] * jnp.einsum('mfw,fwq->mfq', segment_queries, running_state, precision=highest_precision)
    updated_state = segment_decay[:, None, None] * running_state + jnp.einsum('aqc,aqr->qcr', segment_keys * departure_decay.T[:, :, None], segment_values, precision=highest_precision)
    return ((updated_state, last_doc), within_segment_part + carried_over)

def retention(query_rot, key_rot, value_rows, doc_ids):
    blocks = TOKENS // BLOCK
    query_blocks = query_rot.reshape(blocks, BLOCK, HEADS, KEY_DIM)
    key_blocks = key_rot.reshape(blocks, BLOCK, HEADS, KEY_DIM)
    value_blocks = value_rows.reshape(blocks, BLOCK, HEADS, VALUE_DIM)
    doc_blocks = doc_ids.reshape(blocks, BLOCK).astype(jnp.int32)
    start_carry = (jnp.zeros((HEADS, KEY_DIM, VALUE_DIM), query_rot.dtype), jnp.array(-1, jnp.int32))
    _, result = lax.scan(jax.checkpoint(retain_block), start_carry, (query_blocks, key_blocks, value_blocks, doc_blocks))
    return result.reshape(TOKENS, HEADS, VALUE_DIM)

def reference(layer_in, gain1, wq, wk, wv, wg, wo, gain2, w1, w2, starts, cotangent):
    positions = jnp.arange(TOKENS, dtype=jnp.int32)
    member = positions[:, None] >= starts[None, :].astype(jnp.int32)
    doc_ids = (lax.optimization_barrier(jnp.sum(member.astype(jnp.int32), axis=-1)) - 1).astype(jnp.int32)
    last_start = lax.optimization_barrier(jnp.max(jnp.where(member, starts[None, :].astype(jnp.int32), 0), axis=-1)).astype(jnp.int32)
    relative = (positions - last_start).astype(jnp.float32)
    half_dim = KEY_DIM // 2
    frequency = jnp.exp(-math.log(10000.0) * jnp.arange(half_dim, dtype=jnp.float32) / half_dim)
    angles = relative[:, None] * frequency[None, :]
    cosine = jnp.cos(angles)[:, None, :]
    sine_table = jnp.sin(angles)[:, None, :]
    group_floor = float(KEY_DIM)

    def forward(x_in, gain_one, query_w, key_w, value_w, gate_w, out_w, gain_two, up_w, down_w):
        norm_low = low(layer_norm(x_in, gain_one))
        query_rot = low(rotate_pairs(low_back(matmul(norm_low, query_w)).reshape(TOKENS, HEADS, KEY_DIM), cosine, sine_table, 1.0))
        key_rot = low(rotate_pairs(low_back(matmul(norm_low, key_w)).reshape(TOKENS, HEADS, KEY_DIM), cosine, sine_table, 1.0))
        value_rows = low(low_back(matmul(norm_low, value_w))).reshape(TOKENS, HEADS, VALUE_DIM)
        retention_output = retention(query_rot, key_rot, value_rows, doc_ids)
        centered = retention_output - lax.optimization_barrier(jnp.mean(retention_output, axis=-1, keepdims=True))
        grouped = centered * lax.rsqrt(lax.optimization_barrier(jnp.mean(centered * centered, axis=-1, keepdims=True)) + group_floor)
        gate_pre = low_back(matmul(norm_low, gate_w))
        mixed = low(grouped.reshape(TOKENS, VV) * jax.nn.silu(gate_pre))
        middle = x_in + low_back(matmul(mixed, out_w))
        ffn_input = low(layer_norm(middle, gain_two))
        hidden_pre = low_back(matmul(ffn_input, up_w))
        hidden = low(jax.nn.gelu(hidden_pre, approximate=False))
        return middle + low_back(matmul(hidden, down_w))
    floats = tuple((item.astype(jnp.float32) for item in (layer_in, gain1, wq, wk, wv, wg, wo, gain2, w1, w2)))
    output, pullback = jax.vjp(forward, *floats)
    grads = pullback(cotangent.astype(jnp.float32))
    return (output.astype(jnp.bfloat16), grads[0], grads[1], grads[2], grads[3], grads[4], grads[5], grads[6], grads[7], grads[8], grads[9])
```

```python
from functools import partial
import math

import jax
import jax.numpy as jnp
from jax import lax
from jax.sharding import PartitionSpec as P

KEY_DIM = 256
VALUE_DIM = 512
SIDE = 4
CORES = 2
EPSILON = 1e-05
F32 = jnp.float32
BF16 = jnp.bfloat16


def head_shift(step):
    return [(h, (h + step) % SIDE) for h in range(SIDE)]


def seq_index(x, y, core):
    return (x * SIDE + y) * CORES + core


def seq_shift(dx, dy, swap=0):
    return [
        (seq_index(x, y, core), seq_index((x + dx) % SIDE, (y + dy) % SIDE, core ^ swap))
        for x in range(SIDE)
        for y in range(SIDE)
        for core in range(CORES)
    ]


def dot(left, right):
    return jnp.dot(left, right, preferred_element_type=F32)


def dot_t(left, right):
    return lax.dot_general(left, right, (((1,), (1,)), ((), ())), preferred_element_type=F32)


def einsum(form, left, right):
    return jnp.einsum(form, left.astype(BF16), right.astype(BF16), preferred_element_type=F32)


def after(value, *others):
    return lax.optimization_barrier((value, *others))[0]


def gather_parts(block):
    return [block] + [lax.ppermute(block, "head", head_shift(k)) for k in (1, 3, 2)]


def assemble(parts, head_rank):
    rows, width = parts[0].shape
    whole = jnp.zeros((rows, SIDE * width), parts[0].dtype)
    for part, k in zip(parts, (0, 1, 3, 2)):
        at = lax.rem(head_rank + SIDE - k, SIDE)
        whole = lax.dynamic_update_slice(whole, part, (0, at * width))
    return whole


def scatter_cols(partial_sum, head_rank):
    width = partial_sum.shape[1] // SIDE

    def block(k):
        at = lax.rem(head_rank + k, SIDE)
        return lax.dynamic_slice_in_dim(partial_sum, at * width, width, 1)

    received = [lax.ppermute(block(k), "head", head_shift(k)) for k in (2, 1, 3)]
    total = block(0).astype(F32)
    for piece in received:
        total = total + piece.astype(F32)
    return total


def sum_heads(values):
    total = values
    for k in (1, 2, 3):
        total = total + lax.ppermute(values, "head", head_shift(k))
    return total


def axis_phase(blocks, dim, position, shift_of):
    def block(k):
        return lax.dynamic_index_in_dim(blocks, lax.rem(position + k, SIDE), dim, False)

    received = [lax.ppermute(block(k), "seq", shift_of(k)) for k in (2, 1, 3)]
    total = block(0).astype(F32)
    for piece in received:
        total = total + piece.astype(F32)
    return total


def weight_scatter(left_halves, right, place, x_first):
    x, y, core = place
    left_own, left_other = left_halves
    width = right.shape[1]
    other = dot(left_other, right).astype(BF16)
    arrived = lax.ppermute(other, "seq", seq_shift(0, 0, 1))
    own = (dot(left_own, right) + arrived.astype(F32)).astype(BF16)
    own = own.reshape(SIDE, SIDE, -1, width)
    x_of = lambda k: seq_shift(k, 0)
    y_of = lambda k: seq_shift(0, k)
    if x_first:
        half = axis_phase(own, 0, x, x_of).astype(BF16)
        return axis_phase(half, 0, y, y_of)
    half = axis_phase(own, 1, y, y_of).astype(BF16)
    return axis_phase(half, 0, x, x_of)


def state_scan(state, decay, place, reverse):
    x, y, core = place
    swap = seq_shift(0, 0, 1)
    keys, values = state.shape[1:]
    own = lax.dynamic_index_in_dim(state, core, 0, False)
    give = lax.dynamic_index_in_dim(state, 1 - core, 0, False).astype(BF16)
    got = lax.ppermute(give, "seq", swap).astype(F32)
    own_decay = lax.dynamic_index_in_dim(decay, core, 0, False)
    far_core = (core == 0) if not reverse else (core == 1)
    chip_decay = own_decay * own_decay
    total = jnp.where(far_core, own_decay * own + got, own + own_decay * got)
    quarters = total.astype(BF16).reshape(SIDE, keys // SIDE, values)
    row = {}
    for k in (0, 1, 3, 2):
        piece = lax.dynamic_index_in_dim(quarters, lax.rem(y + k, SIDE), 0, False)
        row[k] = piece if k == 0 else lax.ppermute(piece, "seq", seq_shift(0, k))
    pieces = jnp.stack([row[k].astype(F32) for k in range(SIDE)])
    origin = lax.rem(y - jnp.arange(SIDE) + SIDE, SIDE)
    towards = origin if reverse else SIDE - 1 - origin
    row_weight = jnp.exp(jnp.log(chip_decay) * towards.astype(F32))
    row_total = jnp.sum(row_weight[:, None, None] * pieces, axis=0).astype(BF16)
    row_decay = chip_decay**SIDE
    before = jnp.zeros_like(row_total, F32)
    for k in (1, 3, 2):
        piece = lax.ppermute(row_total, "seq", seq_shift(k, 0)).astype(F32)
        if reverse:
            hops = SIDE - k
            counts = x + hops < SIDE
        else:
            hops = k
            counts = x >= k
        before = before + jnp.where(counts, row_decay ** (hops - 1), 0.0) * piece
    targets = jnp.arange(SIDE)
    if reverse:
        gap = origin[None, :] - targets[:, None]
        carry = SIDE - 1 - targets
    else:
        gap = targets[:, None] - origin[None, :]
        carry = targets
    weights = jnp.where(gap > 0, jnp.exp(jnp.log(chip_decay) * (gap - 1).astype(F32)), 0.0)
    carry_weight = jnp.exp(jnp.log(chip_decay) * carry.astype(F32))
    answers = (
        jnp.einsum("tk,kab->tab", weights, pieces, precision=lax.Precision.HIGHEST)
        + carry_weight[:, None, None] * before[None]
    ).astype(BF16)
    back = [None] * SIDE
    for k in (0, 1, 3, 2):
        at = lax.rem(y + k, SIDE)
        piece = lax.dynamic_index_in_dim(answers, at, 0, False)
        back[k] = piece if k == 0 else lax.ppermute(piece, "seq", seq_shift(0, k))
    chip_in = jnp.zeros((SIDE, keys // SIDE, values), BF16)
    for k in range(SIDE):
        at = lax.rem(y - k + SIDE, SIDE)
        chip_in = lax.dynamic_update_index_in_dim(chip_in, back[k], at, 0)
    chip_in = chip_in.reshape(keys, values).astype(F32)
    later = own_decay * chip_in + jnp.where(far_core, own, got)
    mine = jnp.where(far_core, chip_in, later)
    theirs = jnp.where(far_core, later, chip_in).astype(BF16)
    from_sibling = lax.ppermute(theirs, "seq", swap)
    mine = mine.astype(BF16)
    first = jnp.where(core == 0, mine, from_sibling)
    second = jnp.where(core == 0, from_sibling, mine)
    return jnp.stack([first, second])


def norm_forward(rows):
    centered = rows - jnp.mean(rows, axis=-1, keepdims=True)
    inverse = lax.rsqrt(jnp.mean(centered * centered, axis=-1, keepdims=True) + EPSILON)
    return (centered * inverse, inverse)


def rotate_pairs(rows, cosine, sine, direction):
    half = rows.shape[-1] // 2
    first = rows[..., :half]
    second = rows[..., half:]
    return jnp.concatenate(
        [
            first * cosine - direction * second * sine,
            second * cosine + direction * first * sine,
        ],
        axis=-1,
    )


def shards(layer_in, gain1, wq, wk, wv, wg, wo, gain2, w1, w2, starts, cotangent):
    seq_rank = lax.axis_index("seq")
    head_rank = lax.axis_index("head")
    place = (seq_rank // (SIDE * CORES), (seq_rank // CORES) % SIDE, seq_rank % CORES)
    core = place[2]
    rows, width = layer_in.shape
    model = width * SIDE
    heads = wq.shape[1] // KEY_DIM
    value_cols = wv.shape[1]
    col_start = head_rank * width
    gain1_part = lax.dynamic_slice_in_dim(gain1, col_start, width)
    gain2_part = lax.dynamic_slice_in_dim(gain2, col_start, width)

    def part_of(array):
        return lax.dynamic_slice_in_dim(array, col_start, width, 1)

    def halves(array):
        split = array.T.reshape(SIDE * SIDE, CORES, -1, rows)
        pick = lambda at: lax.dynamic_index_in_dim(split, at, 1, False).reshape(-1, rows)
        return pick(core), pick(1 - core)

    offsets = jnp.arange(rows, dtype=jnp.int32)
    positions = seq_rank * rows + offsets
    member = positions[:, None] >= starts[None, :]
    doc_ids = jnp.sum(member.astype(jnp.int32), axis=-1) - 1
    last_start = jnp.max(jnp.where(member, starts[None, :], 0), axis=-1)
    relative = (positions - last_start).astype(F32)
    prior_doc = jnp.sum((seq_rank * rows - 1 >= starts).astype(jnp.int32)) - 1
    half_dim = KEY_DIM // 2
    frequency = jnp.exp(-math.log(10000.0) * jnp.arange(half_dim, dtype=F32) / half_dim)
    angles = relative[:, None] * frequency[None, :]
    cosine = jnp.cos(angles)[:, None, :]
    sine = jnp.sin(angles)[:, None, :]
    head_ids = (head_rank * heads + jnp.arange(heads, dtype=jnp.int32)).astype(F32)
    log_decay = jnp.log1p(-jnp.exp2(-5.0 - head_ids))
    gap_grid = offsets[:, None] - offsets[None, :]
    keep = (gap_grid >= 0) & (doc_ids[:, None] == doc_ids[None, :])
    gap_float = jnp.where(gap_grid >= 0, gap_grid, 0).astype(F32)
    decay_grid = jnp.where(keep[None], jnp.exp(gap_float[None] * log_decay[:, None, None]), 0.0)
    step_float = offsets.astype(F32)
    arrival = jnp.exp((step_float[:, None] + 1.0) * log_decay[None, :]) * (
        doc_ids == prior_doc
    ).astype(F32)[:, None]
    departure = jnp.exp((rows - 1.0 - step_float)[:, None] * log_decay[None, :]) * (
        doc_ids == doc_ids[rows - 1]
    ).astype(F32)[:, None]
    arrival = arrival[:, :, None]
    departure = departure[:, :, None]
    segment_decay = jnp.exp(rows * log_decay)

    whole_rows = assemble(gather_parts(layer_in), head_rank).astype(F32)
    normed1, inverse1 = norm_forward(whole_rows)
    norm_low = (normed1 * gain1).astype(BF16)
    grad_full = lax.all_gather(after(cotangent, norm_low), "head", axis=1, tiled=True)
    key_rows = rotate_pairs(
        dot(norm_low, wk).reshape(rows, heads, KEY_DIM), cosine, sine, 1.0
    ).astype(BF16)
    value_rows = dot(norm_low, wv).astype(BF16).reshape(rows, heads, VALUE_DIM)
    own_state = einsum("thk,thv->hkv", key_rows.astype(F32) * departure, value_rows)
    incoming = state_scan(own_state, segment_decay, place, False)
    query_rows = rotate_pairs(
        dot(norm_low, wq).reshape(rows, heads, KEY_DIM), cosine, sine, 1.0
    ).astype(BF16)
    gate_pre = dot(norm_low, wg)
    scores = einsum("thk,shk->hts", query_rows, key_rows)
    weighted = (scores * decay_grid).astype(BF16)
    within = einsum("hts,shv->thv", weighted, value_rows)
    retained = within + arrival * einsum("thk,hkv->thv", query_rows, incoming)
    centered = retained - jnp.mean(retained, axis=-1, keepdims=True)
    group_inv = lax.rsqrt(jnp.mean(centered * centered, axis=-1, keepdims=True) + float(KEY_DIM))
    grouped = centered * group_inv
    flat_group = grouped.reshape(rows, value_cols)
    gate_sigmoid = jax.nn.sigmoid(gate_pre)
    swish = gate_pre * gate_sigmoid
    mixed = (flat_group * swish).astype(BF16)
    branch_part = scatter_cols(dot(mixed, wo).astype(BF16), head_rank).astype(BF16)
    branch = assemble(gather_parts(branch_part), head_rank).astype(F32)
    middle = whole_rows + branch
    normed2, inverse2 = norm_forward(middle)
    ffn_input = (normed2 * gain2).astype(BF16)
    hidden_pre = dot(ffn_input, w1)
    cdf = 0.5 * (1.0 + lax.erf(hidden_pre * (2.0**-0.5)))
    hidden = (hidden_pre * cdf).astype(BF16)
    pdf = jnp.exp(-0.5 * hidden_pre * hidden_pre) * ((2.0 * math.pi) ** -0.5)
    grad_hidden = dot_t(grad_full, w2)
    grad_pre = ((cdf + hidden_pre * pdf) * grad_hidden).astype(BF16)

    def norm_back(partial_grad, gain, gain_part, normed, normed_part, inverse):
        low = partial_grad.astype(BF16)
        scaled = partial_grad * gain
        sums = sum_heads(
            jnp.stack([jnp.sum(scaled, axis=-1), jnp.sum(scaled * normed, axis=-1)])
        )
        grad = scatter_cols(low, head_rank)
        gain_grad = jnp.sum(grad * normed_part, axis=0)
        back = inverse * (
            grad * gain_part
            - sums[0][:, None] / model
            - normed_part * (sums[1][:, None] / model)
        )
        return back, gain_grad

    normed2_part = part_of(normed2)
    back2, gain2_grad = norm_back(
        dot_t(grad_pre, w1), gain2, gain2_part, normed2, normed2_part, inverse2
    )
    grad_middle = cotangent.astype(F32) + back2
    grad_branch = assemble(gather_parts(grad_middle.astype(BF16)), head_rank)
    cot_halves = halves(grad_full)
    grad_w2 = weight_scatter(cot_halves, hidden, place, True)
    grad_w1 = weight_scatter(halves(ffn_input), grad_pre, place, False)
    ffn_out = dot(hidden, w2).astype(BF16)
    ffn_part = lax.psum_scatter(
        after(ffn_out, grad_branch), "head", scatter_dimension=1, tiled=True
    ).astype(F32)
    output = (part_of(middle) + ffn_part).astype(BF16)

    grad_mixed = dot_t(grad_branch, wo)
    grad_gate = (
        grad_mixed * flat_group * (gate_sigmoid * (1.0 + gate_pre * (1.0 - gate_sigmoid)))
    ).astype(BF16)
    grad_group = (grad_mixed * swish).reshape(rows, heads, VALUE_DIM)
    grad_retained = group_inv * (
        grad_group
        - jnp.mean(grad_group, axis=-1, keepdims=True)
        - grouped * jnp.mean(grad_group * grouped, axis=-1, keepdims=True)
    )
    low_grad = grad_retained.astype(BF16)
    own_back = einsum("thk,thv->hkv", query_rows, grad_retained * arrival)
    outgoing = state_scan(own_back, segment_decay, place, True)
    grad_scores = (einsum("thv,shv->hts", low_grad, value_rows) * decay_grid).astype(BF16)
    grad_query = einsum("hts,shk->thk", grad_scores, key_rows) + arrival * einsum(
        "thv,hkv->thk", low_grad, incoming
    )
    grad_qpre = rotate_pairs(grad_query, cosine, sine, -1.0).reshape(rows, -1).astype(BF16)
    grad_wo = weight_scatter(halves(grad_branch), mixed, place, True)
    norm_halves = halves(norm_low)
    grad_wg = weight_scatter(norm_halves, grad_gate, place, False)
    grad_key = einsum("hts,thk->shk", grad_scores, query_rows) + departure * einsum(
        "shv,hkv->shk", value_rows, outgoing
    )
    grad_value = einsum("hts,thv->shv", weighted, low_grad) + departure * einsum(
        "shk,hkv->shv", key_rows, outgoing
    )
    grad_kpre = rotate_pairs(grad_key, cosine, sine, -1.0).reshape(rows, -1).astype(BF16)
    grad_vpre = grad_value.reshape(rows, -1).astype(BF16)
    grad_wv = weight_scatter(norm_halves, grad_vpre, place, True)
    grad_qk = jnp.concatenate([grad_qpre, grad_kpre], axis=1)
    grad_wqk = weight_scatter(norm_halves, grad_qk, place, False)
    back_terms = (
        dot_t(grad_qpre, wq)
        + dot_t(grad_kpre, wk)
        + dot_t(grad_vpre, wv)
        + dot_t(grad_gate, wg)
    )
    back1, gain1_grad = norm_back(
        back_terms, gain1, gain1_part, normed1, part_of(normed1), inverse1
    )
    grad_x = grad_middle + back1
    gain1_total, gain2_total = lax.psum((gain1_grad, gain2_grad), "seq")
    return (
        output,
        grad_x,
        gain1_total,
        grad_wqk[:, : wq.shape[1]],
        grad_wqk[:, wq.shape[1] :],
        grad_wv,
        grad_wg,
        grad_wo.T,
        gain2_total,
        grad_w1,
        grad_w2.T,
    )


def solution(mesh):
    rows = P("seq", "head")
    return jax.shard_map(
        shards,
        mesh=mesh,
        in_specs=(
            rows,
            P(),
            P(None, "head"),
            P(None, "head"),
            P(None, "head"),
            P(None, "head"),
            P("head", None),
            P(),
            P(None, "head"),
            P("head", None),
            P(),
            rows,
        ),
        out_specs=(
            rows,
            rows,
            P("head"),
            rows,
            rows,
            rows,
            rows,
            P("head", "seq"),
            P("head"),
            rows,
            P("head", "seq"),
        ),
        check_vma=False,
    )
```

```python
import math

import jax
import jax.numpy as jnp
from jax import lax
from jax.experimental import pallas as pl
from jax.experimental.pallas import tpu as pltpu
from jax.sharding import PartitionSpec as P

KEY = 256
VAL = 512
SIDE = 4
CORES = 2
HEADS = 2
ROWS = 512
HALF = 256
PART = 512
MODEL = 2048
EXTRA = 16
EPSILON = 1e-05
F32 = jnp.float32
BF16 = jnp.bfloat16
VMEM_BYTES = 48 * 1024 * 1024
ORDER = (2, 1, 3, 0)


def head_shift(step):
    return [(h, (h + step) % SIDE) for h in range(SIDE)]


def seq_index(x, y, core):
    return (x * SIDE + y) * CORES + core


def seq_shift(dx, dy, swap=0):
    return [
        (seq_index(x, y, core), seq_index((x + dx) % SIDE, (y + dy) % SIDE, core ^ swap))
        for x in range(SIDE)
        for y in range(SIDE)
        for core in range(CORES)
    ]


SWAP = seq_shift(0, 0, 1)


def up(block):
    return lax.ppermute(block, "head", head_shift(1))


def down(block):
    return lax.ppermute(block, "head", head_shift(SIDE - 1))


def add_low(a, b):
    return (a.astype(F32) + b.astype(F32)).astype(BF16)


def ring_gather(a, b):
    r1, l1 = up(a), down(b)
    r2, l2 = up(b), down(a)
    r3, l3 = up(r1), down(l1)
    return [a, b, r1, r2, r3, l3, l2, l1]


def ring_scatter(p2a, p2b, p1a, p1b, pma, pmb):
    t1, t2 = up(p2a), down(p2b)
    rb, la = up(p1b), down(pma)
    ra, lb = up(add_low(p1a, t1)), down(add_low(pmb, t2))
    return [ra, rb, la, lb]


def whole(shape):
    return pl.BlockSpec(shape, lambda *_: (0,) * len(shape))


def call(name, body, grid, scalars, ins, outs, tokens=(), scratch=(), flops=0):
    arrays = [item[0] for item in ins]
    in_specs = [whole(i[0].shape) if len(i) == 1 else pl.BlockSpec(i[1], i[2]) for i in ins]
    out_specs = [whole(o[0]) if len(o) == 2 else pl.BlockSpec(o[2], o[3]) for o in outs]
    out_shape = [jax.ShapeDtypeStruct(o[0], o[1]) for o in outs]
    n_in, n_tok, n_sc = len(arrays), len(tokens), len(scalars)
    in_specs += [pl.BlockSpec(memory_space=pl.ANY)] * n_tok

    def run(*refs):
        body(*refs[: n_sc + n_in], *refs[n_sc + n_in + n_tok :])

    moved = sum(a.size * a.dtype.itemsize for a in arrays) + sum(
        math.prod(o[0]) * jnp.dtype(o[1]).itemsize for o in outs
    )
    return pl.pallas_call(
        run,
        name=name,
        grid_spec=pltpu.PrefetchScalarGridSpec(
            num_scalar_prefetch=n_sc,
            grid=grid,
            in_specs=in_specs,
            out_specs=out_specs,
            scratch_shapes=list(scratch),
        ),
        out_shape=out_shape,
        compiler_params=pltpu.CompilerParams(
            dimension_semantics=("arbitrary",) * len(grid), vmem_limit_bytes=VMEM_BYTES
        ),
        cost_estimate=pl.CostEstimate(flops=flops, bytes_accessed=moved, transcendentals=0),
    )(*scalars, *arrays, *tokens)


def dot(left, right):
    return jnp.dot(left, right, preferred_element_type=F32)


def dot_t(left, right):
    return lax.dot_general(left, right, (((1,), (1,)), ((), ())), preferred_element_type=F32)


def t_dot(left, right):
    return lax.dot_general(left, right, (((0,), (0,)), ((), ())), preferred_element_type=F32)


def rotate(rows, cosine, sine):
    half = rows.shape[-1] // 2
    first, second = rows[:, :half], rows[:, half:]
    return jnp.concatenate([first * cosine - second * sine, second * cosine + first * sine], axis=1)


def head_col(info, k):
    return pl.multiple_of(lax.rem(info[0] + SIDE - k, SIDE) * PART, PART)


CHUNK = 32


def norm_rows(info, load, gain, low, mean_ref, inv_ref, own=None):
    for half in range(2):

        def step(i, _):
            at = pl.multiple_of(i * CHUNK, CHUNK)
            out = pl.ds(pl.multiple_of(half * HALF + i * CHUNK, CHUNK), CHUNK)
            parts = [load(k, half, at) for k in range(SIDE)]
            if own is not None:
                own[out, :] = parts[0]
            mean = sum(jnp.sum(p, axis=1, keepdims=True) for p in parts) / MODEL
            parts = [p - mean for p in parts]
            var = sum(jnp.sum(p * p, axis=1, keepdims=True) for p in parts) / MODEL
            inv = lax.rsqrt(var + EPSILON)
            mean_ref[out, :] = mean
            inv_ref[out, :] = inv
            for k in range(SIDE):
                cols = pl.ds(head_col(info, k), PART)
                low[out, cols] = (parts[k] * inv * gain[:, cols]).astype(BF16)
            return 0

        lax.fori_loop(0, HALF // CHUNK, step, 0)


def norm1(info, parts, gain, cotangent):
    def body(info, *refs):
        x = refs[:8]
        gain, cot, low, mean, inv, cot_out = refs[8:]
        cot_out[...] = cot[...]
        norm_rows(
            info,
            lambda k, half, at: x[2 * k + half][pl.ds(at, CHUNK), :].astype(F32),
            gain,
            low,
            mean,
            inv,
        )

    return call(
        "norm1",
        body,
        (1,),
        [info],
        [(p,) for p in parts] + [(gain,), (cotangent,)],
        [
            ((ROWS, MODEL), BF16),
            ((ROWS, 1), F32),
            ((ROWS, 1), F32),
            ((ROWS, PART), BF16),
        ],
    )


def key_value(info, low, wk, wv, cosine, sine, departure):
    def body(info, low, wk, wv, cosine, sine, departure, key, value, own, give):
        head = pl.program_id(0)
        k = rotate(dot(low[...], wk[...]), cosine[...], sine[...]).astype(BF16)
        key[...] = k
        v = dot(low[...], wv[...]).astype(BF16)
        value[...] = v
        state = t_dot((k.astype(F32) * departure[0]).astype(BF16), v)

        @pl.when(head == info[1])
        def _():
            own[...] = state

        @pl.when(head != info[1])
        def _():
            give[...] = state.astype(BF16)

    by_head = lambda h, *_: (0, h)
    return call(
        "key_value",
        body,
        (HEADS,),
        [info],
        [
            (low,),
            (wk, (MODEL, KEY), by_head),
            (wv, (MODEL, VAL), by_head),
            (cosine,),
            (sine,),
            (departure, (1, ROWS, 1), lambda h, *_: (h, 0, 0)),
        ],
        [
            ((ROWS, HEADS * KEY), BF16, (ROWS, KEY), by_head),
            ((ROWS, HEADS * VAL), BF16, (ROWS, VAL), by_head),
            ((KEY, VAL), F32),
            ((KEY, VAL), BF16),
        ],
        flops=2 * ROWS * MODEL * 1536,
    )


def query_part(low, wq, key, value, decay, cosine, sine, tokens):
    def body(low, wq, key, value, decay, cosine, sine, query, weighted, within):
        q = rotate(dot(low[...], wq[...]), cosine[...], sine[...]).astype(BF16)
        query[...] = q
        w = (dot_t(q, key[...]) * decay[0]).astype(BF16)
        weighted[0] = w
        within[...] = dot(w, value[...])

    by_head = lambda h, *_: (0, h)
    cube = lambda h, *_: (h, 0, 0)
    return call(
        "query_part",
        body,
        (HEADS,),
        [],
        [
            (low,),
            (wq, (MODEL, KEY), by_head),
            (key, (ROWS, KEY), by_head),
            (value, (ROWS, VAL), by_head),
            (decay, (1, ROWS, ROWS), cube),
            (cosine,),
            (sine,),
        ],
        [
            ((ROWS, HEADS * KEY), BF16, (ROWS, KEY), by_head),
            ((HEADS, ROWS, ROWS), BF16, (1, ROWS, ROWS), cube),
            ((ROWS, HEADS * VAL), F32, (ROWS, VAL), by_head),
        ],
        tokens,
        flops=2 * ROWS * MODEL * 512 + 4 * ROWS * ROWS * 768,
    )


def matmul_cols(name, left, right, out_type, tokens=(), block=512):
    def body(left, right, out):
        out[...] = dot(left[...], right[...]).astype(out_type)

    depth, cols = right.shape
    by_col = lambda i, *_: (0, i)
    return call(
        name,
        body,
        (cols // block,),
        [],
        [(left,), (right, (depth, block), by_col)],
        [((left.shape[0], cols), out_type, (left.shape[0], block), by_col)],
        tokens,
        flops=2 * left.shape[0] * depth * cols,
    )[0]


def matmul_rows(name, left, right, out_type, tokens=(), block=256):
    def body(left, right, out):
        out[...] = dot_t(left[...], right[...]).astype(out_type)

    cols, depth = right.shape
    return call(
        name,
        body,
        (cols // block,),
        [],
        [(left,), (right, (block, depth), lambda i, *_: (i, 0))],
        [((left.shape[0], cols), out_type, (left.shape[0], block), lambda i, *_: (0, i))],
        tokens,
        flops=2 * left.shape[0] * depth * cols,
    )[0]


def block_outs(extra):
    tall = HALF + extra
    return [
        ((tall, PART), BF16),
        ((HALF, PART), BF16),
        ((tall, PART), BF16),
        ((HALF, PART), BF16),
        ((tall, PART), BF16),
        ((HALF, PART), BF16),
        ((ROWS, PART), F32),
    ]


def put_block(step, block, outs):
    for k in range(SIDE - 1):

        @pl.when(step == k)
        def _():
            outs[2 * k][:HALF, :] = block[:HALF].astype(BF16)
            outs[2 * k + 1][...] = block[HALF:].astype(BF16)

    @pl.when(step == SIDE - 1)
    def _():
        outs[6][...] = block


def pick(mine, sibling, info, head):
    return jnp.where(info[1] == head, mine[...], sibling[...])


def mix(info, within, gate, query, mine, sibling, arrival, wo):
    def body(info, within, gate, query, mine, sibling, arrival, wo, mixed, grouped, ginv, *outs):
        step = pl.program_id(0)

        @pl.when(step == 0)
        def _():
            for head in range(HEADS):
                cols = slice(head * VAL, (head + 1) * VAL)
                state = pick(mine, sibling, info, head)
                for half in range(2):
                    rows = slice(half * HALF, (half + 1) * HALF)
                    cross = dot(query[rows, head * KEY : (head + 1) * KEY], state)
                    kept = within[rows, cols] + arrival[head, rows] * cross
                    kept = kept - jnp.mean(kept, axis=1, keepdims=True)
                    inv = lax.rsqrt(jnp.mean(kept * kept, axis=1, keepdims=True) + float(KEY))
                    group = kept * inv
                    g = gate[rows, cols]
                    ginv[head, rows] = inv
                    grouped[rows, cols] = group.astype(BF16)
                    mixed[rows, cols] = (group * (g / (1.0 + jnp.exp(-g)))).astype(BF16)

        put_block(step, dot(mixed[...], wo[...]), outs)

    cols = HEADS * VAL
    return call(
        "mix",
        body,
        (SIDE,),
        [info],
        [
            (within,),
            (gate,),
            (query,),
            (mine,),
            (sibling,),
            (arrival,),
            (wo, (cols, PART), lambda i, info: (0, info[2 + i])),
        ],
        [((ROWS, cols), BF16), ((ROWS, cols), BF16), ((HEADS, ROWS, 1), F32)] + block_outs(0),
        flops=2 * ROWS * MODEL * cols,
    )


def sum_branch(p0, pieces):
    def body(p0, ra, rb, la, lb, a, b):
        a[...] = (p0[:HALF] + ra[...].astype(F32) + la[...].astype(F32)).astype(BF16)
        b[...] = (p0[HALF:] + rb[...].astype(F32) + lb[...].astype(F32)).astype(BF16)

    return call(
        "sum_branch",
        body,
        (1,),
        [],
        [(p0,)] + [(p,) for p in pieces],
        [((HALF, PART), BF16), ((HALF, PART), BF16)],
    )


def feed_up(info, x_parts, b_parts, gain, w1, grad_hidden, tokens):
    block = 256

    def body(info, *refs):
        x, b = refs[:8], refs[8:16]
        gain, w1, grad_hidden, ffn_in, mean, inv, own, hidden, grad_pre = refs[16:]

        @pl.when(pl.program_id(0) == 0)
        def _():
            def load(k, half, at):
                rows = pl.ds(at, CHUNK)
                return x[2 * k + half][rows, :].astype(F32) + b[2 * k + half][rows, :].astype(F32)

            norm_rows(info, load, gain, ffn_in, mean, inv, own)

        pre = dot(ffn_in[...], w1[...])
        cdf = 0.5 * (1.0 + lax.erf(pre * (2.0**-0.5)))
        hidden[...] = (pre * cdf).astype(BF16)
        pdf = jnp.exp(-0.5 * pre * pre) * ((2.0 * math.pi) ** -0.5)
        grad_pre[...] = ((cdf + pre * pdf) * grad_hidden[...].astype(F32)).astype(BF16)

    by_col = lambda i, *_: (0, i)
    cols = w1.shape[1]
    tall = ((ROWS, cols), BF16, (ROWS, block), by_col)
    return call(
        "feed_up",
        body,
        (cols // block,),
        [info],
        [(p,) for p in x_parts]
        + [(p,) for p in b_parts]
        + [
            (gain,),
            (w1, (MODEL, block), by_col),
            (grad_hidden, (ROWS, block), by_col),
        ],
        [
            ((ROWS, MODEL), BF16),
            ((ROWS, 1), F32),
            ((ROWS, 1), F32),
            ((ROWS, PART), F32),
            tall,
            tall,
        ],
        tokens,
        flops=2 * ROWS * MODEL * cols,
    )


def back_blocks(name, info, pairs, base, gain, low, tokens=()):
    n = len(pairs)

    def body(info, *refs):
        grads, weights = refs[:n], refs[n : 2 * n]
        rest = refs[2 * n :]
        if base is not None:
            base_ref, rest = rest[0], rest[1:]
        gain, low = rest[:2]
        outs, sums, acc = rest[2:9], rest[9], rest[10]
        step = pl.program_id(0)
        total = dot_t(grads[0][...], weights[0][...])
        for g, w in zip(grads[1:], weights[1:]):
            total = total + dot_t(g[...], w[...])
        if base is not None:
            total = total + base_ref[...]
        put_block(step, total, outs)
        first = jnp.sum(total * gain[...], axis=1, keepdims=True) / MODEL
        second = jnp.sum(total * low[...].astype(F32), axis=1, keepdims=True) / MODEL
        lane = lax.broadcasted_iota(jnp.int32, (ROWS, 128), 1)
        both = jnp.where(lane == 0, first, jnp.where(lane == 1, second, 0.0))

        @pl.when(step == 0)
        def _():
            acc[...] = both

        @pl.when(step > 0)
        def _():
            acc[...] = acc[...] + both

        @pl.when(step == SIDE - 1)
        def _():
            turned = acc[...].T[:EXTRA]
            sums[...] = turned
            for k in range(SIDE - 1):
                outs[2 * k][HALF:, :] = turned.astype(BF16)

    by_row = lambda i, info: (info[2 + i], 0)
    by_col = lambda i, info: (0, info[2 + i])
    return call(
        name,
        body,
        (SIDE,),
        [info],
        [(g,) for g, _ in pairs]
        + [(w, (PART, w.shape[1]), by_row) for _, w in pairs]
        + ([(base, (ROWS, PART), by_col)] if base is not None else [])
        + [(gain, (1, PART), by_col), (low, (ROWS, PART), by_col)],
        block_outs(EXTRA) + [((EXTRA, PART), F32)],
        tokens,
        [pltpu.VMEM((ROWS, 128), F32)],
        flops=sum(2 * ROWS * MODEL * w.shape[1] for _, w in pairs),
    )


def norm_back(name, p0, sums, pieces, gain_part, rows, mean, inv, residual, low_out, tokens):
    def body(p0, sums, ra, rb, la, lb, gain, rows, mean, inv, residual, grad, gain_grad, *low):
        total = sums[...] + ra[HALF:].astype(F32) + la[HALF:].astype(F32)
        total = jnp.concatenate([total, jnp.zeros((128 - EXTRA, PART), F32)], axis=0).T
        acc = jnp.zeros((1, PART), F32)
        for half, (one, two) in enumerate(((ra, la), (rb, lb))):
            for quarter in range(2):
                at = slice(quarter * 128, (quarter + 1) * 128)
                out = slice(half * HALF + quarter * 128, half * HALF + (quarter + 1) * 128)
                g = p0[out] + one[at].astype(F32) + two[at].astype(F32)
                normed = (rows[out].astype(F32) - mean[out]) * inv[out]
                acc = acc + jnp.sum(g * normed, axis=0, keepdims=True)
                back = inv[out] * (g * gain[...] - total[out, 0:1] - normed * total[out, 1:2])
                new = residual[out].astype(F32) + back
                grad[out] = new
                if low_out:
                    low[half][at] = new.astype(BF16)
        gain_grad[...] = acc

    outs = [((ROWS, PART), F32), ((1, PART), F32)]
    if low_out:
        outs += [((HALF, PART), BF16)] * 2
    return call(
        name,
        body,
        (1,),
        [],
        [(p0,), (sums,)]
        + [(p,) for p in pieces]
        + [(gain_part,), (rows,), (mean,), (inv,), (residual,)],
        outs,
        tokens,
    )


def back_mix(info, parts, wo, gate, grouped, ginv, query, arrival, tokens):
    def body(info, *refs):
        parts = refs[:8]
        wo, gate, grouped, ginv, query, arrival, branch, grad_gate, kept, own, give = refs[8:]
        head = pl.program_id(0)

        @pl.when(head == 0)
        def _():
            for k in range(SIDE):
                cols = pl.ds(head_col(info, k), PART)
                branch[:HALF, cols] = parts[2 * k][...]
                branch[HALF:, cols] = parts[2 * k + 1][...]

        for half in range(2):
            rows = slice(half * HALF, (half + 1) * HALF)
            m = dot_t(branch[rows], wo[...])
            g = gate[rows]
            sigmoid = 1.0 / (1.0 + jnp.exp(-g))
            group = grouped[rows].astype(F32)
            slope = sigmoid * (1.0 + g * (1.0 - sigmoid))
            grad_gate[rows] = (m * group * slope).astype(BF16)
            e = m * (g * sigmoid)
            e = ginv[0, rows] * (
                e
                - jnp.mean(e, axis=1, keepdims=True)
                - group * jnp.mean(e * group, axis=1, keepdims=True)
            )
            kept[rows] = e.astype(BF16)
        moved = (query[...].astype(F32) * arrival[0]).astype(BF16)
        state = t_dot(moved, kept[...])

        @pl.when(head == info[1])
        def _():
            own[...] = state

        @pl.when(head != info[1])
        def _():
            give[...] = state.astype(BF16)

    by_head = lambda h, *_: (0, h)
    cube = lambda h, *_: (h, 0, 0)
    cols = HEADS * VAL
    return call(
        "back_mix",
        body,
        (HEADS,),
        [info],
        [(p,) for p in parts]
        + [
            (wo, (VAL, MODEL), lambda h, *_: (h, 0)),
            (gate, (ROWS, VAL), by_head),
            (grouped, (ROWS, VAL), by_head),
            (ginv, (1, ROWS, 1), cube),
            (query, (ROWS, KEY), by_head),
            (arrival, (1, ROWS, 1), cube),
        ],
        [
            ((ROWS, MODEL), BF16),
            ((ROWS, cols), BF16, (ROWS, VAL), by_head),
            ((ROWS, cols), BF16, (ROWS, VAL), by_head),
            ((KEY, VAL), F32),
            ((KEY, VAL), BF16),
        ],
        tokens,
        flops=2 * ROWS * MODEL * cols,
    )


def retain_back(info, kept, value, decay, key, query, weighted, mine, sibling, arrival, cosine, sine, tokens):
    def body(
        info, kept, value, decay, key, query, weighted, mine, sibling, arrival, cosine, sine,
        grad_query, near_key, near_value,
    ):
        head = pl.program_id(0)
        e = kept[...]
        s = (dot_t(e, value[...]) * decay[0]).astype(BF16)
        state = pick(mine, sibling, info, head)
        gq = dot(s, key[...]) + arrival[0] * dot_t(e, state)
        grad_query[...] = rotate(gq, cosine[...], -sine[...]).astype(BF16)
        near_key[...] = t_dot(s, query[...])
        near_value[...] = t_dot(weighted[0], e)

    by_head = lambda h, *_: (0, h)
    cube = lambda h, *_: (h, 0, 0)
    keys, vals = HEADS * KEY, HEADS * VAL
    return call(
        "retain_back",
        body,
        (HEADS,),
        [info],
        [
            (kept, (ROWS, VAL), by_head),
            (value, (ROWS, VAL), by_head),
            (decay, (1, ROWS, ROWS), cube),
            (key, (ROWS, KEY), by_head),
            (query, (ROWS, KEY), by_head),
            (weighted, (1, ROWS, ROWS), cube),
            (mine,),
            (sibling,),
            (arrival, (1, ROWS, 1), cube),
            (cosine,),
            (sine,),
        ],
        [
            ((ROWS, keys), BF16, (ROWS, KEY), by_head),
            ((ROWS, keys), F32, (ROWS, KEY), by_head),
            ((ROWS, vals), F32, (ROWS, VAL), by_head),
        ],
        tokens,
        flops=2 * HEADS * ROWS * ROWS * 1800,
    )


def key_value_back(info, mine, sibling, key, value, departure, near_key, near_value, cosine, sine, tokens):
    def body(
        info, mine, sibling, key, value, departure, near_key, near_value, cosine, sine,
        grad_key, grad_value,
    ):
        state = pick(mine, sibling, info, pl.program_id(0))
        gk = near_key[...] + departure[0] * dot_t(value[...], state)
        grad_key[...] = rotate(gk, cosine[...], -sine[...]).astype(BF16)
        gv = near_value[...] + departure[0] * dot(key[...], state)
        grad_value[...] = gv.astype(BF16)

    by_head = lambda h, *_: (0, h)
    keys, vals = HEADS * KEY, HEADS * VAL
    return call(
        "key_value_back",
        body,
        (HEADS,),
        [info],
        [
            (mine,),
            (sibling,),
            (key, (ROWS, KEY), by_head),
            (value, (ROWS, VAL), by_head),
            (departure, (1, ROWS, 1), lambda h, *_: (h, 0, 0)),
            (near_key, (ROWS, KEY), by_head),
            (near_value, (ROWS, VAL), by_head),
            (cosine,),
            (sine,),
        ],
        [
            ((ROWS, keys), BF16, (ROWS, KEY), by_head),
            ((ROWS, vals), BF16, (ROWS, VAL), by_head),
        ],
        tokens,
        flops=2 * HEADS * ROWS * KEY * VAL * 2,
    )


def turn(name, info, low, x_first, tokens=()):
    def body(info, low, own, other, scratch):
        scratch[...] = low[...].T
        for y in range(SIDE):
            base = y * CORES * 64
            mine = scratch[pl.ds(pl.multiple_of(base + info[1] * 64, 64), 64), :]
            far = scratch[pl.ds(pl.multiple_of(base + (1 - info[1]) * 64, 64), 64), :]
            if x_first:
                own[0, y] = mine
                other[0, y] = far
            else:
                own[y, 0] = mine
                other[y, 0] = far

    if x_first:
        out = ((SIDE, SIDE, 64, ROWS), BF16, (1, SIDE, 64, ROWS), lambda i, *_: (i, 0, 0, 0))
    else:
        out = ((SIDE, SIDE, 64, ROWS), BF16, (SIDE, 1, 64, ROWS), lambda i, *_: (0, i, 0, 0))
    own, other = call(
        name,
        body,
        (SIDE,),
        [info],
        [(low, (ROWS, PART), lambda i, *_: (0, i))],
        [out, out],
        tokens,
        [pltpu.VMEM((PART, ROWS), BF16)],
    )
    return own.reshape(-1, ROWS), other.reshape(-1, ROWS)


def weight_other(name, left, rights, tokens=()):
    n = len(rights)
    width = sum(r.shape[1] for r in rights)

    def body(left, *refs):
        out, at = refs[n], 0
        for r in refs[:n]:
            out[:, at : at + r.shape[1]] = dot(left[...], r[...]).astype(BF16)
            at += r.shape[1]

    return call(
        name,
        body,
        (SIDE,),
        [],
        [(left, (HALF, ROWS), lambda i, *_: (i, 0))] + [(r,) for r in rights],
        [((SIDE * HALF, width), BF16, (HALF, width), lambda i, *_: (i, 0))],
        tokens,
        flops=2 * SIDE * HALF * ROWS * width,
    )[0]


def weight_own(name, info, where, left, rights, arrived, tokens=()):
    n = len(rights)
    width = sum(r.shape[1] for r in rights)

    def body(info, left, *refs):
        arrived, outs, at = refs[n], refs[n + 1 :], 0
        step = pl.program_id(0)
        for r in refs[:n]:
            cols = slice(at, at + r.shape[1])
            total = dot(left[...], r[...]) + arrived[:, cols].astype(F32)
            for k in range(SIDE):

                @pl.when(step == k)
                def _():
                    outs[k][:, cols] = total.astype(outs[k].dtype)

            at += r.shape[1]

    block = lambda i, info: (lax.rem(info[where] + ORDER_OF(i), SIDE), 0)
    return call(
        name,
        body,
        (SIDE,),
        [info],
        [(left, (HALF, ROWS), block)]
        + [(r,) for r in rights]
        + [(arrived, (HALF, width), block)],
        [((HALF, width), BF16)] * 3 + [((HALF, width), F32)],
        tokens,
        flops=2 * SIDE * HALF * ROWS * width,
    )


def ORDER_OF(i):
    return jnp.where(i == 0, 2, jnp.where(i == 1, 1, jnp.where(i == 2, 3, 0)))


def phase_sum(name, info, where, base, received, tokens=()):
    width = base.shape[1]

    def body(info, base, a, b, c, *refs):
        outs, scratch = refs[:SIDE], refs[SIDE]
        scratch[...] = base[...] + a[...].astype(F32) + b[...].astype(F32) + c[...].astype(F32)
        for i, k in enumerate(ORDER):
            at = pl.multiple_of(lax.rem(info[where] + k, SIDE) * 64, 64)
            outs[i][...] = scratch[pl.ds(at, 64), :].astype(outs[i].dtype)

    return call(
        name,
        body,
        (1,),
        [info],
        [(base,)] + [(r,) for r in received],
        [((64, width), BF16)] * 3 + [((64, width), F32)],
        tokens,
        [pltpu.VMEM((HALF, width), F32)],
    )


def shift_of(along_x):
    return (lambda k: seq_shift(k, 0)) if along_x else (lambda k: seq_shift(0, k))


def send_blocks(blocks, along_x):
    shift = shift_of(along_x)
    return [lax.ppermute(b, "seq", shift(k)) for b, k in zip(blocks, ORDER[:3])]


X_AT, Y_AT = 6, 7


def weight_rest(name, info, blocks, x_first, tokens=()):
    received = send_blocks(blocks[:3], x_first)
    subs = phase_sum(name, info, Y_AT if x_first else X_AT, blocks[3], received, tokens)
    received = send_blocks(subs[:3], not x_first)
    return subs[3] + sum(r.astype(F32) for r in received)


def scan_weights(decay, place, reverse):
    x, y, _ = place
    rel = jnp.arange(SIDE)
    origin = lax.rem(y - rel + SIDE, SIDE)
    target = lax.rem(y + rel, SIDE)
    hops = jnp.arange(1, SIDE)
    if reverse:
        row = origin
        before, counts = SIDE * (SIDE - hops - 1), x + (SIDE - hops) < SIDE
        gap = origin[None, :] - target[:, None]
        carry = SIDE - 1 - target
    else:
        row = SIDE - 1 - origin
        before, counts = SIDE * (hops - 1), x >= hops
        gap = target[:, None] - origin[None, :]
        carry = target
    gap = gap.reshape(-1)
    power = jnp.concatenate([row, before, jnp.maximum(gap - 1, 0), carry]).astype(F32)
    keep = jnp.concatenate([row >= 0, counts, gap > 0, carry >= 0]).astype(F32)
    values = keep * jnp.exp(2.0 * jnp.log(decay) * power)
    return jnp.concatenate([decay[None], values, jnp.zeros((4,), F32)])


W_ROW, W_BEFORE, W_ANSWER, W_CARRY = 1, 5, 8, 24
QUARTER = KEY // SIDE


def state_scan(info, weights, own, give, reverse, tag):
    far = 1 if reverse else 0

    def start_body(info, w, own, got, p2, p1, p3, p0, scratch):
        a, b = own[...], got[...].astype(F32)
        scratch[...] = jnp.where(info[1] == far, w[0] * a + b, a + w[0] * b).astype(BF16)
        for k, out in zip(ORDER, (p2, p1, p3, p0)):
            at = pl.multiple_of(lax.rem(info[Y_AT] + k, SIDE) * QUARTER, QUARTER)
            out[...] = scratch[pl.ds(at, QUARTER), :]

    piece = ((QUARTER, VAL), BF16)
    got = lax.ppermute(give, "seq", SWAP)
    sent = call(
        "scan_start" + tag, start_body, (1,), [info, weights], [(own,), (got,)], [piece] * 4,
        scratch=[pltpu.VMEM((KEY, VAL), BF16)],
    )
    at2, at1, at3 = send_blocks(sent[:3], False)
    pieces = [sent[3], at1, at2, at3]

    def row_body(w, p0, p1, p2, p3, total):
        total[...] = sum(
            w[W_ROW + j] * p[...].astype(F32) for j, p in enumerate((p0, p1, p2, p3))
        ).astype(BF16)

    row = call("scan_row" + tag, row_body, (1,), [weights], [(p,) for p in pieces], [piece])[0]
    at2, at1, at3 = send_blocks([row] * 3, True)

    def answer_body(w, p0, p1, p2, p3, b1, b2, b3, *outs):
        p = [r[...].astype(F32) for r in (p0, p1, p2, p3)]
        before = sum(w[W_BEFORE + j] * r[...].astype(F32) for j, r in enumerate((b1, b2, b3)))
        for k, out in zip(ORDER, outs):
            total = w[W_CARRY + k] * before
            for j in range(SIDE):
                total = total + w[W_ANSWER + SIDE * k + j] * p[j]
            out[...] = total.astype(BF16)

    answers = call(
        "scan_answer" + tag, answer_body, (1,), [weights],
        [(p,) for p in pieces] + [(at1,), (at2,), (at3,)], [piece] * 4,
    )
    at2, at1, at3 = send_blocks(answers[:3], False)

    def end_body(info, w, b0, b1, b2, b3, own, got, mine, theirs, scratch):
        for k, b in enumerate((b0, b1, b2, b3)):
            at = pl.multiple_of(lax.rem(info[Y_AT] + SIDE - k, SIDE) * QUARTER, QUARTER)
            scratch[pl.ds(at, QUARTER), :] = b[...].astype(F32)
        chip = scratch[...]
        is_far = info[1] == far
        later = w[0] * chip + jnp.where(is_far, own[...], got[...].astype(F32))
        mine[...] = jnp.where(is_far, chip, later).astype(BF16)
        theirs[...] = jnp.where(is_far, later, chip).astype(BF16)

    state = ((KEY, VAL), BF16)
    mine, theirs = call(
        "scan_end" + tag, end_body, (1,), [info, weights],
        [(answers[3],), (at1,), (at2,), (at3,), (own,), (got,)], [state, state],
        scratch=[pltpu.VMEM((KEY, VAL), F32)],
    )
    return mine, lax.ppermute(theirs, "seq", SWAP)


def sum_seq(values):
    values = values + lax.ppermute(values, "seq", SWAP)
    for along_x in (True, False):
        shift = shift_of(along_x)
        values = values + sum(lax.ppermute(values, "seq", shift(k)) for k in (1, 2, 3))
    return values


def shards(layer_in, gain1, wq, wk, wv, wg, wo, gain2, w1, w2, starts, cotangent):
    seq_rank = lax.axis_index("seq")
    head_rank = lax.axis_index("head")
    x, y, core = (
        seq_rank // (SIDE * CORES),
        (seq_rank // CORES) % SIDE,
        seq_rank % CORES,
    )
    place = (x, y, core)
    info = jnp.stack(
        [head_rank, core] + [(head_rank + k) % SIDE for k in ORDER] + [x, y]
    ).astype(jnp.int32)
    col_start = head_rank * PART
    gain1_part = lax.dynamic_slice_in_dim(gain1, col_start, PART)[None]
    gain2_part = lax.dynamic_slice_in_dim(gain2, col_start, PART)[None]
    gain1, gain2 = gain1[None], gain2[None]

    offsets = jnp.arange(ROWS, dtype=jnp.int32)
    positions = seq_rank * ROWS + offsets
    member = positions[:, None] >= starts[None, :]
    doc_ids = jnp.sum(member.astype(jnp.int32), axis=-1) - 1
    last_start = jnp.max(jnp.where(member, starts[None, :], 0), axis=-1)
    relative = (positions - last_start).astype(F32)
    prior_doc = jnp.sum((seq_rank * ROWS - 1 >= starts).astype(jnp.int32)) - 1
    half_dim = KEY // 2
    frequency = jnp.exp(-math.log(10000.0) * jnp.arange(half_dim, dtype=F32) / half_dim)
    angles = relative[:, None] * frequency[None, :]
    cosine, sine = jnp.cos(angles), jnp.sin(angles)
    head_ids = (head_rank * HEADS + jnp.arange(HEADS, dtype=jnp.int32)).astype(F32)
    log_decay = jnp.log1p(-jnp.exp2(-5.0 - head_ids))
    gap_grid = offsets[:, None] - offsets[None, :]
    keep = (gap_grid >= 0) & (doc_ids[:, None] == doc_ids[None, :])
    gap_float = jnp.where(gap_grid >= 0, gap_grid, 0).astype(F32)
    decay = jnp.where(keep[None], jnp.exp(gap_float[None] * log_decay[:, None, None]), 0.0)
    step_float = offsets.astype(F32)
    arrival = jnp.exp((step_float[None, :] + 1.0) * log_decay[:, None]) * (
        doc_ids == prior_doc
    ).astype(F32)
    departure = jnp.exp((ROWS - 1.0 - step_float)[None, :] * log_decay[:, None]) * (
        doc_ids == doc_ids[ROWS - 1]
    ).astype(F32)
    arrival, departure = arrival[:, :, None], departure[:, :, None]
    rank_decay = lax.dynamic_index_in_dim(jnp.exp(ROWS * log_decay), core, 0, False)
    ahead = scan_weights(rank_decay, place, False)
    behind = scan_weights(rank_decay, place, True)

    x_parts = ring_gather(layer_in[:HALF], layer_in[HALF:])
    low1, mean1, inv1, cot_again = norm1(info, x_parts, gain1, cotangent)
    cot_full = lax.all_gather(cot_again, "head", axis=1, tiled=True)
    key, value, own, give = key_value(info, low1, wk, wv, cosine, sine, departure)
    mine, sibling = state_scan(info, ahead, own, give, False, "_a")
    query, weighted, within = query_part(low1, wq, key, value, decay, cosine, sine, ())
    gate = matmul_cols("gate", low1, wg, F32, (key,))
    mixed, grouped, ginv, *blocks = mix(info, within, gate, query, mine, sibling, arrival, wo)
    pieces = ring_scatter(*blocks[:6])
    grad_hidden = matmul_rows("grad_hidden", cot_full, w2, BF16, (blocks[0],))
    cot_own, cot_other = turn("turn_cot", info, cot_full, True, (blocks[0],))
    b_parts = ring_gather(*sum_branch(blocks[6], pieces))
    low1_own, low1_other = turn("turn_low1", info, low1, True, (b_parts[0],))

    low2, mean2, inv2, middle, hidden, grad_pre = feed_up(
        info, x_parts, b_parts, gain2, w1, grad_hidden, (cot_own, low1_own)
    )
    *blocks, sums = back_blocks("back_feed", info, [(grad_pre, w1)], None, gain2, low2)
    pieces = ring_scatter(*blocks[:6])
    w2_other = weight_other("w2_other", cot_other, [hidden], (blocks[0],))
    low2_own, low2_other = turn("turn_low2", info, low2, False, (blocks[0],))
    w1_other = weight_other("w1_other", low2_other, [grad_pre])
    w2_got, w1_got = lax.ppermute(w2_other, "seq", SWAP), lax.ppermute(w1_other, "seq", SWAP)
    grad_middle, gain2_grad, half_a, half_b = norm_back(
        "norm_back2", blocks[6], sums, pieces, gain2_part, middle, mean2, inv2, cotangent, True,
        (w1_other, w2_other),
    )
    g_parts = ring_gather(half_a, half_b)
    w2_blocks = weight_own("w2_own", info, X_AT, cot_own, [hidden], w2_got, (half_a,))
    w1_blocks = weight_own("w1_own", info, Y_AT, low2_own, [grad_pre], w1_got, (half_a,))

    branch, grad_gate, kept, own, give = back_mix(
        info, g_parts, wo, gate, grouped, ginv, query, arrival, (w2_blocks[0], w1_blocks[0])
    )
    far_mine, far_sibling = state_scan(info, behind, own, give, True, "_b")
    grad_query, near_key, near_value = retain_back(
        info, kept, value, decay, key, query, weighted, mine, sibling, arrival, cosine, sine, ()
    )
    grad_w2 = weight_rest("w2_mid", info, w2_blocks, True)
    grad_w1 = weight_rest("w1_mid", info, w1_blocks, False)
    feed = matmul_cols("feed_down", hidden, w2, BF16, (kept,))
    feed = lax.psum_scatter(feed, "head", scatter_dimension=1, tiled=True)
    branch_own, branch_other = turn("turn_branch", info, branch, False, ())
    wo_other = weight_other("wo_other", branch_other, [mixed])
    wg_other = weight_other("wg_other", low1_other, [grad_gate, grad_query])
    wo_got, wg_got = lax.ppermute(wo_other, "seq", SWAP), lax.ppermute(wg_other, "seq", SWAP)
    grad_key, grad_value = key_value_back(
        info, far_mine, far_sibling, key, value, departure, near_key, near_value, cosine, sine,
        (wo_other, wg_other),
    )
    wv_other = weight_other("wv_other", low1_other, [grad_value])
    wk_other = weight_other("wk_other", low1_other, [grad_key])
    wv_got, wk_got = lax.ppermute(wv_other, "seq", SWAP), lax.ppermute(wk_other, "seq", SWAP)
    *blocks, sums = back_blocks(
        "back_proj", info,
        [(grad_query, wq), (grad_gate, wg), (grad_key, wk), (grad_value, wv)],
        None, gain1, low1, (wv_other, wk_other),
    )
    pieces = ring_scatter(*blocks[:6])
    wo_blocks = weight_own("wo_own", info, Y_AT, branch_own, [mixed], wo_got)
    wg_blocks = weight_own("wg_own", info, X_AT, low1_own, [grad_gate, grad_query], wg_got)
    wv_blocks = weight_own("wv_own", info, X_AT, low1_own, [grad_value], wv_got)
    wk_blocks = weight_own("wk_own", info, X_AT, low1_own, [grad_key], wk_got)
    grad_x, gain1_grad = norm_back(
        "norm_back1", blocks[6], sums, pieces, gain1_part, layer_in, mean1, inv1, grad_middle,
        False, (),
    )
    grad_wo = weight_rest("wo_mid", info, wo_blocks, False)
    grad_wgq = weight_rest("wg_mid", info, wg_blocks, True)
    grad_wv = weight_rest("wv_mid", info, wv_blocks, True)
    grad_wk = weight_rest("wk_mid", info, wk_blocks, True)
    gains = sum_seq(jnp.concatenate([gain1_grad, gain2_grad], axis=0))
    output = (middle + feed.astype(F32)).astype(BF16)
    return (
        output,
        grad_x,
        gains[0],
        grad_wgq[:, HEADS * VAL :],
        grad_wk,
        grad_wv,
        grad_wgq[:, : HEADS * VAL],
        grad_wo.T,
        gains[1],
        grad_w1,
        grad_w2.T,
    )


def solution(mesh):
    rows = P("seq", "head")
    cols = P(None, "head")
    tall = P("head", None)
    return jax.shard_map(
        shards,
        mesh=mesh,
        in_specs=(rows, P(), cols, cols, cols, cols, tall, P(), cols, tall, P(), rows),
        out_specs=(
            rows, rows, P("head"), rows, rows, rows, rows, P("head", "seq"), P("head"), rows,
            P("head", "seq"),
        ),
        check_vma=False,
    )
```

```python
import math

import jax
import jax.numpy as jnp
from jax import lax
from jax.experimental import pallas as pl
from jax.experimental.pallas import tpu as pltpu
from jax.sharding import PartitionSpec as P

KEY = 256
VAL = 512
SIDE = 4
CORES = 2
HEADS = 2
ROWS = 512
HALF = 256
PART = 512
MODEL = 2048
EXTRA = 16
EPSILON = 1e-05
F32 = jnp.float32
BF16 = jnp.bfloat16
VMEM_BYTES = 24 * 1024 * 1024
ORDER = (2, 1, 3, 0)


def head_shift(step):
    return [(h, (h + step) % SIDE) for h in range(SIDE)]


def seq_index(x, y, core):
    return (x * SIDE + y) * CORES + core


def seq_shift(dx, dy, swap=0):
    return [
        (seq_index(x, y, core), seq_index((x + dx) % SIDE, (y + dy) % SIDE, core ^ swap))
        for x in range(SIDE)
        for y in range(SIDE)
        for core in range(CORES)
    ]


SWAP = seq_shift(0, 0, 1)


def up(block):
    return lax.ppermute(block, "head", head_shift(1))


def down(block):
    return lax.ppermute(block, "head", head_shift(SIDE - 1))


def add_low(a, b):
    return (a.astype(F32) + b.astype(F32)).astype(BF16)


def late(value, tokens):
    def body(value, out):
        out[...] = value[...]

    return call("late", body, (1,), [], [(value,)], [(value.shape, value.dtype)], tokens)[0]


def ring_gather(a, b):
    r1, l1 = up(a), down(b)
    r2, l2 = up(b), down(a)
    r3, l3 = up(r1), down(l1)
    return [a, b, r1, r2, r3, l3, l2, l1]


def ring_scatter(p2a, p2b, p1a, p1b, pma, pmb):
    t1, t2 = up(p2a), down(p2b)
    rb, la = up(p1b), down(pma)
    s1, s2 = add_low(p1a, t1), add_low(pmb, t2)
    ra, lb = up(s1), down(s2)
    return [ra, rb, la, lb], (s1, s2)


def whole(shape):
    return pl.BlockSpec(shape, lambda *_: (0,) * len(shape))


def once(shape):
    return pl.BlockSpec(
        shape, lambda *_: (0,) * len(shape), pipeline_mode=pl.Buffered(buffer_count=1)
    )


COST_SCALE = 1.0
COSTS = {
    "norm1": 5,
    "key_value": 8,
    "query_part": 6,
    "gate": 4,
    "mix": 9,
    "grad_hidden": 5,
    "feed_up": 11,
    "back_feed": 7,
    "back_mix": 8,
    "retain_back": 6,
    "feed_down": 5,
    "key_value_back": 3,
    "back_proj": 12,
    "w2_other": 3,
    "wg_other": 4,
    "w2_own": 4,
    "w1_own": 4,
    "wo_own": 4,
    "wg_own": 6,
    "wv_own": 4,
    "norm_back1": 3,
    "norm_back2": 2,
}


def call(name, body, grid, scalars, ins, outs, tokens=(), scratch=()):
    arrays = [item[0] for item in ins]
    in_specs = [once(i[0].shape) if len(i) == 1 else pl.BlockSpec(i[1], i[2]) for i in ins]
    out_specs = [whole(o[0]) if len(o) == 2 else pl.BlockSpec(o[2], o[3]) for o in outs]
    out_shape = [jax.ShapeDtypeStruct(o[0], o[1]) for o in outs]
    n_in, n_tok, n_sc = len(arrays), len(tokens), len(scalars)
    in_specs += [pl.BlockSpec(memory_space=pl.ANY)] * n_tok

    def run(*refs):
        body(*refs[: n_sc + n_in], *refs[n_sc + n_in + n_tok :])

    return pl.pallas_call(
        run,
        name=name,
        grid_spec=pltpu.PrefetchScalarGridSpec(
            num_scalar_prefetch=n_sc,
            grid=grid,
            in_specs=in_specs,
            out_specs=out_specs,
            scratch_shapes=list(scratch),
        ),
        out_shape=out_shape,
        compiler_params=pltpu.CompilerParams(
            dimension_semantics=("arbitrary",) * len(grid), vmem_limit_bytes=VMEM_BYTES
        ),
        cost_estimate=pl.CostEstimate(
            flops=int(COSTS.get(name, 1.5) * COST_SCALE * 1.1e9),
            bytes_accessed=0,
            transcendentals=0,
        ),
    )(*scalars, *arrays, *tokens)


def dot(left, right):
    return jnp.dot(left, right, preferred_element_type=F32)


def dot_t(left, right):
    return lax.dot_general(left, right, (((1,), (1,)), ((), ())), preferred_element_type=F32)


def t_dot(left, right):
    return lax.dot_general(left, right, (((0,), (0,)), ((), ())), preferred_element_type=F32)


def rotate(rows, cosine, sine):
    half = rows.shape[-1] // 2
    first, second = rows[:, :half], rows[:, half:]
    return jnp.concatenate([first * cosine - second * sine, second * cosine + first * sine], axis=1)


def head_col(info, k):
    return pl.multiple_of(lax.rem(info[0] + SIDE - k, SIDE) * PART, PART)


CHUNK = 32


def norm_rows(info, load, gain, low, mean_ref, inv_ref, own=None):
    for half in range(2):

        def step(i, _):
            at = pl.multiple_of(i * CHUNK, CHUNK)
            out = pl.ds(pl.multiple_of(half * HALF + i * CHUNK, CHUNK), CHUNK)
            parts = [load(k, half, at) for k in range(SIDE)]
            if own is not None:
                own[out, :] = parts[0]
            mean = sum(jnp.sum(p, axis=1, keepdims=True) for p in parts) / MODEL
            parts = [p - mean for p in parts]
            var = sum(jnp.sum(p * p, axis=1, keepdims=True) for p in parts) / MODEL
            inv = lax.rsqrt(var + EPSILON)
            mean_ref[out, :] = mean
            inv_ref[out, :] = inv
            for k in range(SIDE):
                cols = pl.ds(head_col(info, k), PART)
                low[out, cols] = (parts[k] * inv * gain[:, cols]).astype(BF16)
            return 0

        lax.fori_loop(0, HALF // CHUNK, step, 0)


def norm1(info, parts, gain, cotangent):
    def body(info, *refs):
        x = refs[:8]
        gain, cot, low, mean, inv, cot_out = refs[8:]
        cot_out[...] = cot[...]
        norm_rows(
            info,
            lambda k, half, at: x[2 * k + half][pl.ds(at, CHUNK), :].astype(F32),
            gain,
            low,
            mean,
            inv,
        )

    return call(
        "norm1",
        body,
        (1,),
        [info],
        [(p,) for p in parts] + [(gain,), (cotangent,)],
        [
            ((ROWS, MODEL), BF16),
            ((ROWS, 1), F32),
            ((ROWS, 1), F32),
            ((ROWS, PART), BF16),
        ],
    )


def key_value(info, low, wk, wv, cosine, sine, departure):
    def body(info, low, wk, wv, cosine, sine, departure, key, value, own, give):
        head = pl.program_id(0)
        k = rotate(dot(low[...], wk[...]), cosine[...], sine[...]).astype(BF16)
        key[...] = k
        v = dot(low[...], wv[...]).astype(BF16)
        value[...] = v
        state = t_dot((k.astype(F32) * departure[0]).astype(BF16), v)

        @pl.when(head == info[1])
        def _():
            own[...] = state

        @pl.when(head != info[1])
        def _():
            give[...] = state.astype(BF16)

    by_head = lambda h, *_: (0, h)
    return call(
        "key_value",
        body,
        (HEADS,),
        [info],
        [
            (low,),
            (wk, (MODEL, KEY), by_head),
            (wv, (MODEL, VAL), by_head),
            (cosine,),
            (sine,),
            (departure, (1, ROWS, 1), lambda h, *_: (h, 0, 0)),
        ],
        [
            ((ROWS, HEADS * KEY), BF16, (ROWS, KEY), by_head),
            ((ROWS, HEADS * VAL), BF16, (ROWS, VAL), by_head),
            ((KEY, VAL), F32),
            ((KEY, VAL), BF16),
        ],
    )


def query_part(low, wq, key, value, decay, cosine, sine, tokens):
    def body(low, wq, key, value, decay, cosine, sine, query, weighted, within):
        q = rotate(dot(low[...], wq[...]), cosine[...], sine[...]).astype(BF16)
        query[...] = q
        w = (dot_t(q, key[...]) * decay[0]).astype(BF16)
        weighted[0] = w
        within[...] = dot(w, value[...])

    by_head = lambda h, *_: (0, h)
    cube = lambda h, *_: (h, 0, 0)
    return call(
        "query_part",
        body,
        (HEADS,),
        [],
        [
            (low,),
            (wq, (MODEL, KEY), by_head),
            (key, (ROWS, KEY), by_head),
            (value, (ROWS, VAL), by_head),
            (decay, (1, ROWS, ROWS), cube),
            (cosine,),
            (sine,),
        ],
        [
            ((ROWS, HEADS * KEY), BF16, (ROWS, KEY), by_head),
            ((HEADS, ROWS, ROWS), BF16, (1, ROWS, ROWS), cube),
            ((ROWS, HEADS * VAL), F32, (ROWS, VAL), by_head),
        ],
        tokens,
    )


def matmul_cols(name, left, right, out_type, tokens=(), block=512):
    def body(left, right, out):
        out[...] = dot(left[...], right[...]).astype(out_type)

    depth, cols = right.shape
    by_col = lambda i, *_: (0, i)
    return call(
        name,
        body,
        (cols // block,),
        [],
        [(left,), (right, (depth, block), by_col)],
        [((left.shape[0], cols), out_type, (left.shape[0], block), by_col)],
        tokens,
    )[0]


def matmul_rows(name, left, right, out_type, tokens=(), block=256):
    def body(left, right, out):
        out[...] = dot_t(left[...], right[...]).astype(out_type)

    cols, depth = right.shape
    return call(
        name,
        body,
        (cols // block,),
        [],
        [(left,), (right, (block, depth), lambda i, *_: (i, 0))],
        [((left.shape[0], cols), out_type, (left.shape[0], block), lambda i, *_: (0, i))],
        tokens,
    )[0]


def block_outs(extra):
    tall = HALF + extra
    return [
        ((tall, PART), BF16),
        ((HALF, PART), BF16),
        ((tall, PART), BF16),
        ((HALF, PART), BF16),
        ((tall, PART), BF16),
        ((HALF, PART), BF16),
        ((ROWS, PART), F32),
    ]


def put_block(step, block, outs):
    for k in range(SIDE - 1):

        @pl.when(step == k)
        def _():
            outs[2 * k][:HALF, :] = block[:HALF].astype(BF16)
            outs[2 * k + 1][...] = block[HALF:].astype(BF16)

    @pl.when(step == SIDE - 1)
    def _():
        outs[6][...] = block


def pick(mine, sibling, info, head):
    return jnp.where(info[1] == head, mine[...], sibling[...])


def mix(info, within, gate, query, mine, sibling, arrival, wo, tokens):
    def body(info, within, gate, query, mine, sibling, arrival, wo, mixed, grouped, ginv, *outs):
        step = pl.program_id(0)

        @pl.when(step == 0)
        def _():
            for head in range(HEADS):
                cols = slice(head * VAL, (head + 1) * VAL)
                state = pick(mine, sibling, info, head)
                for half in range(2):
                    rows = slice(half * HALF, (half + 1) * HALF)
                    cross = dot(query[rows, head * KEY : (head + 1) * KEY], state)
                    kept = within[rows, cols] + arrival[head, rows] * cross
                    kept = kept - jnp.mean(kept, axis=1, keepdims=True)
                    inv = lax.rsqrt(jnp.mean(kept * kept, axis=1, keepdims=True) + float(KEY))
                    group = kept * inv
                    g = gate[rows, cols]
                    ginv[head, rows] = inv
                    grouped[rows, cols] = group.astype(BF16)
                    mixed[rows, cols] = (group * (g / (1.0 + jnp.exp(-g)))).astype(BF16)

        put_block(step, dot(mixed[...], wo[...]), outs)

    cols = HEADS * VAL
    return call(
        "mix",
        body,
        (SIDE,),
        [info],
        [
            (within,),
            (gate,),
            (query,),
            (mine,),
            (sibling,),
            (arrival,),
            (wo, (cols, PART), lambda i, info: (0, info[2 + i])),
        ],
        [((ROWS, cols), BF16), ((ROWS, cols), BF16), ((HEADS, ROWS, 1), F32)] + block_outs(0),
        tokens,
    )


def sum_branch(p0, pieces, tokens):
    def body(p0, ra, rb, la, lb, a, b):
        a[...] = (p0[:HALF] + ra[...].astype(F32) + la[...].astype(F32)).astype(BF16)
        b[...] = (p0[HALF:] + rb[...].astype(F32) + lb[...].astype(F32)).astype(BF16)

    return call(
        "sum_branch",
        body,
        (1,),
        [],
        [(p0,)] + [(p,) for p in pieces],
        [((HALF, PART), BF16), ((HALF, PART), BF16)],
        tokens,
    )


def feed_up(info, x_parts, b_parts, gain, w1, grad_hidden, tokens):
    block = 256

    def body(info, *refs):
        x, b = refs[:8], refs[8:16]
        gain, w1, grad_hidden, ffn_in, mean, inv, own, hidden, grad_pre = refs[16:]

        @pl.when(pl.program_id(0) == 0)
        def _():
            def load(k, half, at):
                rows = pl.ds(at, CHUNK)
                return x[2 * k + half][rows, :].astype(F32) + b[2 * k + half][rows, :].astype(F32)

            norm_rows(info, load, gain, ffn_in, mean, inv, own)

        pre = dot(ffn_in[...], w1[...])
        cdf = 0.5 * (1.0 + lax.erf(pre * (2.0**-0.5)))
        hidden[...] = (pre * cdf).astype(BF16)
        pdf = jnp.exp(-0.5 * pre * pre) * ((2.0 * math.pi) ** -0.5)
        grad_pre[...] = ((cdf + pre * pdf) * grad_hidden[...].astype(F32)).astype(BF16)

    by_col = lambda i, *_: (0, i)
    cols = w1.shape[1]
    tall = ((ROWS, cols), BF16, (ROWS, block), by_col)
    return call(
        "feed_up",
        body,
        (cols // block,),
        [info],
        [(p,) for p in x_parts]
        + [(p,) for p in b_parts]
        + [
            (gain,),
            (w1, (MODEL, block), by_col),
            (grad_hidden, (ROWS, block), by_col),
        ],
        [
            ((ROWS, MODEL), BF16),
            ((ROWS, 1), F32),
            ((ROWS, 1), F32),
            ((ROWS, PART), F32),
            tall,
            tall,
        ],
        tokens,
    )


def back_blocks(name, info, pairs, base, gain, low, tokens=()):
    n = len(pairs)

    def body(info, *refs):
        grads, weights = refs[:n], refs[n : 2 * n]
        rest = refs[2 * n :]
        if base is not None:
            base_ref, rest = rest[0], rest[1:]
        gain, low = rest[:2]
        outs, sums, acc = rest[2:9], rest[9], rest[10]
        step = pl.program_id(0)
        total = dot_t(grads[0][...], weights[0][...])
        for g, w in zip(grads[1:], weights[1:]):
            total = total + dot_t(g[...], w[...])
        if base is not None:
            total = total + base_ref[...]
        put_block(step, total, outs)
        first = jnp.sum(total * gain[...], axis=1, keepdims=True) / MODEL
        second = jnp.sum(total * low[...].astype(F32), axis=1, keepdims=True) / MODEL
        lane = lax.broadcasted_iota(jnp.int32, (ROWS, 128), 1)
        both = jnp.where(lane == 0, first, jnp.where(lane == 1, second, 0.0))

        @pl.when(step == 0)
        def _():
            acc[...] = both

        @pl.when(step > 0)
        def _():
            acc[...] = acc[...] + both

        @pl.when(step == SIDE - 1)
        def _():
            turned = acc[...].T[:EXTRA]
            sums[...] = turned
            for k in range(SIDE - 1):
                outs[2 * k][HALF:, :] = turned.astype(BF16)

    by_row = lambda i, info: (info[2 + i], 0)
    by_col = lambda i, info: (0, info[2 + i])
    return call(
        name,
        body,
        (SIDE,),
        [info],
        [(g,) for g, _ in pairs]
        + [(w, (PART, w.shape[1]), by_row) for _, w in pairs]
        + ([(base, (ROWS, PART), by_col)] if base is not None else [])
        + [(gain, (1, PART), by_col), (low, (ROWS, PART), by_col)],
        block_outs(EXTRA) + [((EXTRA, PART), F32)],
        tokens,
        [pltpu.VMEM((ROWS, 128), F32)],
    )


def norm_back(name, p0, sums, pieces, gain_part, rows, mean, inv, residual, low_out, tokens):
    def body(p0, sums, ra, rb, la, lb, gain, rows, mean, inv, residual, grad, gain_grad, *low):
        total = sums[...] + ra[HALF:].astype(F32) + la[HALF:].astype(F32)
        total = jnp.concatenate([total, jnp.zeros((128 - EXTRA, PART), F32)], axis=0).T
        acc = jnp.zeros((1, PART), F32)
        for half, (one, two) in enumerate(((ra, la), (rb, lb))):
            for quarter in range(2):
                at = slice(quarter * 128, (quarter + 1) * 128)
                out = slice(half * HALF + quarter * 128, half * HALF + (quarter + 1) * 128)
                g = p0[out] + one[at].astype(F32) + two[at].astype(F32)
                normed = (rows[out].astype(F32) - mean[out]) * inv[out]
                acc = acc + jnp.sum(g * normed, axis=0, keepdims=True)
                back = inv[out] * (g * gain[...] - total[out, 0:1] - normed * total[out, 1:2])
                new = residual[out].astype(F32) + back
                grad[out] = new
                if low_out:
                    low[half][at] = new.astype(BF16)
        gain_grad[...] = acc

    outs = [((ROWS, PART), F32), ((1, PART), F32)]
    if low_out:
        outs += [((HALF, PART), BF16)] * 2
    return call(
        name,
        body,
        (1,),
        [],
        [(p0,), (sums,)]
        + [(p,) for p in pieces]
        + [(gain_part,), (rows,), (mean,), (inv,), (residual,)],
        outs,
        tokens,
    )


def back_mix(info, parts, wo, gate, grouped, ginv, query, arrival, tokens):
    def body(info, *refs):
        parts = refs[:8]
        wo, gate, grouped, ginv, query, arrival, branch, grad_gate, kept, own, give = refs[8:]
        head = pl.program_id(0)

        @pl.when(head == 0)
        def _():
            for k in range(SIDE):
                cols = pl.ds(head_col(info, k), PART)
                branch[:HALF, cols] = parts[2 * k][...]
                branch[HALF:, cols] = parts[2 * k + 1][...]

        for half in range(2):
            rows = slice(half * HALF, (half + 1) * HALF)
            m = dot_t(branch[rows], wo[...])
            g = gate[rows]
            sigmoid = 1.0 / (1.0 + jnp.exp(-g))
            group = grouped[rows].astype(F32)
            slope = sigmoid * (1.0 + g * (1.0 - sigmoid))
            grad_gate[rows] = (m * group * slope).astype(BF16)
            e = m * (g * sigmoid)
            e = ginv[0, rows] * (
                e
                - jnp.mean(e, axis=1, keepdims=True)
                - group * jnp.mean(e * group, axis=1, keepdims=True)
            )
            kept[rows] = e.astype(BF16)
        moved = (query[...].astype(F32) * arrival[0]).astype(BF16)
        state = t_dot(moved, kept[...])

        @pl.when(head == info[1])
        def _():
            own[...] = state

        @pl.when(head != info[1])
        def _():
            give[...] = state.astype(BF16)

    by_head = lambda h, *_: (0, h)
    cube = lambda h, *_: (h, 0, 0)
    cols = HEADS * VAL
    return call(
        "back_mix",
        body,
        (HEADS,),
        [info],
        [(p,) for p in parts]
        + [
            (wo, (VAL, MODEL), lambda h, *_: (h, 0)),
            (gate, (ROWS, VAL), by_head),
            (grouped, (ROWS, VAL), by_head),
            (ginv, (1, ROWS, 1), cube),
            (query, (ROWS, KEY), by_head),
            (arrival, (1, ROWS, 1), cube),
        ],
        [
            ((ROWS, MODEL), BF16),
            ((ROWS, cols), BF16, (ROWS, VAL), by_head),
            ((ROWS, cols), BF16, (ROWS, VAL), by_head),
            ((KEY, VAL), F32),
            ((KEY, VAL), BF16),
        ],
        tokens,
    )


def retain_back(info, kept, value, decay, key, query, weighted, mine, sibling, arrival, cosine, sine, tokens):
    def body(
        info, kept, value, decay, key, query, weighted, mine, sibling, arrival, cosine, sine,
        grad_query, near_key, near_value,
    ):
        head = pl.program_id(0)
        e = kept[...]
        s = (dot_t(e, value[...]) * decay[0]).astype(BF16)
        state = pick(mine, sibling, info, head)
        gq = dot(s, key[...]) + arrival[0] * dot_t(e, state)
        grad_query[...] = rotate(gq, cosine[...], -sine[...]).astype(BF16)
        near_key[...] = t_dot(s, query[...])
        near_value[...] = t_dot(weighted[0], e)

    by_head = lambda h, *_: (0, h)
    cube = lambda h, *_: (h, 0, 0)
    keys, vals = HEADS * KEY, HEADS * VAL
    return call(
        "retain_back",
        body,
        (HEADS,),
        [info],
        [
            (kept, (ROWS, VAL), by_head),
            (value, (ROWS, VAL), by_head),
            (decay, (1, ROWS, ROWS), cube),
            (key, (ROWS, KEY), by_head),
            (query, (ROWS, KEY), by_head),
            (weighted, (1, ROWS, ROWS), cube),
            (mine,),
            (sibling,),
            (arrival, (1, ROWS, 1), cube),
            (cosine,),
            (sine,),
        ],
        [
            ((ROWS, keys), BF16, (ROWS, KEY), by_head),
            ((ROWS, keys), F32, (ROWS, KEY), by_head),
            ((ROWS, vals), F32, (ROWS, VAL), by_head),
        ],
        tokens,
    )


def key_value_back(info, mine, sibling, key, value, departure, near_key, near_value, cosine, sine, tokens):
    def body(
        info, mine, sibling, key, value, departure, near_key, near_value, cosine, sine,
        grad_key, grad_value,
    ):
        state = pick(mine, sibling, info, pl.program_id(0))
        gk = near_key[...] + departure[0] * dot_t(value[...], state)
        grad_key[...] = rotate(gk, cosine[...], -sine[...]).astype(BF16)
        gv = near_value[...] + departure[0] * dot(key[...], state)
        grad_value[...] = gv.astype(BF16)

    by_head = lambda h, *_: (0, h)
    keys, vals = HEADS * KEY, HEADS * VAL
    return call(
        "key_value_back",
        body,
        (HEADS,),
        [info],
        [
            (mine,),
            (sibling,),
            (key, (ROWS, KEY), by_head),
            (value, (ROWS, VAL), by_head),
            (departure, (1, ROWS, 1), lambda h, *_: (h, 0, 0)),
            (near_key, (ROWS, KEY), by_head),
            (near_value, (ROWS, VAL), by_head),
            (cosine,),
            (sine,),
        ],
        [
            ((ROWS, keys), BF16, (ROWS, KEY), by_head),
            ((ROWS, vals), BF16, (ROWS, VAL), by_head),
        ],
        tokens,
    )


def turn(name, info, low, x_first, tokens=()):
    def body(info, low, own, other, scratch):
        scratch[...] = low[...].T
        for y in range(SIDE):
            base = y * CORES * 64
            mine = scratch[pl.ds(pl.multiple_of(base + info[1] * 64, 64), 64), :]
            far = scratch[pl.ds(pl.multiple_of(base + (1 - info[1]) * 64, 64), 64), :]
            if x_first:
                own[0, y] = mine
                other[0, y] = far
            else:
                own[y, 0] = mine
                other[y, 0] = far

    if x_first:
        out = ((SIDE, SIDE, 64, ROWS), BF16, (1, SIDE, 64, ROWS), lambda i, *_: (i, 0, 0, 0))
    else:
        out = ((SIDE, SIDE, 64, ROWS), BF16, (SIDE, 1, 64, ROWS), lambda i, *_: (0, i, 0, 0))
    own, other = call(
        name,
        body,
        (SIDE,),
        [info],
        [(low, (ROWS, PART), lambda i, *_: (0, i))],
        [out, out],
        tokens,
        [pltpu.VMEM((PART, ROWS), BF16)],
    )
    return own.reshape(-1, ROWS), other.reshape(-1, ROWS)


def weight_other(name, left, rights, tokens=()):
    n = len(rights)
    width = sum(r.shape[1] for r in rights)

    def body(left, *refs):
        out, at = refs[n], 0
        for r in refs[:n]:
            out[:, at : at + r.shape[1]] = dot(left[...], r[...]).astype(BF16)
            at += r.shape[1]

    return call(
        name,
        body,
        (SIDE,),
        [],
        [(left, (HALF, ROWS), lambda i, *_: (i, 0))] + [(r,) for r in rights],
        [((SIDE * HALF, width), BF16, (HALF, width), lambda i, *_: (i, 0))],
        tokens,
    )[0]


def weight_own(name, info, where, left, rights, arrived, tokens=()):
    n = len(rights)
    width = sum(r.shape[1] for r in rights)

    def body(info, left, *refs):
        arrived, outs, at = refs[n], refs[n + 1 :], 0
        step = pl.program_id(0)
        for r in refs[:n]:
            cols = slice(at, at + r.shape[1])
            total = dot(left[...], r[...]) + arrived[:, cols].astype(F32)
            for k in range(SIDE):

                @pl.when(step == k)
                def _():
                    outs[k][:, cols] = total.astype(outs[k].dtype)

            at += r.shape[1]

    block = lambda i, info: (lax.rem(info[where] + ORDER_OF(i), SIDE), 0)
    return call(
        name,
        body,
        (SIDE,),
        [info],
        [(left, (HALF, ROWS), block)]
        + [(r,) for r in rights]
        + [(arrived, (HALF, width), block)],
        [((HALF, width), BF16)] * 3 + [((HALF, width), F32)],
        tokens,
    )


def weight_whole(name, left, rights, arrived, tokens=()):
    n = len(rights)
    width = sum(r.shape[1] for r in rights)

    def body(left, *refs):
        arrived, out, at = refs[n], refs[n + 1], 0
        for r in refs[:n]:
            cols = slice(at, at + r.shape[1])
            out[:, cols] = (dot(left[...], r[...]) + arrived[:, cols].astype(F32)).astype(BF16)
            at += r.shape[1]

    block = lambda i, *_: (i, 0)
    return call(
        name,
        body,
        (SIDE,),
        [],
        [(left, (HALF, ROWS), block)]
        + [(r,) for r in rights]
        + [(arrived, (HALF, width), block)],
        [((SIDE * HALF, width), BF16, (HALF, width), block)],
        tokens,
    )[0]


def axis_groups(along_x):
    if along_x:
        return [
            [seq_index(x, y, c) for x in range(SIDE)] for y in range(SIDE) for c in range(CORES)
        ]
    return [[seq_index(x, y, c) for y in range(SIDE)] for x in range(SIDE) for c in range(CORES)]


def weight_scatter(total, x_first):
    steps = []
    for along_x in (x_first, not x_first):
        total = lax.psum_scatter(
            total,
            "seq",
            scatter_dimension=0,
            axis_index_groups=axis_groups(along_x),
            tiled=True,
        )
        steps.append(total)
    return total.astype(F32), steps[0]


def ORDER_OF(i):
    return jnp.where(i == 0, 2, jnp.where(i == 1, 1, jnp.where(i == 2, 3, 0)))


def phase_sum(name, info, where, base, received, tokens=()):
    width = base.shape[1]

    def body(info, base, a, b, c, *refs):
        outs, scratch = refs[:SIDE], refs[SIDE]
        scratch[...] = base[...] + a[...].astype(F32) + b[...].astype(F32) + c[...].astype(F32)
        for i, k in enumerate(ORDER):
            at = pl.multiple_of(lax.rem(info[where] + k, SIDE) * 64, 64)
            outs[i][...] = scratch[pl.ds(at, 64), :].astype(outs[i].dtype)

    return call(
        name,
        body,
        (1,),
        [info],
        [(base,)] + [(r,) for r in received],
        [((64, width), BF16)] * 3 + [((64, width), F32)],
        tokens,
        [pltpu.VMEM((HALF, width), F32)],
    )


def shift_of(along_x):
    return (lambda k: seq_shift(k, 0)) if along_x else (lambda k: seq_shift(0, k))


def send_blocks(blocks, along_x):
    shift = shift_of(along_x)
    return [lax.ppermute(b, "seq", shift(k)) for b, k in zip(blocks, ORDER[:3])]


X_AT, Y_AT = 6, 7


def weight_rest(name, info, blocks, x_first, tokens=()):
    received = send_blocks(blocks[:3], x_first)
    subs = phase_sum(name, info, Y_AT if x_first else X_AT, blocks[3], received, tokens)
    received = send_blocks(subs[:3], not x_first)
    return subs[3] + sum(r.astype(F32) for r in received)


def scan_weights(decay, place, reverse):
    x, y, _ = place
    rel = jnp.arange(SIDE)
    origin = lax.rem(y - rel + SIDE, SIDE)
    target = lax.rem(y + rel, SIDE)
    hops = jnp.arange(1, SIDE)
    if reverse:
        row = origin
        before, counts = SIDE * (SIDE - hops - 1), x + (SIDE - hops) < SIDE
        gap = origin[None, :] - target[:, None]
        carry = SIDE - 1 - target
    else:
        row = SIDE - 1 - origin
        before, counts = SIDE * (hops - 1), x >= hops
        gap = target[:, None] - origin[None, :]
        carry = target
    gap = gap.reshape(-1)
    power = jnp.concatenate([row, before, jnp.maximum(gap - 1, 0), carry]).astype(F32)
    keep = jnp.concatenate([row >= 0, counts, gap > 0, carry >= 0]).astype(F32)
    values = keep * jnp.exp(2.0 * jnp.log(decay) * power)
    return jnp.concatenate([decay[None], values, jnp.zeros((4,), F32)])


W_ROW, W_BEFORE, W_ANSWER, W_CARRY = 1, 5, 8, 24
QUARTER = KEY // SIDE


def state_scan(info, weights, own, give, reverse, tag, fills):
    far = 1 if reverse else 0

    def start_body(info, w, own, got, p2, p1, p3, p0, scratch):
        a, b = own[...], got[...].astype(F32)
        scratch[...] = jnp.where(info[1] == far, w[0] * a + b, a + w[0] * b).astype(BF16)
        for k, out in zip(ORDER, (p2, p1, p3, p0)):
            at = pl.multiple_of(lax.rem(info[Y_AT] + k, SIDE) * QUARTER, QUARTER)
            out[...] = scratch[pl.ds(at, QUARTER), :]

    piece = ((QUARTER, VAL), BF16)
    got = lax.ppermute(give, "seq", SWAP)
    sent = call(
        "scan_start" + tag, start_body, (1,), [info, weights], [(own,), (got,)], [piece] * 4,
        fills[0](), scratch=[pltpu.VMEM((KEY, VAL), BF16)],
    )
    at2, at1, at3 = send_blocks(sent[:3], False)
    pieces = [sent[3], at1, at2, at3]

    def row_body(w, p0, p1, p2, p3, total):
        total[...] = sum(
            w[W_ROW + j] * p[...].astype(F32) for j, p in enumerate((p0, p1, p2, p3))
        ).astype(BF16)

    row = call(
        "scan_row" + tag, row_body, (1,), [weights], [(p,) for p in pieces], [piece],
        fills[1](sent[0]),
    )[0]
    at2, at1, at3 = send_blocks([row] * 3, True)

    def answer_body(w, p0, p1, p2, p3, b1, b2, b3, *outs):
        p = [r[...].astype(F32) for r in (p0, p1, p2, p3)]
        before = sum(w[W_BEFORE + j] * r[...].astype(F32) for j, r in enumerate((b1, b2, b3)))
        for k, out in zip(ORDER, outs):
            total = w[W_CARRY + k] * before
            for j in range(SIDE):
                total = total + w[W_ANSWER + SIDE * k + j] * p[j]
            out[...] = total.astype(BF16)

    answers = call(
        "scan_answer" + tag, answer_body, (1,), [weights],
        [(p,) for p in pieces] + [(at1,), (at2,), (at3,)], [piece] * 4, fills[2](row),
    )
    at2, at1, at3 = send_blocks(answers[:3], False)

    def end_body(info, w, b0, b1, b2, b3, own, got, mine, theirs, scratch):
        for k, b in enumerate((b0, b1, b2, b3)):
            at = pl.multiple_of(lax.rem(info[Y_AT] + SIDE - k, SIDE) * QUARTER, QUARTER)
            scratch[pl.ds(at, QUARTER), :] = b[...].astype(F32)
        chip = scratch[...]
        is_far = info[1] == far
        later = w[0] * chip + jnp.where(is_far, own[...], got[...].astype(F32))
        mine[...] = jnp.where(is_far, chip, later).astype(BF16)
        theirs[...] = jnp.where(is_far, later, chip).astype(BF16)

    state = ((KEY, VAL), BF16)
    mine, theirs = call(
        "scan_end" + tag, end_body, (1,), [info, weights],
        [(answers[3],), (at1,), (at2,), (at3,), (own,), (got,)], [state, state],
        fills[3](answers[0]), scratch=[pltpu.VMEM((KEY, VAL), F32)],
    )
    return mine, lax.ppermute(theirs, "seq", SWAP)


def sum_seq(values):
    values = values + lax.ppermute(values, "seq", SWAP)
    for along_x in (True, False):
        shift = shift_of(along_x)
        values = values + sum(lax.ppermute(values, "seq", shift(k)) for k in (1, 2, 3))
    return values


def shards(layer_in, gain1, wq, wk, wv, wg, wo, gain2, w1, w2, starts, cotangent):
    seq_rank = lax.axis_index("seq")
    head_rank = lax.axis_index("head")
    x, y, core = (
        seq_rank // (SIDE * CORES),
        (seq_rank // CORES) % SIDE,
        seq_rank % CORES,
    )
    place = (x, y, core)
    info = jnp.stack(
        [head_rank, core] + [(head_rank + k) % SIDE for k in ORDER] + [x, y]
    ).astype(jnp.int32)
    col_start = head_rank * PART
    gain1_part = lax.dynamic_slice_in_dim(gain1, col_start, PART)[None]
    gain2_part = lax.dynamic_slice_in_dim(gain2, col_start, PART)[None]
    gain1, gain2 = gain1[None], gain2[None]

    x_parts = ring_gather(layer_in[:HALF], layer_in[HALF:])
    starts = late(starts[None], (x_parts[2], x_parts[7]))[0]
    offsets = jnp.arange(ROWS, dtype=jnp.int32)
    positions = seq_rank * ROWS + offsets
    member = positions[:, None] >= starts[None, :]
    doc_ids = jnp.sum(member.astype(jnp.int32), axis=-1) - 1
    last_start = jnp.max(jnp.where(member, starts[None, :], 0), axis=-1)
    relative = (positions - last_start).astype(F32)
    prior_doc = jnp.sum((seq_rank * ROWS - 1 >= starts).astype(jnp.int32)) - 1
    half_dim = KEY // 2
    frequency = jnp.exp(-math.log(10000.0) * jnp.arange(half_dim, dtype=F32) / half_dim)
    angles = relative[:, None] * frequency[None, :]
    cosine, sine = jnp.cos(angles), jnp.sin(angles)
    head_ids = (head_rank * HEADS + jnp.arange(HEADS, dtype=jnp.int32)).astype(F32)
    log_decay = jnp.log1p(-jnp.exp2(-5.0 - head_ids))
    gap_grid = offsets[:, None] - offsets[None, :]
    keep = (gap_grid >= 0) & (doc_ids[:, None] == doc_ids[None, :])
    gap_float = jnp.where(gap_grid >= 0, gap_grid, 0).astype(F32)
    decay = jnp.where(keep[None], jnp.exp(gap_float[None] * log_decay[:, None, None]), 0.0)
    step_float = offsets.astype(F32)
    arrival = jnp.exp((step_float[None, :] + 1.0) * log_decay[:, None]) * (
        doc_ids == prior_doc
    ).astype(F32)
    departure = jnp.exp((ROWS - 1.0 - step_float)[None, :] * log_decay[:, None]) * (
        doc_ids == doc_ids[ROWS - 1]
    ).astype(F32)
    arrival, departure = arrival[:, :, None], departure[:, :, None]
    rank_decay = lax.dynamic_index_in_dim(jnp.exp(ROWS * log_decay), core, 0, False)
    ahead = scan_weights(rank_decay, place, False)
    behind = scan_weights(rank_decay, place, True)

    low1, mean1, inv1, cot_again = norm1(info, x_parts, gain1, cotangent)
    cot_full = lax.all_gather(cot_again, "head", axis=1, tiled=True)
    key, value, own, give = key_value(info, low1, wk, wv, cosine, sine, departure)
    made = {}

    def fill_query():
        made["q"] = query_part(low1, wq, key, value, decay, cosine, sine, (give,))
        return (made["q"][0],)

    def fill_gate(token):
        made["gate"] = matmul_cols("gate", low1, wg, F32, (token,))
        return (made["gate"],)

    def fill_turn(token):
        made["low1_t"] = turn("turn_low1", info, low1, True, (token,))
        return (made["low1_t"][0],)

    mine, sibling = state_scan(
        info, ahead, own, give, False, "_a", (fill_query, fill_gate, fill_turn, lambda token: ())
    )
    query, weighted, within = made["q"]
    gate = made["gate"]
    low1_own, low1_other = made["low1_t"]
    mixed, grouped, ginv, *blocks = mix(
        info, within, gate, query, mine, sibling, arrival, wo, (cot_full,)
    )
    pieces, sent = ring_scatter(*blocks[:6])
    cot_own, cot_other = turn("turn_cot", info, cot_full, True, sent)
    grad_hidden = matmul_rows("grad_hidden", cot_full, w2, BF16, (*sent, cot_own))
    b_parts = ring_gather(*sum_branch(blocks[6], pieces, (grad_hidden,)))

    low2, mean2, inv2, middle, hidden, grad_pre = feed_up(
        info, x_parts, b_parts, gain2, w1, grad_hidden, (cot_own,)
    )
    *blocks, sums = back_blocks("back_feed", info, [(grad_pre, w1)], None, gain2, low2)
    pieces, sent = ring_scatter(*blocks[:6])
    w2_other = weight_other("w2_other", cot_other, [hidden], sent)
    low2_own, low2_other = turn("turn_low2", info, low2, False, (*sent, w2_other))
    w1_other = weight_other("w1_other", low2_other, [grad_pre])
    w2_got, w1_got = lax.ppermute(w2_other, "seq", SWAP), lax.ppermute(w1_other, "seq", SWAP)
    grad_middle, gain2_grad, half_a, half_b = norm_back(
        "norm_back2", blocks[6], sums, pieces, gain2_part, middle, mean2, inv2, cotangent, True,
        (w1_other, w2_other),
    )
    g_parts = ring_gather(half_a, half_b)
    sent = (g_parts[2], g_parts[7])
    w2_total = weight_whole("w2_own", cot_own, [hidden], w2_got, sent)
    w1_total = weight_whole("w1_own", low2_own, [grad_pre], w1_got, (*sent, w2_total))
    grad_w2, w2_step = weight_scatter(w2_total, True)
    grad_w1, w1_step = weight_scatter(w1_total, False)

    branch, grad_gate, kept, own, give = back_mix(
        info, g_parts, wo, gate, grouped, ginv, query, arrival, (w2_total, w1_total)
    )

    def fill_feed(token):
        made["feed"] = matmul_cols("feed_down", hidden, w2, BF16, (token,))
        return (made["feed"],)

    def fill_retain(token):
        made["r"] = retain_back(
            info, kept, value, decay, key, query, weighted, mine, sibling, arrival, cosine, sine,
            (token,),
        )
        return (made["r"][0],)

    def fill_wo(token):
        made["branch_t"] = turn("turn_branch", info, branch, False, (token,))
        made["wo"] = weight_other("wo_other", made["branch_t"][1], [mixed])
        return (made["wo"],)

    far_mine, far_sibling = state_scan(
        info, behind, own, give, True, "_b", (lambda: (), fill_feed, fill_retain, fill_wo)
    )
    wg_other = weight_other("wg_other", low1_other, [grad_gate, made["r"][0]], (far_mine,))
    branch_own, _ = made["branch_t"]
    grad_query, near_key, near_value = made["r"]
    feed = lax.psum_scatter(made["feed"], "head", scatter_dimension=1, tiled=True)
    wo_got, wg_got = lax.ppermute(made["wo"], "seq", SWAP), lax.ppermute(wg_other, "seq", SWAP)
    grad_key, grad_value = key_value_back(
        info, far_mine, far_sibling, key, value, departure, near_key, near_value, cosine, sine,
        (wg_other,),
    )
    wv_other = weight_other("wv_other", low1_other, [grad_value])
    wk_other = weight_other("wk_other", low1_other, [grad_key])
    wv_got, wk_got = lax.ppermute(wv_other, "seq", SWAP), lax.ppermute(wk_other, "seq", SWAP)
    *blocks, sums = back_blocks(
        "back_proj", info,
        [(grad_query, wq), (grad_gate, wg), (grad_key, wk), (grad_value, wv)],
        None, gain1, low1, (wv_other, wk_other, feed),
    )
    pieces, sent = ring_scatter(*blocks[:6])
    wo_total = weight_whole("wo_own", branch_own, [mixed], wo_got, sent)
    wg_total = weight_whole(
        "wg_own", low1_own, [grad_gate, grad_query], wg_got, (*sent, wo_total)
    )
    wv_blocks = weight_own(
        "wv_own", info, X_AT, low1_own, [grad_value], wv_got, (*sent, wg_total)
    )
    wk_blocks = weight_own(
        "wk_own", info, X_AT, low1_own, [grad_key], wk_got, (*sent, wv_blocks[0])
    )
    grad_x, gain1_grad = norm_back(
        "norm_back1", blocks[6], sums, pieces, gain1_part, layer_in, mean1, inv1, grad_middle,
        False, (wo_total, wg_total, wv_blocks[0], wk_blocks[0]),
    )
    grad_wo, wo_step = weight_scatter(wo_total, False)
    grad_wgq, wgq_step = weight_scatter(wg_total, True)
    grad_wv = weight_rest("wv_mid", info, wv_blocks, True)
    grad_wk = weight_rest("wk_mid", info, wk_blocks, True)
    gains = sum_seq(jnp.concatenate([gain1_grad, gain2_grad], axis=0))
    output = (middle + feed.astype(F32)).astype(BF16)
    return (
        output,
        grad_x,
        gains[0],
        grad_wgq[:, HEADS * VAL :],
        grad_wk,
        grad_wv,
        grad_wgq[:, : HEADS * VAL],
        grad_wo.T,
        gains[1],
        grad_w1,
        grad_w2.T,
    )


def solution(mesh):
    rows = P("seq", "head")
    cols = P(None, "head")
    tall = P("head", None)
    return jax.shard_map(
        shards,
        mesh=mesh,
        in_specs=(rows, P(), cols, cols, cols, cols, tall, P(), cols, tall, P(), rows),
        out_specs=(
            rows, rows, P("head"), rows, rows, rows, rows, P("head", "seq"), P("head"), rows,
            P("head", "seq"),
        ),
        check_vma=False,
    )
```

```python
import math

import jax
import jax.numpy as jnp
from jax import lax
from jax.experimental import pallas as pl
from jax.experimental.pallas import tpu as pltpu
from jax.sharding import PartitionSpec as P

KEY = 256
VAL = 512
SIDE = 4
CORES = 2
HEADS = 2
ROWS = 512
HALF = 256
PART = 512
MODEL = 2048
EXTRA = 16
EPSILON = 1e-05
F32 = jnp.float32
BF16 = jnp.bfloat16
VMEM_BYTES = 32 * 1024 * 1024
ORDER = (2, 1, 3, 0)


def head_shift(step):
    return [(h, (h + step) % SIDE) for h in range(SIDE)]


def seq_index(x, y, core):
    return (x * SIDE + y) * CORES + core


def seq_shift(dx, dy, swap=0):
    return [
        (seq_index(x, y, core), seq_index((x + dx) % SIDE, (y + dy) % SIDE, core ^ swap))
        for x in range(SIDE)
        for y in range(SIDE)
        for core in range(CORES)
    ]


SWAP = seq_shift(0, 0, 1)


def up(block):
    return lax.ppermute(block, "head", head_shift(1))


def down(block):
    return lax.ppermute(block, "head", head_shift(SIDE - 1))


def add_low(a, b):
    return (a.astype(F32) + b.astype(F32)).astype(BF16)


def ring_gather(a, b):
    r1, l1 = up(a), down(b)
    r2, l2 = up(b), down(a)
    r3, l3 = up(r1), down(l1)
    return [a, b, r1, r2, r3, l3, l2, l1]


def spread(block):
    copies = jnp.broadcast_to(block[None], (SIDE, *block.shape))
    return lax.all_to_all(copies, "head", 0, 0, tiled=True)


def ring_scatter(p2a, p2b, p1a, p1b, pma, pmb):
    t1, t2 = up(p2a), down(p2b)
    rb, la = up(p1b), down(pma)
    s1, s2 = add_low(p1a, t1), add_low(pmb, t2)
    ra, lb = up(s1), down(s2)
    return [ra, rb, la, lb], (s1, s2)


def whole(shape):
    return pl.BlockSpec(shape, lambda *_: (0,) * len(shape))


def once(shape):
    return pl.BlockSpec(
        shape, lambda *_: (0,) * len(shape), pipeline_mode=pl.Buffered(buffer_count=1)
    )


LARGE = 300 * 1024


def is_large(array):
    return math.prod(array.shape) * array.dtype.itemsize > LARGE


def in_hbm(array):
    return pltpu.with_memory_space_constraint(array, pltpu.HBM)


COST_SCALE = 1.0
COSTS = {
    "norm1": 5,
    "key_value": 8,
    "query_part": 6,
    "gate": 4,
    "mix": 9,
    "grad_hidden": 5,
    "feed_up": 11,
    "back_feed": 7,
    "back_mix": 2.40,
    "retain_back": 1.80,
    "feed_down": 1.50,
    "key_value_back": 0.90,
    "back_proj": 3.60,
    "feed_other": 5,
    "feed_own": 8,
    "mix_other": 1.80,
    "mix_own": 2.70,
    "kv_other": 0.90,
    "kv_own": 1.50,
    "feed_sum": 2,
    "mix_sum": 2,
    "kv_sum": 2,
    "norm_back1": 0.90,
    "norm_back2": 2,
}


def call(name, body, grid, scalars, ins, outs, tokens=(), scratch=()):
    arrays = [in_hbm(item[0]) if is_large(item[0]) else item[0] for item in ins]
    in_specs = [once(i[0].shape) if len(i) == 1 else pl.BlockSpec(i[1], i[2]) for i in ins]
    out_specs = [whole(o[0]) if len(o) == 2 else pl.BlockSpec(o[2], o[3]) for o in outs]
    out_shape = [jax.ShapeDtypeStruct(o[0], o[1]) for o in outs]
    out_shape = [pltpu.HBM(o.shape, o.dtype) if is_large(o) else o for o in out_shape]
    n_in, n_tok, n_sc = len(arrays), len(tokens), len(scalars)
    tokens = [in_hbm(t) if is_large(t) else t for t in tokens]
    in_specs += [pl.BlockSpec(memory_space=pl.ANY)] * n_tok

    def run(*refs):
        body(*refs[: n_sc + n_in], *refs[n_sc + n_in + n_tok :])

    return pl.pallas_call(
        run,
        name=name,
        grid_spec=pltpu.PrefetchScalarGridSpec(
            num_scalar_prefetch=n_sc,
            grid=grid,
            in_specs=in_specs,
            out_specs=out_specs,
            scratch_shapes=list(scratch),
        ),
        out_shape=out_shape,
        compiler_params=pltpu.CompilerParams(
            dimension_semantics=("arbitrary",) * len(grid), vmem_limit_bytes=VMEM_BYTES
        ),
        cost_estimate=pl.CostEstimate(
            flops=int(COSTS.get(name, 1.5) * COST_SCALE * 1.1e9),
            bytes_accessed=0,
            transcendentals=0,
        ),
    )(*scalars, *arrays, *tokens)


def dot(left, right):
    return jnp.dot(left, right, preferred_element_type=F32)


def dot_t(left, right):
    return lax.dot_general(left, right, (((1,), (1,)), ((), ())), preferred_element_type=F32)


def t_dot(left, right):
    return lax.dot_general(left, right, (((0,), (0,)), ((), ())), preferred_element_type=F32)


def rotate(rows, cosine, sine):
    half = rows.shape[-1] // 2
    first, second = rows[:, :half], rows[:, half:]
    return jnp.concatenate([first * cosine - second * sine, second * cosine + first * sine], axis=1)


def head_col(info, k):
    return pl.multiple_of(lax.rem(info[0] + SIDE - k, SIDE) * PART, PART)


CHUNK = 32


def norm_rows(info, load, gain, low, mean_ref, inv_ref, own=None):
    for half in range(2):

        def step(i, _):
            at = pl.multiple_of(i * CHUNK, CHUNK)
            out = pl.ds(pl.multiple_of(half * HALF + i * CHUNK, CHUNK), CHUNK)
            parts = [load(k, half, at) for k in range(SIDE)]
            if own is not None:
                own[out, :] = parts[0]
            mean = sum(jnp.sum(p, axis=1, keepdims=True) for p in parts) / MODEL
            parts = [p - mean for p in parts]
            var = sum(jnp.sum(p * p, axis=1, keepdims=True) for p in parts) / MODEL
            inv = lax.rsqrt(var + EPSILON)
            mean_ref[out, :] = mean
            inv_ref[out, :] = inv
            for k in range(SIDE):
                cols = pl.ds(head_col(info, k), PART)
                low[out, cols] = (parts[k] * inv * gain[:, cols]).astype(BF16)
            return 0

        lax.fori_loop(0, HALF // CHUNK, step, 0)


def of_head(info, x, k, half, at):
    rows = pl.ds(pl.multiple_of(half * HALF + at, CHUNK), CHUNK)
    return x[lax.rem(info[0] + SIDE - k, SIDE), rows, :].astype(F32)


def norm1(info, parts, gain, cotangent):
    def body(info, x, gain, cot, low, mean, inv, cot_out):
        cot_out[...] = cot[...]
        norm_rows(
            info,
            lambda k, half, at: of_head(info, x, k, half, at),
            gain,
            low,
            mean,
            inv,
        )

    return call(
        "norm1",
        body,
        (1,),
        [info],
        [(parts,), (gain,), (cotangent,)],
        [
            ((ROWS, MODEL), BF16),
            ((ROWS, 1), F32),
            ((ROWS, 1), F32),
            ((ROWS, PART), BF16),
        ],
    )


def key_value(info, low, wk, wv, cosine, sine, departure):
    def body(info, low, wk, wv, cosine, sine, departure, key, value, own, give):
        head = pl.program_id(0)
        k = rotate(dot(low[...], wk[...]), cosine[...], sine[...]).astype(BF16)
        key[...] = k
        v = dot(low[...], wv[...]).astype(BF16)
        value[...] = v
        state = t_dot((k.astype(F32) * departure[0]).astype(BF16), v)

        @pl.when(head == info[1])
        def _():
            own[...] = state

        @pl.when(head != info[1])
        def _():
            give[...] = state.astype(BF16)

    by_head = lambda h, *_: (0, h)
    return call(
        "key_value",
        body,
        (HEADS,),
        [info],
        [
            (low,),
            (wk, (MODEL, KEY), by_head),
            (wv, (MODEL, VAL), by_head),
            (cosine,),
            (sine,),
            (departure, (1, ROWS, 1), lambda h, *_: (h, 0, 0)),
        ],
        [
            ((ROWS, HEADS * KEY), BF16, (ROWS, KEY), by_head),
            ((ROWS, HEADS * VAL), BF16, (ROWS, VAL), by_head),
            ((KEY, VAL), F32),
            ((KEY, VAL), BF16),
        ],
    )


def query_part(low, wq, key, value, decay, cosine, sine, tokens):
    def body(low, wq, key, value, decay, cosine, sine, query, weighted, within):
        q = rotate(dot(low[...], wq[...]), cosine[...], sine[...]).astype(BF16)
        query[...] = q
        w = (dot_t(q, key[...]) * decay[0]).astype(BF16)
        weighted[0] = w
        within[...] = dot(w, value[...])

    by_head = lambda h, *_: (0, h)
    cube = lambda h, *_: (h, 0, 0)
    return call(
        "query_part",
        body,
        (HEADS,),
        [],
        [
            (low,),
            (wq, (MODEL, KEY), by_head),
            (key, (ROWS, KEY), by_head),
            (value, (ROWS, VAL), by_head),
            (decay, (1, ROWS, ROWS), cube),
            (cosine,),
            (sine,),
        ],
        [
            ((ROWS, HEADS * KEY), BF16, (ROWS, KEY), by_head),
            ((HEADS, ROWS, ROWS), BF16, (1, ROWS, ROWS), cube),
            ((ROWS, HEADS * VAL), F32, (ROWS, VAL), by_head),
        ],
        tokens,
    )


def matmul_cols(name, left, right, out_type, tokens=(), block=512):
    def body(left, right, out):
        out[...] = dot(left[...], right[...]).astype(out_type)

    depth, cols = right.shape
    by_col = lambda i, *_: (0, i)
    return call(
        name,
        body,
        (cols // block,),
        [],
        [(left,), (right, (depth, block), by_col)],
        [((left.shape[0], cols), out_type, (left.shape[0], block), by_col)],
        tokens,
    )[0]


def matmul_rows(name, left, right, out_type, tokens=(), block=256):
    def body(left, right, out):
        out[...] = dot_t(left[...], right[...]).astype(out_type)

    cols, depth = right.shape
    return call(
        name,
        body,
        (cols // block,),
        [],
        [(left,), (right, (block, depth), lambda i, *_: (i, 0))],
        [((left.shape[0], cols), out_type, (left.shape[0], block), lambda i, *_: (0, i))],
        tokens,
    )[0]


def block_outs(extra):
    tall = HALF + extra
    return [
        ((tall, PART), BF16),
        ((HALF, PART), BF16),
        ((tall, PART), BF16),
        ((HALF, PART), BF16),
        ((tall, PART), BF16),
        ((HALF, PART), BF16),
        ((ROWS, PART), F32),
    ]


def put_block(step, block, outs):
    for k in range(SIDE - 1):

        @pl.when(step == k)
        def _():
            outs[2 * k][:HALF, :] = block[:HALF].astype(BF16)
            outs[2 * k + 1][...] = block[HALF:].astype(BF16)

    @pl.when(step == SIDE - 1)
    def _():
        outs[6][...] = block


def pick(mine, sibling, info, head):
    return jnp.where(info[1] == head, mine[...], sibling[...])


def mix(info, within, gate, query, mine, sibling, arrival, wo, tokens):
    def body(info, within, gate, query, mine, sibling, arrival, wo, mixed, grouped, ginv, *outs):
        step = pl.program_id(0)

        @pl.when(step == 0)
        def _():
            for head in range(HEADS):
                cols = slice(head * VAL, (head + 1) * VAL)
                state = pick(mine, sibling, info, head)
                for half in range(2):
                    rows = slice(half * HALF, (half + 1) * HALF)
                    cross = dot(query[rows, head * KEY : (head + 1) * KEY], state)
                    kept = within[rows, cols] + arrival[head, rows] * cross
                    kept = kept - jnp.mean(kept, axis=1, keepdims=True)
                    inv = lax.rsqrt(jnp.mean(kept * kept, axis=1, keepdims=True) + float(KEY))
                    group = kept * inv
                    g = gate[rows, cols]
                    ginv[head, rows] = inv
                    grouped[rows, cols] = group.astype(BF16)
                    mixed[rows, cols] = (group * (g / (1.0 + jnp.exp(-g)))).astype(BF16)

        put_block(step, dot(mixed[...], wo[...]), outs)

    cols = HEADS * VAL
    return call(
        "mix",
        body,
        (SIDE,),
        [info],
        [
            (within,),
            (gate,),
            (query,),
            (mine,),
            (sibling,),
            (arrival,),
            (wo, (cols, PART), lambda i, info: (0, info[2 + i])),
        ],
        [((ROWS, cols), BF16), ((ROWS, cols), BF16), ((HEADS, ROWS, 1), F32)] + block_outs(0),
        tokens,
    )


def sum_branch(p0, pieces, tokens):
    def body(p0, ra, rb, la, lb, a, b):
        a[...] = (p0[:HALF] + ra[...].astype(F32) + la[...].astype(F32)).astype(BF16)
        b[...] = (p0[HALF:] + rb[...].astype(F32) + lb[...].astype(F32)).astype(BF16)

    return call(
        "sum_branch",
        body,
        (1,),
        [],
        [(p0,)] + [(p,) for p in pieces],
        [((HALF, PART), BF16), ((HALF, PART), BF16)],
        tokens,
    )


def feed_up(info, x_parts, b_parts, gain, w1, grad_hidden, tokens):
    block = 256

    def body(info, *refs):
        x, b = refs[0], refs[1:9]
        gain, w1, grad_hidden, ffn_in, mean, inv, own, hidden, grad_pre = refs[9:]

        @pl.when(pl.program_id(0) == 0)
        def _():
            def load(k, half, at):
                branch = b[2 * k + half][pl.ds(at, CHUNK), :].astype(F32)
                return of_head(info, x, k, half, at) + branch

            norm_rows(info, load, gain, ffn_in, mean, inv, own)

        pre = dot(ffn_in[...], w1[...])
        cdf = 0.5 * (1.0 + lax.erf(pre * (2.0**-0.5)))
        hidden[...] = (pre * cdf).astype(BF16)
        pdf = jnp.exp(-0.5 * pre * pre) * ((2.0 * math.pi) ** -0.5)
        grad_pre[...] = ((cdf + pre * pdf) * grad_hidden[...].astype(F32)).astype(BF16)

    by_col = lambda i, *_: (0, i)
    cols = w1.shape[1]
    tall = ((ROWS, cols), BF16, (ROWS, block), by_col)
    return call(
        "feed_up",
        body,
        (cols // block,),
        [info],
        [(x_parts,)]
        + [(p,) for p in b_parts]
        + [
            (gain,),
            (w1, (MODEL, block), by_col),
            (grad_hidden, (ROWS, block), by_col),
        ],
        [
            ((ROWS, MODEL), BF16),
            ((ROWS, 1), F32),
            ((ROWS, 1), F32),
            ((ROWS, PART), F32),
            tall,
            tall,
        ],
        tokens,
    )


def back_blocks(name, info, pairs, base, gain, low, tokens=()):
    n = len(pairs)

    def body(info, *refs):
        grads, weights = refs[:n], refs[n : 2 * n]
        rest = refs[2 * n :]
        if base is not None:
            base_ref, rest = rest[0], rest[1:]
        gain, low = rest[:2]
        outs, sums, acc = rest[2:9], rest[9], rest[10]
        step = pl.program_id(0)
        total = dot_t(grads[0][...], weights[0][...])
        for g, w in zip(grads[1:], weights[1:]):
            total = total + dot_t(g[...], w[...])
        if base is not None:
            total = total + base_ref[...]
        put_block(step, total, outs)
        first = jnp.sum(total * gain[...], axis=1, keepdims=True) / MODEL
        second = jnp.sum(total * low[...].astype(F32), axis=1, keepdims=True) / MODEL
        lane = lax.broadcasted_iota(jnp.int32, (ROWS, 128), 1)
        both = jnp.where(lane == 0, first, jnp.where(lane == 1, second, 0.0))

        @pl.when(step == 0)
        def _():
            acc[...] = both

        @pl.when(step > 0)
        def _():
            acc[...] = acc[...] + both

        @pl.when(step == SIDE - 1)
        def _():
            turned = acc[...].T[:EXTRA]
            sums[...] = turned
            for k in range(SIDE - 1):
                outs[2 * k][HALF:, :] = turned.astype(BF16)

    by_row = lambda i, info: (info[2 + i], 0)
    by_col = lambda i, info: (0, info[2 + i])
    return call(
        name,
        body,
        (SIDE,),
        [info],
        [(g,) for g, _ in pairs]
        + [(w, (PART, w.shape[1]), by_row) for _, w in pairs]
        + ([(base, (ROWS, PART), by_col)] if base is not None else [])
        + [(gain, (1, PART), by_col), (low, (ROWS, PART), by_col)],
        block_outs(EXTRA) + [((EXTRA, PART), F32)],
        tokens,
        [pltpu.VMEM((ROWS, 128), F32)],
    )


def norm_back(name, p0, sums, pieces, gain_part, rows, mean, inv, residual, low_out, tokens):
    def body(p0, sums, ra, rb, la, lb, gain, rows, mean, inv, residual, grad, gain_grad, *low):
        total = sums[...] + ra[HALF:].astype(F32) + la[HALF:].astype(F32)
        total = jnp.concatenate([total, jnp.zeros((128 - EXTRA, PART), F32)], axis=0).T
        acc = jnp.zeros((1, PART), F32)
        for half, (one, two) in enumerate(((ra, la), (rb, lb))):
            for quarter in range(2):
                at = slice(quarter * 128, (quarter + 1) * 128)
                out = slice(half * HALF + quarter * 128, half * HALF + (quarter + 1) * 128)
                g = p0[out] + one[at].astype(F32) + two[at].astype(F32)
                normed = (rows[out].astype(F32) - mean[out]) * inv[out]
                acc = acc + jnp.sum(g * normed, axis=0, keepdims=True)
                back = inv[out] * (g * gain[...] - total[out, 0:1] - normed * total[out, 1:2])
                new = residual[out].astype(F32) + back
                grad[out] = new
                if low_out:
                    low[half][at] = new.astype(BF16)
        gain_grad[...] = acc

    outs = [((ROWS, PART), F32), ((1, PART), F32)]
    if low_out:
        outs += [((HALF, PART), BF16)] * 2
    return call(
        name,
        body,
        (1,),
        [],
        [(p0,), (sums,)]
        + [(p,) for p in pieces]
        + [(gain_part,), (rows,), (mean,), (inv,), (residual,)],
        outs,
        tokens,
    )


def back_mix(info, parts, wo, gate, grouped, ginv, query, arrival, tokens):
    def body(info, *refs):
        parts = refs[:8]
        wo, gate, grouped, ginv, query, arrival, branch, grad_gate, kept, own, give = refs[8:]
        head = pl.program_id(0)

        @pl.when(head == 0)
        def _():
            for k in range(SIDE):
                cols = pl.ds(head_col(info, k), PART)
                branch[:HALF, cols] = parts[2 * k][...]
                branch[HALF:, cols] = parts[2 * k + 1][...]

        for half in range(2):
            rows = slice(half * HALF, (half + 1) * HALF)
            m = dot_t(branch[rows], wo[...])
            g = gate[rows]
            sigmoid = 1.0 / (1.0 + jnp.exp(-g))
            group = grouped[rows].astype(F32)
            slope = sigmoid * (1.0 + g * (1.0 - sigmoid))
            grad_gate[rows] = (m * group * slope).astype(BF16)
            e = m * (g * sigmoid)
            e = ginv[0, rows] * (
                e
                - jnp.mean(e, axis=1, keepdims=True)
                - group * jnp.mean(e * group, axis=1, keepdims=True)
            )
            kept[rows] = e.astype(BF16)
        moved = (query[...].astype(F32) * arrival[0]).astype(BF16)
        state = t_dot(moved, kept[...])

        @pl.when(head == info[1])
        def _():
            own[...] = state

        @pl.when(head != info[1])
        def _():
            give[...] = state.astype(BF16)

    by_head = lambda h, *_: (0, h)
    cube = lambda h, *_: (h, 0, 0)
    cols = HEADS * VAL
    return call(
        "back_mix",
        body,
        (HEADS,),
        [info],
        [(p,) for p in parts]
        + [
            (wo, (VAL, MODEL), lambda h, *_: (h, 0)),
            (gate, (ROWS, VAL), by_head),
            (grouped, (ROWS, VAL), by_head),
            (ginv, (1, ROWS, 1), cube),
            (query, (ROWS, KEY), by_head),
            (arrival, (1, ROWS, 1), cube),
        ],
        [
            ((ROWS, MODEL), BF16),
            ((ROWS, cols), BF16, (ROWS, VAL), by_head),
            ((ROWS, cols), BF16, (ROWS, VAL), by_head),
            ((KEY, VAL), F32),
            ((KEY, VAL), BF16),
        ],
        tokens,
    )


def retain_back(info, kept, value, decay, key, query, weighted, mine, sibling, arrival, cosine, sine, tokens):
    def body(
        info, kept, value, decay, key, query, weighted, mine, sibling, arrival, cosine, sine,
        grad_query, near_key, near_value,
    ):
        head = pl.program_id(0)
        e = kept[...]
        s = (dot_t(e, value[...]) * decay[0]).astype(BF16)
        state = pick(mine, sibling, info, head)
        gq = dot(s, key[...]) + arrival[0] * dot_t(e, state)
        grad_query[...] = rotate(gq, cosine[...], -sine[...]).astype(BF16)
        near_key[...] = t_dot(s, query[...])
        near_value[...] = t_dot(weighted[0], e)

    by_head = lambda h, *_: (0, h)
    cube = lambda h, *_: (h, 0, 0)
    keys, vals = HEADS * KEY, HEADS * VAL
    return call(
        "retain_back",
        body,
        (HEADS,),
        [info],
        [
            (kept, (ROWS, VAL), by_head),
            (value, (ROWS, VAL), by_head),
            (decay, (1, ROWS, ROWS), cube),
            (key, (ROWS, KEY), by_head),
            (query, (ROWS, KEY), by_head),
            (weighted, (1, ROWS, ROWS), cube),
            (mine,),
            (sibling,),
            (arrival, (1, ROWS, 1), cube),
            (cosine,),
            (sine,),
        ],
        [
            ((ROWS, keys), BF16, (ROWS, KEY), by_head),
            ((ROWS, keys), F32, (ROWS, KEY), by_head),
            ((ROWS, vals), F32, (ROWS, VAL), by_head),
        ],
        tokens,
    )


def key_value_back(info, mine, sibling, key, value, departure, near_key, near_value, cosine, sine, tokens):
    def body(
        info, mine, sibling, key, value, departure, near_key, near_value, cosine, sine,
        grad_key, grad_value,
    ):
        state = pick(mine, sibling, info, pl.program_id(0))
        gk = near_key[...] + departure[0] * dot_t(value[...], state)
        grad_key[...] = rotate(gk, cosine[...], -sine[...]).astype(BF16)
        gv = near_value[...] + departure[0] * dot(key[...], state)
        grad_value[...] = gv.astype(BF16)

    by_head = lambda h, *_: (0, h)
    keys, vals = HEADS * KEY, HEADS * VAL
    return call(
        "key_value_back",
        body,
        (HEADS,),
        [info],
        [
            (mine,),
            (sibling,),
            (key, (ROWS, KEY), by_head),
            (value, (ROWS, VAL), by_head),
            (departure, (1, ROWS, 1), lambda h, *_: (h, 0, 0)),
            (near_key, (ROWS, KEY), by_head),
            (near_value, (ROWS, VAL), by_head),
            (cosine,),
            (sine,),
        ],
        [
            ((ROWS, keys), BF16, (ROWS, KEY), by_head),
            ((ROWS, vals), BF16, (ROWS, VAL), by_head),
        ],
        tokens,
    )


def turn(name, info, low, x_first, tokens=()):
    def body(info, low, own, other, scratch):
        scratch[...] = low[...].T
        for y in range(SIDE):
            base = y * CORES * 64
            mine = scratch[pl.ds(pl.multiple_of(base + info[1] * 64, 64), 64), :]
            far = scratch[pl.ds(pl.multiple_of(base + (1 - info[1]) * 64, 64), 64), :]
            if x_first:
                own[0, y] = mine
                other[0, y] = far
            else:
                own[y, 0] = mine
                other[y, 0] = far

    if x_first:
        out = ((SIDE, SIDE, 64, ROWS), BF16, (1, SIDE, 64, ROWS), lambda i, *_: (i, 0, 0, 0))
    else:
        out = ((SIDE, SIDE, 64, ROWS), BF16, (SIDE, 1, 64, ROWS), lambda i, *_: (0, i, 0, 0))
    own, other = call(
        name,
        body,
        (SIDE,),
        [info],
        [(low, (ROWS, PART), lambda i, *_: (0, i))],
        [out, out],
        tokens,
        [pltpu.VMEM((PART, ROWS), BF16)],
    )
    return own.reshape(-1, ROWS), other.reshape(-1, ROWS)


def widths(groups):
    return [sum(r.shape[1] for r in rights) for _, rights in groups]


def weight_half(name, groups, arrived=None, tokens=()):
    n_left = len(groups)
    rights = [r for _, rs in groups for r in rs]
    counts = [len(rs) for _, rs in groups]
    n = len(rights)
    width = sum(widths(groups))

    def body(*refs):
        lefts, rest = refs[:n_left], refs[n_left : n_left + n]
        out = refs[-1]
        at = 0
        which = 0
        for left, count in zip(lefts, counts):
            for r in rest[which : which + count]:
                cols = slice(at, at + r.shape[1])
                total = dot(left[...], r[...])
                if arrived is not None:
                    total = total + refs[n_left + n][:, cols].astype(F32)
                out[:, cols] = total.astype(BF16)
                at += r.shape[1]
            which += count

    block = lambda i, *_: (i, 0)
    return call(
        name,
        body,
        (SIDE,),
        [],
        [(left, (HALF, ROWS), block) for left, _ in groups]
        + [(r,) for r in rights]
        + ([(arrived, (HALF, width), block)] if arrived is not None else []),
        [((SIDE * HALF, width), BF16, (HALF, width), block)],
        tokens,
    )[0]


PLANE = [
    [seq_index(x, y, c) for x in range(SIDE) for y in range(SIDE)] for c in range(CORES)
]


def weight_exchange(total):
    blocks = total.reshape(SIDE * SIDE, 64, -1)
    return lax.all_to_all(blocks, "seq", 0, 0, axis_index_groups=PLANE, tiled=True)


def axis_groups(along_x):
    if along_x:
        return [
            [seq_index(x, y, c) for x in range(SIDE)] for y in range(SIDE) for c in range(CORES)
        ]
    return [[seq_index(x, y, c) for y in range(SIDE)] for x in range(SIDE) for c in range(CORES)]


def weight_scatter(total):
    for along_x in (True, False):
        total = lax.psum_scatter(
            total,
            "seq",
            scatter_dimension=0,
            axis_index_groups=axis_groups(along_x),
            tiled=True,
        )
    return total.astype(F32)


def weight_sum(name, blocks, parts, tokens=()):
    step = 512
    cols = sum(w for w, _ in parts)
    firsts = [sum(w for w, _ in parts[:i]) // step for i in range(len(parts))]

    def body(blocks, *outs):
        i = pl.program_id(0)
        total = blocks[0].astype(F32)
        for k in range(1, SIDE * SIDE):
            total = total + blocks[k].astype(F32)
        for (width, turned), first, out in zip(parts, firsts, outs):

            @pl.when((i >= first) & (i < first + width // step))
            def _():
                out[...] = total.T if turned else total

    def place(first, count, turned):
        def at(i, *_):
            j = jnp.clip(i - first, 0, count - 1)
            return (j, 0) if turned else (0, j)

        return at

    outs = []
    for (width, turned), first in zip(parts, firsts):
        at = place(first, width // step, turned)
        if turned:
            outs.append(((width, 64), F32, (step, 64), at))
        else:
            outs.append(((64, width), F32, (64, step), at))
    return call(
        name,
        body,
        (cols // step,),
        [],
        [(blocks, (SIDE * SIDE, 64, step), lambda i, *_: (0, 0, i))],
        outs,
        tokens,
    )


def shift_of(along_x):
    return (lambda k: seq_shift(k, 0)) if along_x else (lambda k: seq_shift(0, k))


def send_blocks(blocks, along_x):
    shift = shift_of(along_x)
    return [lax.ppermute(b, "seq", shift(k)) for b, k in zip(blocks, ORDER[:3])]


X_AT, Y_AT = 6, 7


def scan_weights(decay, place, reverse):
    x, y, _ = place
    rel = jnp.arange(SIDE)
    origin = lax.rem(y - rel + SIDE, SIDE)
    target = lax.rem(y + rel, SIDE)
    hops = jnp.arange(1, SIDE)
    if reverse:
        row = origin
        before, counts = SIDE * (SIDE - hops - 1), x + (SIDE - hops) < SIDE
        gap = origin[None, :] - target[:, None]
        carry = SIDE - 1 - target
    else:
        row = SIDE - 1 - origin
        before, counts = SIDE * (hops - 1), x >= hops
        gap = target[:, None] - origin[None, :]
        carry = target
    gap = gap.reshape(-1)
    power = jnp.concatenate([row, before, jnp.maximum(gap - 1, 0), carry]).astype(F32)
    keep = jnp.concatenate([row >= 0, counts, gap > 0, carry >= 0]).astype(F32)
    values = keep * jnp.exp(2.0 * jnp.log(decay) * power)
    return jnp.concatenate([decay[None], values, jnp.zeros((4,), F32)])


W_ROW, W_BEFORE, W_ANSWER, W_CARRY = 1, 5, 8, 24
QUARTER = KEY // SIDE


def state_scan(info, weights, own, give, reverse, tag, fills):
    far = 1 if reverse else 0

    def start_body(info, w, own, got, p2, p1, p3, p0, scratch):
        a, b = own[...], got[...].astype(F32)
        scratch[...] = jnp.where(info[1] == far, w[0] * a + b, a + w[0] * b).astype(BF16)
        for k, out in zip(ORDER, (p2, p1, p3, p0)):
            at = pl.multiple_of(lax.rem(info[Y_AT] + k, SIDE) * QUARTER, QUARTER)
            out[...] = scratch[pl.ds(at, QUARTER), :]

    piece = ((QUARTER, VAL), BF16)
    got = lax.ppermute(give, "seq", SWAP)
    sent = call(
        "scan_start" + tag, start_body, (1,), [info, weights], [(own,), (got,)], [piece] * 4,
        fills[0](), scratch=[pltpu.VMEM((KEY, VAL), BF16)],
    )
    at2, at1, at3 = send_blocks(sent[:3], False)
    pieces = [sent[3], at1, at2, at3]

    def row_body(w, p0, p1, p2, p3, total):
        total[...] = sum(
            w[W_ROW + j] * p[...].astype(F32) for j, p in enumerate((p0, p1, p2, p3))
        ).astype(BF16)

    row = call(
        "scan_row" + tag, row_body, (1,), [weights], [(p,) for p in pieces], [piece],
        fills[1](sent[0]),
    )[0]
    at2, at1, at3 = send_blocks([row] * 3, True)

    def answer_body(w, p0, p1, p2, p3, b1, b2, b3, *outs):
        p = [r[...].astype(F32) for r in (p0, p1, p2, p3)]
        before = sum(w[W_BEFORE + j] * r[...].astype(F32) for j, r in enumerate((b1, b2, b3)))
        for k, out in zip(ORDER, outs):
            total = w[W_CARRY + k] * before
            for j in range(SIDE):
                total = total + w[W_ANSWER + SIDE * k + j] * p[j]
            out[...] = total.astype(BF16)

    answers = call(
        "scan_answer" + tag, answer_body, (1,), [weights],
        [(p,) for p in pieces] + [(at1,), (at2,), (at3,)], [piece] * 4, fills[2](row),
    )
    at2, at1, at3 = send_blocks(answers[:3], False)

    def end_body(info, w, b0, b1, b2, b3, own, got, mine, theirs, scratch):
        for k, b in enumerate((b0, b1, b2, b3)):
            at = pl.multiple_of(lax.rem(info[Y_AT] + SIDE - k, SIDE) * QUARTER, QUARTER)
            scratch[pl.ds(at, QUARTER), :] = b[...].astype(F32)
        chip = scratch[...]
        is_far = info[1] == far
        later = w[0] * chip + jnp.where(is_far, own[...], got[...].astype(F32))
        mine[...] = jnp.where(is_far, chip, later).astype(BF16)
        theirs[...] = jnp.where(is_far, later, chip).astype(BF16)

    state = ((KEY, VAL), BF16)
    mine, theirs = call(
        "scan_end" + tag, end_body, (1,), [info, weights],
        [(answers[3],), (at1,), (at2,), (at3,), (own,), (got,)], [state, state],
        fills[3](answers[0]), scratch=[pltpu.VMEM((KEY, VAL), F32)],
    )
    return mine, lax.ppermute(theirs, "seq", SWAP)


def sum_seq(values):
    values = values + lax.ppermute(values, "seq", SWAP)
    for along_x in (True, False):
        shift = shift_of(along_x)
        values = values + sum(lax.ppermute(values, "seq", shift(k)) for k in (1, 2, 3))
    return values


def shards(layer_in, gain1, wq, wk, wv, wg, wo, gain2, w1, w2, starts, cotangent):
    seq_rank = lax.axis_index("seq")
    head_rank = lax.axis_index("head")
    x, y, core = (
        seq_rank // (SIDE * CORES),
        (seq_rank // CORES) % SIDE,
        seq_rank % CORES,
    )
    place = (x, y, core)
    info = jnp.stack(
        [head_rank, core] + [(head_rank + k) % SIDE for k in ORDER] + [x, y]
    ).astype(jnp.int32)
    col_start = head_rank * PART
    gain1_part = lax.dynamic_slice_in_dim(gain1, col_start, PART)[None]
    gain2_part = lax.dynamic_slice_in_dim(gain2, col_start, PART)[None]
    gain1, gain2 = gain1[None], gain2[None]

    x_parts = spread(layer_in)
    offsets = jnp.arange(ROWS, dtype=jnp.int32)
    positions = seq_rank * ROWS + offsets
    member = positions[:, None] >= starts[None, :]
    doc_ids = jnp.sum(member.astype(jnp.int32), axis=-1) - 1
    last_start = jnp.max(jnp.where(member, starts[None, :], 0), axis=-1)
    relative = (positions - last_start).astype(F32)
    prior_doc = jnp.sum((seq_rank * ROWS - 1 >= starts).astype(jnp.int32)) - 1
    half_dim = KEY // 2
    frequency = jnp.exp(-math.log(10000.0) * jnp.arange(half_dim, dtype=F32) / half_dim)
    angles = relative[:, None] * frequency[None, :]
    cosine, sine = jnp.cos(angles), jnp.sin(angles)
    head_ids = (head_rank * HEADS + jnp.arange(HEADS, dtype=jnp.int32)).astype(F32)
    log_decay = jnp.log1p(-jnp.exp2(-5.0 - head_ids))
    gap_grid = offsets[:, None] - offsets[None, :]
    keep = (gap_grid >= 0) & (doc_ids[:, None] == doc_ids[None, :])
    gap_float = jnp.where(gap_grid >= 0, gap_grid, 0).astype(F32)
    decay = jnp.where(keep[None], jnp.exp(gap_float[None] * log_decay[:, None, None]), 0.0)
    step_float = offsets.astype(F32)
    arrival = jnp.exp((step_float[None, :] + 1.0) * log_decay[:, None]) * (
        doc_ids == prior_doc
    ).astype(F32)
    departure = jnp.exp((ROWS - 1.0 - step_float)[None, :] * log_decay[:, None]) * (
        doc_ids == doc_ids[ROWS - 1]
    ).astype(F32)
    arrival, departure = arrival[:, :, None], departure[:, :, None]
    rank_decay = lax.dynamic_index_in_dim(jnp.exp(ROWS * log_decay), core, 0, False)
    ahead = scan_weights(rank_decay, place, False)
    behind = scan_weights(rank_decay, place, True)

    low1, mean1, inv1, cot_again = norm1(info, x_parts, gain1, cotangent)
    cot_full = lax.all_gather(cot_again, "head", axis=1, tiled=True)
    key, value, own, give = key_value(info, low1, wk, wv, cosine, sine, departure)
    made = {}

    def fill_query():
        made["q"] = query_part(low1, wq, key, value, decay, cosine, sine, (give,))
        return (made["q"][0],)

    def fill_gate(token):
        made["gate"] = matmul_cols("gate", low1, wg, F32, (token,))
        return (made["gate"],)

    def fill_turn(token):
        made["low1_t"] = turn("turn_low1", info, low1, True, (token,))
        return (made["low1_t"][0],)

    mine, sibling = state_scan(
        info, ahead, own, give, False, "_a", (fill_query, fill_gate, fill_turn, lambda token: ())
    )
    query, weighted, within = made["q"]
    gate = made["gate"]
    low1_own, low1_other = made["low1_t"]
    mixed, grouped, ginv, *blocks = mix(
        info, within, gate, query, mine, sibling, arrival, wo, (cot_full,)
    )
    pieces, sent = ring_scatter(*blocks[:6])
    cot_own, cot_other = turn("turn_cot", info, cot_full, True, sent)
    grad_hidden = matmul_rows("grad_hidden", cot_full, w2, BF16, (*sent, cot_own))
    b_parts = ring_gather(*sum_branch(blocks[6], pieces, (grad_hidden,)))

    low2, mean2, inv2, middle, hidden, grad_pre = feed_up(
        info, x_parts, b_parts, gain2, w1, grad_hidden, (cot_own,)
    )
    *blocks, sums = back_blocks("back_feed", info, [(grad_pre, w1)], None, gain2, low2)
    pieces, sent = ring_scatter(*blocks[:6])
    low2_own, low2_other = turn("turn_low2", info, low2, True, (blocks[0],))
    feed_other = weight_half(
        "feed_other", [(cot_other, [hidden]), (low2_other, [grad_pre])], None, (blocks[0],)
    )
    feed_got = lax.ppermute(feed_other, "seq", SWAP)
    feed_total = weight_half(
        "feed_own", [(cot_own, [hidden]), (low2_own, [grad_pre])], feed_got, sent
    )
    grad_middle, gain2_grad, half_a, half_b = norm_back(
        "norm_back2", blocks[6], sums, pieces, gain2_part, middle, mean2, inv2, cotangent, True,
        (feed_total,),
    )
    g_parts = ring_gather(half_a, half_b)
    feed_blocks = weight_exchange(feed_total)
    feed = matmul_cols("feed_down", hidden, w2, BF16, (g_parts[2], g_parts[7]))

    branch, grad_gate, kept, own, give = back_mix(
        info, g_parts, wo, gate, grouped, ginv, query, arrival, (feed_total, feed)
    )

    def fill_turn():
        made["branch_t"] = turn("turn_branch", info, branch, True, (give,))
        return (made["branch_t"][0],)

    def fill_retain(token):
        made["r"] = retain_back(
            info, kept, value, decay, key, query, weighted, mine, sibling, arrival, cosine, sine,
            (token,),
        )
        return (made["r"][0],)

    def fill_other(token):
        made["other"] = weight_half(
            "mix_other",
            [
                (made["branch_t"][1], [mixed]),
                (low1_other, [grad_gate, made["r"][0]]),
            ],
            None,
            (token,),
        )
        return (made["other"],)

    far_mine, far_sibling = state_scan(
        info, behind, own, give, True, "_b",
        (fill_turn, fill_retain, fill_other, lambda token: ()),
    )
    branch_own, _ = made["branch_t"]
    grad_query, near_key, near_value = made["r"]
    feed = lax.psum_scatter(feed, "head", scatter_dimension=1, tiled=True)
    mix_got = lax.ppermute(made["other"], "seq", SWAP)
    grad_key, grad_value = key_value_back(
        info, far_mine, far_sibling, key, value, departure, near_key, near_value, cosine, sine,
        (),
    )
    kv_other = weight_half("kv_other", [(low1_other, [grad_key, grad_value])])
    kv_got = lax.ppermute(kv_other, "seq", SWAP)
    *blocks, sums = back_blocks(
        "back_proj", info,
        [(grad_query, wq), (grad_gate, wg), (grad_key, wk), (grad_value, wv)],
        None, gain1, low1, (kv_other, feed_blocks),
    )
    pieces, sent = ring_scatter(*blocks[:6])
    kv_total = weight_half("kv_own", [(low1_own, [grad_key, grad_value])], kv_got, sent)
    mix_total = weight_half(
        "mix_own",
        [(branch_own, [mixed]), (low1_own, [grad_gate, grad_query])],
        mix_got,
        (kv_total,),
    )
    grad_x, gain1_grad = norm_back(
        "norm_back1", blocks[6], sums, pieces, gain1_part, layer_in, mean1, inv1, grad_middle,
        False, (mix_total, feed),
    )
    mix_blocks = weight_exchange(mix_total)
    grad_kv = weight_scatter(kv_total)
    keys, vals = HEADS * KEY, HEADS * VAL
    grad_w2, grad_w1 = weight_sum("feed_sum", feed_blocks, [(vals, True), (vals, False)])
    grad_wo, grad_wg, grad_wq = weight_sum(
        "mix_sum", mix_blocks, [(vals, True), (vals, False), (keys, False)]
    )
    gains = sum_seq(jnp.concatenate([gain1_grad, gain2_grad], axis=0))
    output = (middle + feed.astype(F32)).astype(BF16)
    return (
        output,
        grad_x,
        gains[0],
        grad_wq,
        grad_kv[:, :keys],
        grad_kv[:, keys:],
        grad_wg,
        grad_wo,
        gains[1],
        grad_w1,
        grad_w2,
    )


def solution(mesh):
    rows = P("seq", "head")
    cols = P(None, "head")
    tall = P("head", None)
    return jax.shard_map(
        shards,
        mesh=mesh,
        in_specs=(rows, P(), cols, cols, cols, cols, tall, P(), cols, tall, P(), rows),
        out_specs=(
            rows, rows, P("head"), rows, rows, rows, rows, P("head", "seq"), P("head"), rows,
            P("head", "seq"),
        ),
        check_vma=False,
    )
```

```python
import math

import jax
import jax.numpy as jnp
from jax import lax
from jax.experimental import pallas as pl
from jax.experimental.pallas import tpu as pltpu
from jax.sharding import PartitionSpec as P

KEY = 256
VAL = 512
SIDE = 4
CORES = 2
HEADS = 2
ROWS = 512
HALF = 256
PART = 512
MODEL = 2048
EXTRA = 16
EPSILON = 1e-05
F32 = jnp.float32
BF16 = jnp.bfloat16
VMEM_BYTES = 26 * 1024 * 1024
ORDER = (2, 1, 3, 0)


def head_shift(step):
    return [(h, (h + step) % SIDE) for h in range(SIDE)]


def seq_index(x, y, core):
    return (x * SIDE + y) * CORES + core


def seq_shift(dx, dy, swap=0):
    return [
        (seq_index(x, y, core), seq_index((x + dx) % SIDE, (y + dy) % SIDE, core ^ swap))
        for x in range(SIDE)
        for y in range(SIDE)
        for core in range(CORES)
    ]


SWAP = seq_shift(0, 0, 1)


def up(block):
    return lax.ppermute(block, "head", head_shift(1))


def down(block):
    return lax.ppermute(block, "head", head_shift(SIDE - 1))


def add_low(a, b):
    return (a.astype(F32) + b.astype(F32)).astype(BF16)


def late(value, tokens):
    def body(value, out):
        out[...] = value[...]

    return call("late", body, (1,), [], [(value,)], [(value.shape, value.dtype)], tokens)[0]


def hold(tokens):
    def body(out):
        out[...] = jnp.zeros_like(out)

    return call("hold", body, (1,), [], [], [((8, 128), F32)], tokens)[0]


def gather_direct(block):
    got = {k: lax.ppermute(block, "head", head_shift(k)) for k in (2, 1, 3)}
    return [block, got[1], got[2], got[3]]


def ring_gather(a, b):
    r1, l1 = up(a), down(b)
    r2, l2 = up(b), down(a)
    r3, l3 = up(r1), down(l1)
    return [a, b, r1, r2, r3, l3, l2, l1]


def ring_scatter(p2a, p2b, p1a, p1b, pma, pmb):
    t1, t2 = up(p2a), down(p2b)
    rb, la = up(p1b), down(pma)
    s1, s2 = add_low(p1a, t1), add_low(pmb, t2)
    ra, lb = up(s1), down(s2)
    return [ra, rb, la, lb], (s1, s2)


def whole(shape):
    return pl.BlockSpec(shape, lambda *_: (0,) * len(shape))


def once(shape):
    return pl.BlockSpec(
        shape, lambda *_: (0,) * len(shape), pipeline_mode=pl.Buffered(buffer_count=1)
    )


PINNED = []


def pin(*arrays):
    PINNED.extend(arrays)


def is_pinned(array):
    return any(array is other for other in PINNED)


def in_hbm(array):
    return pltpu.with_memory_space_constraint(array, pltpu.HBM)


COST_SCALE = 1.0
COSTS = {
    "hold": 100,
    "turn_low2": 2,
    "late": 100,
    "scan_end_b": 50,
    "norm1": 5,
    "key_value": 8,
    "query_part": 6,
    "gate": 4,
    "mix": 9,
    "cot_pass": 100,
    "feed_up": 11,
    "back_feed": 7,
    "back_mix": 6,
    "retain_back": 0.6,
    "feed_down": 2,
    "key_value_back": 100,
    "back_proj": 1,
    "feed_other": 5,
    "feed_own": 8,
    "mix_other": 0.180,
    "mix_own": 0.270,
    "kv_other": 0.90,
    "kv_own": 1,
    "feed_sum": 2,
    "mix_sum": 2,
    "kv_sum": 2,
    "norm_back1": 0.90,
    "norm_back2": 100,
}


def call(name, body, grid, scalars, ins, outs, tokens=(), scratch=(), keep=False):
    arrays = [in_hbm(item[0]) if is_pinned(item[0]) else item[0] for item in ins]
    in_specs = [once(i[0].shape) if len(i) == 1 else pl.BlockSpec(i[1], i[2]) for i in ins]
    out_specs = [whole(o[0]) if len(o) == 2 else pl.BlockSpec(o[2], o[3]) for o in outs]
    out_shape = [jax.ShapeDtypeStruct(o[0], o[1]) for o in outs]
    keep = range(len(outs)) if keep is True else (keep or ())
    out_shape = [
        pltpu.HBM(o.shape, o.dtype) if i in keep else o for i, o in enumerate(out_shape)
    ]
    n_in, n_tok, n_sc = len(arrays), len(tokens), len(scalars)
    tokens = [in_hbm(t) if is_pinned(t) else t for t in tokens]
    in_specs += [pl.BlockSpec(memory_space=pl.ANY)] * n_tok

    def run(*refs):
        body(*refs[: n_sc + n_in], *refs[n_sc + n_in + n_tok :])

    results = pl.pallas_call(
        run,
        name=name,
        grid_spec=pltpu.PrefetchScalarGridSpec(
            num_scalar_prefetch=n_sc,
            grid=grid,
            in_specs=in_specs,
            out_specs=out_specs,
            scratch_shapes=list(scratch),
        ),
        out_shape=out_shape,
        compiler_params=pltpu.CompilerParams(
            dimension_semantics=("arbitrary",) * len(grid), vmem_limit_bytes=VMEM_BYTES
        ),
        cost_estimate=pl.CostEstimate(
            flops=int(COSTS.get(name, 0.1) * COST_SCALE * 1.1e9),
            bytes_accessed=0,
            transcendentals=0,
        ),
    )(*scalars, *arrays, *tokens)
    pin(*[results[i] for i in keep])
    return results


def dot(left, right):
    return jnp.dot(left, right, preferred_element_type=F32)


def dot_t(left, right):
    return lax.dot_general(left, right, (((1,), (1,)), ((), ())), preferred_element_type=F32)


def t_dot(left, right):
    return lax.dot_general(left, right, (((0,), (0,)), ((), ())), preferred_element_type=F32)


def rotate(rows, cosine, sine):
    half = rows.shape[-1] // 2
    first, second = rows[:, :half], rows[:, half:]
    return jnp.concatenate([first * cosine - second * sine, second * cosine + first * sine], axis=1)


def head_col(info, k):
    return pl.multiple_of(lax.rem(info[0] + SIDE - k, SIDE) * PART, PART)


CHUNK = 16


def norm_rows(info, load, gain, low, mean_ref, inv_ref, own=None):
    for half in range(2):

        def step(i, _):
            at = pl.multiple_of(i * CHUNK, CHUNK)
            out = pl.ds(pl.multiple_of(half * HALF + i * CHUNK, CHUNK), CHUNK)
            parts = [load(k, half, at) for k in range(SIDE)]
            if own is not None:
                own[out, :] = parts[0]
            mean = sum(jnp.sum(p, axis=1, keepdims=True) for p in parts) / MODEL
            parts = [p - mean for p in parts]
            var = sum(jnp.sum(p * p, axis=1, keepdims=True) for p in parts) / MODEL
            inv = lax.rsqrt(var + EPSILON)
            mean_ref[out, :] = mean
            inv_ref[out, :] = inv
            for k in range(SIDE):
                cols = pl.ds(head_col(info, k), PART)
                low[out, cols] = (parts[k] * inv * gain[:, cols]).astype(BF16)
            return 0

        lax.fori_loop(0, HALF // CHUNK, step, 0, unroll=4)


def chunk_of(part, half, at):
    return part[pl.ds(pl.multiple_of(half * HALF + at, CHUNK), CHUNK), :].astype(F32)


def norm1(info, parts, gain, cotangent):
    def body(info, *refs):
        x = refs[:8]
        gain, cot, low, mean, inv, cot_out, rows = refs[8:]
        cot_out[...] = cot[...]
        for k in range(SIDE):
            rows[k, :HALF] = x[2 * k][...]
            rows[k, HALF:] = x[2 * k + 1][...]
        norm_rows(
            info,
            lambda k, half, at: x[2 * k + half][pl.ds(at, CHUNK), :].astype(F32),
            gain,
            low,
            mean,
            inv,
        )

    return call(
        "norm1",
        body,
        (1,),
        [info],
        [(p,) for p in parts] + [(gain,), (cotangent,)],
        [
            ((ROWS, MODEL), BF16),
            ((ROWS, 1), F32),
            ((ROWS, 1), F32),
            ((ROWS, PART), BF16),
            ((SIDE, ROWS, PART), BF16),
        ],
        keep=(4,),
    )


def key_value(info, low, wk, wv, cosine, sine, departure):
    def body(info, low, wk, wv, cosine, sine, departure, key, value, own, give):
        head = pl.program_id(0)
        k = rotate(dot(low[...], wk[...]), cosine[...], sine[...]).astype(BF16)
        key[...] = k
        v = dot(low[...], wv[...]).astype(BF16)
        value[...] = v
        state = t_dot((k.astype(F32) * departure[0]).astype(BF16), v)

        @pl.when(head == info[1])
        def _():
            own[...] = state

        @pl.when(head != info[1])
        def _():
            give[...] = state.astype(BF16)

    by_head = lambda h, *_: (0, h)
    return call(
        "key_value",
        body,
        (HEADS,),
        [info],
        [
            (low,),
            (wk, (MODEL, KEY), by_head),
            (wv, (MODEL, VAL), by_head),
            (cosine,),
            (sine,),
            (departure, (1, ROWS, 1), lambda h, *_: (h, 0, 0)),
        ],
        [
            ((ROWS, HEADS * KEY), BF16, (ROWS, KEY), by_head),
            ((ROWS, HEADS * VAL), BF16, (ROWS, VAL), by_head),
            ((KEY, VAL), F32),
            ((KEY, VAL), BF16),
        ],
        keep=(0, 1),
    )


def query_part(low, wq, key, value, decay, cosine, sine, tokens):
    def body(low, wq, key, value, decay, cosine, sine, query, weighted, within):
        q = rotate(dot(low[...], wq[...]), cosine[...], sine[...]).astype(BF16)
        query[...] = q
        w = (dot_t(q, key[...]) * decay[0]).astype(BF16)
        weighted[0] = w
        within[...] = dot(w, value[...])

    by_head = lambda h, *_: (0, h)
    cube = lambda h, *_: (h, 0, 0)
    return call(
        "query_part",
        body,
        (HEADS,),
        [],
        [
            (low,),
            (wq, (MODEL, KEY), by_head),
            (key, (ROWS, KEY), by_head),
            (value, (ROWS, VAL), by_head),
            (decay, (1, ROWS, ROWS), cube),
            (cosine,),
            (sine,),
        ],
        [
            ((ROWS, HEADS * KEY), BF16, (ROWS, KEY), by_head),
            ((HEADS, ROWS, ROWS), BF16, (1, ROWS, ROWS), cube),
            ((ROWS, HEADS * VAL), F32, (ROWS, VAL), by_head),
        ],
        tokens,
        keep=(0, 1),
    )


def matmul_cols(name, left, right, out_type, tokens=(), block=512):
    def body(left, right, out):
        out[...] = dot(left[...], right[...]).astype(out_type)

    depth, cols = right.shape
    by_col = lambda i, *_: (0, i)
    return call(
        name,
        body,
        (cols // block,),
        [],
        [(left,), (right, (depth, block), by_col)],
        [((left.shape[0], cols), out_type, (left.shape[0], block), by_col)],
        tokens,
        keep=True,
    )[0]


def block_outs(extra):
    tall = ((HALF + extra, PART), BF16)
    return [tall, ((HALF, PART), BF16)] * 3 + [((ROWS, PART), F32)]


def put_blocks(step, make, outs):
    for i in range(2):
        block = make(i)
        for s in range(2):
            k = 2 * s + i

            @pl.when(step == s)
            def _():
                if k == SIDE - 1:
                    outs[6][...] = block
                else:
                    outs[2 * k][:HALF, :] = block[:HALF].astype(BF16)
                    outs[2 * k + 1][...] = block[HALF:].astype(BF16)


def pick(mine, sibling, info, head):
    return jnp.where(info[1] == head, mine[...], sibling[...])


def mix(info, within, gate, query, mine, sibling, arrival, wo, tokens):
    def body(
        info, within, gate, query, mine, sibling, arrival, wo_a, wo_b, mixed, grouped, ginv, *outs
    ):
        step = pl.program_id(0)

        @pl.when(step == 0)
        def _():
            for head in range(HEADS):
                cols = slice(head * VAL, (head + 1) * VAL)
                state = pick(mine, sibling, info, head)
                for half in range(2):
                    rows = slice(half * HALF, (half + 1) * HALF)
                    cross = dot(query[rows, head * KEY : (head + 1) * KEY], state)
                    kept = within[rows, cols] + arrival[head, rows] * cross
                    kept = kept - jnp.mean(kept, axis=1, keepdims=True)
                    inv = lax.rsqrt(jnp.mean(kept * kept, axis=1, keepdims=True) + float(KEY))
                    group = kept * inv
                    g = gate[rows, cols].astype(F32)
                    ginv[head, rows] = inv
                    grouped[rows, cols] = group.astype(BF16)
                    mixed[rows, cols] = (group * (g / (1.0 + jnp.exp(-g)))).astype(BF16)

        put_blocks(step, lambda i: dot(mixed[...], (wo_a, wo_b)[i][...]), outs)

    cols = HEADS * VAL
    return call(
        "mix",
        body,
        (2,),
        [info],
        [
            (within,),
            (gate,),
            (query,),
            (mine,),
            (sibling,),
            (arrival,),
            (wo, (cols, PART), lambda i, info: (0, info[2 + 2 * i])),
            (wo, (cols, PART), lambda i, info: (0, info[3 + 2 * i])),
        ],
        [((ROWS, cols), BF16), ((ROWS, cols), BF16), ((HEADS, ROWS, 1), F32)] + block_outs(0),
        tokens,
        keep=(0, 1),
    )


def sum_branch(p0, pieces, tokens):
    def body(p0, ra, rb, la, lb, a, b):
        a[...] = (p0[:HALF] + ra[...].astype(F32) + la[...].astype(F32)).astype(BF16)
        b[...] = (p0[HALF:] + rb[...].astype(F32) + lb[...].astype(F32)).astype(BF16)

    return call(
        "sum_branch",
        body,
        (1,),
        [],
        [(p0,)] + [(p,) for p in pieces],
        [((HALF, PART), BF16), ((HALF, PART), BF16)],
        tokens,
    )


def feed_up(info, x_rows, b_parts, gain, w1, grad_hidden, tokens):
    block = 512

    def body(info, *refs):
        x, b = refs[0], refs[1:9]
        gain, w1, grad_hidden, ffn_in, mean, inv, own, hidden, grad_pre = refs[9:]

        @pl.when(pl.program_id(0) == 0)
        def _():
            def load(k, half, at):
                branch = b[2 * k + half][pl.ds(at, CHUNK), :].astype(F32)
                return chunk_of(x.at[k], half, at) + branch

            norm_rows(info, load, gain, ffn_in, mean, inv, own)

        pre = dot(ffn_in[...], w1[...])
        cdf = 0.5 * (1.0 + lax.erf(pre * (2.0**-0.5)))
        hidden[...] = (pre * cdf).astype(BF16)
        pdf = jnp.exp(-0.5 * pre * pre) * ((2.0 * math.pi) ** -0.5)
        grad_pre[...] = ((cdf + pre * pdf) * grad_hidden[...].astype(F32)).astype(BF16)

    by_col = lambda i, *_: (0, i)
    cols = w1.shape[1]
    tall = ((ROWS, cols), BF16, (ROWS, block), by_col)
    return call(
        "feed_up",
        body,
        (cols // block,),
        [info],
        [(x_rows,)]
        + [(p,) for p in b_parts]
        + [
            (gain,),
            (w1, (MODEL, block), by_col),
            (grad_hidden, (ROWS, block), by_col),
        ],
        [
            ((ROWS, MODEL), BF16),
            ((ROWS, 1), F32),
            ((ROWS, 1), F32),
            ((ROWS, PART), F32),
            tall,
            tall,
        ],
        tokens,
    )


def back_blocks(name, info, pairs, gain, low, tokens=()):
    n = len(pairs)

    def body(info, *refs):
        grads, weights = refs[:n], refs[n : 3 * n]
        gains, lows = refs[3 * n : 3 * n + 2], refs[3 * n + 2 : 3 * n + 4]
        outs, sums, acc = refs[3 * n + 4 : 3 * n + 11], refs[3 * n + 11], refs[3 * n + 12]
        step = pl.program_id(0)
        lane = lax.broadcasted_iota(jnp.int32, (ROWS, 128), 1)

        @pl.when(step == 0)
        def _():
            acc[...] = jnp.zeros_like(acc)

        def make(i):
            total = dot_t(grads[0][...], weights[2 * 0 + i][...])
            for j in range(1, n):
                total = total + dot_t(grads[j][...], weights[2 * j + i][...])
            first = jnp.sum(total * gains[i][...], axis=1, keepdims=True) / MODEL
            second = jnp.sum(total * lows[i][...].astype(F32), axis=1, keepdims=True) / MODEL
            acc[...] += jnp.where(lane == 0, first, jnp.where(lane == 1, second, 0.0))
            return total

        put_blocks(step, make, outs)

        @pl.when(step == 1)
        def _():
            turned = acc[...].T[:EXTRA]
            sums[...] = turned
            for k in range(SIDE - 1):
                outs[2 * k][HALF:, :] = turned.astype(BF16)

    def by_row(j):
        return lambda i, info: (info[2 + j + 2 * i], 0)

    def by_col(j):
        return lambda i, info: (0, info[2 + j + 2 * i])

    return call(
        name,
        body,
        (2,),
        [info],
        [(g,) for g, _ in pairs]
        + [(w, (PART, w.shape[1]), by_row(j)) for _, w in pairs for j in range(2)]
        + [(gain, (1, PART), by_col(j)) for j in range(2)]
        + [(low, (ROWS, PART), by_col(j)) for j in range(2)],
        block_outs(EXTRA) + [((EXTRA, PART), F32)],
        tokens,
        [pltpu.VMEM((ROWS, 128), F32)],
    )


def norm_back(
    name, info, p0, sums, pieces, gain, rows, mean, inv, residual, low_out, tokens
):
    def body(
        info, p0, sums, ra, rb, la, lb, gain, rows, mean, inv, residual, grad, gain_grad, *low
    ):
        scale = gain[:, pl.ds(head_col(info, 0), PART)]
        total = sums[...] + ra[HALF:].astype(F32) + la[HALF:].astype(F32)
        total = jnp.concatenate([total, jnp.zeros((128 - EXTRA, PART), F32)], axis=0).T
        acc = jnp.zeros((1, PART), F32)
        for half, (one, two) in enumerate(((ra, la), (rb, lb))):
            for quarter in range(2):
                at = slice(quarter * 128, (quarter + 1) * 128)
                out = slice(half * HALF + quarter * 128, half * HALF + (quarter + 1) * 128)
                g = p0[out] + one[at].astype(F32) + two[at].astype(F32)
                normed = (rows[out].astype(F32) - mean[out]) * inv[out]
                acc = acc + jnp.sum(g * normed, axis=0, keepdims=True)
                back = inv[out] * (g * scale - total[out, 0:1] - normed * total[out, 1:2])
                new = residual[out].astype(F32) + back
                grad[out] = new
                if low_out:
                    low[half][at] = new.astype(BF16)
        gain_grad[...] = acc

    outs = [((ROWS, PART), F32), ((1, PART), F32)]
    if low_out:
        outs += [((HALF, PART), BF16)] * 2
    return call(
        name,
        body,
        (1,),
        [info],
        [(p0,), (sums,)]
        + [(p,) for p in pieces]
        + [(gain,), (rows,), (mean,), (inv,), (residual,)],
        outs,
        tokens,
    )


def back_mix(info, parts, wo, gate, grouped, ginv, query, arrival, tokens):
    def body(info, *refs):
        parts = refs[:8]
        wo, gate, grouped, ginv, query, arrival, branch, grad_gate, kept, own, give = refs[8:]
        head = pl.program_id(0)

        @pl.when(head == 0)
        def _():
            for k in range(SIDE):
                cols = pl.ds(head_col(info, k), PART)
                branch[:HALF, cols] = parts[2 * k][...]
                branch[HALF:, cols] = parts[2 * k + 1][...]

        for half in range(2):
            rows = slice(half * HALF, (half + 1) * HALF)
            m = dot_t(branch[rows], wo[...])
            g = gate[rows].astype(F32)
            sigmoid = 1.0 / (1.0 + jnp.exp(-g))
            group = grouped[rows].astype(F32)
            slope = sigmoid * (1.0 + g * (1.0 - sigmoid))
            grad_gate[rows] = (m * group * slope).astype(BF16)
            e = m * (g * sigmoid)
            e = ginv[0, rows] * (
                e
                - jnp.mean(e, axis=1, keepdims=True)
                - group * jnp.mean(e * group, axis=1, keepdims=True)
            )
            kept[rows] = e.astype(BF16)
        moved = (query[...].astype(F32) * arrival[0]).astype(BF16)
        state = t_dot(moved, kept[...])

        @pl.when(head == info[1])
        def _():
            own[...] = state

        @pl.when(head != info[1])
        def _():
            give[...] = state.astype(BF16)

    by_head = lambda h, *_: (0, h)
    cube = lambda h, *_: (h, 0, 0)
    cols = HEADS * VAL
    return call(
        "back_mix",
        body,
        (HEADS,),
        [info],
        [(p,) for p in parts]
        + [
            (wo, (VAL, MODEL), lambda h, *_: (h, 0)),
            (gate, (ROWS, VAL), by_head),
            (grouped, (ROWS, VAL), by_head),
            (ginv, (1, ROWS, 1), cube),
            (query, (ROWS, KEY), by_head),
            (arrival, (1, ROWS, 1), cube),
        ],
        [
            ((ROWS, MODEL), BF16),
            ((ROWS, cols), BF16, (ROWS, VAL), by_head),
            ((ROWS, cols), BF16, (ROWS, VAL), by_head),
            ((KEY, VAL), F32),
            ((KEY, VAL), BF16),
        ],
        tokens,
        keep=(1, 2),
    )


def retain_back(info, kept, value, decay, key, query, weighted, mine, sibling, arrival, cosine, sine, tokens):
    def body(
        info, kept, value, decay, key, query, weighted, mine, sibling, arrival, cosine, sine,
        grad_query, near_key, near_value,
    ):
        head = pl.program_id(0)
        e = kept[...]
        s = (dot_t(e, value[...]) * decay[0]).astype(BF16)
        state = pick(mine, sibling, info, head)
        gq = dot(s, key[...]) + arrival[0] * dot_t(e, state)
        grad_query[...] = rotate(gq, cosine[...], -sine[...]).astype(BF16)
        near_key[...] = t_dot(s, query[...])
        near_value[...] = t_dot(weighted[0], e)

    by_head = lambda h, *_: (0, h)
    cube = lambda h, *_: (h, 0, 0)
    keys, vals = HEADS * KEY, HEADS * VAL
    return call(
        "retain_back",
        body,
        (HEADS,),
        [info],
        [
            (kept, (ROWS, VAL), by_head),
            (value, (ROWS, VAL), by_head),
            (decay, (1, ROWS, ROWS), cube),
            (key, (ROWS, KEY), by_head),
            (query, (ROWS, KEY), by_head),
            (weighted, (1, ROWS, ROWS), cube),
            (mine,),
            (sibling,),
            (arrival, (1, ROWS, 1), cube),
            (cosine,),
            (sine,),
        ],
        [
            ((ROWS, keys), BF16, (ROWS, KEY), by_head),
            ((ROWS, keys), F32, (ROWS, KEY), by_head),
            ((ROWS, vals), F32, (ROWS, VAL), by_head),
        ],
        tokens,
        keep=True,
    )


def key_value_back(info, mine, sibling, key, value, departure, near_key, near_value, cosine, sine, tokens):
    def body(
        info, mine, sibling, key, value, departure, near_key, near_value, cosine, sine,
        grad_key, grad_value,
    ):
        state = pick(mine, sibling, info, pl.program_id(0))
        gk = near_key[...] + departure[0] * dot_t(value[...], state)
        grad_key[...] = rotate(gk, cosine[...], -sine[...]).astype(BF16)
        gv = near_value[...] + departure[0] * dot(key[...], state)
        grad_value[...] = gv.astype(BF16)

    by_head = lambda h, *_: (0, h)
    keys, vals = HEADS * KEY, HEADS * VAL
    return call(
        "key_value_back",
        body,
        (HEADS,),
        [info],
        [
            (mine,),
            (sibling,),
            (key, (ROWS, KEY), by_head),
            (value, (ROWS, VAL), by_head),
            (departure, (1, ROWS, 1), lambda h, *_: (h, 0, 0)),
            (near_key, (ROWS, KEY), by_head),
            (near_value, (ROWS, VAL), by_head),
            (cosine,),
            (sine,),
        ],
        [
            ((ROWS, keys), BF16, (ROWS, KEY), by_head),
            ((ROWS, vals), BF16, (ROWS, VAL), by_head),
        ],
        tokens,
    )


def turn(name, info, low, tokens=(), keep=False):
    xs = 2

    def body(info, low, own, other, scratch):
        scratch[...] = low[...].T
        for x in range(xs):
            for y in range(SIDE):
                base = (x * SIDE + y) * CORES * 64
                mine = pl.ds(pl.multiple_of(base + info[1] * 64, 64), 64)
                far = pl.ds(pl.multiple_of(base + (1 - info[1]) * 64, 64), 64)
                own[x, y] = scratch[mine, :]
                other[x, y] = scratch[far, :]

    out = ((SIDE, SIDE, 64, ROWS), BF16, (xs, SIDE, 64, ROWS), lambda i, *_: (i, 0, 0, 0))
    own, other = call(
        name,
        body,
        (SIDE // xs,),
        [info],
        [(low, (ROWS, xs * PART), lambda i, *_: (0, i))],
        [out, out],
        tokens,
        [pltpu.VMEM((xs * PART, ROWS), BF16)],
        keep=keep,
    )
    flat = own.reshape(-1, ROWS), other.reshape(-1, ROWS)
    if keep:
        pin(*flat)
    return flat


def cot_pass(info, parts, w2, tokens):
    xs = 2

    def body(info, a, b, c, d, w2, own, other, out, whole_rows, scratch):
        step = pl.program_id(0)

        @pl.when(step == 0)
        def _():
            for k, part in enumerate((a, b, c, d)):
                whole_rows[:, pl.ds(head_col(info, k), PART)] = part[...]

        out[...] = dot_t(whole_rows[...], w2[...]).astype(BF16)
        cols = pl.ds(pl.multiple_of(step * xs * PART, PART), xs * PART)
        scratch[...] = whole_rows[:, cols].T
        for x in range(xs):
            for y in range(SIDE):
                base = (x * SIDE + y) * CORES * 64
                mine = pl.ds(pl.multiple_of(base + info[1] * 64, 64), 64)
                far = pl.ds(pl.multiple_of(base + (1 - info[1]) * 64, 64), 64)
                own[x, y] = scratch[mine, :]
                other[x, y] = scratch[far, :]

    turned = ((SIDE, SIDE, 64, ROWS), BF16, (xs, SIDE, 64, ROWS), lambda i, *_: (i, 0, 0, 0))
    cols = w2.shape[0]
    own, other, out = call(
        "cot_pass",
        body,
        (2,),
        [info],
        [(p,) for p in parts] + [(w2, (cols // 2, MODEL), lambda i, *_: (i, 0))],
        [turned, turned, ((ROWS, cols), BF16, (ROWS, cols // 2), lambda i, *_: (0, i))],
        tokens,
        [pltpu.VMEM((ROWS, MODEL), BF16), pltpu.VMEM((xs * PART, ROWS), BF16)],
    )
    return own.reshape(-1, ROWS), other.reshape(-1, ROWS), out


def widths(groups):
    return [sum(r.shape[1] for r in rights) for _, rights in groups]


def weight_half(name, groups, arrived=None, tokens=()):
    n_left = len(groups)
    rights = [r for _, rs in groups for r in rs]
    counts = [len(rs) for _, rs in groups]
    n = len(rights)
    width = sum(widths(groups))

    def body(*refs):
        lefts, rest = refs[:n_left], refs[n_left : n_left + n]
        out = refs[-1]
        at = 0
        which = 0
        for left, count in zip(lefts, counts):
            for r in rest[which : which + count]:
                cols = slice(at, at + r.shape[1])
                total = dot(left[...], r[...])
                if arrived is not None:
                    total = total + refs[n_left + n][:, cols].astype(F32)
                out[:, cols] = total.astype(BF16)
                at += r.shape[1]
            which += count

    block = lambda i, *_: (i, 0)
    return call(
        name,
        body,
        (2,),
        [],
        [(left, (ROWS, ROWS), block) for left, _ in groups]
        + [(r,) for r in rights]
        + ([(arrived, (ROWS, width), block)] if arrived is not None else []),
        [((2 * ROWS, width), BF16, (ROWS, width), block)],
        tokens,
        keep=True,
    )[0]


PLANE = [
    [seq_index(x, y, c) for x in range(SIDE) for y in range(SIDE)] for c in range(CORES)
]


def axis_groups(along_x):
    if along_x:
        return [
            [seq_index(x, y, c) for x in range(SIDE)] for y in range(SIDE) for c in range(CORES)
        ]
    return [[seq_index(x, y, c) for y in range(SIDE)] for x in range(SIDE) for c in range(CORES)]


def exchange(total, groups):
    blocks = total
    if total.ndim == 2:
        blocks = total.reshape(len(groups[0]), -1, total.shape[-1])
    blocks = lax.all_to_all(blocks, "seq", 0, 0, axis_index_groups=groups, tiled=True)
    pin(blocks)
    return blocks


def weight_mid(name, blocks, gains, tokens=()):
    count, rows, width = blocks.shape
    step = width // 2
    part = rows // SIDE
    gains = jnp.pad(gains, ((0, EXTRA - gains.shape[0]), (0, step - gains.shape[1])))

    def body(blocks, gains, out):
        total = blocks[0].astype(F32)
        for k in range(1, count):
            total = total + blocks[k].astype(F32)
        for y in range(SIDE):
            out[y, :part] = total[y * part : (y + 1) * part].astype(BF16)
            out[y, part:] = gains[...].astype(BF16)

    return call(
        name,
        body,
        (2,),
        [],
        [(blocks, (count, rows, step), lambda i, *_: (0, 0, i)), (gains,)],
        [
            (
                (SIDE, part + EXTRA, width),
                BF16,
                (SIDE, part + EXTRA, step),
                lambda i, *_: (0, 0, i),
            )
        ],
        tokens,
        keep=True,
    )[0]


def weight_sum(name, blocks, parts, tokens=()):
    count, rows, width = blocks.shape
    extra = rows - 64

    def body(blocks, *outs):
        at = 0
        for out, part in zip(outs, parts):
            cols = slice(at, at + part)
            total = blocks[0, :64, cols].astype(F32)
            for k in range(1, count):
                total = total + blocks[k, :64, cols].astype(F32)
            out[...] = total
            at += part
        if extra:
            total = blocks[0, 64:, :PART].astype(F32)
            for k in range(1, count):
                total = total + blocks[k, 64:, :PART].astype(F32)
            outs[-1][...] = total

    return call(
        name,
        body,
        (1,),
        [],
        [(blocks,)],
        [((64, part), F32) for part in parts] + ([((extra, PART), F32)] if extra else []),
        tokens,
    )


def weight_own_y(name, info, left, rights, arrived, tokens=()):
    n = len(rights)
    width = sum(r.shape[1] for r in rights)
    left = left.reshape(SIDE, SIDE, 64, ROWS)
    arrived = arrived.reshape(SIDE, SIDE, 64, width)
    pin(left, arrived)

    def body(info, *refs):
        lefts, rights, got, outs = refs[:2], refs[2 : 2 + n], refs[2 + n : 4 + n], refs[4 + n :]
        step = pl.program_id(0)
        for i in range(2):
            at = 0
            for r in rights:
                cols = slice(at, at + r.shape[1])
                total = dot(lefts[i][...].reshape(HALF, ROWS), r[...])
                total = total + got[i][:, :, :, cols].reshape(HALF, r.shape[1]).astype(F32)
                for s in range(2):

                    @pl.when(step == s)
                    def _():
                        out = outs[2 * s + i]
                        out[:, cols] = total.astype(out.dtype)

                at += r.shape[1]

    def block(j):
        def at(i, info):
            return (0, lax.rem(info[Y_AT] + ORDER_OF(2 * i + j), SIDE), 0, 0)

        return at

    return call(
        name,
        body,
        (2,),
        [info],
        [(left, (SIDE, 1, 64, ROWS), block(j)) for j in range(2)]
        + [(r,) for r in rights]
        + [(arrived, (SIDE, 1, 64, width), block(j)) for j in range(2)],
        [((HALF, width), BF16)] * 3 + [((HALF, width), F32)],
        tokens,
    )


def ORDER_OF(i):
    return jnp.where(i == 0, 2, jnp.where(i == 1, 1, jnp.where(i == 2, 3, 0)))


def phase_sum(name, info, where, base, received, tokens=()):
    width = base.shape[1]

    def body(info, base, a, b, c, *refs):
        outs, scratch = refs[:SIDE], refs[SIDE]
        scratch[...] = base[...] + a[...].astype(F32) + b[...].astype(F32) + c[...].astype(F32)
        for i, k in enumerate(ORDER):
            at = pl.multiple_of(lax.rem(info[where] + k, SIDE) * 64, 64)
            outs[i][...] = scratch[pl.ds(at, 64), :].astype(outs[i].dtype)

    return call(
        name,
        body,
        (1,),
        [info],
        [(base,)] + [(r,) for r in received],
        [((64, width), BF16)] * 3 + [((64, width), F32)],
        tokens,
        [pltpu.VMEM((HALF, width), F32)],
    )


def last_sum(name, base, received, parts):
    def body(base, a, b, c, *outs):
        at = 0
        for out in outs:
            cols = slice(at, at + out.shape[1])
            out[...] = base[:, cols] + sum(r[:, cols].astype(F32) for r in (a, b, c))
            at += out.shape[1]

    return call(
        name,
        body,
        (1,),
        [],
        [(base,)] + [(r,) for r in received],
        [((64, w), F32) for w in parts],
    )


def shift_of(along_x):
    return (lambda k: seq_shift(k, 0)) if along_x else (lambda k: seq_shift(0, k))


def send_blocks(blocks, along_x):
    shift = shift_of(along_x)
    return [lax.ppermute(b, "seq", shift(k)) for b, k in zip(blocks, ORDER[:3])]


X_AT, Y_AT = 6, 7


def scan_weights(decay, place, reverse):
    x, y, _ = place
    rel = jnp.arange(SIDE)
    origin = lax.rem(y - rel + SIDE, SIDE)
    target = lax.rem(y + rel, SIDE)
    hops = jnp.arange(1, SIDE)
    if reverse:
        row = origin
        before, counts = SIDE * (SIDE - hops - 1), x + (SIDE - hops) < SIDE
        gap = origin[None, :] - target[:, None]
        carry = SIDE - 1 - target
    else:
        row = SIDE - 1 - origin
        before, counts = SIDE * (hops - 1), x >= hops
        gap = target[:, None] - origin[None, :]
        carry = target
    gap = gap.reshape(-1)
    power = jnp.concatenate([row, before, jnp.maximum(gap - 1, 0), carry]).astype(F32)
    keep = jnp.concatenate([row >= 0, counts, gap > 0, carry >= 0]).astype(F32)
    values = keep * jnp.exp(2.0 * jnp.log(decay) * power)
    return jnp.concatenate([decay[None], values, jnp.zeros((4,), F32)])


W_ROW, W_BEFORE, W_ANSWER, W_CARRY = 1, 5, 8, 24
QUARTER = KEY // SIDE


def state_scan(info, weights, own, give, reverse, tag, fills):
    far = 1 if reverse else 0

    def start_body(info, w, own, got, p2, p1, p3, p0, scratch):
        a, b = own[...], got[...].astype(F32)
        scratch[...] = jnp.where(info[1] == far, w[0] * a + b, a + w[0] * b).astype(BF16)
        for k, out in zip(ORDER, (p2, p1, p3, p0)):
            at = pl.multiple_of(lax.rem(info[Y_AT] + k, SIDE) * QUARTER, QUARTER)
            out[...] = scratch[pl.ds(at, QUARTER), :]

    piece = ((QUARTER, VAL), BF16)
    got = lax.ppermute(give, "seq", SWAP)
    sent = call(
        "scan_start" + tag, start_body, (1,), [info, weights], [(own,), (got,)], [piece] * 4,
        fills[0](), scratch=[pltpu.VMEM((KEY, VAL), BF16)],
    )
    at2, at1, at3 = send_blocks(sent[:3], False)
    pieces = [sent[3], at1, at2, at3]

    def row_body(w, p0, p1, p2, p3, total):
        total[...] = sum(
            w[W_ROW + j] * p[...].astype(F32) for j, p in enumerate((p0, p1, p2, p3))
        ).astype(BF16)

    row = call(
        "scan_row" + tag, row_body, (1,), [weights], [(p,) for p in pieces], [piece],
        fills[1](sent[0]),
    )[0]
    at2, at1, at3 = send_blocks([row] * 3, True)

    def answer_body(w, p0, p1, p2, p3, b1, b2, b3, *outs):
        p = [r[...].astype(F32) for r in (p0, p1, p2, p3)]
        before = sum(w[W_BEFORE + j] * r[...].astype(F32) for j, r in enumerate((b1, b2, b3)))
        for k, out in zip(ORDER, outs):
            total = w[W_CARRY + k] * before
            for j in range(SIDE):
                total = total + w[W_ANSWER + SIDE * k + j] * p[j]
            out[...] = total.astype(BF16)

    answers = call(
        "scan_answer" + tag, answer_body, (1,), [weights],
        [(p,) for p in pieces] + [(at1,), (at2,), (at3,)], [piece] * 4, fills[2](row),
    )
    at2, at1, at3 = send_blocks(answers[:3], False)

    def end_body(info, w, b0, b1, b2, b3, own, got, mine, theirs, scratch):
        for k, b in enumerate((b0, b1, b2, b3)):
            at = pl.multiple_of(lax.rem(info[Y_AT] + SIDE - k, SIDE) * QUARTER, QUARTER)
            scratch[pl.ds(at, QUARTER), :] = b[...].astype(F32)
        chip = scratch[...]
        is_far = info[1] == far
        later = w[0] * chip + jnp.where(is_far, own[...], got[...].astype(F32))
        mine[...] = jnp.where(is_far, chip, later).astype(BF16)
        theirs[...] = jnp.where(is_far, later, chip).astype(BF16)

    state = ((KEY, VAL), BF16)
    mine, theirs = call(
        "scan_end" + tag, end_body, (1,), [info, weights],
        [(answers[3],), (at1,), (at2,), (at3,), (own,), (got,)], [state, state],
        fills[3](answers[0]), scratch=[pltpu.VMEM((KEY, VAL), F32)],
    )
    return mine, lax.ppermute(theirs, "seq", SWAP)


def sum_core_x(values):
    values = values + lax.ppermute(values, "seq", SWAP)
    return values + sum(lax.ppermute(values, "seq", seq_shift(k, 0)) for k in (1, 2, 3))


def shards(layer_in, gain1, wq, wk, wv, wg, wo, gain2, w1, w2, starts, cotangent):
    seq_rank = lax.axis_index("seq")
    head_rank = lax.axis_index("head")
    x, y, core = (
        seq_rank // (SIDE * CORES),
        (seq_rank // CORES) % SIDE,
        seq_rank % CORES,
    )
    place = (x, y, core)
    PINNED.clear()
    pin(wq, wk, wv, wg, wo, w1, w2)
    info = jnp.stack(
        [head_rank, core] + [(head_rank + k) % SIDE for k in ORDER] + [x, y]
    ).astype(jnp.int32)
    gain1, gain2 = gain1[None], gain2[None]

    x_parts = ring_gather(layer_in[:HALF], layer_in[HALF:])
    starts = late(starts[None], (x_parts[2], x_parts[7]))[0]
    offsets = jnp.arange(ROWS, dtype=jnp.int32)
    positions = seq_rank * ROWS + offsets
    member = positions[:, None] >= starts[None, :]
    doc_ids = jnp.sum(member.astype(jnp.int32), axis=-1) - 1
    last_start = jnp.max(jnp.where(member, starts[None, :], 0), axis=-1)
    relative = (positions - last_start).astype(F32)
    prior_doc = jnp.sum((seq_rank * ROWS - 1 >= starts).astype(jnp.int32)) - 1
    half_dim = KEY // 2
    frequency = jnp.exp(-math.log(10000.0) * jnp.arange(half_dim, dtype=F32) / half_dim)
    angles = relative[:, None] * frequency[None, :]
    cosine, sine = jnp.cos(angles), jnp.sin(angles)
    head_ids = (head_rank * HEADS + jnp.arange(HEADS, dtype=jnp.int32)).astype(F32)
    log_decay = jnp.log1p(-jnp.exp2(-5.0 - head_ids))
    gap_grid = offsets[:, None] - offsets[None, :]
    keep = (gap_grid >= 0) & (doc_ids[:, None] == doc_ids[None, :])
    gap_float = jnp.where(gap_grid >= 0, gap_grid, 0).astype(F32)
    decay = jnp.where(keep[None], jnp.exp(gap_float[None] * log_decay[:, None, None]), 0.0)
    step_float = offsets.astype(F32)
    arrival = jnp.exp((step_float[None, :] + 1.0) * log_decay[:, None]) * (
        doc_ids == prior_doc
    ).astype(F32)
    departure = jnp.exp((ROWS - 1.0 - step_float)[None, :] * log_decay[:, None]) * (
        doc_ids == doc_ids[ROWS - 1]
    ).astype(F32)
    arrival, departure = arrival[:, :, None], departure[:, :, None]
    pin(decay)
    rank_decay = lax.dynamic_index_in_dim(jnp.exp(ROWS * log_decay), core, 0, False)
    ahead = scan_weights(rank_decay, place, False)
    behind = scan_weights(rank_decay, place, True)

    low1, mean1, inv1, cot_again, x_rows = norm1(info, x_parts, gain1, cotangent)
    cot_parts = gather_direct(cot_again)
    key, value, own, give = key_value(info, low1, wk, wv, cosine, sine, departure)
    made = {}

    def fill_query():
        made["q"] = query_part(low1, wq, key, value, decay, cosine, sine, (give,))
        return (made["q"][0],)

    def fill_gate(token):
        made["gate"] = matmul_cols("gate", low1, wg, BF16, (token, *cot_parts[1:]))
        return (made["gate"],)

    def fill_turn(token):
        made["low1_t"] = turn("turn_low1", info, low1, (token,), True)
        return (made["low1_t"][0],)

    mine, sibling = state_scan(
        info, ahead, own, give, False, "_a", (fill_query, fill_gate, fill_turn, lambda token: ())
    )
    query, weighted, within = made["q"]
    gate = made["gate"]
    low1_own, low1_other = made["low1_t"]
    mixed, grouped, ginv, *blocks = mix(
        info, within, gate, query, mine, sibling, arrival, wo, ()
    )
    pieces, sent = ring_scatter(*blocks[:6])
    cot_own, cot_other, grad_hidden = cot_pass(info, cot_parts, w2, sent)
    b_parts = ring_gather(*sum_branch(blocks[6], pieces, (grad_hidden,)))

    low2, mean2, inv2, middle, hidden, grad_pre = feed_up(
        info, x_rows, b_parts, gain2, w1, grad_hidden, (cot_own,)
    )
    *blocks, sums = back_blocks("back_feed", info, [(grad_pre, w1)], gain2, low2)
    pieces, sent = ring_scatter(*blocks[:6])
    low2_own, low2_other = turn("turn_low2", info, low2, (blocks[0],))
    feed_other = weight_half(
        "feed_other", [(cot_other, [hidden]), (low2_other, [grad_pre])], None, (blocks[0],)
    )
    feed_got = lax.ppermute(feed_other, "seq", SWAP)
    pin(feed_got)
    feed_total = weight_half(
        "feed_own", [(cot_own, [hidden]), (low2_own, [grad_pre])], feed_got, (hold(sent),)
    )
    grad_middle, gain2_grad, half_a, half_b = norm_back(
        "norm_back2", info, blocks[6], sums, pieces, gain2, middle, mean2, inv2, cotangent, True,
        (feed_total,),
    )
    g_parts = ring_gather(half_a, half_b)
    feed_blocks = exchange(feed_total, PLANE)

    branch, grad_gate, kept, own, give = back_mix(
        info, g_parts, wo, gate, grouped, ginv, query, arrival, (feed_total,)
    )

    def fill_turn():
        made["branch_t"] = turn("turn_branch", info, branch, (give,), True)
        made["feed"] = matmul_cols(
            "feed_down", hidden, w2, BF16, (made["branch_t"][0],), 1024
        )
        return (made["feed"], feed_blocks)

    def fill_retain(token):
        made["r"] = retain_back(
            info, kept, value, decay, key, query, weighted, mine, sibling, arrival, cosine, sine,
            (token,),
        )
        return (made["r"][0],)

    def fill_other(token):
        made["other"] = weight_half(
            "mix_other",
            [
                (made["branch_t"][1], [mixed]),
                (low1_other, [grad_gate, made["r"][0]]),
            ],
            None,
            (token,),
        )
        return (made["other"],)

    far_mine, far_sibling = state_scan(
        info, behind, own, give, True, "_b",
        (fill_turn, fill_retain, fill_other, lambda token: ()),
    )
    feed = lax.psum_scatter(made["feed"], "head", scatter_dimension=1, tiled=True)
    mix_got = lax.ppermute(made["other"], "seq", SWAP)
    pin(mix_got)
    mix_total = weight_half(
        "mix_own",
        [(made["branch_t"][0], [mixed]), (low1_own, [grad_gate, made["r"][0]])],
        mix_got,
        (far_mine,),
    )
    grad_query, near_key, near_value = made["r"]
    grad_key, grad_value = key_value_back(
        info, far_mine, far_sibling, key, value, departure, near_key, near_value, cosine, sine,
        (mix_total,),
    )
    kv_other = weight_half(
        "kv_other", [(low1_other, [grad_key, grad_value])], None, (feed,)
    )
    kv_got = lax.ppermute(kv_other, "seq", SWAP)
    pin(kv_got)
    *blocks, sums = back_blocks(
        "back_proj", info,
        [(grad_query, wq), (grad_gate, wg), (grad_key, wk), (grad_value, wv)],
        gain1, low1, (kv_other, feed_blocks),
    )
    pieces, sent = ring_scatter(*blocks[:6])
    kv_blocks = weight_own_y(
        "kv_own", info, low1_own, [grad_key, grad_value], kv_got, sent
    )
    grad_w2, grad_w1 = weight_sum("feed_sum", feed_blocks, [HEADS * VAL] * 2, (kv_blocks[0],))
    mix_x = exchange(mix_total, axis_groups(True))
    grad_x, gain1_grad = norm_back(
        "norm_back1", info, blocks[6], sums, pieces, gain1, layer_in, mean1, inv1, grad_middle,
        False, (kv_blocks[0], grad_w1, mix_x),
    )
    keys, vals = HEADS * KEY, HEADS * VAL
    kv_half = phase_sum("kv_mid", info, X_AT, kv_blocks[3], send_blocks(kv_blocks[:3], False))
    gains = sum_core_x(jnp.concatenate([gain1_grad, gain2_grad], axis=0))
    mix_half = weight_mid(
        "mix_mid", mix_x, gains, (kv_half[0],)
    )
    grad_wo, grad_wg, grad_wq, gains = weight_sum(
        "mix_sum", exchange(mix_half, axis_groups(False)), [vals, vals, keys]
    )
    grad_wk, grad_wv = last_sum(
        "kv_sum", kv_half[3], send_blocks(kv_half[:3], True), (keys, vals)
    )
    output = (middle + feed.astype(F32)).astype(BF16)
    return (
        output,
        grad_x,
        gains[0],
        grad_wq,
        grad_wk,
        grad_wv,
        grad_wg,
        grad_wo.T,
        gains[1],
        grad_w1,
        grad_w2.T,
    )


def solution(mesh):
    rows = P("seq", "head")
    cols = P(None, "head")
    tall = P("head", None)
    return jax.shard_map(
        shards,
        mesh=mesh,
        in_specs=(rows, P(), cols, cols, cols, cols, tall, P(), cols, tall, P(), rows),
        out_specs=(
            rows, rows, P("head"), rows, rows, rows, rows, P("head", "seq"), P("head"), rows,
            P("head", "seq"),
        ),
        check_vma=False,
    )
```

```python
import math

import jax
import jax.numpy as jnp
from jax import lax
from jax.experimental import pallas as pl
from jax.experimental.pallas import tpu as pltpu
from jax.sharding import PartitionSpec as P

KEY = 256
VAL = 512
SIDE = 4
CORES = 2
HEADS = 2
ROWS = 512
HALF = 256
PART = 512
MODEL = 2048
EXTRA = 16
EPSILON = 1e-05
F32 = jnp.float32
BF16 = jnp.bfloat16
VMEM_BYTES = 26 * 1024 * 1024
ORDER = (2, 1, 3, 0)


def head_shift(step):
    return [(h, (h + step) % SIDE) for h in range(SIDE)]


def seq_index(x, y, core):
    return (x * SIDE + y) * CORES + core


def seq_shift(dx, dy, swap=0):
    return [
        (seq_index(x, y, core), seq_index((x + dx) % SIDE, (y + dy) % SIDE, core ^ swap))
        for x in range(SIDE)
        for y in range(SIDE)
        for core in range(CORES)
    ]


SWAP = seq_shift(0, 0, 1)


def up(block):
    return lax.ppermute(block, "head", head_shift(1))


def down(block):
    return lax.ppermute(block, "head", head_shift(SIDE - 1))


def add_low(a, b):
    return (a.astype(F32) + b.astype(F32)).astype(BF16)


def relay(a, b, tokens):
    def body(a, b, to_a, to_b):
        to_a[...] = a[...]
        to_b[...] = b[...]

    return call(
        "relay", body, (1,), [], [(a,), (b,)], [(a.shape, a.dtype), (b.shape, b.dtype)], tokens
    )


def gated(array, tokens):
    n = len(tokens)

    def body(*refs):
        del refs

    out = pl.pallas_call(
        body,
        name="gated",
        in_specs=[pl.BlockSpec(memory_space=pl.ANY)] * (1 + n),
        out_specs=pl.BlockSpec(memory_space=pl.ANY),
        out_shape=pltpu.HBM(array.shape, array.dtype),
        input_output_aliases={0: 0},
    )(in_hbm(array), *[in_hbm(t) if is_pinned(t) else t for t in tokens])
    pin(out)
    return out


def hold(tokens):
    def body(out):
        out[...] = jnp.zeros_like(out)

    return call("hold", body, (1,), [], [], [((8, 128), F32)], tokens)[0]


def gather_direct(block):
    got = {k: lax.ppermute(block, "head", head_shift(k)) for k in (2, 1, 3)}
    return [block, got[1], got[2], got[3]]


def ring_gather(a, b, first=None):
    r1, l1 = up(a), down(b)
    r2, l2 = up(b), down(a)
    on_r, on_l = first(r1, l1) if first else (r1, l1)
    r3, l3 = up(on_r), down(on_l)
    return [a, b, r1, r2, r3, l3, l2, l1]


def ring_scatter(p2a, p2b, p1a, p1b, pma, pmb):
    t1, t2 = up(p2a), down(p2b)
    rb, la = up(p1b), down(pma)
    s1, s2 = add_low(p1a, t1), add_low(pmb, t2)
    ra, lb = up(s1), down(s2)
    return [ra, rb, la, lb], (s1, s2)


def whole(shape):
    return pl.BlockSpec(shape, lambda *_: (0,) * len(shape))


def once(shape):
    return pl.BlockSpec(
        shape, lambda *_: (0,) * len(shape), pipeline_mode=pl.Buffered(buffer_count=1)
    )


PINNED = []


def pin(*arrays):
    PINNED.extend(arrays)


def is_pinned(array):
    return any(array is other for other in PINNED)


def in_hbm(array):
    return pltpu.with_memory_space_constraint(array, pltpu.HBM)


COST_SCALE = 1.0
COSTS = {
    "kv_mid": 100,
    "scan_start_b": 100,
    "relay": 1,
    "hold": 0.1,
    "turn_low2": 1.5,
    "late": 100,
    "scan_end_b": 50,
    "norm1": 5,
    "key_value": 8,
    "query_part": 6,
    "gate": 4,
    "mix": 9,
    "cot_pass": 100,
    "feed_up": 11,
    "back_feed": 7,
    "back_mix": 6,
    "retain_back": 0.6,
    "feed_down": 2,
    "key_value_back": 100,
    "back_proj": 0.1,
    "feed_other": 5,
    "feed_own": 8,
    "mix_other": 0.180,
    "mix_own": 1,
    "kv_other": 0.90,
    "kv_own": 0.1,
    "feed_sum": 0.1,
    "mix_sum": 2,
    "kv_sum": 0.1,
    "norm_back1": 0.1,
    "norm_back2": 100,
}


def call(name, body, grid, scalars, ins, outs, tokens=(), scratch=(), keep=False):
    arrays = [in_hbm(item[0]) if is_pinned(item[0]) else item[0] for item in ins]
    in_specs = [once(i[0].shape) if len(i) == 1 else pl.BlockSpec(i[1], i[2]) for i in ins]
    out_specs = [whole(o[0]) if len(o) == 2 else pl.BlockSpec(o[2], o[3]) for o in outs]
    out_shape = [jax.ShapeDtypeStruct(o[0], o[1]) for o in outs]
    keep = range(len(outs)) if keep is True else (keep or ())
    out_shape = [
        pltpu.HBM(o.shape, o.dtype) if i in keep else o for i, o in enumerate(out_shape)
    ]
    n_in, n_tok, n_sc = len(arrays), len(tokens), len(scalars)
    tokens = [in_hbm(t) if is_pinned(t) else t for t in tokens]
    in_specs += [pl.BlockSpec(memory_space=pl.ANY)] * n_tok

    def run(*refs):
        body(*refs[: n_sc + n_in], *refs[n_sc + n_in + n_tok :])

    results = pl.pallas_call(
        run,
        name=name,
        grid_spec=pltpu.PrefetchScalarGridSpec(
            num_scalar_prefetch=n_sc,
            grid=grid,
            in_specs=in_specs,
            out_specs=out_specs,
            scratch_shapes=list(scratch),
        ),
        out_shape=out_shape,
        compiler_params=pltpu.CompilerParams(
            dimension_semantics=("arbitrary",) * len(grid), vmem_limit_bytes=VMEM_BYTES
        ),
        cost_estimate=pl.CostEstimate(
            flops=int(COSTS.get(name, 0.1) * COST_SCALE * 1.1e9),
            bytes_accessed=0,
            transcendentals=0,
        ),
    )(*scalars, *arrays, *tokens)
    pin(*[results[i] for i in keep])
    return results


def dot(left, right):
    return jnp.dot(left, right, preferred_element_type=F32)


def dot_t(left, right):
    return lax.dot_general(left, right, (((1,), (1,)), ((), ())), preferred_element_type=F32)


def t_dot(left, right):
    return lax.dot_general(left, right, (((0,), (0,)), ((), ())), preferred_element_type=F32)


def rotate(rows, cosine, sine):
    half = rows.shape[-1] // 2
    first, second = rows[:, :half], rows[:, half:]
    return jnp.concatenate([first * cosine - second * sine, second * cosine + first * sine], axis=1)


def sigmoid(v):
    return 0.5 + 0.5 * jnp.tanh(0.5 * v)


def head_col(info, k):
    return pl.multiple_of(lax.rem(info[0] + SIDE - k, SIDE) * PART, PART)


CHUNK = 16


def norm_rows(info, load, gain, low, mean_ref, inv_ref, own=None):
    for half in range(2):

        def step(i, _):
            at = pl.multiple_of(i * CHUNK, CHUNK)
            out = pl.ds(pl.multiple_of(half * HALF + i * CHUNK, CHUNK), CHUNK)
            parts = [load(k, half, at) for k in range(SIDE)]
            if own is not None:
                own[out, :] = parts[0]
            mean = sum(jnp.sum(p, axis=1, keepdims=True) for p in parts) / MODEL
            parts = [p - mean for p in parts]
            var = sum(jnp.sum(p * p, axis=1, keepdims=True) for p in parts) / MODEL
            inv = lax.rsqrt(var + EPSILON)
            mean_ref[out, :] = mean
            inv_ref[out, :] = inv
            for k in range(SIDE):
                cols = pl.ds(head_col(info, k), PART)
                low[out, cols] = (parts[k] * inv * gain[:, cols]).astype(BF16)
            return 0

        lax.fori_loop(0, HALF // CHUNK, step, 0, unroll=4)


def chunk_of(part, half, at):
    return part[pl.ds(pl.multiple_of(half * HALF + at, CHUNK), CHUNK), :].astype(F32)


def norm1(info, parts, gain, cotangent):
    def body(info, *refs):
        x = refs[:8]
        gain, cot, low, mean, inv, cot_out, rows = refs[8:]
        cot_out[...] = cot[...]
        for k in range(SIDE):
            rows[k, :HALF] = x[2 * k][...]
            rows[k, HALF:] = x[2 * k + 1][...]
        norm_rows(
            info,
            lambda k, half, at: x[2 * k + half][pl.ds(at, CHUNK), :].astype(F32),
            gain,
            low,
            mean,
            inv,
        )

    return call(
        "norm1",
        body,
        (1,),
        [info],
        [(p,) for p in parts] + [(gain,), (cotangent,)],
        [
            ((ROWS, MODEL), BF16),
            ((ROWS, 1), F32),
            ((ROWS, 1), F32),
            ((ROWS, PART), BF16),
            ((SIDE, ROWS, PART), BF16),
        ],
        keep=(4,),
    )


def key_value(info, low, wk, wv, cosine, sine, departure):
    def body(info, low, wk, wv, cosine, sine, departure, key, value, own, give):
        head = pl.program_id(0)
        k = rotate(dot(low[...], wk[...]), cosine[...], sine[...]).astype(BF16)
        key[...] = k
        v = dot(low[...], wv[...]).astype(BF16)
        value[...] = v
        state = t_dot((k.astype(F32) * departure[0]).astype(BF16), v)

        @pl.when(head == info[1])
        def _():
            own[...] = state

        @pl.when(head != info[1])
        def _():
            give[...] = state.astype(BF16)

    by_head = lambda h, *_: (0, h)
    return call(
        "key_value",
        body,
        (HEADS,),
        [info],
        [
            (low,),
            (wk, (MODEL, KEY), by_head),
            (wv, (MODEL, VAL), by_head),
            (cosine,),
            (sine,),
            (departure, (1, ROWS, 1), lambda h, *_: (h, 0, 0)),
        ],
        [
            ((ROWS, HEADS * KEY), BF16, (ROWS, KEY), by_head),
            ((ROWS, HEADS * VAL), BF16, (ROWS, VAL), by_head),
            ((KEY, VAL), F32),
            ((KEY, VAL), BF16),
        ],
        keep=(0, 1),
    )


def query_part(low, wq, key, value, decay, cosine, sine, tokens):
    def body(low, wq, key, value, decay, cosine, sine, query, weighted, within):
        q = rotate(dot(low[...], wq[...]), cosine[...], sine[...]).astype(BF16)
        query[...] = q
        w = (dot_t(q, key[...]) * decay[0]).astype(BF16)
        weighted[0] = w
        within[...] = dot(w, value[...])

    by_head = lambda h, *_: (0, h)
    cube = lambda h, *_: (h, 0, 0)
    return call(
        "query_part",
        body,
        (HEADS,),
        [],
        [
            (low,),
            (wq, (MODEL, KEY), by_head),
            (key, (ROWS, KEY), by_head),
            (value, (ROWS, VAL), by_head),
            (decay, (1, ROWS, ROWS), cube),
            (cosine,),
            (sine,),
        ],
        [
            ((ROWS, HEADS * KEY), BF16, (ROWS, KEY), by_head),
            ((HEADS, ROWS, ROWS), BF16, (1, ROWS, ROWS), cube),
            ((ROWS, HEADS * VAL), F32, (ROWS, VAL), by_head),
        ],
        tokens,
        keep=(0, 1),
    )


def matmul_cols(name, left, right, out_type, tokens=(), block=512):
    def body(left, right, out):
        out[...] = dot(left[...], right[...]).astype(out_type)

    depth, cols = right.shape
    by_col = lambda i, *_: (0, i)
    return call(
        name,
        body,
        (cols // block,),
        [],
        [(left,), (right, (depth, block), by_col)],
        [((left.shape[0], cols), out_type, (left.shape[0], block), by_col)],
        tokens,
        keep=True,
    )[0]


def block_outs(extra):
    tall = ((HALF + extra, PART), BF16)
    return [tall, ((HALF, PART), BF16)] * 3 + [((ROWS, PART), F32)]


def put_blocks(step, make, outs):
    for i in range(2):
        block = make(i)
        for s in range(2):
            k = 2 * s + i

            @pl.when(step == s)
            def _():
                if k == SIDE - 1:
                    outs[6][...] = block
                else:
                    outs[2 * k][:HALF, :] = block[:HALF].astype(BF16)
                    outs[2 * k + 1][...] = block[HALF:].astype(BF16)


def pick(mine, sibling, info, head):
    return jnp.where(info[1] == head, mine[...], sibling[...])


def mix(info, within, gate, query, mine, sibling, arrival, wo, tokens):
    def body(
        info, within, gate, query, mine, sibling, arrival, wo_a, wo_b, mixed, grouped, ginv, *outs
    ):
        step = pl.program_id(0)

        @pl.when(step == 0)
        def _():
            for head in range(HEADS):
                cols = slice(head * VAL, (head + 1) * VAL)
                state = pick(mine, sibling, info, head)
                for half in range(2):
                    rows = slice(half * HALF, (half + 1) * HALF)
                    cross = dot(query[rows, head * KEY : (head + 1) * KEY], state)
                    kept = within[rows, cols] + arrival[head, rows] * cross
                    kept = kept - jnp.mean(kept, axis=1, keepdims=True)
                    inv = lax.rsqrt(jnp.mean(kept * kept, axis=1, keepdims=True) + float(KEY))
                    group = kept * inv
                    g = gate[rows, cols].astype(F32)
                    ginv[head, rows] = inv
                    grouped[rows, cols] = group.astype(BF16)
                    mixed[rows, cols] = (group * (g * sigmoid(g))).astype(BF16)

        put_blocks(step, lambda i: dot(mixed[...], (wo_a, wo_b)[i][...]), outs)

    cols = HEADS * VAL
    return call(
        "mix",
        body,
        (2,),
        [info],
        [
            (within,),
            (gate,),
            (query,),
            (mine,),
            (sibling,),
            (arrival,),
            (wo, (cols, PART), lambda i, info: (0, info[2 + 2 * i])),
            (wo, (cols, PART), lambda i, info: (0, info[3 + 2 * i])),
        ],
        [((ROWS, cols), BF16), ((ROWS, cols), BF16), ((HEADS, ROWS, 1), F32)] + block_outs(0),
        tokens,
        keep=(0, 1),
    )


def sum_branch(p0, pieces, tokens):
    def body(p0, ra, rb, la, lb, a, b):
        a[...] = (p0[:HALF] + ra[...].astype(F32) + la[...].astype(F32)).astype(BF16)
        b[...] = (p0[HALF:] + rb[...].astype(F32) + lb[...].astype(F32)).astype(BF16)

    return call(
        "sum_branch",
        body,
        (1,),
        [],
        [(p0,)] + [(p,) for p in pieces],
        [((HALF, PART), BF16), ((HALF, PART), BF16)],
        tokens,
    )


def feed_up(info, x_rows, b_parts, gain, w1, grad_hidden, tokens):
    block = 512

    def body(info, *refs):
        x, b = refs[0], refs[1:9]
        gain, w1, grad_hidden, ffn_in, mean, inv, own, hidden, grad_pre = refs[9:]

        @pl.when(pl.program_id(0) == 0)
        def _():
            def load(k, half, at):
                branch = b[2 * k + half][pl.ds(at, CHUNK), :].astype(F32)
                return chunk_of(x.at[k], half, at) + branch

            norm_rows(info, load, gain, ffn_in, mean, inv, own)

        pre = dot(ffn_in[...], w1[...])
        cdf = 0.5 * (1.0 + lax.erf(pre * (2.0**-0.5)))
        hidden[...] = (pre * cdf).astype(BF16)
        pdf = jnp.exp(-0.5 * pre * pre) * ((2.0 * math.pi) ** -0.5)
        grad_pre[...] = ((cdf + pre * pdf) * grad_hidden[...].astype(F32)).astype(BF16)

    by_col = lambda i, *_: (0, i)
    cols = w1.shape[1]
    tall = ((ROWS, cols), BF16, (ROWS, block), by_col)
    return call(
        "feed_up",
        body,
        (cols // block,),
        [info],
        [(x_rows,)]
        + [(p,) for p in b_parts]
        + [
            (gain,),
            (w1, (MODEL, block), by_col),
            (grad_hidden, (ROWS, block), by_col),
        ],
        [
            ((ROWS, MODEL), BF16),
            ((ROWS, 1), F32),
            ((ROWS, 1), F32),
            ((ROWS, PART), F32),
            tall,
            tall,
        ],
        tokens,
        keep=(1, 2, 3),
    )


def back_blocks(name, info, pairs, gain, low, tokens=()):
    n = len(pairs)

    def body(info, *refs):
        grads, weights = refs[:n], refs[n : 3 * n]
        gains, lows = refs[3 * n : 3 * n + 2], refs[3 * n + 2 : 3 * n + 4]
        outs, sums, acc = refs[3 * n + 4 : 3 * n + 11], refs[3 * n + 11], refs[3 * n + 12]
        step = pl.program_id(0)
        lane = lax.broadcasted_iota(jnp.int32, (ROWS, 128), 1)

        @pl.when(step == 0)
        def _():
            acc[...] = jnp.zeros_like(acc)

        def make(i):
            total = dot_t(grads[0][...], weights[2 * 0 + i][...])
            for j in range(1, n):
                total = total + dot_t(grads[j][...], weights[2 * j + i][...])
            first = jnp.sum(total * gains[i][...], axis=1, keepdims=True) / MODEL
            second = jnp.sum(total * lows[i][...].astype(F32), axis=1, keepdims=True) / MODEL
            acc[...] += jnp.where(lane == 0, first, jnp.where(lane == 1, second, 0.0))
            return total

        put_blocks(step, make, outs)

        @pl.when(step == 1)
        def _():
            turned = acc[...].T[:EXTRA]
            sums[...] = turned
            for k in range(SIDE - 1):
                outs[2 * k][HALF:, :] = turned.astype(BF16)

    def by_row(j):
        return lambda i, info: (info[2 + j + 2 * i], 0)

    def by_col(j):
        return lambda i, info: (0, info[2 + j + 2 * i])

    return call(
        name,
        body,
        (2,),
        [info],
        [(g,) for g, _ in pairs]
        + [(in_hbm(w), (PART, w.shape[1]), by_row(j)) for _, w in pairs for j in range(2)]
        + [(gain, (1, PART), by_col(j)) for j in range(2)]
        + [(low, (ROWS, PART), by_col(j)) for j in range(2)],
        block_outs(EXTRA) + [((EXTRA, PART), F32)],
        tokens,
        [pltpu.VMEM((ROWS, 128), F32)],
        keep=(6,),
    )


def norm_back(
    name, info, p0, sums, pieces, gain, rows, mean, inv, residual, low_out, tokens
):
    def body(
        info, p0, sums, ra, rb, la, lb, gain, rows, mean, inv, residual, grad, gain_grad, *low
    ):
        scale = gain[:, pl.ds(head_col(info, 0), PART)]
        total = sums[...] + ra[HALF:].astype(F32) + la[HALF:].astype(F32)
        total = jnp.concatenate([total, jnp.zeros((128 - EXTRA, PART), F32)], axis=0).T
        acc = jnp.zeros((1, PART), F32)
        for half, (one, two) in enumerate(((ra, la), (rb, lb))):
            for quarter in range(2):
                at = slice(quarter * 128, (quarter + 1) * 128)
                out = slice(half * HALF + quarter * 128, half * HALF + (quarter + 1) * 128)
                g = p0[out] + one[at].astype(F32) + two[at].astype(F32)
                normed = (rows[out].astype(F32) - mean[out]) * inv[out]
                acc = acc + jnp.sum(g * normed, axis=0, keepdims=True)
                back = inv[out] * (g * scale - total[out, 0:1] - normed * total[out, 1:2])
                new = residual[out].astype(F32) + back
                grad[out] = new
                if low_out:
                    low[half][at] = new.astype(BF16)
        gain_grad[...] = acc

    outs = [((ROWS, PART), F32), ((1, PART), F32)]
    if low_out:
        outs += [((HALF, PART), BF16)] * 2
    return call(
        name,
        body,
        (1,),
        [info],
        [(p0,), (sums,)]
        + [(p,) for p in pieces]
        + [(gain,), (rows,), (mean,), (inv,), (residual,)],
        outs,
        tokens,
    )


def back_mix(info, parts, wo, gate, grouped, ginv, query, arrival, tokens):
    def body(info, *refs):
        parts = refs[:8]
        wo, gate, grouped, ginv, query, arrival, branch, grad_gate, kept, own, give = refs[8:]
        head = pl.program_id(0)

        @pl.when(head == 0)
        def _():
            for k in range(SIDE):
                cols = pl.ds(head_col(info, k), PART)
                branch[:HALF, cols] = parts[2 * k][...]
                branch[HALF:, cols] = parts[2 * k + 1][...]

        for half in range(2):
            rows = slice(half * HALF, (half + 1) * HALF)
            m = dot_t(branch[rows], wo[...])
            g = gate[rows].astype(F32)
            gate_s = sigmoid(g)
            group = grouped[rows].astype(F32)
            slope = gate_s * (1.0 + g * (1.0 - gate_s))
            grad_gate[rows] = (m * group * slope).astype(BF16)
            e = m * (g * gate_s)
            e = ginv[0, rows] * (
                e
                - jnp.mean(e, axis=1, keepdims=True)
                - group * jnp.mean(e * group, axis=1, keepdims=True)
            )
            kept[rows] = e.astype(BF16)
        moved = (query[...].astype(F32) * arrival[0]).astype(BF16)
        state = t_dot(moved, kept[...])

        @pl.when(head == info[1])
        def _():
            own[...] = state

        @pl.when(head != info[1])
        def _():
            give[...] = state.astype(BF16)

    by_head = lambda h, *_: (0, h)
    cube = lambda h, *_: (h, 0, 0)
    cols = HEADS * VAL
    return call(
        "back_mix",
        body,
        (HEADS,),
        [info],
        [(p,) for p in parts]
        + [
            (wo, (VAL, MODEL), lambda h, *_: (h, 0)),
            (gate, (ROWS, VAL), by_head),
            (grouped, (ROWS, VAL), by_head),
            (ginv, (1, ROWS, 1), cube),
            (query, (ROWS, KEY), by_head),
            (arrival, (1, ROWS, 1), cube),
        ],
        [
            ((ROWS, MODEL), BF16),
            ((ROWS, cols), BF16, (ROWS, VAL), by_head),
            ((ROWS, cols), BF16, (ROWS, VAL), by_head),
            ((KEY, VAL), F32),
            ((KEY, VAL), BF16),
        ],
        tokens,
        keep=(1, 2),
    )


def retain_back(info, kept, value, decay, key, query, weighted, mine, sibling, arrival, cosine, sine, tokens):
    def body(
        info, kept, value, decay, key, query, weighted, mine, sibling, arrival, cosine, sine,
        grad_query, near_key, near_value,
    ):
        head = pl.program_id(0)
        e = kept[...]
        s = (dot_t(e, value[...]) * decay[0]).astype(BF16)
        state = pick(mine, sibling, info, head)
        gq = dot(s, key[...]) + arrival[0] * dot_t(e, state)
        grad_query[...] = rotate(gq, cosine[...], -sine[...]).astype(BF16)
        near_key[...] = t_dot(s, query[...])
        near_value[...] = t_dot(weighted[0], e)

    by_head = lambda h, *_: (0, h)
    cube = lambda h, *_: (h, 0, 0)
    keys, vals = HEADS * KEY, HEADS * VAL
    return call(
        "retain_back",
        body,
        (HEADS,),
        [info],
        [
            (kept, (ROWS, VAL), by_head),
            (value, (ROWS, VAL), by_head),
            (decay, (1, ROWS, ROWS), cube),
            (key, (ROWS, KEY), by_head),
            (query, (ROWS, KEY), by_head),
            (weighted, (1, ROWS, ROWS), cube),
            (mine,),
            (sibling,),
            (arrival, (1, ROWS, 1), cube),
            (cosine,),
            (sine,),
        ],
        [
            ((ROWS, keys), BF16, (ROWS, KEY), by_head),
            ((ROWS, keys), F32, (ROWS, KEY), by_head),
            ((ROWS, vals), F32, (ROWS, VAL), by_head),
        ],
        tokens,
        keep=True,
    )


def key_value_back(info, mine, sibling, key, value, departure, near_key, near_value, cosine, sine, tokens):
    def body(
        info, mine, sibling, key, value, departure, near_key, near_value, cosine, sine,
        grad_key, grad_value,
    ):
        state = pick(mine, sibling, info, pl.program_id(0))
        gk = near_key[...] + departure[0] * dot_t(value[...], state)
        grad_key[...] = rotate(gk, cosine[...], -sine[...]).astype(BF16)
        gv = near_value[...] + departure[0] * dot(key[...], state)
        grad_value[...] = gv.astype(BF16)

    by_head = lambda h, *_: (0, h)
    keys, vals = HEADS * KEY, HEADS * VAL
    return call(
        "key_value_back",
        body,
        (HEADS,),
        [info],
        [
            (mine,),
            (sibling,),
            (key, (ROWS, KEY), by_head),
            (value, (ROWS, VAL), by_head),
            (departure, (1, ROWS, 1), lambda h, *_: (h, 0, 0)),
            (near_key, (ROWS, KEY), by_head),
            (near_value, (ROWS, VAL), by_head),
            (cosine,),
            (sine,),
        ],
        [
            ((ROWS, keys), BF16, (ROWS, KEY), by_head),
            ((ROWS, vals), BF16, (ROWS, VAL), by_head),
        ],
        tokens,
    )


def turn(name, info, low, tokens=(), keep=False):
    xs = 2

    def body(info, low, own, other, scratch):
        scratch[...] = low[...].T
        for x in range(xs):
            for y in range(SIDE):
                base = (x * SIDE + y) * CORES * 64
                mine = pl.ds(pl.multiple_of(base + info[1] * 64, 64), 64)
                far = pl.ds(pl.multiple_of(base + (1 - info[1]) * 64, 64), 64)
                own[x, y] = scratch[mine, :]
                other[x, y] = scratch[far, :]

    out = ((SIDE, SIDE, 64, ROWS), BF16, (xs, SIDE, 64, ROWS), lambda i, *_: (i, 0, 0, 0))
    own, other = call(
        name,
        body,
        (SIDE // xs,),
        [info],
        [(low, (ROWS, xs * PART), lambda i, *_: (0, i))],
        [out, out],
        tokens,
        [pltpu.VMEM((xs * PART, ROWS), BF16)],
        keep=keep,
    )
    flat = own.reshape(-1, ROWS), other.reshape(-1, ROWS)
    if keep:
        pin(*flat)
    return flat


def cot_pass(info, parts, w2, tokens):
    xs = 2

    def body(info, a, b, c, d, w2, own, other, out, whole_rows, scratch):
        step = pl.program_id(0)

        @pl.when(step == 0)
        def _():
            for k, part in enumerate((a, b, c, d)):
                whole_rows[:, pl.ds(head_col(info, k), PART)] = part[...]

        out[...] = dot_t(whole_rows[...], w2[...]).astype(BF16)
        cols = pl.ds(pl.multiple_of(step * xs * PART, PART), xs * PART)
        scratch[...] = whole_rows[:, cols].T
        for x in range(xs):
            for y in range(SIDE):
                base = (x * SIDE + y) * CORES * 64
                mine = pl.ds(pl.multiple_of(base + info[1] * 64, 64), 64)
                far = pl.ds(pl.multiple_of(base + (1 - info[1]) * 64, 64), 64)
                own[x, y] = scratch[mine, :]
                other[x, y] = scratch[far, :]

    turned = ((SIDE, SIDE, 64, ROWS), BF16, (xs, SIDE, 64, ROWS), lambda i, *_: (i, 0, 0, 0))
    cols = w2.shape[0]
    own, other, out = call(
        "cot_pass",
        body,
        (2,),
        [info],
        [(p,) for p in parts] + [(w2, (cols // 2, MODEL), lambda i, *_: (i, 0))],
        [turned, turned, ((ROWS, cols), BF16, (ROWS, cols // 2), lambda i, *_: (0, i))],
        tokens,
        [pltpu.VMEM((ROWS, MODEL), BF16), pltpu.VMEM((xs * PART, ROWS), BF16)],
    )
    return own.reshape(-1, ROWS), other.reshape(-1, ROWS), out


def widths(groups):
    return [sum(r.shape[1] for r in rights) for _, rights in groups]


def weight_half(name, groups, arrived=None, tokens=()):
    n_left = len(groups)
    rights = [r for _, rs in groups for r in rs]
    counts = [len(rs) for _, rs in groups]
    n = len(rights)
    width = sum(widths(groups))

    def body(*refs):
        lefts, rest = refs[:n_left], refs[n_left : n_left + n]
        out = refs[-1]
        at = 0
        which = 0
        for left, count in zip(lefts, counts):
            for r in rest[which : which + count]:
                cols = slice(at, at + r.shape[1])
                total = dot(left[...], r[...])
                if arrived is not None:
                    total = total + refs[n_left + n][:, cols].astype(F32)
                out[:, cols] = total.astype(BF16)
                at += r.shape[1]
            which += count

    block = lambda i, *_: (i, 0)
    return call(
        name,
        body,
        (2,),
        [],
        [(left, (ROWS, ROWS), block) for left, _ in groups]
        + [(r,) for r in rights]
        + ([(arrived, (ROWS, width), block)] if arrived is not None else []),
        [((2 * ROWS, width), BF16, (ROWS, width), block)],
        tokens,
        keep=True,
    )[0]


PLANE = [
    [seq_index(x, y, c) for x in range(SIDE) for y in range(SIDE)] for c in range(CORES)
]


def axis_groups(along_x):
    if along_x:
        return [
            [seq_index(x, y, c) for x in range(SIDE)] for y in range(SIDE) for c in range(CORES)
        ]
    return [[seq_index(x, y, c) for y in range(SIDE)] for x in range(SIDE) for c in range(CORES)]


def exchange(total, groups):
    blocks = total
    if total.ndim == 2:
        blocks = total.reshape(len(groups[0]), -1, total.shape[-1])
    blocks = lax.all_to_all(blocks, "seq", 0, 0, axis_index_groups=groups, tiled=True)
    pin(blocks)
    return blocks


def weight_mid(name, blocks, gains, tokens=()):
    count, rows, width = blocks.shape
    step = width // 2
    part = rows // SIDE
    gains = jnp.pad(gains, ((0, EXTRA - gains.shape[0]), (0, step - gains.shape[1])))

    def body(blocks, gains, out):
        total = blocks[0].astype(F32)
        for k in range(1, count):
            total = total + blocks[k].astype(F32)
        for y in range(SIDE):
            out[y, :part] = total[y * part : (y + 1) * part].astype(BF16)
            out[y, part:] = gains[...].astype(BF16)

    return call(
        name,
        body,
        (2,),
        [],
        [(blocks, (count, rows, step), lambda i, *_: (0, 0, i)), (gains,)],
        [
            (
                (SIDE, part + EXTRA, width),
                BF16,
                (SIDE, part + EXTRA, step),
                lambda i, *_: (0, 0, i),
            )
        ],
        tokens,
        keep=True,
    )[0]


def weight_sum(name, blocks, parts, tokens=()):
    count, rows, width = blocks.shape
    extra = rows - 64

    def body(blocks, *outs):
        at = 0
        for out, part in zip(outs, parts):
            cols = slice(at, at + part)
            total = blocks[0, :64, cols].astype(F32)
            for k in range(1, count):
                total = total + blocks[k, :64, cols].astype(F32)
            out[...] = total
            at += part
        if extra:
            total = blocks[0, 64:, :PART].astype(F32)
            for k in range(1, count):
                total = total + blocks[k, 64:, :PART].astype(F32)
            outs[-1][...] = total

    return call(
        name,
        body,
        (1,),
        [],
        [(blocks,)],
        [((64, part), F32) for part in parts] + ([((extra, PART), F32)] if extra else []),
        tokens,
    )


def weight_own_y(name, info, left, rights, arrived, tokens=()):
    n = len(rights)
    width = sum(r.shape[1] for r in rights)
    left = left.reshape(SIDE, SIDE, 64, ROWS)
    arrived = arrived.reshape(SIDE, SIDE, 64, width)
    pin(left)

    def body(info, *refs):
        lefts, rights, got, outs = refs[:2], refs[2 : 2 + n], refs[2 + n : 4 + n], refs[4 + n :]
        step = pl.program_id(0)
        for i in range(2):
            at = 0
            for r in rights:
                cols = slice(at, at + r.shape[1])
                total = dot(lefts[i][...].reshape(HALF, ROWS), r[...])
                total = total + got[i][:, :, :, cols].reshape(HALF, r.shape[1]).astype(F32)
                for s in range(2):

                    @pl.when(step == s)
                    def _():
                        out = outs[2 * s + i]
                        out[:, cols] = total.astype(out.dtype)

                at += r.shape[1]

    def block(j):
        def at(i, info):
            return (0, lax.rem(info[Y_AT] + ORDER_OF(2 * i + j), SIDE), 0, 0)

        return at

    return call(
        name,
        body,
        (2,),
        [info],
        [(left, (SIDE, 1, 64, ROWS), block(j)) for j in range(2)]
        + [(r,) for r in rights]
        + [(arrived, (SIDE, 1, 64, width), block(j)) for j in range(2)],
        [((HALF, width), BF16)] * 3 + [((HALF, width), F32)],
        tokens,
    )


def ORDER_OF(i):
    return jnp.where(i == 0, 2, jnp.where(i == 1, 1, jnp.where(i == 2, 3, 0)))


def phase_sum(name, info, where, base, received, tokens=()):
    width = base.shape[1]

    def body(info, base, a, b, c, *refs):
        outs, scratch = refs[:SIDE], refs[SIDE]
        scratch[...] = base[...] + a[...].astype(F32) + b[...].astype(F32) + c[...].astype(F32)
        for i, k in enumerate(ORDER):
            at = pl.multiple_of(lax.rem(info[where] + k, SIDE) * 64, 64)
            outs[i][...] = scratch[pl.ds(at, 64), :].astype(outs[i].dtype)

    return call(
        name,
        body,
        (1,),
        [info],
        [(base,)] + [(r,) for r in received],
        [((64, width), BF16)] * 3 + [((64, width), F32)],
        tokens,
        [pltpu.VMEM((HALF, width), F32)],
    )


def last_sum(name, base, received, parts):
    def body(base, a, b, c, *outs):
        at = 0
        for out in outs:
            cols = slice(at, at + out.shape[1])
            out[...] = base[:, cols] + sum(r[:, cols].astype(F32) for r in (a, b, c))
            at += out.shape[1]

    return call(
        name,
        body,
        (1,),
        [],
        [(base,)] + [(r,) for r in received],
        [((64, w), F32) for w in parts],
    )


def shift_of(along_x):
    return (lambda k: seq_shift(k, 0)) if along_x else (lambda k: seq_shift(0, k))


def send_blocks(blocks, along_x):
    shift = shift_of(along_x)
    return [lax.ppermute(b, "seq", shift(k)) for b, k in zip(blocks, ORDER[:3])]


X_AT, Y_AT = 6, 7


def scan_weights(decay, place, reverse):
    x, y, _ = place
    rel = jnp.arange(SIDE)
    origin = lax.rem(y - rel + SIDE, SIDE)
    target = lax.rem(y + rel, SIDE)
    hops = jnp.arange(1, SIDE)
    if reverse:
        row = origin
        before, counts = SIDE * (SIDE - hops - 1), x + (SIDE - hops) < SIDE
        gap = origin[None, :] - target[:, None]
        carry = SIDE - 1 - target
    else:
        row = SIDE - 1 - origin
        before, counts = SIDE * (hops - 1), x >= hops
        gap = target[:, None] - origin[None, :]
        carry = target
    gap = gap.reshape(-1)
    power = jnp.concatenate([row, before, jnp.maximum(gap - 1, 0), carry]).astype(F32)
    keep = jnp.concatenate([row >= 0, counts, gap > 0, carry >= 0]).astype(F32)
    values = keep * jnp.exp(2.0 * jnp.log(decay) * power)
    return jnp.concatenate([decay[None], values, jnp.zeros((4,), F32)])


W_ROW, W_BEFORE, W_ANSWER, W_CARRY = 1, 5, 8, 24
QUARTER = KEY // SIDE


def state_scan(info, weights, own, give, reverse, tag, fills):
    far = 1 if reverse else 0

    def start_body(info, w, own, got, p2, p1, p3, p0, scratch):
        a, b = own[...], got[...].astype(F32)
        scratch[...] = jnp.where(info[1] == far, w[0] * a + b, a + w[0] * b).astype(BF16)
        for k, out in zip(ORDER, (p2, p1, p3, p0)):
            at = pl.multiple_of(lax.rem(info[Y_AT] + k, SIDE) * QUARTER, QUARTER)
            out[...] = scratch[pl.ds(at, QUARTER), :]

    piece = ((QUARTER, VAL), BF16)
    got = lax.ppermute(give, "seq", SWAP)
    sent = call(
        "scan_start" + tag, start_body, (1,), [info, weights], [(own,), (got,)], [piece] * 4,
        fills[0](), scratch=[pltpu.VMEM((KEY, VAL), BF16)],
    )
    at2, at1, at3 = send_blocks(sent[:3], False)
    pieces = [sent[3], at1, at2, at3]

    def row_body(w, p0, p1, p2, p3, total):
        total[...] = sum(
            w[W_ROW + j] * p[...].astype(F32) for j, p in enumerate((p0, p1, p2, p3))
        ).astype(BF16)

    row = call(
        "scan_row" + tag, row_body, (1,), [weights], [(p,) for p in pieces], [piece],
        fills[1](sent[0]),
    )[0]
    at2, at1, at3 = send_blocks([row] * 3, True)

    def answer_body(w, p0, p1, p2, p3, b1, b2, b3, *outs):
        p = [r[...].astype(F32) for r in (p0, p1, p2, p3)]
        before = sum(w[W_BEFORE + j] * r[...].astype(F32) for j, r in enumerate((b1, b2, b3)))
        for k, out in zip(ORDER, outs):
            total = w[W_CARRY + k] * before
            for j in range(SIDE):
                total = total + w[W_ANSWER + SIDE * k + j] * p[j]
            out[...] = total.astype(BF16)

    answers = call(
        "scan_answer" + tag, answer_body, (1,), [weights],
        [(p,) for p in pieces] + [(at1,), (at2,), (at3,)], [piece] * 4, fills[2](row),
    )
    at2, at1, at3 = send_blocks(answers[:3], False)

    def end_body(info, w, b0, b1, b2, b3, own, got, mine, theirs, scratch):
        for k, b in enumerate((b0, b1, b2, b3)):
            at = pl.multiple_of(lax.rem(info[Y_AT] + SIDE - k, SIDE) * QUARTER, QUARTER)
            scratch[pl.ds(at, QUARTER), :] = b[...].astype(F32)
        chip = scratch[...]
        is_far = info[1] == far
        later = w[0] * chip + jnp.where(is_far, own[...], got[...].astype(F32))
        mine[...] = jnp.where(is_far, chip, later).astype(BF16)
        theirs[...] = jnp.where(is_far, later, chip).astype(BF16)

    state = ((KEY, VAL), BF16)
    mine, theirs = call(
        "scan_end" + tag, end_body, (1,), [info, weights],
        [(answers[3],), (at1,), (at2,), (at3,), (own,), (got,)], [state, state],
        fills[3](answers[0]), scratch=[pltpu.VMEM((KEY, VAL), F32)],
    )
    return mine, lax.ppermute(theirs, "seq", SWAP)


def sum_core_x(values):
    values = values + lax.ppermute(values, "seq", SWAP)
    return values + sum(lax.ppermute(values, "seq", seq_shift(k, 0)) for k in (1, 2, 3))


def shards(layer_in, gain1, wq, wk, wv, wg, wo, gain2, w1, w2, starts, cotangent):
    seq_rank = lax.axis_index("seq")
    head_rank = lax.axis_index("head")
    x, y, core = (
        seq_rank // (SIDE * CORES),
        (seq_rank // CORES) % SIDE,
        seq_rank % CORES,
    )
    place = (x, y, core)
    PINNED.clear()
    info = jnp.stack(
        [head_rank, core] + [(head_rank + k) % SIDE for k in ORDER] + [x, y]
    ).astype(jnp.int32)
    gain1, gain2 = gain1[None], gain2[None]

    offsets = jnp.arange(ROWS, dtype=jnp.int32)
    positions = seq_rank * ROWS + offsets
    member = positions[:, None] >= starts[None, :]
    doc_ids = jnp.sum(member.astype(jnp.int32), axis=-1) - 1
    last_start = jnp.max(jnp.where(member, starts[None, :], 0), axis=-1)
    relative = (positions - last_start).astype(F32)
    prior_doc = jnp.sum((seq_rank * ROWS - 1 >= starts).astype(jnp.int32)) - 1
    half_dim = KEY // 2
    frequency = jnp.exp(-math.log(10000.0) * jnp.arange(half_dim, dtype=F32) / half_dim)
    angles = relative[:, None] * frequency[None, :]
    cosine, sine = jnp.cos(angles), jnp.sin(angles)
    head_ids = (head_rank * HEADS + jnp.arange(HEADS, dtype=jnp.int32)).astype(F32)
    log_decay = jnp.log1p(-jnp.exp2(-5.0 - head_ids))
    gap_grid = offsets[:, None] - offsets[None, :]
    keep = (gap_grid >= 0) & (doc_ids[:, None] == doc_ids[None, :])
    gap_float = jnp.where(gap_grid >= 0, gap_grid, 0).astype(F32)
    decay = jnp.where(keep[None], jnp.exp(gap_float[None] * log_decay[:, None, None]), 0.0)
    step_float = offsets.astype(F32)
    arrival = jnp.exp((step_float[None, :] + 1.0) * log_decay[:, None]) * (
        doc_ids == prior_doc
    ).astype(F32)
    departure = jnp.exp((ROWS - 1.0 - step_float)[None, :] * log_decay[:, None]) * (
        doc_ids == doc_ids[ROWS - 1]
    ).astype(F32)
    arrival, departure = arrival[:, :, None], departure[:, :, None]
    pin(decay)
    rank_decay = lax.dynamic_index_in_dim(jnp.exp(ROWS * log_decay), core, 0, False)
    ahead = scan_weights(rank_decay, place, False)
    behind = scan_weights(rank_decay, place, True)

    tables = (arrival, departure, ahead, behind, info)
    x_parts = ring_gather(
        layer_in[:HALF], layer_in[HALF:], lambda r, l: relay(r, l, tables)
    )
    low1, mean1, inv1, cot_again, x_rows = norm1(info, x_parts, gain1, cotangent)
    cot_parts = gather_direct(cot_again)
    key, value, own, give = key_value(info, low1, wk, wv, cosine, sine, departure)
    made = {}

    def fill_query():
        made["q"] = query_part(low1, wq, key, value, decay, cosine, sine, (give,))
        return (made["q"][0],)

    def fill_gate(token):
        made["gate"] = matmul_cols("gate", low1, wg, BF16, (token, *cot_parts[1:]))
        return (made["gate"],)

    def fill_turn(token):
        made["low1_t"] = turn("turn_low1", info, low1, (token,), True)
        return (made["low1_t"][0],)

    mine, sibling = state_scan(
        info, ahead, own, give, False, "_a", (fill_query, fill_gate, fill_turn, lambda token: ())
    )
    query, weighted, within = made["q"]
    gate = made["gate"]
    low1_own, low1_other = made["low1_t"]
    mixed, grouped, ginv, *blocks = mix(
        info, within, gate, query, mine, sibling, arrival, wo, ()
    )
    pieces, sent = ring_scatter(*blocks[:6])
    cot_own, cot_other, grad_hidden = cot_pass(info, cot_parts, w2, sent)
    b_parts = ring_gather(*sum_branch(blocks[6], pieces, (grad_hidden,)))

    low2, mean2, inv2, middle, hidden, grad_pre = feed_up(
        info, x_rows, b_parts, gain2, w1, grad_hidden, (cot_own,)
    )
    low2_own, low2_other = turn("turn_low2", info, low2)
    feed_other = weight_half(
        "feed_other", [(cot_other, [hidden]), (low2_other, [grad_pre])], None, (low2_own,)
    )
    *blocks, sums = back_blocks(
        "back_feed", info, [(grad_pre, w1)], gain2, low2, (feed_other,)
    )
    pieces, sent = ring_scatter(*blocks[:6])
    feed_got = lax.ppermute(feed_other, "seq", SWAP)
    feed_total = weight_half(
        "feed_own", [(cot_own, [hidden]), (low2_own, [grad_pre])], feed_got
    )
    grad_middle, gain2_grad, half_a, half_b = norm_back(
        "norm_back2", info, blocks[6], sums, pieces, gain2, middle, mean2, inv2, cotangent, True,
        (feed_total,),
    )
    g_parts = ring_gather(half_a, half_b)
    feed_blocks = exchange(feed_total, PLANE)

    branch, grad_gate, kept, own, give = back_mix(
        info, g_parts, wo, gate, grouped, ginv, query, arrival, (feed_total,)
    )

    branch_own, branch_other = turn("turn_branch", info, branch, (give,), True)
    grad_query, near_key, near_value = retain_back(
        info, kept, value, decay, key, query, weighted, mine, sibling, arrival, cosine, sine,
        (branch_own,),
    )
    mix_other = weight_half(
        "mix_other",
        [(branch_other, [mixed]), (low1_other, [grad_gate, grad_query])],
        None,
        (grad_query,),
    )
    mix_got = lax.ppermute(mix_other, "seq", SWAP)

    def fill_own(token):
        made["own"] = weight_half(
            "mix_own",
            [(branch_own, [mixed]), (low1_own, [grad_gate, grad_query])],
            mix_got,
            (token,),
        )
        return (made["own"],)

    feed = matmul_cols("feed_down", hidden, w2, BF16, (mix_other,), 1024)

    far_mine, far_sibling = state_scan(
        info, behind, own, give, True, "_b",
        (lambda: (feed, feed_blocks), fill_own, lambda token: (), lambda token: ()),
    )
    feed = lax.psum_scatter(feed, "head", scatter_dimension=1, tiled=True)
    mix_x = exchange(gated(made["own"], (far_mine,)), axis_groups(True))
    grad_key, grad_value = key_value_back(
        info, far_mine, far_sibling, key, value, departure, near_key, near_value, cosine, sine,
        (),
    )
    kv_other = weight_half(
        "kv_other", [(low1_other, [grad_key, grad_value])]
    )
    kv_got = lax.ppermute(kv_other, "seq", SWAP)
    *blocks, sums = back_blocks(
        "back_proj", info,
        [(grad_query, wq), (grad_gate, wg), (grad_key, wk), (grad_value, wv)],
        gain1, low1, (kv_other, feed_blocks),
    )
    pieces, sent = ring_scatter(*blocks[:6])
    kv_blocks = weight_own_y(
        "kv_own", info, low1_own, [grad_key, grad_value], kv_got, (*sent, feed)
    )
    grad_w2, grad_w1 = weight_sum("feed_sum", feed_blocks, [HEADS * VAL] * 2, (kv_blocks[0],))
    grad_x, gain1_grad = norm_back(
        "norm_back1", info, blocks[6], sums, pieces, gain1, layer_in, mean1, inv1, grad_middle,
        False, (kv_blocks[0], grad_w1),
    )
    keys, vals = HEADS * KEY, HEADS * VAL
    kv_sent = send_blocks(kv_blocks[:3], False)
    kv_half = phase_sum("kv_mid", info, X_AT, kv_blocks[3], kv_sent)
    gains = sum_core_x(jnp.concatenate([gain1_grad, gain2_grad], axis=0))
    mix_half = weight_mid("mix_mid", mix_x, gains)
    grad_wo, grad_wg, grad_wq, gains = weight_sum(
        "mix_sum", exchange(mix_half, axis_groups(False)), [vals, vals, keys]
    )
    grad_wk, grad_wv = last_sum(
        "kv_sum", kv_half[3], send_blocks(kv_half[:3], True), (keys, vals)
    )
    output = (middle + feed.astype(F32)).astype(BF16)
    return (
        output,
        grad_x,
        gains[0],
        grad_wq,
        grad_wk,
        grad_wv,
        grad_wg,
        grad_wo.T,
        gains[1],
        grad_w1,
        grad_w2.T,
    )


def solution(mesh):
    rows = P("seq", "head")
    cols = P(None, "head")
    tall = P("head", None)
    return jax.shard_map(
        shards,
        mesh=mesh,
        in_specs=(rows, P(), cols, cols, cols, cols, tall, P(), cols, tall, P(), rows),
        out_specs=(
            rows, rows, P("head"), rows, rows, rows, rows, P("head", "seq"), P("head"), rows,
            P("head", "seq"),
        ),
        check_vma=False,
    )
```

```python
import math

import jax
import jax.numpy as jnp
from jax import lax
from jax.experimental import pallas as pl
from jax.experimental.pallas import tpu as pltpu
from jax.sharding import PartitionSpec as P

KEY = 256
VAL = 512
SIDE = 4
CORES = 2
HEADS = 2
ROWS = 512
HALF = 256
PART = 512
MODEL = 2048
EXTRA = 16
EPSILON = 1e-05
F32 = jnp.float32
BF16 = jnp.bfloat16
VMEM_BYTES = 26 * 1024 * 1024
ORDER = (2, 1, 3, 0)


def head_shift(step):
    return [(h, (h + step) % SIDE) for h in range(SIDE)]


def seq_index(x, y, core):
    return (x * SIDE + y) * CORES + core


def seq_shift(dx, dy, swap=0):
    return [
        (seq_index(x, y, core), seq_index((x + dx) % SIDE, (y + dy) % SIDE, core ^ swap))
        for x in range(SIDE)
        for y in range(SIDE)
        for core in range(CORES)
    ]


SWAP = seq_shift(0, 0, 1)


def up(block):
    return lax.ppermute(block, "head", head_shift(1))


def down(block):
    return lax.ppermute(block, "head", head_shift(SIDE - 1))


def add_low(a, b):
    return (a.astype(F32) + b.astype(F32)).astype(BF16)


def relay(a, b, tokens):
    def body(a, b, to_a, to_b):
        to_a[...] = a[...]
        to_b[...] = b[...]

    return call(
        "relay", body, (1,), [], [(a,), (b,)], [(a.shape, a.dtype), (b.shape, b.dtype)], tokens
    )


def gated(array, tokens):
    n = len(tokens)

    def body(*refs):
        del refs

    out = pl.pallas_call(
        body,
        name="gated",
        in_specs=[pl.BlockSpec(memory_space=pl.ANY)] * (1 + n),
        out_specs=pl.BlockSpec(memory_space=pl.ANY),
        out_shape=pltpu.HBM(array.shape, array.dtype),
        input_output_aliases={0: 0},
    )(in_hbm(array), *[in_hbm(t) if is_pinned(t) else t for t in tokens])
    pin(out)
    return out


def hold(tokens):
    def body(out):
        out[...] = jnp.zeros_like(out)

    return call("hold", body, (1,), [], [], [((8, 128), F32)], tokens)[0]


def gather_direct(block):
    got = {k: lax.ppermute(block, "head", head_shift(k)) for k in (2, 1, 3)}
    return [block, got[1], got[2], got[3]]


def ring_gather(a, b, first=None):
    r1, l1 = up(a), down(b)
    r2, l2 = up(b), down(a)
    on_r, on_l = first(r1, l1) if first else (r1, l1)
    r3, l3 = up(on_r), down(on_l)
    return [a, b, r1, r2, r3, l3, l2, l1]


def ring_scatter(p2a, p2b, p1a, p1b, pma, pmb):
    t1, t2 = up(p2a), down(p2b)
    rb, la = up(p1b), down(pma)
    s1, s2 = add_low(p1a, t1), add_low(pmb, t2)
    ra, lb = up(s1), down(s2)
    return [ra, rb, la, lb], (s1, s2)


def whole(shape):
    return pl.BlockSpec(shape, lambda *_: (0,) * len(shape))


def once(shape):
    return pl.BlockSpec(
        shape, lambda *_: (0,) * len(shape), pipeline_mode=pl.Buffered(buffer_count=1)
    )


PINNED = []


def pin(*arrays):
    PINNED.extend(arrays)


def is_pinned(array):
    return any(array is other for other in PINNED)


def in_hbm(array):
    return pltpu.with_memory_space_constraint(array, pltpu.HBM)


COST_SCALE = 1.0
COSTS = {
    "kv_mid": 100,
    "scan_start_b": 100,
    "relay": 1,
    "hold": 0.1,
    "turn_low2": 1.5,
    "late": 100,
    "scan_end_b": 50,
    "norm1": 5,
    "key_value": 8,
    "query_part": 6,
    "gate": 4,
    "mix": 9,
    "cot_pass": 100,
    "feed_up": 11,
    "back_feed": 7,
    "back_mix": 6,
    "retain_back": 0.6,
    "feed_down": 2,
    "key_value_back": 100,
    "back_proj": 0.1,
    "feed_other": 5,
    "feed_own": 8,
    "mix_other": 0.180,
    "mix_own": 1,
    "kv_other": 0.90,
    "kv_own": 0.1,
    "feed_sum": 0.1,
    "mix_sum": 2,
    "kv_sum": 0.1,
    "norm_back1": 0.1,
    "norm_back2": 100,
}


def call(name, body, grid, scalars, ins, outs, tokens=(), scratch=(), keep=False):
    arrays = [in_hbm(item[0]) if is_pinned(item[0]) else item[0] for item in ins]
    in_specs = [once(i[0].shape) if len(i) == 1 else pl.BlockSpec(i[1], i[2]) for i in ins]
    out_specs = [whole(o[0]) if len(o) == 2 else pl.BlockSpec(o[2], o[3]) for o in outs]
    out_shape = [jax.ShapeDtypeStruct(o[0], o[1]) for o in outs]
    keep = range(len(outs)) if keep is True else (keep or ())
    out_shape = [
        pltpu.HBM(o.shape, o.dtype) if i in keep else o for i, o in enumerate(out_shape)
    ]
    n_in, n_tok, n_sc = len(arrays), len(tokens), len(scalars)
    tokens = [in_hbm(t) if is_pinned(t) else t for t in tokens]
    in_specs += [pl.BlockSpec(memory_space=pl.ANY)] * n_tok

    def run(*refs):
        body(*refs[: n_sc + n_in], *refs[n_sc + n_in + n_tok :])

    results = pl.pallas_call(
        run,
        name=name,
        grid_spec=pltpu.PrefetchScalarGridSpec(
            num_scalar_prefetch=n_sc,
            grid=grid,
            in_specs=in_specs,
            out_specs=out_specs,
            scratch_shapes=list(scratch),
        ),
        out_shape=out_shape,
        compiler_params=pltpu.CompilerParams(
            dimension_semantics=("arbitrary",) * len(grid), vmem_limit_bytes=VMEM_BYTES
        ),
        cost_estimate=pl.CostEstimate(
            flops=int(COSTS.get(name, 0.1) * COST_SCALE * 1.1e9),
            bytes_accessed=0,
            transcendentals=0,
        ),
    )(*scalars, *arrays, *tokens)
    pin(*[results[i] for i in keep])
    return results


def dot(left, right):
    return jnp.dot(left, right, preferred_element_type=F32)


def dot_t(left, right):
    return lax.dot_general(left, right, (((1,), (1,)), ((), ())), preferred_element_type=F32)


def t_dot(left, right):
    return lax.dot_general(left, right, (((0,), (0,)), ((), ())), preferred_element_type=F32)


def rotate(rows, cosine, sine):
    half = rows.shape[-1] // 2
    first, second = rows[:, :half], rows[:, half:]
    return jnp.concatenate([first * cosine - second * sine, second * cosine + first * sine], axis=1)


def sigmoid(v):
    return 0.5 + 0.5 * jnp.tanh(0.5 * v)


def head_col(info, k):
    return pl.multiple_of(lax.rem(info[0] + SIDE - k, SIDE) * PART, PART)


CHUNK = 16


def norm_rows(info, load, gain, low, mean_ref, inv_ref, own=None):
    for half in range(2):

        def step(i, _):
            at = pl.multiple_of(i * CHUNK, CHUNK)
            out = pl.ds(pl.multiple_of(half * HALF + i * CHUNK, CHUNK), CHUNK)
            parts = [load(k, half, at) for k in range(SIDE)]
            if own is not None:
                own[out, :] = parts[0]
            mean = sum(jnp.sum(p, axis=1, keepdims=True) for p in parts) / MODEL
            parts = [p - mean for p in parts]
            var = sum(jnp.sum(p * p, axis=1, keepdims=True) for p in parts) / MODEL
            inv = lax.rsqrt(var + EPSILON)
            mean_ref[out, :] = mean
            inv_ref[out, :] = inv
            for k in range(SIDE):
                cols = pl.ds(head_col(info, k), PART)
                low[out, cols] = (parts[k] * inv * gain[:, cols]).astype(BF16)
            return 0

        lax.fori_loop(0, HALF // CHUNK, step, 0, unroll=4)


def chunk_of(part, half, at):
    return part[pl.ds(pl.multiple_of(half * HALF + at, CHUNK), CHUNK), :].astype(F32)


def norm1(info, parts, gain, cotangent):
    def body(info, *refs):
        x = refs[:8]
        gain, cot, low, mean, inv, cot_out, rows = refs[8:]
        cot_out[...] = cot[...]
        for k in range(SIDE):
            rows[k, :HALF] = x[2 * k][...]
            rows[k, HALF:] = x[2 * k + 1][...]
        norm_rows(
            info,
            lambda k, half, at: x[2 * k + half][pl.ds(at, CHUNK), :].astype(F32),
            gain,
            low,
            mean,
            inv,
        )

    return call(
        "norm1",
        body,
        (1,),
        [info],
        [(p,) for p in parts] + [(gain,), (cotangent,)],
        [
            ((ROWS, MODEL), BF16),
            ((ROWS, 1), F32),
            ((ROWS, 1), F32),
            ((ROWS, PART), BF16),
            ((SIDE, ROWS, PART), BF16),
        ],
        keep=(4,),
    )


def key_value(info, low, wk, wv, cosine, sine, departure):
    def body(info, low, wk, wv, cosine, sine, departure, key, value, own, give):
        head = pl.program_id(0)
        k = rotate(dot(low[...], wk[...]), cosine[...], sine[...]).astype(BF16)
        key[...] = k
        v = dot(low[...], wv[...]).astype(BF16)
        value[...] = v
        state = t_dot((k.astype(F32) * departure[0]).astype(BF16), v)

        @pl.when(head == info[1])
        def _():
            own[...] = state

        @pl.when(head != info[1])
        def _():
            give[...] = state.astype(BF16)

    by_head = lambda h, *_: (0, h)
    return call(
        "key_value",
        body,
        (HEADS,),
        [info],
        [
            (low,),
            (wk, (MODEL, KEY), by_head),
            (wv, (MODEL, VAL), by_head),
            (cosine,),
            (sine,),
            (departure, (1, ROWS, 1), lambda h, *_: (h, 0, 0)),
        ],
        [
            ((ROWS, HEADS * KEY), BF16, (ROWS, KEY), by_head),
            ((ROWS, HEADS * VAL), BF16, (ROWS, VAL), by_head),
            ((KEY, VAL), F32),
            ((KEY, VAL), BF16),
        ],
        keep=(0, 1),
    )


def query_part(low, wq, key, value, decay, cosine, sine, tokens):
    def body(low, wq, key, value, decay, cosine, sine, query, weighted, within):
        q = rotate(dot(low[...], wq[...]), cosine[...], sine[...]).astype(BF16)
        query[...] = q
        w = (dot_t(q, key[...]) * decay[0]).astype(BF16)
        weighted[0] = w
        within[...] = dot(w, value[...])

    by_head = lambda h, *_: (0, h)
    cube = lambda h, *_: (h, 0, 0)
    return call(
        "query_part",
        body,
        (HEADS,),
        [],
        [
            (low,),
            (wq, (MODEL, KEY), by_head),
            (key, (ROWS, KEY), by_head),
            (value, (ROWS, VAL), by_head),
            (decay, (1, ROWS, ROWS), cube),
            (cosine,),
            (sine,),
        ],
        [
            ((ROWS, HEADS * KEY), BF16, (ROWS, KEY), by_head),
            ((HEADS, ROWS, ROWS), BF16, (1, ROWS, ROWS), cube),
            ((ROWS, HEADS * VAL), F32, (ROWS, VAL), by_head),
        ],
        tokens,
        keep=(0, 1),
    )


def matmul_cols(name, left, right, out_type, tokens=(), block=512):
    def body(left, right, out):
        out[...] = dot(left[...], right[...]).astype(out_type)

    depth, cols = right.shape
    by_col = lambda i, *_: (0, i)
    return call(
        name,
        body,
        (cols // block,),
        [],
        [(left,), (right, (depth, block), by_col)],
        [((left.shape[0], cols), out_type, (left.shape[0], block), by_col)],
        tokens,
        keep=True,
    )[0]


def block_outs(extra):
    tall = ((HALF + extra, PART), BF16)
    return [tall, ((HALF, PART), BF16)] * 3 + [((ROWS, PART), F32)]


def put_blocks(step, make, outs):
    for i in range(2):
        block = make(i)
        for s in range(2):
            k = 2 * s + i

            @pl.when(step == s)
            def _():
                if k == SIDE - 1:
                    outs[6][...] = block
                else:
                    outs[2 * k][:HALF, :] = block[:HALF].astype(BF16)
                    outs[2 * k + 1][...] = block[HALF:].astype(BF16)


def pick(mine, sibling, info, head):
    return jnp.where(info[1] == head, mine[...], sibling[...])


def mix(info, within, gate, query, mine, sibling, arrival, wo, tokens):
    def body(
        info, within, gate, query, mine, sibling, arrival, wo_a, wo_b, mixed, grouped, ginv, *outs
    ):
        step = pl.program_id(0)

        @pl.when(step == 0)
        def _():
            for head in range(HEADS):
                cols = slice(head * VAL, (head + 1) * VAL)
                state = pick(mine, sibling, info, head)
                for half in range(2):
                    rows = slice(half * HALF, (half + 1) * HALF)
                    cross = dot(query[rows, head * KEY : (head + 1) * KEY], state)
                    kept = within[rows, cols] + arrival[head, rows] * cross
                    kept = kept - jnp.mean(kept, axis=1, keepdims=True)
                    inv = lax.rsqrt(jnp.mean(kept * kept, axis=1, keepdims=True) + float(KEY))
                    group = kept * inv
                    g = gate[rows, cols].astype(F32)
                    ginv[head, rows] = inv
                    grouped[rows, cols] = group.astype(BF16)
                    mixed[rows, cols] = (group * (g * sigmoid(g))).astype(BF16)

        put_blocks(step, lambda i: dot(mixed[...], (wo_a, wo_b)[i][...]), outs)

    cols = HEADS * VAL
    return call(
        "mix",
        body,
        (2,),
        [info],
        [
            (within,),
            (gate,),
            (query,),
            (mine,),
            (sibling,),
            (arrival,),
            (wo, (cols, PART), lambda i, info: (0, info[2 + 2 * i])),
            (wo, (cols, PART), lambda i, info: (0, info[3 + 2 * i])),
        ],
        [((ROWS, cols), BF16), ((ROWS, cols), BF16), ((HEADS, ROWS, 1), F32)] + block_outs(0),
        tokens,
        keep=(0, 1),
    )


def sum_branch(p0, pieces, tokens):
    def body(p0, ra, rb, la, lb, a, b):
        a[...] = (p0[:HALF] + ra[...].astype(F32) + la[...].astype(F32)).astype(BF16)
        b[...] = (p0[HALF:] + rb[...].astype(F32) + lb[...].astype(F32)).astype(BF16)

    return call(
        "sum_branch",
        body,
        (1,),
        [],
        [(p0,)] + [(p,) for p in pieces],
        [((HALF, PART), BF16), ((HALF, PART), BF16)],
        tokens,
    )


def feed_up(info, x_rows, b_parts, gain, w1, grad_hidden, tokens):
    block = 512

    def body(info, *refs):
        x, b = refs[0], refs[1:9]
        gain, w1, grad_hidden, ffn_in, mean, inv, own, hidden, grad_pre = refs[9:]

        @pl.when(pl.program_id(0) == 0)
        def _():
            def load(k, half, at):
                branch = b[2 * k + half][pl.ds(at, CHUNK), :].astype(F32)
                return chunk_of(x.at[k], half, at) + branch

            norm_rows(info, load, gain, ffn_in, mean, inv, own)

        pre = dot(ffn_in[...], w1[...])
        cdf = 0.5 * (1.0 + lax.erf(pre * (2.0**-0.5)))
        hidden[...] = (pre * cdf).astype(BF16)
        pdf = jnp.exp(-0.5 * pre * pre) * ((2.0 * math.pi) ** -0.5)
        grad_pre[...] = ((cdf + pre * pdf) * grad_hidden[...].astype(F32)).astype(BF16)

    by_col = lambda i, *_: (0, i)
    cols = w1.shape[1]
    tall = ((ROWS, cols), BF16, (ROWS, block), by_col)
    return call(
        "feed_up",
        body,
        (cols // block,),
        [info],
        [(x_rows,)]
        + [(p,) for p in b_parts]
        + [
            (gain,),
            (w1, (MODEL, block), by_col),
            (grad_hidden, (ROWS, block), by_col),
        ],
        [
            ((ROWS, MODEL), BF16),
            ((ROWS, 1), F32),
            ((ROWS, 1), F32),
            ((ROWS, PART), F32),
            tall,
            tall,
        ],
        tokens,
        keep=(1, 2, 3),
    )


def back_blocks(name, info, pairs, gain, low, tokens=()):
    n = len(pairs)

    def body(info, *refs):
        grads, weights = refs[:n], refs[n : 3 * n]
        gains, lows = refs[3 * n : 3 * n + 2], refs[3 * n + 2 : 3 * n + 4]
        outs, sums, acc = refs[3 * n + 4 : 3 * n + 11], refs[3 * n + 11], refs[3 * n + 12]
        step = pl.program_id(0)
        lane = lax.broadcasted_iota(jnp.int32, (ROWS, 128), 1)

        @pl.when(step == 0)
        def _():
            acc[...] = jnp.zeros_like(acc)

        def make(i):
            total = dot_t(grads[0][...], weights[2 * 0 + i][...])
            for j in range(1, n):
                total = total + dot_t(grads[j][...], weights[2 * j + i][...])
            first = jnp.sum(total * gains[i][...], axis=1, keepdims=True) / MODEL
            second = jnp.sum(total * lows[i][...].astype(F32), axis=1, keepdims=True) / MODEL
            acc[...] += jnp.where(lane == 0, first, jnp.where(lane == 1, second, 0.0))
            return total

        put_blocks(step, make, outs)

        @pl.when(step == 1)
        def _():
            turned = acc[...].T[:EXTRA]
            sums[...] = turned
            for k in range(SIDE - 1):
                outs[2 * k][HALF:, :] = turned.astype(BF16)

    def by_row(j):
        return lambda i, info: (info[2 + j + 2 * i], 0)

    def by_col(j):
        return lambda i, info: (0, info[2 + j + 2 * i])

    return call(
        name,
        body,
        (2,),
        [info],
        [(g,) for g, _ in pairs]
        + [(w, (PART, w.shape[1]), by_row(j)) for _, w in pairs for j in range(2)]
        + [(gain, (1, PART), by_col(j)) for j in range(2)]
        + [(low, (ROWS, PART), by_col(j)) for j in range(2)],
        block_outs(EXTRA) + [((EXTRA, PART), F32)],
        tokens,
        [pltpu.VMEM((ROWS, 128), F32)],
        keep=(6,),
    )


def norm_back(
    name, info, p0, sums, pieces, gain, rows, mean, inv, residual, low_out, tokens
):
    def body(
        info, p0, sums, ra, rb, la, lb, gain, rows, mean, inv, residual, grad, gain_grad, *low
    ):
        scale = gain[:, pl.ds(head_col(info, 0), PART)]
        total = sums[...] + ra[HALF:].astype(F32) + la[HALF:].astype(F32)
        total = jnp.concatenate([total, jnp.zeros((128 - EXTRA, PART), F32)], axis=0).T
        acc = jnp.zeros((1, PART), F32)
        for half, (one, two) in enumerate(((ra, la), (rb, lb))):
            for quarter in range(2):
                at = slice(quarter * 128, (quarter + 1) * 128)
                out = slice(half * HALF + quarter * 128, half * HALF + (quarter + 1) * 128)
                g = p0[out] + one[at].astype(F32) + two[at].astype(F32)
                normed = (rows[out].astype(F32) - mean[out]) * inv[out]
                acc = acc + jnp.sum(g * normed, axis=0, keepdims=True)
                back = inv[out] * (g * scale - total[out, 0:1] - normed * total[out, 1:2])
                new = residual[out].astype(F32) + back
                grad[out] = new
                if low_out:
                    low[half][at] = new.astype(BF16)
        gain_grad[...] = acc

    outs = [((ROWS, PART), F32), ((1, PART), F32)]
    if low_out:
        outs += [((HALF, PART), BF16)] * 2
    return call(
        name,
        body,
        (1,),
        [info],
        [(p0,), (sums,)]
        + [(p,) for p in pieces]
        + [(gain,), (rows,), (mean,), (inv,), (residual,)],
        outs,
        tokens,
        keep=(0,) if low_out else (),
    )


def back_mix(info, parts, wo, gate, grouped, ginv, query, arrival, tokens):
    def body(info, *refs):
        parts = refs[:8]
        wo, gate, grouped, ginv, query, arrival, branch, grad_gate, kept, own, give = refs[8:]
        head = pl.program_id(0)

        @pl.when(head == 0)
        def _():
            for k in range(SIDE):
                cols = pl.ds(head_col(info, k), PART)
                branch[:HALF, cols] = parts[2 * k][...]
                branch[HALF:, cols] = parts[2 * k + 1][...]

        for half in range(2):
            rows = slice(half * HALF, (half + 1) * HALF)
            m = dot_t(branch[rows], wo[...])
            g = gate[rows].astype(F32)
            gate_s = sigmoid(g)
            group = grouped[rows].astype(F32)
            slope = gate_s * (1.0 + g * (1.0 - gate_s))
            grad_gate[rows] = (m * group * slope).astype(BF16)
            e = m * (g * gate_s)
            e = ginv[0, rows] * (
                e
                - jnp.mean(e, axis=1, keepdims=True)
                - group * jnp.mean(e * group, axis=1, keepdims=True)
            )
            kept[rows] = e.astype(BF16)
        moved = (query[...].astype(F32) * arrival[0]).astype(BF16)
        state = t_dot(moved, kept[...])

        @pl.when(head == info[1])
        def _():
            own[...] = state

        @pl.when(head != info[1])
        def _():
            give[...] = state.astype(BF16)

    by_head = lambda h, *_: (0, h)
    cube = lambda h, *_: (h, 0, 0)
    cols = HEADS * VAL
    return call(
        "back_mix",
        body,
        (HEADS,),
        [info],
        [(p,) for p in parts]
        + [
            (wo, (VAL, MODEL), lambda h, *_: (h, 0)),
            (gate, (ROWS, VAL), by_head),
            (grouped, (ROWS, VAL), by_head),
            (ginv, (1, ROWS, 1), cube),
            (query, (ROWS, KEY), by_head),
            (arrival, (1, ROWS, 1), cube),
        ],
        [
            ((ROWS, MODEL), BF16),
            ((ROWS, cols), BF16, (ROWS, VAL), by_head),
            ((ROWS, cols), BF16, (ROWS, VAL), by_head),
            ((KEY, VAL), F32),
            ((KEY, VAL), BF16),
        ],
        tokens,
        keep=(1, 2),
    )


def retain_back(info, kept, value, decay, key, query, weighted, mine, sibling, arrival, cosine, sine, tokens):
    def body(
        info, kept, value, decay, key, query, weighted, mine, sibling, arrival, cosine, sine,
        grad_query, near_key, near_value,
    ):
        head = pl.program_id(0)
        e = kept[...]
        s = (dot_t(e, value[...]) * decay[0]).astype(BF16)
        state = pick(mine, sibling, info, head)
        gq = dot(s, key[...]) + arrival[0] * dot_t(e, state)
        grad_query[...] = rotate(gq, cosine[...], -sine[...]).astype(BF16)
        near_key[...] = t_dot(s, query[...])
        near_value[...] = t_dot(weighted[0], e)

    by_head = lambda h, *_: (0, h)
    cube = lambda h, *_: (h, 0, 0)
    keys, vals = HEADS * KEY, HEADS * VAL
    return call(
        "retain_back",
        body,
        (HEADS,),
        [info],
        [
            (kept, (ROWS, VAL), by_head),
            (value, (ROWS, VAL), by_head),
            (decay, (1, ROWS, ROWS), cube),
            (key, (ROWS, KEY), by_head),
            (query, (ROWS, KEY), by_head),
            (weighted, (1, ROWS, ROWS), cube),
            (mine,),
            (sibling,),
            (arrival, (1, ROWS, 1), cube),
            (cosine,),
            (sine,),
        ],
        [
            ((ROWS, keys), BF16, (ROWS, KEY), by_head),
            ((ROWS, keys), F32, (ROWS, KEY), by_head),
            ((ROWS, vals), F32, (ROWS, VAL), by_head),
        ],
        tokens,
        keep=True,
    )


def key_value_back(info, mine, sibling, key, value, departure, near_key, near_value, cosine, sine, tokens):
    def body(
        info, mine, sibling, key, value, departure, near_key, near_value, cosine, sine,
        grad_key, grad_value,
    ):
        state = pick(mine, sibling, info, pl.program_id(0))
        gk = near_key[...] + departure[0] * dot_t(value[...], state)
        grad_key[...] = rotate(gk, cosine[...], -sine[...]).astype(BF16)
        gv = near_value[...] + departure[0] * dot(key[...], state)
        grad_value[...] = gv.astype(BF16)

    by_head = lambda h, *_: (0, h)
    keys, vals = HEADS * KEY, HEADS * VAL
    return call(
        "key_value_back",
        body,
        (HEADS,),
        [info],
        [
            (mine,),
            (sibling,),
            (key, (ROWS, KEY), by_head),
            (value, (ROWS, VAL), by_head),
            (departure, (1, ROWS, 1), lambda h, *_: (h, 0, 0)),
            (near_key, (ROWS, KEY), by_head),
            (near_value, (ROWS, VAL), by_head),
            (cosine,),
            (sine,),
        ],
        [
            ((ROWS, keys), BF16, (ROWS, KEY), by_head),
            ((ROWS, vals), BF16, (ROWS, VAL), by_head),
        ],
        tokens,
        keep=True,
    )


def turn(name, info, low, tokens=(), keep=False):
    xs = 2

    def body(info, low, own, other, scratch):
        scratch[...] = low[...].T
        for x in range(xs):
            for y in range(SIDE):
                base = (x * SIDE + y) * CORES * 64
                mine = pl.ds(pl.multiple_of(base + info[1] * 64, 64), 64)
                far = pl.ds(pl.multiple_of(base + (1 - info[1]) * 64, 64), 64)
                own[x, y] = scratch[mine, :]
                other[x, y] = scratch[far, :]

    out = ((SIDE, SIDE, 64, ROWS), BF16, (xs, SIDE, 64, ROWS), lambda i, *_: (i, 0, 0, 0))
    own, other = call(
        name,
        body,
        (SIDE // xs,),
        [info],
        [(low, (ROWS, xs * PART), lambda i, *_: (0, i))],
        [out, out],
        tokens,
        [pltpu.VMEM((xs * PART, ROWS), BF16)],
        keep=keep,
    )
    flat = own.reshape(-1, ROWS), other.reshape(-1, ROWS)
    if keep:
        pin(*flat)
    return flat


def cot_pass(info, parts, w2, tokens):
    xs = 2

    def body(info, a, b, c, d, w2, own, other, out, whole_rows, scratch):
        step = pl.program_id(0)

        @pl.when(step == 0)
        def _():
            for k, part in enumerate((a, b, c, d)):
                whole_rows[:, pl.ds(head_col(info, k), PART)] = part[...]

        out[...] = dot_t(whole_rows[...], w2[...]).astype(BF16)
        cols = pl.ds(pl.multiple_of(step * xs * PART, PART), xs * PART)
        scratch[...] = whole_rows[:, cols].T
        for x in range(xs):
            for y in range(SIDE):
                base = (x * SIDE + y) * CORES * 64
                mine = pl.ds(pl.multiple_of(base + info[1] * 64, 64), 64)
                far = pl.ds(pl.multiple_of(base + (1 - info[1]) * 64, 64), 64)
                own[x, y] = scratch[mine, :]
                other[x, y] = scratch[far, :]

    turned = ((SIDE, SIDE, 64, ROWS), BF16, (xs, SIDE, 64, ROWS), lambda i, *_: (i, 0, 0, 0))
    cols = w2.shape[0]
    own, other, out = call(
        "cot_pass",
        body,
        (2,),
        [info],
        [(p,) for p in parts] + [(w2, (cols // 2, MODEL), lambda i, *_: (i, 0))],
        [turned, turned, ((ROWS, cols), BF16, (ROWS, cols // 2), lambda i, *_: (0, i))],
        tokens,
        [pltpu.VMEM((ROWS, MODEL), BF16), pltpu.VMEM((xs * PART, ROWS), BF16)],
    )
    return own.reshape(-1, ROWS), other.reshape(-1, ROWS), out


def widths(groups):
    return [sum(r.shape[1] for r in rights) for _, rights in groups]


def weight_half(name, groups, arrived=None, tokens=()):
    n_left = len(groups)
    rights = [r for _, rs in groups for r in rs]
    counts = [len(rs) for _, rs in groups]
    n = len(rights)
    width = sum(widths(groups))

    def body(*refs):
        lefts, rest = refs[:n_left], refs[n_left : n_left + n]
        out = refs[-1]
        at = 0
        which = 0
        for left, count in zip(lefts, counts):
            for r in rest[which : which + count]:
                cols = slice(at, at + r.shape[1])
                total = dot(left[...], r[...])
                if arrived is not None:
                    total = total + refs[n_left + n][:, cols].astype(F32)
                out[:, cols] = total.astype(BF16)
                at += r.shape[1]
            which += count

    block = lambda i, *_: (i, 0)
    return call(
        name,
        body,
        (2,),
        [],
        [(left, (ROWS, ROWS), block) for left, _ in groups]
        + [(r,) for r in rights]
        + ([(arrived, (ROWS, width), block)] if arrived is not None else []),
        [((2 * ROWS, width), BF16, (ROWS, width), block)],
        tokens,
        keep=True,
    )[0]


PLANE = [
    [seq_index(x, y, c) for x in range(SIDE) for y in range(SIDE)] for c in range(CORES)
]


def axis_groups(along_x):
    if along_x:
        return [
            [seq_index(x, y, c) for x in range(SIDE)] for y in range(SIDE) for c in range(CORES)
        ]
    return [[seq_index(x, y, c) for y in range(SIDE)] for x in range(SIDE) for c in range(CORES)]


def exchange(total, groups):
    blocks = total
    if total.ndim == 2:
        blocks = total.reshape(len(groups[0]), -1, total.shape[-1])
    blocks = lax.all_to_all(blocks, "seq", 0, 0, axis_index_groups=groups, tiled=True)
    pin(blocks)
    return blocks


def weight_mid(name, blocks, gains, tokens=()):
    count, rows, width = blocks.shape
    step = width // 2
    part = rows // SIDE
    gains = jnp.pad(gains, ((0, EXTRA - gains.shape[0]), (0, step - gains.shape[1])))

    def body(blocks, gains, out):
        total = blocks[0].astype(F32)
        for k in range(1, count):
            total = total + blocks[k].astype(F32)
        for y in range(SIDE):
            out[y, :part] = total[y * part : (y + 1) * part].astype(BF16)
            out[y, part:] = gains[...].astype(BF16)

    return call(
        name,
        body,
        (2,),
        [],
        [(blocks, (count, rows, step), lambda i, *_: (0, 0, i)), (gains,)],
        [
            (
                (SIDE, part + EXTRA, width),
                BF16,
                (SIDE, part + EXTRA, step),
                lambda i, *_: (0, 0, i),
            )
        ],
        tokens,
        keep=True,
    )[0]


def weight_sum(name, blocks, parts, tokens=()):
    count, rows, width = blocks.shape
    extra = rows - 64

    def body(blocks, *outs):
        at = 0
        for out, part in zip(outs, parts):
            cols = slice(at, at + part)
            total = blocks[0, :64, cols].astype(F32)
            for k in range(1, count):
                total = total + blocks[k, :64, cols].astype(F32)
            out[...] = total
            at += part
        if extra:
            total = blocks[0, 64:, :PART].astype(F32)
            for k in range(1, count):
                total = total + blocks[k, 64:, :PART].astype(F32)
            outs[-1][...] = total

    return call(
        name,
        body,
        (1,),
        [],
        [(blocks,)],
        [((64, part), F32) for part in parts] + ([((extra, PART), F32)] if extra else []),
        tokens,
    )


def weight_own_y(name, info, left, rights, arrived, tokens=()):
    n = len(rights)
    width = sum(r.shape[1] for r in rights)
    left = left.reshape(SIDE, SIDE, 64, ROWS)
    arrived = arrived.reshape(SIDE, SIDE, 64, width)
    pin(left)

    def body(info, *refs):
        lefts, rights, got, outs = refs[:2], refs[2 : 2 + n], refs[2 + n : 4 + n], refs[4 + n :]
        step = pl.program_id(0)
        for i in range(2):
            at = 0
            for r in rights:
                cols = slice(at, at + r.shape[1])
                total = dot(lefts[i][...].reshape(HALF, ROWS), r[...])
                total = total + got[i][:, :, :, cols].reshape(HALF, r.shape[1]).astype(F32)
                for s in range(2):

                    @pl.when(step == s)
                    def _():
                        out = outs[2 * s + i]
                        out[:, cols] = total.astype(out.dtype)

                at += r.shape[1]

    def block(j):
        def at(i, info):
            return (0, lax.rem(info[Y_AT] + ORDER_OF(2 * i + j), SIDE), 0, 0)

        return at

    return call(
        name,
        body,
        (2,),
        [info],
        [(left, (SIDE, 1, 64, ROWS), block(j)) for j in range(2)]
        + [(r,) for r in rights]
        + [(arrived, (SIDE, 1, 64, width), block(j)) for j in range(2)],
        [((HALF, width), BF16)] * 3 + [((HALF, width), F32)],
        tokens,
    )


def ORDER_OF(i):
    return jnp.where(i == 0, 2, jnp.where(i == 1, 1, jnp.where(i == 2, 3, 0)))


def phase_sum(name, info, where, base, received, tokens=()):
    width = base.shape[1]

    def body(info, base, a, b, c, *refs):
        outs, scratch = refs[:SIDE], refs[SIDE]
        scratch[...] = base[...] + a[...].astype(F32) + b[...].astype(F32) + c[...].astype(F32)
        for i, k in enumerate(ORDER):
            at = pl.multiple_of(lax.rem(info[where] + k, SIDE) * 64, 64)
            outs[i][...] = scratch[pl.ds(at, 64), :].astype(outs[i].dtype)

    return call(
        name,
        body,
        (1,),
        [info],
        [(base,)] + [(r,) for r in received],
        [((64, width), BF16)] * 3 + [((64, width), F32)],
        tokens,
        [pltpu.VMEM((HALF, width), F32)],
    )


def last_sum(name, base, received, parts):
    def body(base, a, b, c, *outs):
        at = 0
        for out in outs:
            cols = slice(at, at + out.shape[1])
            out[...] = base[:, cols] + sum(r[:, cols].astype(F32) for r in (a, b, c))
            at += out.shape[1]

    return call(
        name,
        body,
        (1,),
        [],
        [(base,)] + [(r,) for r in received],
        [((64, w), F32) for w in parts],
    )


def shift_of(along_x):
    return (lambda k: seq_shift(k, 0)) if along_x else (lambda k: seq_shift(0, k))


def send_blocks(blocks, along_x):
    shift = shift_of(along_x)
    return [lax.ppermute(b, "seq", shift(k)) for b, k in zip(blocks, ORDER[:3])]


X_AT, Y_AT = 6, 7


def scan_weights(decay, place, reverse):
    x, y, _ = place
    rel = jnp.arange(SIDE)
    origin = lax.rem(y - rel + SIDE, SIDE)
    target = lax.rem(y + rel, SIDE)
    hops = jnp.arange(1, SIDE)
    if reverse:
        row = origin
        before, counts = SIDE * (SIDE - hops - 1), x + (SIDE - hops) < SIDE
        gap = origin[None, :] - target[:, None]
        carry = SIDE - 1 - target
    else:
        row = SIDE - 1 - origin
        before, counts = SIDE * (hops - 1), x >= hops
        gap = target[:, None] - origin[None, :]
        carry = target
    gap = gap.reshape(-1)
    power = jnp.concatenate([row, before, jnp.maximum(gap - 1, 0), carry]).astype(F32)
    keep = jnp.concatenate([row >= 0, counts, gap > 0, carry >= 0]).astype(F32)
    values = keep * jnp.exp(2.0 * jnp.log(decay) * power)
    return jnp.concatenate([decay[None], values, jnp.zeros((4,), F32)])


W_ROW, W_BEFORE, W_ANSWER, W_CARRY = 1, 5, 8, 24
QUARTER = KEY // SIDE


def state_scan(info, weights, own, give, reverse, tag, fills):
    far = 1 if reverse else 0

    def start_body(info, w, own, got, p2, p1, p3, p0, scratch):
        a, b = own[...], got[...].astype(F32)
        scratch[...] = jnp.where(info[1] == far, w[0] * a + b, a + w[0] * b).astype(BF16)
        for k, out in zip(ORDER, (p2, p1, p3, p0)):
            at = pl.multiple_of(lax.rem(info[Y_AT] + k, SIDE) * QUARTER, QUARTER)
            out[...] = scratch[pl.ds(at, QUARTER), :]

    piece = ((QUARTER, VAL), BF16)
    got = lax.ppermute(give, "seq", SWAP)
    sent = call(
        "scan_start" + tag, start_body, (1,), [info, weights], [(own,), (got,)], [piece] * 4,
        fills[0](), scratch=[pltpu.VMEM((KEY, VAL), BF16)],
    )
    at2, at1, at3 = send_blocks(sent[:3], False)
    pieces = [sent[3], at1, at2, at3]

    def row_body(w, p0, p1, p2, p3, total):
        total[...] = sum(
            w[W_ROW + j] * p[...].astype(F32) for j, p in enumerate((p0, p1, p2, p3))
        ).astype(BF16)

    row = call(
        "scan_row" + tag, row_body, (1,), [weights], [(p,) for p in pieces], [piece],
        fills[1](sent[0]),
    )[0]
    at2, at1, at3 = send_blocks([row] * 3, True)

    def answer_body(w, p0, p1, p2, p3, b1, b2, b3, *outs):
        p = [r[...].astype(F32) for r in (p0, p1, p2, p3)]
        before = sum(w[W_BEFORE + j] * r[...].astype(F32) for j, r in enumerate((b1, b2, b3)))
        for k, out in zip(ORDER, outs):
            total = w[W_CARRY + k] * before
            for j in range(SIDE):
                total = total + w[W_ANSWER + SIDE * k + j] * p[j]
            out[...] = total.astype(BF16)

    answers = call(
        "scan_answer" + tag, answer_body, (1,), [weights],
        [(p,) for p in pieces] + [(at1,), (at2,), (at3,)], [piece] * 4, fills[2](row),
    )
    at2, at1, at3 = send_blocks(answers[:3], False)

    def end_body(info, w, b0, b1, b2, b3, own, got, mine, theirs, scratch):
        for k, b in enumerate((b0, b1, b2, b3)):
            at = pl.multiple_of(lax.rem(info[Y_AT] + SIDE - k, SIDE) * QUARTER, QUARTER)
            scratch[pl.ds(at, QUARTER), :] = b[...].astype(F32)
        chip = scratch[...]
        is_far = info[1] == far
        later = w[0] * chip + jnp.where(is_far, own[...], got[...].astype(F32))
        mine[...] = jnp.where(is_far, chip, later).astype(BF16)
        theirs[...] = jnp.where(is_far, later, chip).astype(BF16)

    state = ((KEY, VAL), BF16)
    mine, theirs = call(
        "scan_end" + tag, end_body, (1,), [info, weights],
        [(answers[3],), (at1,), (at2,), (at3,), (own,), (got,)], [state, state],
        fills[3](answers[0]), scratch=[pltpu.VMEM((KEY, VAL), F32)],
    )
    return mine, lax.ppermute(theirs, "seq", SWAP)


def sum_core_x(values, tokens):
    def body(a, b, out):
        out[...] = a[...] + b[...]

    got = lax.ppermute(values, "seq", SWAP)
    values = call(
        "gain_pair", body, (1,), [], [(values,), (got,)], [(values.shape, F32)], tokens
    )[0]
    return values + sum(lax.ppermute(values, "seq", seq_shift(k, 0)) for k in (1, 2, 3))


def shards(layer_in, gain1, wq, wk, wv, wg, wo, gain2, w1, w2, starts, cotangent):
    seq_rank = lax.axis_index("seq")
    head_rank = lax.axis_index("head")
    x, y, core = (
        seq_rank // (SIDE * CORES),
        (seq_rank // CORES) % SIDE,
        seq_rank % CORES,
    )
    place = (x, y, core)
    PINNED.clear()
    info = jnp.stack(
        [head_rank, core] + [(head_rank + k) % SIDE for k in ORDER] + [x, y]
    ).astype(jnp.int32)
    gain1, gain2 = gain1[None], gain2[None]

    offsets = jnp.arange(ROWS, dtype=jnp.int32)
    positions = seq_rank * ROWS + offsets
    member = positions[:, None] >= starts[None, :]
    doc_ids = jnp.sum(member.astype(jnp.int32), axis=-1) - 1
    last_start = jnp.max(jnp.where(member, starts[None, :], 0), axis=-1)
    relative = (positions - last_start).astype(F32)
    prior_doc = jnp.sum((seq_rank * ROWS - 1 >= starts).astype(jnp.int32)) - 1
    half_dim = KEY // 2
    frequency = jnp.exp(-math.log(10000.0) * jnp.arange(half_dim, dtype=F32) / half_dim)
    angles = relative[:, None] * frequency[None, :]
    cosine, sine = jnp.cos(angles), jnp.sin(angles)
    head_ids = (head_rank * HEADS + jnp.arange(HEADS, dtype=jnp.int32)).astype(F32)
    log_decay = jnp.log1p(-jnp.exp2(-5.0 - head_ids))
    gap_grid = offsets[:, None] - offsets[None, :]
    keep = (gap_grid >= 0) & (doc_ids[:, None] == doc_ids[None, :])
    gap_float = jnp.where(gap_grid >= 0, gap_grid, 0).astype(F32)
    decay = jnp.where(keep[None], jnp.exp(gap_float[None] * log_decay[:, None, None]), 0.0)
    step_float = offsets.astype(F32)
    arrival = jnp.exp((step_float[None, :] + 1.0) * log_decay[:, None]) * (
        doc_ids == prior_doc
    ).astype(F32)
    departure = jnp.exp((ROWS - 1.0 - step_float)[None, :] * log_decay[:, None]) * (
        doc_ids == doc_ids[ROWS - 1]
    ).astype(F32)
    arrival, departure = arrival[:, :, None], departure[:, :, None]
    pin(decay)
    rank_decay = lax.dynamic_index_in_dim(jnp.exp(ROWS * log_decay), core, 0, False)
    ahead = scan_weights(rank_decay, place, False)
    behind = scan_weights(rank_decay, place, True)

    tables = (arrival, departure, ahead, behind, info)
    x_parts = ring_gather(
        layer_in[:HALF], layer_in[HALF:], lambda r, l: relay(r, l, tables)
    )
    low1, mean1, inv1, cot_again, x_rows = norm1(info, x_parts, gain1, cotangent)
    cot_parts = gather_direct(cot_again)
    key, value, own, give = key_value(info, low1, wk, wv, cosine, sine, departure)
    made = {}

    def fill_query():
        made["q"] = query_part(low1, wq, key, value, decay, cosine, sine, (give,))
        return (made["q"][0],)

    def fill_gate(token):
        made["gate"] = matmul_cols("gate", low1, wg, BF16, (token, *cot_parts[1:]))
        return (made["gate"],)

    mine, sibling = state_scan(
        info, ahead, own, give, False, "_a", (fill_query, fill_gate, lambda token: (), lambda token: ())
    )
    query, weighted, within = made["q"]
    gate = made["gate"]
    mixed, grouped, ginv, *blocks = mix(
        info, within, gate, query, mine, sibling, arrival, wo, ()
    )
    pieces, sent = ring_scatter(*blocks[:6])
    cot_own, cot_other, grad_hidden = cot_pass(info, cot_parts, w2, sent)
    low1_own, low1_other = turn("turn_low1", info, low1, (cot_own,), True)
    b_parts = ring_gather(*sum_branch(blocks[6], pieces, (grad_hidden, low1_own)))

    low2, mean2, inv2, middle, hidden, grad_pre = feed_up(
        info, x_rows, b_parts, gain2, w1, grad_hidden, (cot_own,)
    )
    low2_own, low2_other = turn("turn_low2", info, low2)
    feed_other = weight_half(
        "feed_other", [(cot_other, [hidden]), (low2_other, [grad_pre])], None, (low2_own,)
    )
    *blocks, sums = back_blocks(
        "back_feed", info, [(grad_pre, w1)], gain2, low2, (feed_other,)
    )
    pieces, sent = ring_scatter(*blocks[:6])
    feed_got = lax.ppermute(feed_other, "seq", SWAP)
    feed_total = weight_half(
        "feed_own", [(cot_own, [hidden]), (low2_own, [grad_pre])], feed_got
    )
    grad_middle, gain2_grad, half_a, half_b = norm_back(
        "norm_back2", info, blocks[6], sums, pieces, gain2, middle, mean2, inv2, cotangent, True,
        (feed_total,),
    )
    g_parts = ring_gather(half_a, half_b)
    feed_blocks = exchange(feed_total, PLANE)

    branch, grad_gate, kept, own, give = back_mix(
        info, g_parts, wo, gate, grouped, ginv, query, arrival, (feed_total,)
    )

    branch_own, branch_other = turn("turn_branch", info, branch, (give,), True)
    grad_query, near_key, near_value = retain_back(
        info, kept, value, decay, key, query, weighted, mine, sibling, arrival, cosine, sine,
        (branch_own,),
    )
    mix_other = weight_half(
        "mix_other",
        [(branch_other, [mixed]), (low1_other, [grad_gate, grad_query])],
        None,
        (grad_query,),
    )
    mix_got = lax.ppermute(mix_other, "seq", SWAP)

    def fill_own(token):
        made["own"] = weight_half(
            "mix_own",
            [(branch_own, [mixed]), (low1_own, [grad_gate, grad_query])],
            mix_got,
            (token,),
        )
        return (made["own"],)

    feed = matmul_cols("feed_down", hidden, w2, BF16, (mix_other,), 1024)
    fed = lax.psum_scatter(feed, "head", scatter_dimension=1, tiled=True)

    far_mine, far_sibling = state_scan(
        info, behind, own, give, True, "_b",
        (lambda: (feed, feed_blocks), fill_own, lambda token: (), lambda token: (fed,)),
    )
    mix_x = exchange(gated(made["own"], (far_mine,)), axis_groups(True))
    grad_key, grad_value = key_value_back(
        info, far_mine, far_sibling, key, value, departure, near_key, near_value, cosine, sine,
        (),
    )
    kv_other = weight_half(
        "kv_other", [(low1_other, [grad_key, grad_value])]
    )
    kv_got = lax.ppermute(kv_other, "seq", SWAP)
    *blocks, sums = back_blocks(
        "back_proj", info,
        [(grad_query, wq), (grad_gate, wg), (grad_key, wk), (grad_value, wv)],
        gain1, low1, (kv_other, feed_blocks),
    )
    pieces, sent = ring_scatter(*blocks[:6])
    kv_blocks = weight_own_y(
        "kv_own", info, low1_own, [grad_key, grad_value], kv_got, sent
    )

    grad_x, gain1_grad = norm_back(
        "norm_back1", info, blocks[6], sums, pieces, gain1, layer_in, mean1, inv1, grad_middle,
        False, (kv_blocks[0],),
    )
    keys, vals = HEADS * KEY, HEADS * VAL
    kv_sent = send_blocks(kv_blocks[:3], False)
    kv_half = phase_sum("kv_mid", info, X_AT, kv_blocks[3], kv_sent)
    gains = sum_core_x(jnp.concatenate([gain1_grad, gain2_grad], axis=0), (mix_x,))
    mix_half = weight_mid("mix_mid", mix_x, gains)
    grad_w2, grad_w1 = weight_sum("feed_sum", feed_blocks, [vals, vals], (mix_half,))
    grad_wo, grad_wg, grad_wq, gains = weight_sum(
        "mix_sum", exchange(mix_half, axis_groups(False)), [vals, vals, keys]
    )
    grad_wk, grad_wv = last_sum(
        "kv_sum", kv_half[3], send_blocks(kv_half[:3], True), (keys, vals)
    )
    output = (middle + fed.astype(F32)).astype(BF16)
    return (
        output,
        grad_x,
        gains[0],
        grad_wq,
        grad_wk,
        grad_wv,
        grad_wg,
        grad_wo.T,
        gains[1],
        grad_w1,
        grad_w2.T,
    )


def solution(mesh):
    rows = P("seq", "head")
    cols = P(None, "head")
    tall = P("head", None)
    return jax.shard_map(
        shards,
        mesh=mesh,
        in_specs=(rows, P(), cols, cols, cols, cols, tall, P(), cols, tall, P(), rows),
        out_specs=(
            rows, rows, P("head"), rows, rows, rows, rows, P("head", "seq"), P("head"), rows,
            P("head", "seq"),
        ),
        check_vma=False,
    )
```

```python
import math

import jax
import jax.numpy as jnp
from jax import lax
from jax.experimental import pallas as pl
from jax.experimental.pallas import tpu as pltpu
from jax.sharding import PartitionSpec as P

KEY = 256
VAL = 512
SIDE = 4
CORES = 2
HEADS = 2
ROWS = 512
HALF = 256
PART = 512
MODEL = 2048
EXTRA = 16
EPSILON = 1e-05
F32 = jnp.float32
BF16 = jnp.bfloat16
VMEM_BYTES = 26 * 1024 * 1024
ORDER = (2, 1, 3, 0)


def head_shift(step):
    return [(h, (h + step) % SIDE) for h in range(SIDE)]


def seq_index(x, y, core):
    return (x * SIDE + y) * CORES + core


def seq_shift(dx, dy, swap=0):
    return [
        (seq_index(x, y, core), seq_index((x + dx) % SIDE, (y + dy) % SIDE, core ^ swap))
        for x in range(SIDE)
        for y in range(SIDE)
        for core in range(CORES)
    ]


SWAP = seq_shift(0, 0, 1)


def up(block):
    return lax.ppermute(block, "head", head_shift(1))


def down(block):
    return lax.ppermute(block, "head", head_shift(SIDE - 1))


def add_low(a, b):
    return (a.astype(F32) + b.astype(F32)).astype(BF16)


def relay(a, b, tokens):
    def body(a, b, to_a, to_b):
        to_a[...] = a[...]
        to_b[...] = b[...]

    return call(
        "relay", body, (1,), [], [(a,), (b,)], [(a.shape, a.dtype), (b.shape, b.dtype)], tokens
    )


def gated(array, tokens):
    n = len(tokens)

    def body(*refs):
        del refs

    out = pl.pallas_call(
        body,
        name="gated",
        in_specs=[pl.BlockSpec(memory_space=pl.ANY)] * (1 + n),
        out_specs=pl.BlockSpec(memory_space=pl.ANY),
        out_shape=pltpu.HBM(array.shape, array.dtype),
        input_output_aliases={0: 0},
    )(in_hbm(array), *[in_hbm(t) if is_pinned(t) else t for t in tokens])
    pin(out)
    return out


def hold(tokens):
    def body(out):
        out[...] = jnp.zeros_like(out)

    return call("hold", body, (1,), [], [], [((8, 128), F32)], tokens)[0]


def gather_direct(block):
    got = {k: lax.ppermute(block, "head", head_shift(k)) for k in (2, 1, 3)}
    return [block, got[1], got[2], got[3]]


def ring_gather(a, b, first=None):
    r1, l1 = up(a), down(b)
    r2, l2 = up(b), down(a)
    on_r, on_l = first(r1, l1) if first else (r1, l1)
    r3, l3 = up(on_r), down(on_l)
    return [a, b, r1, r2, r3, l3, l2, l1]


def ring_scatter(p2a, p2b, p1a, p1b, pma, pmb):
    t1, t2 = up(p2a), down(p2b)
    rb, la = up(p1b), down(pma)
    s1, s2 = add_low(p1a, t1), add_low(pmb, t2)
    ra, lb = up(s1), down(s2)
    return [ra, rb, la, lb], (s1, s2)


def whole(shape):
    return pl.BlockSpec(shape, lambda *_: (0,) * len(shape))


def once(shape):
    return pl.BlockSpec(
        shape, lambda *_: (0,) * len(shape), pipeline_mode=pl.Buffered(buffer_count=1)
    )


PINNED = []


def pin(*arrays):
    PINNED.extend(arrays)


def is_pinned(array):
    return any(array is other for other in PINNED)


def in_hbm(array):
    return pltpu.with_memory_space_constraint(array, pltpu.HBM)


COST_SCALE = 1.0
COSTS = {
    "kv_mid": 100,
    "scan_start_b": 100,
    "relay": 1,
    "hold": 0.1,
    "turn_low2": 1.5,
    "late": 100,
    "scan_end_b": 50,
    "norm1": 5,
    "key_value": 8,
    "query_part": 6,
    "gate": 4,
    "mix": 9,
    "cot_pass": 100,
    "feed_up": 11,
    "back_feed": 7,
    "back_mix": 6,
    "retain_back": 0.6,
    "feed_down": 2,
    "key_value_back": 100,
    "back_proj": 0.1,
    "feed_other": 5,
    "feed_own": 8,
    "mix_other": 0.180,
    "mix_own": 1,
    "kv_other": 0.90,
    "kv_own": 0.1,
    "feed_sum": 0.1,
    "mix_sum": 2,
    "kv_sum": 0.1,
    "norm_back1": 0.1,
    "norm_back2": 100,
}


def call(name, body, grid, scalars, ins, outs, tokens=(), scratch=(), keep=False):
    arrays = [in_hbm(item[0]) if is_pinned(item[0]) else item[0] for item in ins]
    in_specs = [once(i[0].shape) if len(i) == 1 else pl.BlockSpec(i[1], i[2]) for i in ins]
    out_specs = [whole(o[0]) if len(o) == 2 else pl.BlockSpec(o[2], o[3]) for o in outs]
    out_shape = [jax.ShapeDtypeStruct(o[0], o[1]) for o in outs]
    keep = range(len(outs)) if keep is True else (keep or ())
    out_shape = [
        pltpu.HBM(o.shape, o.dtype) if i in keep else o for i, o in enumerate(out_shape)
    ]
    n_in, n_tok, n_sc = len(arrays), len(tokens), len(scalars)
    tokens = [in_hbm(t) if is_pinned(t) else t for t in tokens]
    in_specs += [pl.BlockSpec(memory_space=pl.ANY)] * n_tok

    def run(*refs):
        body(*refs[: n_sc + n_in], *refs[n_sc + n_in + n_tok :])

    results = pl.pallas_call(
        run,
        name=name,
        grid_spec=pltpu.PrefetchScalarGridSpec(
            num_scalar_prefetch=n_sc,
            grid=grid,
            in_specs=in_specs,
            out_specs=out_specs,
            scratch_shapes=list(scratch),
        ),
        out_shape=out_shape,
        compiler_params=pltpu.CompilerParams(
            dimension_semantics=("arbitrary",) * len(grid), vmem_limit_bytes=VMEM_BYTES
        ),
        cost_estimate=pl.CostEstimate(
            flops=int(COSTS.get(name, 0.1) * COST_SCALE * 1.1e9),
            bytes_accessed=0,
            transcendentals=0,
        ),
    )(*scalars, *arrays, *tokens)
    pin(*[results[i] for i in keep])
    return results


def dot(left, right):
    return jnp.dot(left, right, preferred_element_type=F32)


def dot_t(left, right):
    return lax.dot_general(left, right, (((1,), (1,)), ((), ())), preferred_element_type=F32)


def t_dot(left, right):
    return lax.dot_general(left, right, (((0,), (0,)), ((), ())), preferred_element_type=F32)


def rotate(rows, cosine, sine):
    half = rows.shape[-1] // 2
    first, second = rows[:, :half], rows[:, half:]
    return jnp.concatenate([first * cosine - second * sine, second * cosine + first * sine], axis=1)


def sigmoid(v):
    return 0.5 + 0.5 * jnp.tanh(0.5 * v)


def head_col(info, k):
    return pl.multiple_of(lax.rem(info[0] + SIDE - k, SIDE) * PART, PART)


CHUNK = 16


def norm_rows(info, load, gain, low, mean_ref, inv_ref, own=None):
    for half in range(2):

        def step(i, _):
            at = pl.multiple_of(i * CHUNK, CHUNK)
            out = pl.ds(pl.multiple_of(half * HALF + i * CHUNK, CHUNK), CHUNK)
            parts = [load(k, half, at) for k in range(SIDE)]
            if own is not None:
                own[out, :] = parts[0]
            mean = sum(jnp.sum(p, axis=1, keepdims=True) for p in parts) / MODEL
            parts = [p - mean for p in parts]
            var = sum(jnp.sum(p * p, axis=1, keepdims=True) for p in parts) / MODEL
            inv = lax.rsqrt(var + EPSILON)
            mean_ref[out, :] = mean
            inv_ref[out, :] = inv
            for k in range(SIDE):
                cols = pl.ds(head_col(info, k), PART)
                low[out, cols] = (parts[k] * inv * gain[:, cols]).astype(BF16)
            return 0

        lax.fori_loop(0, HALF // CHUNK, step, 0, unroll=8)


def chunk_of(part, half, at):
    return part[pl.ds(pl.multiple_of(half * HALF + at, CHUNK), CHUNK), :].astype(F32)


def norm1(info, parts, gain, cotangent):
    def body(info, *refs):
        x = refs[:8]
        gain, cot, low, mean, inv, cot_out, rows = refs[8:]
        cot_out[...] = cot[...]
        for k in range(SIDE):
            rows[k, :HALF] = x[2 * k][...]
            rows[k, HALF:] = x[2 * k + 1][...]
        norm_rows(
            info,
            lambda k, half, at: x[2 * k + half][pl.ds(at, CHUNK), :].astype(F32),
            gain,
            low,
            mean,
            inv,
        )

    return call(
        "norm1",
        body,
        (1,),
        [info],
        [(p,) for p in parts] + [(gain,), (cotangent,)],
        [
            ((ROWS, MODEL), BF16),
            ((ROWS, 1), F32),
            ((ROWS, 1), F32),
            ((ROWS, PART), BF16),
            ((SIDE, ROWS, PART), BF16),
        ],
        keep=(4,),
    )


def key_value(info, low, wk, wv, cosine, sine, departure):
    def body(info, low, wk, wv, cosine, sine, departure, key, value, own, give):
        head = pl.program_id(0)
        k = rotate(dot(low[...], wk[...]), cosine[...], sine[...]).astype(BF16)
        key[...] = k
        v = dot(low[...], wv[...]).astype(BF16)
        value[...] = v
        state = t_dot((k.astype(F32) * departure[0]).astype(BF16), v)

        @pl.when(head == info[1])
        def _():
            own[...] = state

        @pl.when(head != info[1])
        def _():
            give[...] = state.astype(BF16)

    by_head = lambda h, *_: (0, h)
    return call(
        "key_value",
        body,
        (HEADS,),
        [info],
        [
            (low,),
            (wk, (MODEL, KEY), by_head),
            (wv, (MODEL, VAL), by_head),
            (cosine,),
            (sine,),
            (departure, (1, ROWS, 1), lambda h, *_: (h, 0, 0)),
        ],
        [
            ((ROWS, HEADS * KEY), BF16, (ROWS, KEY), by_head),
            ((ROWS, HEADS * VAL), BF16, (ROWS, VAL), by_head),
            ((KEY, VAL), F32),
            ((KEY, VAL), BF16),
        ],
        keep=(0, 1),
    )


def query_part(low, wq, key, value, decay, cosine, sine, tokens):
    def body(low, wq, key, value, decay, cosine, sine, query, weighted, within):
        q = rotate(dot(low[...], wq[...]), cosine[...], sine[...]).astype(BF16)
        query[...] = q
        w = (dot_t(q, key[...]) * decay[0]).astype(BF16)
        weighted[0] = w
        within[...] = dot(w, value[...])

    by_head = lambda h, *_: (0, h)
    cube = lambda h, *_: (h, 0, 0)
    return call(
        "query_part",
        body,
        (HEADS,),
        [],
        [
            (low,),
            (wq, (MODEL, KEY), by_head),
            (key, (ROWS, KEY), by_head),
            (value, (ROWS, VAL), by_head),
            (decay, (1, ROWS, ROWS), cube),
            (cosine,),
            (sine,),
        ],
        [
            ((ROWS, HEADS * KEY), BF16, (ROWS, KEY), by_head),
            ((HEADS, ROWS, ROWS), BF16, (1, ROWS, ROWS), cube),
            ((ROWS, HEADS * VAL), F32, (ROWS, VAL), by_head),
        ],
        tokens,
        keep=(0, 1),
    )


def matmul_cols(name, left, right, out_type, tokens=(), block=512):
    def body(left, right, out):
        out[...] = dot(left[...], right[...]).astype(out_type)

    depth, cols = right.shape
    by_col = lambda i, *_: (0, i)
    return call(
        name,
        body,
        (cols // block,),
        [],
        [(left,), (right, (depth, block), by_col)],
        [((left.shape[0], cols), out_type, (left.shape[0], block), by_col)],
        tokens,
        keep=True,
    )[0]


def block_outs(extra):
    tall = ((HALF + extra, PART), BF16)
    return [tall, ((HALF, PART), BF16)] * 3 + [((ROWS, PART), F32)]


def put_blocks(step, make, outs):
    for i in range(2):
        block = make(i)
        for s in range(2):
            k = 2 * s + i

            @pl.when(step == s)
            def _():
                if k == SIDE - 1:
                    outs[6][...] = block
                else:
                    outs[2 * k][:HALF, :] = block[:HALF].astype(BF16)
                    outs[2 * k + 1][...] = block[HALF:].astype(BF16)


def pick(mine, sibling, info, head):
    return jnp.where(info[1] == head, mine[...], sibling[...])


def mix(info, within, gate, query, mine, sibling, arrival, wo, tokens):
    def body(info, within, gate, query, mine, sibling, arrival, wo, mixed, grouped, ginv, *outs):
        for half in range(2):
            rows = slice(half * HALF, (half + 1) * HALF)
            for head in range(HEADS):
                cols = slice(head * VAL, (head + 1) * VAL)
                state = pick(mine, sibling, info, head)
                cross = dot(query[rows, head * KEY : (head + 1) * KEY], state)
                kept = within[rows, cols] + arrival[head, rows] * cross
                kept = kept - jnp.mean(kept, axis=1, keepdims=True)
                inv = lax.rsqrt(jnp.mean(kept * kept, axis=1, keepdims=True) + float(KEY))
                group = kept * inv
                g = gate[rows, cols].astype(F32)
                ginv[head, rows] = inv
                grouped[rows, cols] = group.astype(BF16)
                mixed[rows, cols] = (group * (g * sigmoid(g))).astype(BF16)
            for i in range(SIDE):
                at = pl.ds(pl.multiple_of(info[2 + i] * PART, PART), PART)
                block = dot(mixed[rows], wo[:, at])
                if i == SIDE - 1:
                    outs[6][rows] = block
                else:
                    outs[2 * i + half][...] = block.astype(BF16)

    cols = HEADS * VAL
    return call(
        "mix",
        body,
        (1,),
        [info],
        [(within,), (gate,), (query,), (mine,), (sibling,), (arrival,), (wo,)],
        [((ROWS, cols), BF16), ((ROWS, cols), BF16), ((HEADS, ROWS, 1), F32)] + block_outs(0),
        tokens,
        keep=(0, 1),
    )


def sum_branch(p0, pieces, tokens):
    def body(p0, ra, rb, la, lb, a, b):
        a[...] = (p0[:HALF] + ra[...].astype(F32) + la[...].astype(F32)).astype(BF16)
        b[...] = (p0[HALF:] + rb[...].astype(F32) + lb[...].astype(F32)).astype(BF16)

    return call(
        "sum_branch",
        body,
        (1,),
        [],
        [(p0,)] + [(p,) for p in pieces],
        [((HALF, PART), BF16), ((HALF, PART), BF16)],
        tokens,
    )


def feed_up(info, x_rows, b_parts, gain, w1, grad_hidden, tokens):
    block = 512

    def body(info, *refs):
        x, b = refs[0], refs[1:9]
        gain, w1, grad_hidden, ffn_in, mean, inv, own, hidden, grad_pre = refs[9:]

        @pl.when(pl.program_id(0) == 0)
        def _():
            def load(k, half, at):
                branch = b[2 * k + half][pl.ds(at, CHUNK), :].astype(F32)
                return chunk_of(x.at[k], half, at) + branch

            norm_rows(info, load, gain, ffn_in, mean, inv, own)

        pre = dot(ffn_in[...], w1[...])
        cdf = 0.5 * (1.0 + lax.erf(pre * (2.0**-0.5)))
        hidden[...] = (pre * cdf).astype(BF16)
        pdf = jnp.exp(-0.5 * pre * pre) * ((2.0 * math.pi) ** -0.5)
        grad_pre[...] = ((cdf + pre * pdf) * grad_hidden[...].astype(F32)).astype(BF16)

    by_col = lambda i, *_: (0, i)
    cols = w1.shape[1]
    tall = ((ROWS, cols), BF16, (ROWS, block), by_col)
    return call(
        "feed_up",
        body,
        (cols // block,),
        [info],
        [(x_rows,)]
        + [(p,) for p in b_parts]
        + [
            (gain,),
            (w1, (MODEL, block), by_col),
            (grad_hidden, (ROWS, block), by_col),
        ],
        [
            ((ROWS, MODEL), BF16),
            ((ROWS, 1), F32),
            ((ROWS, 1), F32),
            ((ROWS, PART), F32),
            tall,
            tall,
        ],
        tokens,
        keep=(1, 2, 3),
    )


def back_blocks(name, info, pairs, gain, low, tokens=()):
    n = len(pairs)

    def body(info, *refs):
        grads, weights = refs[:n], refs[n : 3 * n]
        gains, lows = refs[3 * n : 3 * n + 2], refs[3 * n + 2 : 3 * n + 4]
        outs, sums, acc = refs[3 * n + 4 : 3 * n + 11], refs[3 * n + 11], refs[3 * n + 12]
        step = pl.program_id(0)
        lane = lax.broadcasted_iota(jnp.int32, (ROWS, 128), 1)

        @pl.when(step == 0)
        def _():
            acc[...] = jnp.zeros_like(acc)

        def make(i):
            total = dot_t(grads[0][...], weights[2 * 0 + i][...])
            for j in range(1, n):
                total = total + dot_t(grads[j][...], weights[2 * j + i][...])
            first = jnp.sum(total * gains[i][...], axis=1, keepdims=True) / MODEL
            second = jnp.sum(total * lows[i][...].astype(F32), axis=1, keepdims=True) / MODEL
            acc[...] += jnp.where(lane == 0, first, jnp.where(lane == 1, second, 0.0))
            return total

        put_blocks(step, make, outs)

        @pl.when(step == 1)
        def _():
            turned = acc[...].T[:EXTRA]
            sums[...] = turned
            for k in range(SIDE - 1):
                outs[2 * k][HALF:, :] = turned.astype(BF16)

    def by_row(j):
        return lambda i, info: (info[2 + j + 2 * i], 0)

    def by_col(j):
        return lambda i, info: (0, info[2 + j + 2 * i])

    return call(
        name,
        body,
        (2,),
        [info],
        [(g,) for g, _ in pairs]
        + [(w, (PART, w.shape[1]), by_row(j)) for _, w in pairs for j in range(2)]
        + [(gain, (1, PART), by_col(j)) for j in range(2)]
        + [(low, (ROWS, PART), by_col(j)) for j in range(2)],
        block_outs(EXTRA) + [((EXTRA, PART), F32)],
        tokens,
        [pltpu.VMEM((ROWS, 128), F32)],
        keep=(6,),
    )


def norm_back(
    name, info, p0, sums, pieces, gain, rows, mean, inv, residual, low_out, tokens
):
    def body(
        info, p0, sums, ra, rb, la, lb, gain, rows, mean, inv, residual, grad, gain_grad, *low
    ):
        scale = gain[:, pl.ds(head_col(info, 0), PART)]
        total = sums[...] + ra[HALF:].astype(F32) + la[HALF:].astype(F32)
        total = jnp.concatenate([total, jnp.zeros((128 - EXTRA, PART), F32)], axis=0).T
        acc = jnp.zeros((1, PART), F32)
        for half, (one, two) in enumerate(((ra, la), (rb, lb))):
            for quarter in range(2):
                at = slice(quarter * 128, (quarter + 1) * 128)
                out = slice(half * HALF + quarter * 128, half * HALF + (quarter + 1) * 128)
                g = p0[out] + one[at].astype(F32) + two[at].astype(F32)
                normed = (rows[out].astype(F32) - mean[out]) * inv[out]
                acc = acc + jnp.sum(g * normed, axis=0, keepdims=True)
                back = inv[out] * (g * scale - total[out, 0:1] - normed * total[out, 1:2])
                new = residual[out].astype(F32) + back
                grad[out] = new
                if low_out:
                    low[half][at] = new.astype(BF16)
        gain_grad[...] = acc

    outs = [((ROWS, PART), F32), ((1, PART), F32)]
    if low_out:
        outs += [((HALF, PART), BF16)] * 2
    return call(
        name,
        body,
        (1,),
        [info],
        [(p0,), (sums,)]
        + [(p,) for p in pieces]
        + [(gain,), (rows,), (mean,), (inv,), (residual,)],
        outs,
        tokens,
        keep=(0,) if low_out else (),
    )


def back_mix(info, parts, wo, gate, grouped, ginv, query, arrival, tokens):
    def body(info, *refs):
        parts = refs[:8]
        wo, gate, grouped, ginv, query, arrival, branch, grad_gate, kept, own, give = refs[8:]
        head = pl.program_id(0)

        @pl.when(head == 0)
        def _():
            for k in range(SIDE):
                cols = pl.ds(head_col(info, k), PART)
                branch[:HALF, cols] = parts[2 * k][...]
                branch[HALF:, cols] = parts[2 * k + 1][...]

        for half in range(2):
            rows = slice(half * HALF, (half + 1) * HALF)
            m = dot_t(branch[rows], wo[...])
            g = gate[rows].astype(F32)
            gate_s = sigmoid(g)
            group = grouped[rows].astype(F32)
            slope = gate_s * (1.0 + g * (1.0 - gate_s))
            grad_gate[rows] = (m * group * slope).astype(BF16)
            e = m * (g * gate_s)
            e = ginv[0, rows] * (
                e
                - jnp.mean(e, axis=1, keepdims=True)
                - group * jnp.mean(e * group, axis=1, keepdims=True)
            )
            kept[rows] = e.astype(BF16)
        moved = (query[...].astype(F32) * arrival[0]).astype(BF16)
        state = t_dot(moved, kept[...])

        @pl.when(head == info[1])
        def _():
            own[...] = state

        @pl.when(head != info[1])
        def _():
            give[...] = state.astype(BF16)

    by_head = lambda h, *_: (0, h)
    cube = lambda h, *_: (h, 0, 0)
    cols = HEADS * VAL
    return call(
        "back_mix",
        body,
        (HEADS,),
        [info],
        [(p,) for p in parts]
        + [
            (wo, (VAL, MODEL), lambda h, *_: (h, 0)),
            (gate, (ROWS, VAL), by_head),
            (grouped, (ROWS, VAL), by_head),
            (ginv, (1, ROWS, 1), cube),
            (query, (ROWS, KEY), by_head),
            (arrival, (1, ROWS, 1), cube),
        ],
        [
            ((ROWS, MODEL), BF16),
            ((ROWS, cols), BF16, (ROWS, VAL), by_head),
            ((ROWS, cols), BF16, (ROWS, VAL), by_head),
            ((KEY, VAL), F32),
            ((KEY, VAL), BF16),
        ],
        tokens,
        keep=(1, 2),
    )


def retain_back(info, kept, value, decay, key, query, weighted, mine, sibling, arrival, cosine, sine, tokens):
    def body(
        info, kept, value, decay, key, query, weighted, mine, sibling, arrival, cosine, sine,
        grad_query, near_key, near_value,
    ):
        head = pl.program_id(0)
        e = kept[...]
        s = (dot_t(e, value[...]) * decay[0]).astype(BF16)
        state = pick(mine, sibling, info, head)
        gq = dot(s, key[...]) + arrival[0] * dot_t(e, state)
        grad_query[...] = rotate(gq, cosine[...], -sine[...]).astype(BF16)
        near_key[...] = t_dot(s, query[...])
        near_value[...] = t_dot(weighted[0], e)

    by_head = lambda h, *_: (0, h)
    cube = lambda h, *_: (h, 0, 0)
    keys, vals = HEADS * KEY, HEADS * VAL
    return call(
        "retain_back",
        body,
        (HEADS,),
        [info],
        [
            (kept, (ROWS, VAL), by_head),
            (value, (ROWS, VAL), by_head),
            (decay, (1, ROWS, ROWS), cube),
            (key, (ROWS, KEY), by_head),
            (query, (ROWS, KEY), by_head),
            (weighted, (1, ROWS, ROWS), cube),
            (mine,),
            (sibling,),
            (arrival, (1, ROWS, 1), cube),
            (cosine,),
            (sine,),
        ],
        [
            ((ROWS, keys), BF16, (ROWS, KEY), by_head),
            ((ROWS, keys), F32, (ROWS, KEY), by_head),
            ((ROWS, vals), F32, (ROWS, VAL), by_head),
        ],
        tokens,
        keep=True,
    )


def key_value_back(info, mine, sibling, key, value, departure, near_key, near_value, cosine, sine, tokens):
    def body(
        info, mine, sibling, key, value, departure, near_key, near_value, cosine, sine,
        grad_key, grad_value,
    ):
        state = pick(mine, sibling, info, pl.program_id(0))
        gk = near_key[...] + departure[0] * dot_t(value[...], state)
        grad_key[...] = rotate(gk, cosine[...], -sine[...]).astype(BF16)
        gv = near_value[...] + departure[0] * dot(key[...], state)
        grad_value[...] = gv.astype(BF16)

    by_head = lambda h, *_: (0, h)
    keys, vals = HEADS * KEY, HEADS * VAL
    return call(
        "key_value_back",
        body,
        (HEADS,),
        [info],
        [
            (mine,),
            (sibling,),
            (key, (ROWS, KEY), by_head),
            (value, (ROWS, VAL), by_head),
            (departure, (1, ROWS, 1), lambda h, *_: (h, 0, 0)),
            (near_key, (ROWS, KEY), by_head),
            (near_value, (ROWS, VAL), by_head),
            (cosine,),
            (sine,),
        ],
        [
            ((ROWS, keys), BF16, (ROWS, KEY), by_head),
            ((ROWS, vals), BF16, (ROWS, VAL), by_head),
        ],
        tokens,
        keep=True,
    )


def turn(name, info, low, tokens=(), keep=False):
    xs = 2

    def body(info, low, own, other, scratch):
        scratch[...] = low[...].T
        for x in range(xs):
            for y in range(SIDE):
                base = (x * SIDE + y) * CORES * 64
                mine = pl.ds(pl.multiple_of(base + info[1] * 64, 64), 64)
                far = pl.ds(pl.multiple_of(base + (1 - info[1]) * 64, 64), 64)
                own[x, y] = scratch[mine, :]
                other[x, y] = scratch[far, :]

    out = ((SIDE, SIDE, 64, ROWS), BF16, (xs, SIDE, 64, ROWS), lambda i, *_: (i, 0, 0, 0))
    own, other = call(
        name,
        body,
        (SIDE // xs,),
        [info],
        [(low, (ROWS, xs * PART), lambda i, *_: (0, i))],
        [out, out],
        tokens,
        [pltpu.VMEM((xs * PART, ROWS), BF16)],
        keep=keep,
    )
    flat = own.reshape(-1, ROWS), other.reshape(-1, ROWS)
    if keep:
        pin(*flat)
    return flat


def cot_pass(info, parts, w2, tokens):
    xs = 2

    def body(info, a, b, c, d, w2, own, other, out, whole_rows, scratch):
        step = pl.program_id(0)

        @pl.when(step == 0)
        def _():
            for k, part in enumerate((a, b, c, d)):
                whole_rows[:, pl.ds(head_col(info, k), PART)] = part[...]

        out[...] = dot_t(whole_rows[...], w2[...]).astype(BF16)
        cols = pl.ds(pl.multiple_of(step * xs * PART, PART), xs * PART)
        scratch[...] = whole_rows[:, cols].T
        for x in range(xs):
            for y in range(SIDE):
                base = (x * SIDE + y) * CORES * 64
                mine = pl.ds(pl.multiple_of(base + info[1] * 64, 64), 64)
                far = pl.ds(pl.multiple_of(base + (1 - info[1]) * 64, 64), 64)
                own[x, y] = scratch[mine, :]
                other[x, y] = scratch[far, :]

    turned = ((SIDE, SIDE, 64, ROWS), BF16, (xs, SIDE, 64, ROWS), lambda i, *_: (i, 0, 0, 0))
    cols = w2.shape[0]
    own, other, out = call(
        "cot_pass",
        body,
        (2,),
        [info],
        [(p,) for p in parts] + [(w2, (cols // 2, MODEL), lambda i, *_: (i, 0))],
        [turned, turned, ((ROWS, cols), BF16, (ROWS, cols // 2), lambda i, *_: (0, i))],
        tokens,
        [pltpu.VMEM((ROWS, MODEL), BF16), pltpu.VMEM((xs * PART, ROWS), BF16)],
    )
    return own.reshape(-1, ROWS), other.reshape(-1, ROWS), out


def widths(groups):
    return [sum(r.shape[1] for r in rights) for _, rights in groups]


def weight_half(name, groups, arrived=None, tokens=()):
    n_left = len(groups)
    rights = [r for _, rs in groups for r in rs]
    counts = [len(rs) for _, rs in groups]
    n = len(rights)
    width = sum(widths(groups))

    def body(*refs):
        lefts, rest = refs[:n_left], refs[n_left : n_left + n]
        out = refs[-1]
        at = 0
        which = 0
        for left, count in zip(lefts, counts):
            for r in rest[which : which + count]:
                cols = slice(at, at + r.shape[1])
                total = dot(left[...], r[...])
                if arrived is not None:
                    total = total + refs[n_left + n][:, cols].astype(F32)
                out[:, cols] = total.astype(BF16)
                at += r.shape[1]
            which += count

    block = lambda i, *_: (i, 0)
    return call(
        name,
        body,
        (2,),
        [],
        [(left, (ROWS, ROWS), block) for left, _ in groups]
        + [(r,) for r in rights]
        + ([(arrived, (ROWS, width), block)] if arrived is not None else []),
        [((2 * ROWS, width), BF16, (ROWS, width), block)],
        tokens,
        keep=True,
    )[0]


PLANE = [
    [seq_index(x, y, c) for x in range(SIDE) for y in range(SIDE)] for c in range(CORES)
]


def axis_groups(along_x):
    if along_x:
        return [
            [seq_index(x, y, c) for x in range(SIDE)] for y in range(SIDE) for c in range(CORES)
        ]
    return [[seq_index(x, y, c) for y in range(SIDE)] for x in range(SIDE) for c in range(CORES)]


def exchange(total, groups):
    blocks = total
    if total.ndim == 2:
        blocks = total.reshape(len(groups[0]), -1, total.shape[-1])
    blocks = lax.all_to_all(blocks, "seq", 0, 0, axis_index_groups=groups, tiled=True)
    pin(blocks)
    return blocks


def weight_mid(name, blocks, gains, tokens=()):
    count, rows, width = blocks.shape
    step = width // 2
    part = rows // SIDE
    gains = jnp.pad(gains, ((0, EXTRA - gains.shape[0]), (0, step - gains.shape[1])))

    def body(blocks, gains, out):
        total = blocks[0].astype(F32)
        for k in range(1, count):
            total = total + blocks[k].astype(F32)
        for y in range(SIDE):
            out[y, :part] = total[y * part : (y + 1) * part].astype(BF16)
            out[y, part:] = gains[...].astype(BF16)

    return call(
        name,
        body,
        (2,),
        [],
        [(blocks, (count, rows, step), lambda i, *_: (0, 0, i)), (gains,)],
        [
            (
                (SIDE, part + EXTRA, width),
                BF16,
                (SIDE, part + EXTRA, step),
                lambda i, *_: (0, 0, i),
            )
        ],
        tokens,
        keep=True,
    )[0]


def weight_sum(name, blocks, parts, tokens=()):
    count, rows, width = blocks.shape
    extra = rows - 64

    def body(blocks, *outs):
        at = 0
        for out, part in zip(outs, parts):
            cols = slice(at, at + part)
            total = blocks[0, :64, cols].astype(F32)
            for k in range(1, count):
                total = total + blocks[k, :64, cols].astype(F32)
            out[...] = total
            at += part
        if extra:
            total = blocks[0, 64:, :PART].astype(F32)
            for k in range(1, count):
                total = total + blocks[k, 64:, :PART].astype(F32)
            outs[-1][...] = total

    return call(
        name,
        body,
        (1,),
        [],
        [(blocks,)],
        [((64, part), F32) for part in parts] + ([((extra, PART), F32)] if extra else []),
        tokens,
    )


def weight_own_y(name, info, left, rights, arrived, tokens=()):
    n = len(rights)
    width = sum(r.shape[1] for r in rights)
    left = left.reshape(SIDE, SIDE, 64, ROWS)
    arrived = arrived.reshape(SIDE, SIDE, 64, width)
    pin(left)

    def body(info, *refs):
        lefts, rights, got, outs = refs[:2], refs[2 : 2 + n], refs[2 + n : 4 + n], refs[4 + n :]
        step = pl.program_id(0)
        for i in range(2):
            at = 0
            for r in rights:
                cols = slice(at, at + r.shape[1])
                total = dot(lefts[i][...].reshape(HALF, ROWS), r[...])
                total = total + got[i][:, :, :, cols].reshape(HALF, r.shape[1]).astype(F32)
                for s in range(2):

                    @pl.when(step == s)
                    def _():
                        out = outs[2 * s + i]
                        out[:, cols] = total.astype(out.dtype)

                at += r.shape[1]

    def block(j):
        def at(i, info):
            return (0, lax.rem(info[Y_AT] + ORDER_OF(2 * i + j), SIDE), 0, 0)

        return at

    return call(
        name,
        body,
        (2,),
        [info],
        [(left, (SIDE, 1, 64, ROWS), block(j)) for j in range(2)]
        + [(r,) for r in rights]
        + [(arrived, (SIDE, 1, 64, width), block(j)) for j in range(2)],
        [((HALF, width), BF16)] * 3 + [((HALF, width), F32)],
        tokens,
    )


def ORDER_OF(i):
    return jnp.where(i == 0, 2, jnp.where(i == 1, 1, jnp.where(i == 2, 3, 0)))


def phase_sum(name, info, where, base, received, tokens=()):
    width = base.shape[1]

    def body(info, base, a, b, c, *refs):
        outs, scratch = refs[:SIDE], refs[SIDE]
        scratch[...] = base[...] + a[...].astype(F32) + b[...].astype(F32) + c[...].astype(F32)
        for i, k in enumerate(ORDER):
            at = pl.multiple_of(lax.rem(info[where] + k, SIDE) * 64, 64)
            outs[i][...] = scratch[pl.ds(at, 64), :].astype(outs[i].dtype)

    return call(
        name,
        body,
        (1,),
        [info],
        [(base,)] + [(r,) for r in received],
        [((64, width), BF16)] * 3 + [((64, width), F32)],
        tokens,
        [pltpu.VMEM((HALF, width), F32)],
    )


def last_sum(name, base, received, parts):
    def body(base, a, b, c, *outs):
        at = 0
        for out in outs:
            cols = slice(at, at + out.shape[1])
            out[...] = base[:, cols] + sum(r[:, cols].astype(F32) for r in (a, b, c))
            at += out.shape[1]

    return call(
        name,
        body,
        (1,),
        [],
        [(base,)] + [(r,) for r in received],
        [((64, w), F32) for w in parts],
    )


def shift_of(along_x):
    return (lambda k: seq_shift(k, 0)) if along_x else (lambda k: seq_shift(0, k))


def send_blocks(blocks, along_x):
    shift = shift_of(along_x)
    return [lax.ppermute(b, "seq", shift(k)) for b, k in zip(blocks, ORDER[:3])]


X_AT, Y_AT = 6, 7


def scan_weights(decay, place, reverse):
    x, y, _ = place
    rel = jnp.arange(SIDE)
    origin = lax.rem(y - rel + SIDE, SIDE)
    target = lax.rem(y + rel, SIDE)
    hops = jnp.arange(1, SIDE)
    if reverse:
        row = origin
        before, counts = SIDE * (SIDE - hops - 1), x + (SIDE - hops) < SIDE
        gap = origin[None, :] - target[:, None]
        carry = SIDE - 1 - target
    else:
        row = SIDE - 1 - origin
        before, counts = SIDE * (hops - 1), x >= hops
        gap = target[:, None] - origin[None, :]
        carry = target
    gap = gap.reshape(-1)
    power = jnp.concatenate([row, before, jnp.maximum(gap - 1, 0), carry]).astype(F32)
    keep = jnp.concatenate([row >= 0, counts, gap > 0, carry >= 0]).astype(F32)
    values = keep * jnp.exp(2.0 * jnp.log(decay) * power)
    return jnp.concatenate([decay[None], values, jnp.zeros((4,), F32)])


W_ROW, W_BEFORE, W_ANSWER, W_CARRY = 1, 5, 8, 24
QUARTER = KEY // SIDE


def state_scan(info, weights, own, give, reverse, tag, fills):
    far = 1 if reverse else 0

    def start_body(info, w, own, got, p2, p1, p3, p0, scratch):
        a, b = own[...], got[...].astype(F32)
        scratch[...] = jnp.where(info[1] == far, w[0] * a + b, a + w[0] * b).astype(BF16)
        for k, out in zip(ORDER, (p2, p1, p3, p0)):
            at = pl.multiple_of(lax.rem(info[Y_AT] + k, SIDE) * QUARTER, QUARTER)
            out[...] = scratch[pl.ds(at, QUARTER), :]

    piece = ((QUARTER, VAL), BF16)
    got = lax.ppermute(give, "seq", SWAP)
    sent = call(
        "scan_start" + tag, start_body, (1,), [info, weights], [(own,), (got,)], [piece] * 4,
        fills[0](), scratch=[pltpu.VMEM((KEY, VAL), BF16)],
    )
    at2, at1, at3 = send_blocks(sent[:3], False)
    pieces = [sent[3], at1, at2, at3]

    def row_body(w, p0, p1, p2, p3, total):
        total[...] = sum(
            w[W_ROW + j] * p[...].astype(F32) for j, p in enumerate((p0, p1, p2, p3))
        ).astype(BF16)

    row = call(
        "scan_row" + tag, row_body, (1,), [weights], [(p,) for p in pieces], [piece],
        fills[1](sent[0]),
    )[0]
    at2, at1, at3 = send_blocks([row] * 3, True)

    def answer_body(w, p0, p1, p2, p3, b1, b2, b3, *outs):
        p = [r[...].astype(F32) for r in (p0, p1, p2, p3)]
        before = sum(w[W_BEFORE + j] * r[...].astype(F32) for j, r in enumerate((b1, b2, b3)))
        for k, out in zip(ORDER, outs):
            total = w[W_CARRY + k] * before
            for j in range(SIDE):
                total = total + w[W_ANSWER + SIDE * k + j] * p[j]
            out[...] = total.astype(BF16)

    answers = call(
        "scan_answer" + tag, answer_body, (1,), [weights],
        [(p,) for p in pieces] + [(at1,), (at2,), (at3,)], [piece] * 4, fills[2](row),
    )
    at2, at1, at3 = send_blocks(answers[:3], False)

    def end_body(info, w, b0, b1, b2, b3, own, got, mine, theirs, scratch):
        for k, b in enumerate((b0, b1, b2, b3)):
            at = pl.multiple_of(lax.rem(info[Y_AT] + SIDE - k, SIDE) * QUARTER, QUARTER)
            scratch[pl.ds(at, QUARTER), :] = b[...].astype(F32)
        chip = scratch[...]
        is_far = info[1] == far
        later = w[0] * chip + jnp.where(is_far, own[...], got[...].astype(F32))
        mine[...] = jnp.where(is_far, chip, later).astype(BF16)
        theirs[...] = jnp.where(is_far, later, chip).astype(BF16)

    state = ((KEY, VAL), BF16)
    mine, theirs = call(
        "scan_end" + tag, end_body, (1,), [info, weights],
        [(answers[3],), (at1,), (at2,), (at3,), (own,), (got,)], [state, state],
        fills[3](answers[0]), scratch=[pltpu.VMEM((KEY, VAL), F32)],
    )
    return mine, lax.ppermute(theirs, "seq", SWAP)


def sum_core_x(values, tokens):
    def body(a, b, out):
        out[...] = a[...] + b[...]

    got = lax.ppermute(values, "seq", SWAP)
    values = call(
        "gain_pair", body, (1,), [], [(values,), (got,)], [(values.shape, F32)], tokens
    )[0]
    return values + sum(lax.ppermute(values, "seq", seq_shift(k, 0)) for k in (1, 2, 3))


def shards(layer_in, gain1, wq, wk, wv, wg, wo, gain2, w1, w2, starts, cotangent):
    seq_rank = lax.axis_index("seq")
    head_rank = lax.axis_index("head")
    x, y, core = (
        seq_rank // (SIDE * CORES),
        (seq_rank // CORES) % SIDE,
        seq_rank % CORES,
    )
    place = (x, y, core)
    PINNED.clear()
    info = jnp.stack(
        [head_rank, core] + [(head_rank + k) % SIDE for k in ORDER] + [x, y]
    ).astype(jnp.int32)
    gain1, gain2 = gain1[None], gain2[None]

    offsets = jnp.arange(ROWS, dtype=jnp.int32)
    positions = seq_rank * ROWS + offsets
    member = positions[:, None] >= starts[None, :]
    doc_ids = jnp.sum(member.astype(jnp.int32), axis=-1) - 1
    last_start = jnp.max(jnp.where(member, starts[None, :], 0), axis=-1)
    relative = (positions - last_start).astype(F32)
    prior_doc = jnp.sum((seq_rank * ROWS - 1 >= starts).astype(jnp.int32)) - 1
    half_dim = KEY // 2
    frequency = jnp.exp(-math.log(10000.0) * jnp.arange(half_dim, dtype=F32) / half_dim)
    angles = relative[:, None] * frequency[None, :]
    cosine, sine = jnp.cos(angles), jnp.sin(angles)
    head_ids = (head_rank * HEADS + jnp.arange(HEADS, dtype=jnp.int32)).astype(F32)
    log_decay = jnp.log1p(-jnp.exp2(-5.0 - head_ids))
    gap_grid = offsets[:, None] - offsets[None, :]
    keep = (gap_grid >= 0) & (doc_ids[:, None] == doc_ids[None, :])
    gap_float = jnp.where(gap_grid >= 0, gap_grid, 0).astype(F32)
    decay = jnp.where(keep[None], jnp.exp(gap_float[None] * log_decay[:, None, None]), 0.0)
    step_float = offsets.astype(F32)
    arrival = jnp.exp((step_float[None, :] + 1.0) * log_decay[:, None]) * (
        doc_ids == prior_doc
    ).astype(F32)
    departure = jnp.exp((ROWS - 1.0 - step_float)[None, :] * log_decay[:, None]) * (
        doc_ids == doc_ids[ROWS - 1]
    ).astype(F32)
    arrival, departure = arrival[:, :, None], departure[:, :, None]
    pin(decay)
    rank_decay = lax.dynamic_index_in_dim(jnp.exp(ROWS * log_decay), core, 0, False)
    ahead = scan_weights(rank_decay, place, False)
    behind = scan_weights(rank_decay, place, True)

    tables = (arrival, departure, ahead, behind, info)
    x_parts = ring_gather(
        layer_in[:HALF], layer_in[HALF:], lambda r, l: relay(r, l, tables)
    )
    low1, mean1, inv1, cot_again, x_rows = norm1(info, x_parts, gain1, cotangent)
    cot_parts = gather_direct(cot_again)
    key, value, own, give = key_value(info, low1, wk, wv, cosine, sine, departure)
    made = {}

    def fill_query():
        made["q"] = query_part(low1, wq, key, value, decay, cosine, sine, (give,))
        return (made["q"][0],)

    def fill_gate(token):
        made["gate"] = matmul_cols("gate", low1, wg, BF16, (token, *cot_parts[1:]))
        return (made["gate"],)

    mine, sibling = state_scan(
        info, ahead, own, give, False, "_a", (fill_query, fill_gate, lambda token: (), lambda token: ())
    )
    query, weighted, within = made["q"]
    gate = made["gate"]
    mixed, grouped, ginv, *blocks = mix(
        info, within, gate, query, mine, sibling, arrival, wo, ()
    )
    pieces, sent = ring_scatter(*blocks[:6])
    cot_own, cot_other, grad_hidden = cot_pass(info, cot_parts, w2, sent)
    low1_own, low1_other = turn("turn_low1", info, low1, (cot_own,), True)
    b_parts = ring_gather(*sum_branch(blocks[6], pieces, (grad_hidden, low1_own)))

    low2, mean2, inv2, middle, hidden, grad_pre = feed_up(
        info, x_rows, b_parts, gain2, w1, grad_hidden, (cot_own,)
    )
    low2_own, low2_other = turn("turn_low2", info, low2)
    feed_other = weight_half(
        "feed_other", [(cot_other, [hidden]), (low2_other, [grad_pre])], None, (low2_own,)
    )
    *blocks, sums = back_blocks(
        "back_feed", info, [(grad_pre, w1)], gain2, low2, (feed_other,)
    )
    pieces, sent = ring_scatter(*blocks[:6])
    feed_got = lax.ppermute(feed_other, "seq", SWAP)
    feed_total = weight_half(
        "feed_own", [(cot_own, [hidden]), (low2_own, [grad_pre])], feed_got
    )
    grad_middle, gain2_grad, half_a, half_b = norm_back(
        "norm_back2", info, blocks[6], sums, pieces, gain2, middle, mean2, inv2, cotangent, True,
        (feed_total,),
    )
    g_parts = ring_gather(half_a, half_b)
    feed_blocks = exchange(feed_total, PLANE)

    branch, grad_gate, kept, own, give = back_mix(
        info, g_parts, wo, gate, grouped, ginv, query, arrival, (feed_total,)
    )

    branch_own, branch_other = turn("turn_branch", info, branch, (give,), True)
    grad_query, near_key, near_value = retain_back(
        info, kept, value, decay, key, query, weighted, mine, sibling, arrival, cosine, sine,
        (branch_own,),
    )
    mix_other = weight_half(
        "mix_other",
        [(branch_other, [mixed]), (low1_other, [grad_gate, grad_query])],
        None,
        (grad_query,),
    )
    mix_got = lax.ppermute(mix_other, "seq", SWAP)

    def fill_own(token):
        made["own"] = weight_half(
            "mix_own",
            [(branch_own, [mixed]), (low1_own, [grad_gate, grad_query])],
            mix_got,
            (token,),
        )
        return (made["own"],)

    feed = matmul_cols("feed_down", hidden, w2, BF16, (mix_other,), 1024)
    fed = lax.psum_scatter(feed, "head", scatter_dimension=1, tiled=True)

    far_mine, far_sibling = state_scan(
        info, behind, own, give, True, "_b",
        (lambda: (feed, feed_blocks), fill_own, lambda token: (), lambda token: (fed,)),
    )
    mix_x = exchange(gated(made["own"], (far_mine,)), axis_groups(True))
    grad_key, grad_value = key_value_back(
        info, far_mine, far_sibling, key, value, departure, near_key, near_value, cosine, sine,
        (),
    )
    kv_other = weight_half(
        "kv_other", [(low1_other, [grad_key, grad_value])]
    )
    kv_got = lax.ppermute(kv_other, "seq", SWAP)
    *blocks, sums = back_blocks(
        "back_proj", info,
        [(grad_query, wq), (grad_gate, wg), (grad_key, wk), (grad_value, wv)],
        gain1, low1, (kv_other, feed_blocks),
    )
    pieces, sent = ring_scatter(*blocks[:6])
    kv_blocks = weight_own_y(
        "kv_own", info, low1_own, [grad_key, grad_value], kv_got, sent
    )

    grad_x, gain1_grad = norm_back(
        "norm_back1", info, blocks[6], sums, pieces, gain1, layer_in, mean1, inv1, grad_middle,
        False, (kv_blocks[0],),
    )
    keys, vals = HEADS * KEY, HEADS * VAL
    kv_sent = send_blocks(kv_blocks[:3], False)
    kv_half = phase_sum("kv_mid", info, X_AT, kv_blocks[3], kv_sent)
    gains = sum_core_x(jnp.concatenate([gain1_grad, gain2_grad], axis=0), (mix_x,))
    mix_half = weight_mid("mix_mid", mix_x, gains)
    grad_w2, grad_w1 = weight_sum("feed_sum", feed_blocks, [vals, vals], (mix_half,))
    grad_wo, grad_wg, grad_wq, gains = weight_sum(
        "mix_sum", exchange(mix_half, axis_groups(False)), [vals, vals, keys]
    )
    grad_wk, grad_wv = last_sum(
        "kv_sum", kv_half[3], send_blocks(kv_half[:3], True), (keys, vals)
    )
    output = (middle + fed.astype(F32)).astype(BF16)
    return (
        output,
        grad_x,
        gains[0],
        grad_wq,
        grad_wk,
        grad_wv,
        grad_wg,
        grad_wo.T,
        gains[1],
        grad_w1,
        grad_w2.T,
    )


def solution(mesh):
    rows = P("seq", "head")
    cols = P(None, "head")
    tall = P("head", None)
    return jax.shard_map(
        shards,
        mesh=mesh,
        in_specs=(rows, P(), cols, cols, cols, cols, tall, P(), cols, tall, P(), rows),
        out_specs=(
            rows, rows, P("head"), rows, rows, rows, rows, P("head", "seq"), P("head"), rows,
            P("head", "seq"),
        ),
        check_vma=False,
    )
```

```python
import math

import jax
import jax.numpy as jnp
from jax import lax
from jax.experimental import pallas as pl
from jax.experimental.pallas import tpu as pltpu
from jax.sharding import PartitionSpec as P

KEY = 256
VAL = 512
SIDE = 4
CORES = 2
HEADS = 2
ROWS = 512
HALF = 256
PART = 512
MODEL = 2048
EXTRA = 16
EPSILON = 1e-05
F32 = jnp.float32
BF16 = jnp.bfloat16
VMEM_BYTES = 26 * 1024 * 1024
ORDER = (2, 1, 3, 0)


def head_shift(step):
    return [(h, (h + step) % SIDE) for h in range(SIDE)]


def seq_index(x, y, core):
    return (x * SIDE + y) * CORES + core


def seq_shift(dx, dy, swap=0):
    return [
        (seq_index(x, y, core), seq_index((x + dx) % SIDE, (y + dy) % SIDE, core ^ swap))
        for x in range(SIDE)
        for y in range(SIDE)
        for core in range(CORES)
    ]


SWAP = seq_shift(0, 0, 1)


def up(block):
    return lax.ppermute(block, "head", head_shift(1))


def down(block):
    return lax.ppermute(block, "head", head_shift(SIDE - 1))


def add_low(a, b):
    return (a.astype(F32) + b.astype(F32)).astype(BF16)


def relay(a, b, tokens):
    def body(a, b, to_a, to_b):
        to_a[...] = a[...]
        to_b[...] = b[...]

    return call(
        "relay", body, (1,), [], [(a,), (b,)], [(a.shape, a.dtype), (b.shape, b.dtype)], tokens
    )


def gated(array, tokens):
    n = len(tokens)

    def body(*refs):
        del refs

    out = pl.pallas_call(
        body,
        name="gated",
        in_specs=[pl.BlockSpec(memory_space=pl.ANY)] * (1 + n),
        out_specs=pl.BlockSpec(memory_space=pl.ANY),
        out_shape=pltpu.HBM(array.shape, array.dtype),
        input_output_aliases={0: 0},
    )(in_hbm(array), *[in_hbm(t) if is_pinned(t) else t for t in tokens])
    pin(out)
    return out


def hold(tokens):
    def body(out):
        out[...] = jnp.zeros_like(out)

    return call("hold", body, (1,), [], [], [((8, 128), F32)], tokens)[0]


def gather_direct(block):
    got = {k: lax.ppermute(block, "head", head_shift(k)) for k in (2, 1, 3)}
    return [block, got[1], got[2], got[3]]


def ring_gather(a, b, first=None):
    r1, l1 = up(a), down(b)
    r2, l2 = up(b), down(a)
    on_r, on_l = first(r1, l1) if first else (r1, l1)
    r3, l3 = up(on_r), down(on_l)
    return [a, b, r1, r2, r3, l3, l2, l1]


def ring_scatter(p2a, p2b, p1a, p1b, pma, pmb):
    t1, t2 = up(p2a), down(p2b)
    rb, la = up(p1b), down(pma)
    s1, s2 = add_low(p1a, t1), add_low(pmb, t2)
    ra, lb = up(s1), down(s2)
    return [ra, rb, la, lb], (s1, s2)


def whole(shape):
    return pl.BlockSpec(shape, lambda *_: (0,) * len(shape))


def once(shape):
    return pl.BlockSpec(
        shape, lambda *_: (0,) * len(shape), pipeline_mode=pl.Buffered(buffer_count=1)
    )


PINNED = []


def pin(*arrays):
    PINNED.extend(arrays)


def is_pinned(array):
    return any(array is other for other in PINNED)


def in_hbm(array):
    return pltpu.with_memory_space_constraint(array, pltpu.HBM)


COST_SCALE = 1.0
COSTS = {
    "kv_mid": 100,
    "scan_start_b": 100,
    "relay": 1,
    "hold": 0.1,
    "turn_low2": 1.5,
    "late": 100,
    "scan_end_b": 50,
    "norm1": 5,
    "key_value": 8,
    "query_part": 6,
    "gate": 4,
    "mix": 9,
    "cot_pass": 100,
    "feed_up": 11,
    "back_feed": 7,
    "back_mix": 6,
    "retain_back": 0.6,
    "feed_down": 2,
    "key_value_back": 100,
    "back_proj": 0.1,
    "feed_other": 5,
    "feed_own": 8,
    "mix_other": 0.180,
    "mix_own": 1,
    "kv_other": 0.90,
    "kv_own": 0.1,
    "feed_sum": 0.1,
    "mix_sum": 2,
    "kv_sum": 0.1,
    "norm_back1": 0.1,
    "norm_back2": 100,
}


def call(name, body, grid, scalars, ins, outs, tokens=(), scratch=(), keep=False):
    arrays = [in_hbm(item[0]) if is_pinned(item[0]) else item[0] for item in ins]
    in_specs = [once(i[0].shape) if len(i) == 1 else pl.BlockSpec(i[1], i[2]) for i in ins]
    out_specs = [whole(o[0]) if len(o) == 2 else pl.BlockSpec(o[2], o[3]) for o in outs]
    out_shape = [jax.ShapeDtypeStruct(o[0], o[1]) for o in outs]
    keep = range(len(outs)) if keep is True else (keep or ())
    out_shape = [
        pltpu.HBM(o.shape, o.dtype) if i in keep else o for i, o in enumerate(out_shape)
    ]
    n_in, n_tok, n_sc = len(arrays), len(tokens), len(scalars)
    tokens = [in_hbm(t) if is_pinned(t) else t for t in tokens]
    in_specs += [pl.BlockSpec(memory_space=pl.ANY)] * n_tok

    def run(*refs):
        body(*refs[: n_sc + n_in], *refs[n_sc + n_in + n_tok :])

    results = pl.pallas_call(
        run,
        name=name,
        grid_spec=pltpu.PrefetchScalarGridSpec(
            num_scalar_prefetch=n_sc,
            grid=grid,
            in_specs=in_specs,
            out_specs=out_specs,
            scratch_shapes=list(scratch),
        ),
        out_shape=out_shape,
        compiler_params=pltpu.CompilerParams(
            dimension_semantics=("arbitrary",) * len(grid), vmem_limit_bytes=VMEM_BYTES
        ),
        cost_estimate=pl.CostEstimate(
            flops=int(COSTS.get(name, 0.1) * COST_SCALE * 1.1e9),
            bytes_accessed=0,
            transcendentals=0,
        ),
    )(*scalars, *arrays, *tokens)
    pin(*[results[i] for i in keep])
    return results


def dot(left, right):
    return jnp.dot(left, right, preferred_element_type=F32)


def dot_t(left, right):
    return lax.dot_general(left, right, (((1,), (1,)), ((), ())), preferred_element_type=F32)


def t_dot(left, right):
    return lax.dot_general(left, right, (((0,), (0,)), ((), ())), preferred_element_type=F32)


def rotate(rows, cosine, sine):
    half = rows.shape[-1] // 2
    first, second = rows[:, :half], rows[:, half:]
    return jnp.concatenate([first * cosine - second * sine, second * cosine + first * sine], axis=1)


def sigmoid(v):
    return 0.5 + 0.5 * jnp.tanh(0.5 * v)


def head_col(info, k):
    return pl.multiple_of(lax.rem(info[0] + SIDE - k, SIDE) * PART, PART)


CHUNK = 16


def norm_rows(info, load, gain, low, mean_ref, inv_ref, own=None):
    for half in range(2):

        def step(i, _):
            at = pl.multiple_of(i * CHUNK, CHUNK)
            out = pl.ds(pl.multiple_of(half * HALF + i * CHUNK, CHUNK), CHUNK)
            parts = [load(k, half, at) for k in range(SIDE)]
            if own is not None:
                own[out, :] = parts[0]
            mean = sum(jnp.sum(p, axis=1, keepdims=True) for p in parts) / MODEL
            parts = [p - mean for p in parts]
            var = sum(jnp.sum(p * p, axis=1, keepdims=True) for p in parts) / MODEL
            inv = lax.rsqrt(var + EPSILON)
            mean_ref[out, :] = mean
            inv_ref[out, :] = inv
            for k in range(SIDE):
                cols = pl.ds(head_col(info, k), PART)
                low[out, cols] = (parts[k] * inv * gain[:, cols]).astype(BF16)
            return 0

        lax.fori_loop(0, HALF // CHUNK, step, 0, unroll=8)


def chunk_of(part, half, at):
    return part[pl.ds(pl.multiple_of(half * HALF + at, CHUNK), CHUNK), :].astype(F32)


def norm1(info, parts, gain, cotangent):
    def body(info, *refs):
        x = refs[:8]
        gain, cot, low, mean, inv, cot_out, rows = refs[8:]
        cot_out[...] = cot[...]
        for k in range(SIDE):
            rows[k, :HALF] = x[2 * k][...]
            rows[k, HALF:] = x[2 * k + 1][...]
        norm_rows(
            info,
            lambda k, half, at: x[2 * k + half][pl.ds(at, CHUNK), :].astype(F32),
            gain,
            low,
            mean,
            inv,
        )

    return call(
        "norm1",
        body,
        (1,),
        [info],
        [(p,) for p in parts] + [(gain,), (cotangent,)],
        [
            ((ROWS, MODEL), BF16),
            ((ROWS, 1), F32),
            ((ROWS, 1), F32),
            ((ROWS, PART), BF16),
            ((SIDE, ROWS, PART), BF16),
        ],
        keep=(4,),
    )


def key_value(info, low, wk, wv, cosine, sine, departure):
    def body(info, low, wk, wv, cosine, sine, departure, key, value, own, give):
        head = pl.program_id(0)
        k = rotate(dot(low[...], wk[...]), cosine[...], sine[...]).astype(BF16)
        key[...] = k
        v = dot(low[...], wv[...]).astype(BF16)
        value[...] = v
        state = t_dot((k.astype(F32) * departure[0]).astype(BF16), v)

        @pl.when(head == info[1])
        def _():
            own[...] = state

        @pl.when(head != info[1])
        def _():
            give[...] = state.astype(BF16)

    by_head = lambda h, *_: (0, h)
    return call(
        "key_value",
        body,
        (HEADS,),
        [info],
        [
            (low,),
            (wk, (MODEL, KEY), by_head),
            (wv, (MODEL, VAL), by_head),
            (cosine,),
            (sine,),
            (departure, (1, ROWS, 1), lambda h, *_: (h, 0, 0)),
        ],
        [
            ((ROWS, HEADS * KEY), BF16, (ROWS, KEY), by_head),
            ((ROWS, HEADS * VAL), BF16, (ROWS, VAL), by_head),
            ((KEY, VAL), F32),
            ((KEY, VAL), BF16),
        ],
        keep=(0, 1),
    )


def query_part(low, wq, key, value, decay, cosine, sine, tokens):
    def body(low, wq, key, value, decay, cosine, sine, query, weighted, within):
        q = rotate(dot(low[...], wq[...]), cosine[...], sine[...]).astype(BF16)
        query[...] = q
        w = (dot_t(q, key[...]) * decay[0]).astype(BF16)
        weighted[0] = w
        within[...] = dot(w, value[...])

    by_head = lambda h, *_: (0, h)
    cube = lambda h, *_: (h, 0, 0)
    return call(
        "query_part",
        body,
        (HEADS,),
        [],
        [
            (low,),
            (wq, (MODEL, KEY), by_head),
            (key, (ROWS, KEY), by_head),
            (value, (ROWS, VAL), by_head),
            (decay, (1, ROWS, ROWS), cube),
            (cosine,),
            (sine,),
        ],
        [
            ((ROWS, HEADS * KEY), BF16, (ROWS, KEY), by_head),
            ((HEADS, ROWS, ROWS), BF16, (1, ROWS, ROWS), cube),
            ((ROWS, HEADS * VAL), F32, (ROWS, VAL), by_head),
        ],
        tokens,
        keep=(0, 1),
    )


def matmul_cols(name, left, right, out_type, tokens=(), block=512):
    def body(left, right, out):
        out[...] = dot(left[...], right[...]).astype(out_type)

    depth, cols = right.shape
    by_col = lambda i, *_: (0, i)
    return call(
        name,
        body,
        (cols // block,),
        [],
        [(left,), (right, (depth, block), by_col)],
        [((left.shape[0], cols), out_type, (left.shape[0], block), by_col)],
        tokens,
        keep=True,
    )[0]


def block_outs(extra):
    tall = ((HALF + extra, PART), BF16)
    return [tall, ((HALF, PART), BF16)] * 3 + [((ROWS, PART), F32)]


def put_blocks(step, make, outs):
    for i in range(2):
        block = make(i)
        for s in range(2):
            k = 2 * s + i

            @pl.when(step == s)
            def _():
                if k == SIDE - 1:
                    outs[6][...] = block
                else:
                    outs[2 * k][:HALF, :] = block[:HALF].astype(BF16)
                    outs[2 * k + 1][...] = block[HALF:].astype(BF16)


def pick(mine, sibling, info, head):
    return jnp.where(info[1] == head, mine[...], sibling[...])


def mix(info, within, gate, query, mine, sibling, arrival, wo, tokens):
    def body(info, within, gate, query, mine, sibling, arrival, wo, mixed, grouped, ginv, *outs):
        for half in range(2):
            rows = slice(half * HALF, (half + 1) * HALF)
            for head in range(HEADS):
                cols = slice(head * VAL, (head + 1) * VAL)
                state = pick(mine, sibling, info, head)
                cross = dot(query[rows, head * KEY : (head + 1) * KEY], state)
                kept = within[rows, cols] + arrival[head, rows] * cross
                kept = kept - jnp.mean(kept, axis=1, keepdims=True)
                inv = lax.rsqrt(jnp.mean(kept * kept, axis=1, keepdims=True) + float(KEY))
                group = kept * inv
                g = gate[rows, cols].astype(F32)
                ginv[head, rows] = inv
                grouped[rows, cols] = group.astype(BF16)
                mixed[rows, cols] = (group * (g * sigmoid(g))).astype(BF16)
            for i in range(SIDE):
                at = pl.ds(pl.multiple_of(info[2 + i] * PART, PART), PART)
                block = dot(mixed[rows], wo[:, at])
                if i == SIDE - 1:
                    outs[6][rows] = block
                else:
                    outs[2 * i + half][...] = block.astype(BF16)

    cols = HEADS * VAL
    return call(
        "mix",
        body,
        (1,),
        [info],
        [(within,), (gate,), (query,), (mine,), (sibling,), (arrival,), (wo,)],
        [((ROWS, cols), BF16), ((ROWS, cols), BF16), ((HEADS, ROWS, 1), F32)] + block_outs(0),
        tokens,
        keep=(0, 1),
    )


def sum_branch(p0, pieces, tokens):
    def body(p0, ra, rb, la, lb, a, b):
        a[...] = (p0[:HALF] + ra[...].astype(F32) + la[...].astype(F32)).astype(BF16)
        b[...] = (p0[HALF:] + rb[...].astype(F32) + lb[...].astype(F32)).astype(BF16)

    return call(
        "sum_branch",
        body,
        (1,),
        [],
        [(p0,)] + [(p,) for p in pieces],
        [((HALF, PART), BF16), ((HALF, PART), BF16)],
        tokens,
    )


def feed_up(info, x_rows, b_parts, gain, w1, grad_hidden, tokens):
    block = 512

    def body(info, *refs):
        x, b = refs[0], refs[1:9]
        gain, w1, grad_hidden, ffn_in, mean, inv, own, hidden, grad_pre = refs[9:]

        @pl.when(pl.program_id(0) == 0)
        def _():
            def load(k, half, at):
                branch = b[2 * k + half][pl.ds(at, CHUNK), :].astype(F32)
                return chunk_of(x.at[k], half, at) + branch

            norm_rows(info, load, gain, ffn_in, mean, inv, own)

        pre = dot(ffn_in[...], w1[...])
        cdf = 0.5 * (1.0 + lax.erf(pre * (2.0**-0.5)))
        hidden[...] = (pre * cdf).astype(BF16)
        pdf = jnp.exp(-0.5 * pre * pre) * ((2.0 * math.pi) ** -0.5)
        grad_pre[...] = ((cdf + pre * pdf) * grad_hidden[...].astype(F32)).astype(BF16)

    by_col = lambda i, *_: (0, i)
    cols = w1.shape[1]
    tall = ((ROWS, cols), BF16, (ROWS, block), by_col)
    return call(
        "feed_up",
        body,
        (cols // block,),
        [info],
        [(x_rows,)]
        + [(p,) for p in b_parts]
        + [
            (gain,),
            (w1, (MODEL, block), by_col),
            (grad_hidden, (ROWS, block), by_col),
        ],
        [
            ((ROWS, MODEL), BF16),
            ((ROWS, 1), F32),
            ((ROWS, 1), F32),
            ((ROWS, PART), F32),
            tall,
            tall,
        ],
        tokens,
        keep=(1, 2, 3),
    )


def back_blocks(name, info, pairs, gain, low, tokens=()):
    n = len(pairs)

    def body(info, *refs):
        grads, weights = refs[:n], refs[n : 3 * n]
        gains, lows = refs[3 * n : 3 * n + 2], refs[3 * n + 2 : 3 * n + 4]
        outs, sums, acc = refs[3 * n + 4 : 3 * n + 11], refs[3 * n + 11], refs[3 * n + 12]
        step = pl.program_id(0)
        lane = lax.broadcasted_iota(jnp.int32, (ROWS, 128), 1)

        @pl.when(step == 0)
        def _():
            acc[...] = jnp.zeros_like(acc)

        def make(i):
            total = dot_t(grads[0][...], weights[2 * 0 + i][...])
            for j in range(1, n):
                total = total + dot_t(grads[j][...], weights[2 * j + i][...])
            first = jnp.sum(total * gains[i][...], axis=1, keepdims=True) / MODEL
            second = jnp.sum(total * lows[i][...].astype(F32), axis=1, keepdims=True) / MODEL
            acc[...] += jnp.where(lane == 0, first, jnp.where(lane == 1, second, 0.0))
            return total

        put_blocks(step, make, outs)

        @pl.when(step == 1)
        def _():
            turned = acc[...].T[:EXTRA]
            sums[...] = turned
            for k in range(SIDE - 1):
                outs[2 * k][HALF:, :] = turned.astype(BF16)

    def by_row(j):
        return lambda i, info: (info[2 + j + 2 * i], 0)

    def by_col(j):
        return lambda i, info: (0, info[2 + j + 2 * i])

    return call(
        name,
        body,
        (2,),
        [info],
        [(g,) for g, _ in pairs]
        + [(in_hbm(w), (PART, w.shape[1]), by_row(j)) for _, w in pairs for j in range(2)]
        + [(gain, (1, PART), by_col(j)) for j in range(2)]
        + [(low, (ROWS, PART), by_col(j)) for j in range(2)],
        block_outs(EXTRA) + [((EXTRA, PART), F32)],
        tokens,
        [pltpu.VMEM((ROWS, 128), F32)],
        keep=(6,),
    )


def norm_back(
    name, info, p0, sums, pieces, gain, rows, mean, inv, residual, low_out, tokens
):
    def body(
        info, p0, sums, ra, rb, la, lb, gain, rows, mean, inv, residual, grad, gain_grad, *low
    ):
        scale = gain[:, pl.ds(head_col(info, 0), PART)]
        total = sums[...] + ra[HALF:].astype(F32) + la[HALF:].astype(F32)
        total = jnp.concatenate([total, jnp.zeros((128 - EXTRA, PART), F32)], axis=0).T
        acc = jnp.zeros((1, PART), F32)
        for half, (one, two) in enumerate(((ra, la), (rb, lb))):
            for quarter in range(2):
                at = slice(quarter * 128, (quarter + 1) * 128)
                out = slice(half * HALF + quarter * 128, half * HALF + (quarter + 1) * 128)
                g = p0[out] + one[at].astype(F32) + two[at].astype(F32)
                normed = (rows[out].astype(F32) - mean[out]) * inv[out]
                acc = acc + jnp.sum(g * normed, axis=0, keepdims=True)
                back = inv[out] * (g * scale - total[out, 0:1] - normed * total[out, 1:2])
                new = residual[out].astype(F32) + back
                grad[out] = new
                if low_out:
                    low[half][at] = new.astype(BF16)
        gain_grad[...] = acc

    outs = [((ROWS, PART), F32), ((1, PART), F32)]
    if low_out:
        outs += [((HALF, PART), BF16)] * 2
    return call(
        name,
        body,
        (1,),
        [info],
        [(p0,), (sums,)]
        + [(p,) for p in pieces]
        + [(gain,), (rows,), (mean,), (inv,), (residual,)],
        outs,
        tokens,
        keep=(0,) if low_out else (),
    )


def back_mix(info, parts, wo, gate, grouped, ginv, query, arrival, tokens):
    def body(info, *refs):
        parts = refs[:8]
        wo, gate, grouped, ginv, query, arrival, branch, grad_gate, kept, own, give = refs[8:]
        head = pl.program_id(0)

        @pl.when(head == 0)
        def _():
            for k in range(SIDE):
                cols = pl.ds(head_col(info, k), PART)
                branch[:HALF, cols] = parts[2 * k][...]
                branch[HALF:, cols] = parts[2 * k + 1][...]

        for half in range(2):
            rows = slice(half * HALF, (half + 1) * HALF)
            m = dot_t(branch[rows], wo[...])
            g = gate[rows].astype(F32)
            gate_s = sigmoid(g)
            group = grouped[rows].astype(F32)
            slope = gate_s * (1.0 + g * (1.0 - gate_s))
            grad_gate[rows] = (m * group * slope).astype(BF16)
            e = m * (g * gate_s)
            e = ginv[0, rows] * (
                e
                - jnp.mean(e, axis=1, keepdims=True)
                - group * jnp.mean(e * group, axis=1, keepdims=True)
            )
            kept[rows] = e.astype(BF16)
        moved = (query[...].astype(F32) * arrival[0]).astype(BF16)
        state = t_dot(moved, kept[...])

        @pl.when(head == info[1])
        def _():
            own[...] = state

        @pl.when(head != info[1])
        def _():
            give[...] = state.astype(BF16)

    by_head = lambda h, *_: (0, h)
    cube = lambda h, *_: (h, 0, 0)
    cols = HEADS * VAL
    return call(
        "back_mix",
        body,
        (HEADS,),
        [info],
        [(p,) for p in parts]
        + [
            (wo, (VAL, MODEL), lambda h, *_: (h, 0)),
            (gate, (ROWS, VAL), by_head),
            (grouped, (ROWS, VAL), by_head),
            (ginv, (1, ROWS, 1), cube),
            (query, (ROWS, KEY), by_head),
            (arrival, (1, ROWS, 1), cube),
        ],
        [
            ((ROWS, MODEL), BF16),
            ((ROWS, cols), BF16, (ROWS, VAL), by_head),
            ((ROWS, cols), BF16, (ROWS, VAL), by_head),
            ((KEY, VAL), F32),
            ((KEY, VAL), BF16),
        ],
        tokens,
        keep=(1, 2),
    )


def retain_back(info, kept, value, decay, key, query, weighted, mine, sibling, arrival, cosine, sine, tokens):
    def body(
        info, kept, value, decay, key, query, weighted, mine, sibling, arrival, cosine, sine,
        grad_query, near_key, near_value,
    ):
        head = pl.program_id(0)
        e = kept[...]
        s = (dot_t(e, value[...]) * decay[0]).astype(BF16)
        state = pick(mine, sibling, info, head)
        gq = dot(s, key[...]) + arrival[0] * dot_t(e, state)
        grad_query[...] = rotate(gq, cosine[...], -sine[...]).astype(BF16)
        near_key[...] = t_dot(s, query[...])
        near_value[...] = t_dot(weighted[0], e)

    by_head = lambda h, *_: (0, h)
    cube = lambda h, *_: (h, 0, 0)
    keys, vals = HEADS * KEY, HEADS * VAL
    return call(
        "retain_back",
        body,
        (HEADS,),
        [info],
        [
            (kept, (ROWS, VAL), by_head),
            (value, (ROWS, VAL), by_head),
            (decay, (1, ROWS, ROWS), cube),
            (key, (ROWS, KEY), by_head),
            (query, (ROWS, KEY), by_head),
            (weighted, (1, ROWS, ROWS), cube),
            (mine,),
            (sibling,),
            (arrival, (1, ROWS, 1), cube),
            (cosine,),
            (sine,),
        ],
        [
            ((ROWS, keys), BF16, (ROWS, KEY), by_head),
            ((ROWS, keys), F32, (ROWS, KEY), by_head),
            ((ROWS, vals), F32, (ROWS, VAL), by_head),
        ],
        tokens,
        keep=True,
    )


def key_value_back(info, mine, sibling, key, value, departure, near_key, near_value, cosine, sine, tokens):
    def body(
        info, mine, sibling, key, value, departure, near_key, near_value, cosine, sine,
        grad_key, grad_value,
    ):
        state = pick(mine, sibling, info, pl.program_id(0))
        gk = near_key[...] + departure[0] * dot_t(value[...], state)
        grad_key[...] = rotate(gk, cosine[...], -sine[...]).astype(BF16)
        gv = near_value[...] + departure[0] * dot(key[...], state)
        grad_value[...] = gv.astype(BF16)

    by_head = lambda h, *_: (0, h)
    keys, vals = HEADS * KEY, HEADS * VAL
    return call(
        "key_value_back",
        body,
        (HEADS,),
        [info],
        [
            (mine,),
            (sibling,),
            (key, (ROWS, KEY), by_head),
            (value, (ROWS, VAL), by_head),
            (departure, (1, ROWS, 1), lambda h, *_: (h, 0, 0)),
            (near_key, (ROWS, KEY), by_head),
            (near_value, (ROWS, VAL), by_head),
            (cosine,),
            (sine,),
        ],
        [
            ((ROWS, keys), BF16, (ROWS, KEY), by_head),
            ((ROWS, vals), BF16, (ROWS, VAL), by_head),
        ],
        tokens,
        keep=True,
    )


def turn(name, info, low, tokens=(), keep=False):
    xs = 2

    def body(info, low, own, other, scratch):
        scratch[...] = low[...].T
        for x in range(xs):
            for y in range(SIDE):
                base = (x * SIDE + y) * CORES * 64
                mine = pl.ds(pl.multiple_of(base + info[1] * 64, 64), 64)
                far = pl.ds(pl.multiple_of(base + (1 - info[1]) * 64, 64), 64)
                own[x, y] = scratch[mine, :]
                other[x, y] = scratch[far, :]

    out = ((SIDE, SIDE, 64, ROWS), BF16, (xs, SIDE, 64, ROWS), lambda i, *_: (i, 0, 0, 0))
    own, other = call(
        name,
        body,
        (SIDE // xs,),
        [info],
        [(low, (ROWS, xs * PART), lambda i, *_: (0, i))],
        [out, out],
        tokens,
        [pltpu.VMEM((xs * PART, ROWS), BF16)],
        keep=keep,
    )
    flat = own.reshape(-1, ROWS), other.reshape(-1, ROWS)
    if keep:
        pin(*flat)
    return flat


def cot_pass(info, parts, w2, tokens):
    xs = 2

    def body(info, a, b, c, d, w2, own, other, out, whole_rows, scratch):
        step = pl.program_id(0)

        @pl.when(step == 0)
        def _():
            for k, part in enumerate((a, b, c, d)):
                whole_rows[:, pl.ds(head_col(info, k), PART)] = part[...]

        out[...] = dot_t(whole_rows[...], w2[...]).astype(BF16)
        cols = pl.ds(pl.multiple_of(step * xs * PART, PART), xs * PART)
        scratch[...] = whole_rows[:, cols].T
        for x in range(xs):
            for y in range(SIDE):
                base = (x * SIDE + y) * CORES * 64
                mine = pl.ds(pl.multiple_of(base + info[1] * 64, 64), 64)
                far = pl.ds(pl.multiple_of(base + (1 - info[1]) * 64, 64), 64)
                own[x, y] = scratch[mine, :]
                other[x, y] = scratch[far, :]

    turned = ((SIDE, SIDE, 64, ROWS), BF16, (xs, SIDE, 64, ROWS), lambda i, *_: (i, 0, 0, 0))
    cols = w2.shape[0]
    own, other, out = call(
        "cot_pass",
        body,
        (2,),
        [info],
        [(p,) for p in parts] + [(w2, (cols // 2, MODEL), lambda i, *_: (i, 0))],
        [turned, turned, ((ROWS, cols), BF16, (ROWS, cols // 2), lambda i, *_: (0, i))],
        tokens,
        [pltpu.VMEM((ROWS, MODEL), BF16), pltpu.VMEM((xs * PART, ROWS), BF16)],
    )
    return own.reshape(-1, ROWS), other.reshape(-1, ROWS), out


def widths(groups):
    return [sum(r.shape[1] for r in rights) for _, rights in groups]


def weight_half(name, groups, arrived=None, tokens=()):
    n_left = len(groups)
    rights = [r for _, rs in groups for r in rs]
    counts = [len(rs) for _, rs in groups]
    n = len(rights)
    width = sum(widths(groups))

    def body(*refs):
        lefts, rest = refs[:n_left], refs[n_left : n_left + n]
        out = refs[-1]
        at = 0
        which = 0
        for left, count in zip(lefts, counts):
            for r in rest[which : which + count]:
                cols = slice(at, at + r.shape[1])
                total = dot(left[...], r[...])
                if arrived is not None:
                    total = total + refs[n_left + n][:, cols].astype(F32)
                out[:, cols] = total.astype(BF16)
                at += r.shape[1]
            which += count

    block = lambda i, *_: (i, 0)
    return call(
        name,
        body,
        (2,),
        [],
        [(left, (ROWS, ROWS), block) for left, _ in groups]
        + [(r,) for r in rights]
        + ([(arrived, (ROWS, width), block)] if arrived is not None else []),
        [((2 * ROWS, width), BF16, (ROWS, width), block)],
        tokens,
        keep=True,
    )[0]


def axis_groups(along_x):
    if along_x:
        return [
            [seq_index(x, y, c) for x in range(SIDE)] for y in range(SIDE) for c in range(CORES)
        ]
    return [[seq_index(x, y, c) for y in range(SIDE)] for x in range(SIDE) for c in range(CORES)]


def exchange(total, groups):
    blocks = total
    if total.ndim == 2:
        blocks = total.reshape(len(groups[0]), -1, total.shape[-1])
    blocks = lax.all_to_all(blocks, "seq", 0, 0, axis_index_groups=groups, tiled=True)
    pin(blocks)
    return blocks


def weight_mid(name, blocks, gains, tokens=()):
    count, rows, width = blocks.shape
    part = rows // SIDE
    gains = jnp.pad(gains, ((0, EXTRA - gains.shape[0]), (0, 0)))

    def body(blocks, gains, out):
        total = blocks[0].astype(F32)
        for k in range(1, count):
            total = total + blocks[k].astype(F32)
        for y in range(SIDE):
            out[y, :, :width] = total[y * part : (y + 1) * part].astype(BF16)
            out[y, :EXTRA, width:] = gains[...].astype(BF16)
            out[y, EXTRA:, width:] = jnp.zeros((part - EXTRA, PART), BF16)

    return call(
        name,
        body,
        (1,),
        [],
        [(blocks,), (gains,)],
        [((SIDE, part, width + PART), BF16)],
        tokens,
        keep=True,
    )[0]


def weight_sum(name, blocks, parts, tokens=()):
    def body(blocks, *outs):
        at = 0
        for out, part in zip(outs, parts):
            cols = slice(at, at + part)
            rows = slice(0, out.shape[0])
            total = blocks[0, rows, cols].astype(F32)
            for k in range(1, blocks.shape[0]):
                total = total + blocks[k, rows, cols].astype(F32)
            out[...] = total
            at += part

    return call(
        name,
        body,
        (1,),
        [],
        [(blocks,)],
        [((64, part), F32) for part in parts[:-1]] + [((EXTRA, parts[-1]), F32)],
        tokens,
    )

def weight_own_y(name, info, left, rights, arrived, tokens=()):
    n = len(rights)
    width = sum(r.shape[1] for r in rights)
    left = left.reshape(SIDE, SIDE, 64, ROWS)
    arrived = arrived.reshape(SIDE, SIDE, 64, width)
    pin(left)

    def body(info, *refs):
        lefts, rights, got, outs = refs[:2], refs[2 : 2 + n], refs[2 + n : 4 + n], refs[4 + n :]
        step = pl.program_id(0)
        for i in range(2):
            at = 0
            for r in rights:
                cols = slice(at, at + r.shape[1])
                total = dot(lefts[i][...].reshape(HALF, ROWS), r[...])
                total = total + got[i][:, :, :, cols].reshape(HALF, r.shape[1]).astype(F32)
                for s in range(2):

                    @pl.when(step == s)
                    def _():
                        out = outs[2 * s + i]
                        out[:, cols] = total.astype(out.dtype)

                at += r.shape[1]

    def block(j):
        def at(i, info):
            return (0, lax.rem(info[Y_AT] + ORDER_OF(2 * i + j), SIDE), 0, 0)

        return at

    return call(
        name,
        body,
        (2,),
        [info],
        [(left, (SIDE, 1, 64, ROWS), block(j)) for j in range(2)]
        + [(r,) for r in rights]
        + [(arrived, (SIDE, 1, 64, width), block(j)) for j in range(2)],
        [((HALF, width), BF16)] * 3 + [((HALF, width), F32)],
        tokens,
    )


def ORDER_OF(i):
    return jnp.where(i == 0, 2, jnp.where(i == 1, 1, jnp.where(i == 2, 3, 0)))


def phase_sum(name, info, where, base, received, tokens=()):
    width = base.shape[1]

    def body(info, base, a, b, c, *refs):
        outs, scratch = refs[:SIDE], refs[SIDE]
        scratch[...] = base[...] + a[...].astype(F32) + b[...].astype(F32) + c[...].astype(F32)
        for i, k in enumerate(ORDER):
            at = pl.multiple_of(lax.rem(info[where] + k, SIDE) * 64, 64)
            outs[i][...] = scratch[pl.ds(at, 64), :].astype(outs[i].dtype)

    return call(
        name,
        body,
        (1,),
        [info],
        [(base,)] + [(r,) for r in received],
        [((64, width), BF16)] * 3 + [((64, width), F32)],
        tokens,
        [pltpu.VMEM((HALF, width), F32)],
    )


def plain_mid(name, blocks, tokens=()):
    def body(blocks, out):
        total = blocks[0].astype(F32)
        for k in range(1, blocks.shape[0]):
            total = total + blocks[k].astype(F32)
        out[...] = total.astype(BF16)

    shape = blocks.shape[1:]
    return call(
        name, body, (1,), [], [(blocks,)], [(shape, BF16)], tokens, keep=True
    )[0]


def last_sum(name, base, received, parts, tokens=()):
    def body(base, a, b, c, *outs):
        at = 0
        for out in outs:
            cols = slice(at, at + out.shape[1])
            out[...] = base[:, cols] + sum(r[:, cols].astype(F32) for r in (a, b, c))
            at += out.shape[1]

    return call(
        name,
        body,
        (1,),
        [],
        [(base,)] + [(r,) for r in received],
        [((64, w), F32) for w in parts],
        tokens,
    )


def shift_of(along_x):
    return (lambda k: seq_shift(k, 0)) if along_x else (lambda k: seq_shift(0, k))


def send_blocks(blocks, along_x):
    shift = shift_of(along_x)
    return [lax.ppermute(b, "seq", shift(k)) for b, k in zip(blocks, ORDER[:3])]


X_AT, Y_AT = 6, 7


def scan_weights(decay, place, reverse):
    x, y, _ = place
    rel = jnp.arange(SIDE)
    origin = lax.rem(y - rel + SIDE, SIDE)
    target = lax.rem(y + rel, SIDE)
    hops = jnp.arange(1, SIDE)
    if reverse:
        row = origin
        before, counts = SIDE * (SIDE - hops - 1), x + (SIDE - hops) < SIDE
        gap = origin[None, :] - target[:, None]
        carry = SIDE - 1 - target
    else:
        row = SIDE - 1 - origin
        before, counts = SIDE * (hops - 1), x >= hops
        gap = target[:, None] - origin[None, :]
        carry = target
    gap = gap.reshape(-1)
    power = jnp.concatenate([row, before, jnp.maximum(gap - 1, 0), carry]).astype(F32)
    keep = jnp.concatenate([row >= 0, counts, gap > 0, carry >= 0]).astype(F32)
    values = keep * jnp.exp(2.0 * jnp.log(decay) * power)
    return jnp.concatenate([decay[None], values, jnp.zeros((4,), F32)])


W_ROW, W_BEFORE, W_ANSWER, W_CARRY = 1, 5, 8, 24
QUARTER = KEY // SIDE


def state_scan(info, weights, own, give, reverse, tag, fills):
    far = 1 if reverse else 0

    def start_body(info, w, own, got, p2, p1, p3, p0, scratch):
        a, b = own[...], got[...].astype(F32)
        scratch[...] = jnp.where(info[1] == far, w[0] * a + b, a + w[0] * b).astype(BF16)
        for k, out in zip(ORDER, (p2, p1, p3, p0)):
            at = pl.multiple_of(lax.rem(info[Y_AT] + k, SIDE) * QUARTER, QUARTER)
            out[...] = scratch[pl.ds(at, QUARTER), :]

    piece = ((QUARTER, VAL), BF16)
    got = lax.ppermute(give, "seq", SWAP)
    sent = call(
        "scan_start" + tag, start_body, (1,), [info, weights], [(own,), (got,)], [piece] * 4,
        fills[0](), scratch=[pltpu.VMEM((KEY, VAL), BF16)],
    )
    at2, at1, at3 = send_blocks(sent[:3], False)
    pieces = [sent[3], at1, at2, at3]

    def row_body(w, p0, p1, p2, p3, total):
        total[...] = sum(
            w[W_ROW + j] * p[...].astype(F32) for j, p in enumerate((p0, p1, p2, p3))
        ).astype(BF16)

    row = call(
        "scan_row" + tag, row_body, (1,), [weights], [(p,) for p in pieces], [piece],
        fills[1](sent[0]),
    )[0]
    at2, at1, at3 = send_blocks([row] * 3, True)

    def answer_body(w, p0, p1, p2, p3, b1, b2, b3, *outs):
        p = [r[...].astype(F32) for r in (p0, p1, p2, p3)]
        before = sum(w[W_BEFORE + j] * r[...].astype(F32) for j, r in enumerate((b1, b2, b3)))
        for k, out in zip(ORDER, outs):
            total = w[W_CARRY + k] * before
            for j in range(SIDE):
                total = total + w[W_ANSWER + SIDE * k + j] * p[j]
            out[...] = total.astype(BF16)

    answers = call(
        "scan_answer" + tag, answer_body, (1,), [weights],
        [(p,) for p in pieces] + [(at1,), (at2,), (at3,)], [piece] * 4, fills[2](row),
    )
    at2, at1, at3 = send_blocks(answers[:3], False)

    def end_body(info, w, b0, b1, b2, b3, own, got, mine, theirs, scratch):
        for k, b in enumerate((b0, b1, b2, b3)):
            at = pl.multiple_of(lax.rem(info[Y_AT] + SIDE - k, SIDE) * QUARTER, QUARTER)
            scratch[pl.ds(at, QUARTER), :] = b[...].astype(F32)
        chip = scratch[...]
        is_far = info[1] == far
        later = w[0] * chip + jnp.where(is_far, own[...], got[...].astype(F32))
        mine[...] = jnp.where(is_far, chip, later).astype(BF16)
        theirs[...] = jnp.where(is_far, later, chip).astype(BF16)

    state = ((KEY, VAL), BF16)
    mine, theirs = call(
        "scan_end" + tag, end_body, (1,), [info, weights],
        [(answers[3],), (at1,), (at2,), (at3,), (own,), (got,)], [state, state],
        fills[3](answers[0]), scratch=[pltpu.VMEM((KEY, VAL), F32)],
    )
    return mine, lax.ppermute(theirs, "seq", SWAP)


def sum_core_x(values, tokens):
    def body(a, b, out):
        out[...] = a[...] + b[...]

    got = lax.ppermute(values, "seq", SWAP)
    values = call(
        "gain_pair", body, (1,), [], [(values,), (got,)], [(values.shape, F32)], tokens
    )[0]
    return values + sum(lax.ppermute(values, "seq", seq_shift(k, 0)) for k in (1, 2, 3))


def shards(layer_in, gain1, wq, wk, wv, wg, wo, gain2, w1, w2, starts, cotangent):
    seq_rank = lax.axis_index("seq")
    head_rank = lax.axis_index("head")
    x, y, core = (
        seq_rank // (SIDE * CORES),
        (seq_rank // CORES) % SIDE,
        seq_rank % CORES,
    )
    place = (x, y, core)
    PINNED.clear()
    info = jnp.stack(
        [head_rank, core] + [(head_rank + k) % SIDE for k in ORDER] + [x, y]
    ).astype(jnp.int32)
    gain1, gain2 = gain1[None], gain2[None]

    offsets = jnp.arange(ROWS, dtype=jnp.int32)
    positions = seq_rank * ROWS + offsets
    member = positions[:, None] >= starts[None, :]
    doc_ids = jnp.sum(member.astype(jnp.int32), axis=-1) - 1
    last_start = jnp.max(jnp.where(member, starts[None, :], 0), axis=-1)
    relative = (positions - last_start).astype(F32)
    prior_doc = jnp.sum((seq_rank * ROWS - 1 >= starts).astype(jnp.int32)) - 1
    half_dim = KEY // 2
    frequency = jnp.exp(-math.log(10000.0) * jnp.arange(half_dim, dtype=F32) / half_dim)
    angles = relative[:, None] * frequency[None, :]
    cosine, sine = jnp.cos(angles), jnp.sin(angles)
    head_ids = (head_rank * HEADS + jnp.arange(HEADS, dtype=jnp.int32)).astype(F32)
    log_decay = jnp.log1p(-jnp.exp2(-5.0 - head_ids))
    gap_grid = offsets[:, None] - offsets[None, :]
    keep = (gap_grid >= 0) & (doc_ids[:, None] == doc_ids[None, :])
    gap_float = jnp.where(gap_grid >= 0, gap_grid, 0).astype(F32)
    decay = jnp.where(keep[None], jnp.exp(gap_float[None] * log_decay[:, None, None]), 0.0)
    step_float = offsets.astype(F32)
    arrival = jnp.exp((step_float[None, :] + 1.0) * log_decay[:, None]) * (
        doc_ids == prior_doc
    ).astype(F32)
    departure = jnp.exp((ROWS - 1.0 - step_float)[None, :] * log_decay[:, None]) * (
        doc_ids == doc_ids[ROWS - 1]
    ).astype(F32)
    arrival, departure = arrival[:, :, None], departure[:, :, None]
    pin(decay)
    rank_decay = lax.dynamic_index_in_dim(jnp.exp(ROWS * log_decay), core, 0, False)
    ahead = scan_weights(rank_decay, place, False)
    behind = scan_weights(rank_decay, place, True)

    tables = (arrival, departure, ahead, behind, info)
    x_parts = ring_gather(
        layer_in[:HALF], layer_in[HALF:], lambda r, l: relay(r, l, tables)
    )
    low1, mean1, inv1, cot_again, x_rows = norm1(info, x_parts, gain1, cotangent)
    cot_parts = gather_direct(cot_again)
    key, value, own, give = key_value(info, low1, wk, wv, cosine, sine, departure)
    made = {}

    def fill_query():
        made["q"] = query_part(low1, wq, key, value, decay, cosine, sine, (give,))
        return (made["q"][0],)

    def fill_gate(token):
        made["gate"] = matmul_cols("gate", low1, wg, BF16, (token, *cot_parts[1:]))
        return (made["gate"],)

    mine, sibling = state_scan(
        info, ahead, own, give, False, "_a", (fill_query, fill_gate, lambda token: (), lambda token: ())
    )
    query, weighted, within = made["q"]
    gate = made["gate"]
    mixed, grouped, ginv, *blocks = mix(
        info, within, gate, query, mine, sibling, arrival, wo, ()
    )
    pieces, sent = ring_scatter(*blocks[:6])
    cot_own, cot_other, grad_hidden = cot_pass(info, cot_parts, w2, sent)
    low1_own, low1_other = turn("turn_low1", info, low1, (cot_own,), True)
    b_parts = ring_gather(*sum_branch(blocks[6], pieces, (grad_hidden, low1_own)))

    low2, mean2, inv2, middle, hidden, grad_pre = feed_up(
        info, x_rows, b_parts, gain2, w1, grad_hidden, (cot_own,)
    )
    low2_own, low2_other = turn("turn_low2", info, low2)
    feed_other = weight_half(
        "feed_other", [(cot_other, [hidden]), (low2_other, [grad_pre])], None, (low2_own,)
    )
    *blocks, sums = back_blocks(
        "back_feed", info, [(grad_pre, w1)], gain2, low2, (feed_other,)
    )
    pieces, sent = ring_scatter(*blocks[:6])
    feed_got = lax.ppermute(feed_other, "seq", SWAP)
    feed_total = weight_half(
        "feed_own", [(cot_own, [hidden]), (low2_own, [grad_pre])], feed_got
    )
    grad_middle, gain2_grad, half_a, half_b = norm_back(
        "norm_back2", info, blocks[6], sums, pieces, gain2, middle, mean2, inv2, cotangent, True,
        (feed_total,),
    )
    g_parts = ring_gather(half_a, half_b)
    feed_blocks = exchange(feed_total, axis_groups(True))

    branch, grad_gate, kept, own, give = back_mix(
        info, g_parts, wo, gate, grouped, ginv, query, arrival, (feed_total,)
    )

    branch_own, branch_other = turn("turn_branch", info, branch, (give,), True)
    grad_query, near_key, near_value = retain_back(
        info, kept, value, decay, key, query, weighted, mine, sibling, arrival, cosine, sine,
        (branch_own,),
    )
    mix_other = weight_half(
        "mix_other",
        [(branch_other, [mixed]), (low1_other, [grad_gate, grad_query])],
        None,
        (grad_query,),
    )
    mix_got = lax.ppermute(mix_other, "seq", SWAP)

    def fill_own(token):
        made["own"] = weight_half(
            "mix_own",
            [(branch_own, [mixed]), (low1_own, [grad_gate, grad_query])],
            mix_got,
            (token,),
        )
        return (made["own"],)

    feed = matmul_cols("feed_down", hidden, w2, BF16, (mix_other,), 1024)
    fed = lax.psum_scatter(feed, "head", scatter_dimension=1, tiled=True)
    pin(fed)

    far_mine, far_sibling = state_scan(
        info, behind, own, give, True, "_b",
        (lambda: (feed, feed_blocks), fill_own, lambda token: (), lambda token: (fed,)),
    )
    mix_x = exchange(gated(made["own"], (far_mine,)), axis_groups(True))
    feed_mid = plain_mid("feed_mid", feed_blocks, (far_mine,))
    feed_grad = lax.psum_scatter(
        feed_mid, "seq", scatter_dimension=0, axis_index_groups=axis_groups(False), tiled=True
    )
    pin(feed_grad)
    grad_key, grad_value = key_value_back(
        info, far_mine, far_sibling, key, value, departure, near_key, near_value, cosine, sine,
        (feed_mid,),
    )
    kv_other = weight_half(
        "kv_other", [(low1_other, [grad_key, grad_value])]
    )
    kv_got = lax.ppermute(kv_other, "seq", SWAP)
    *blocks, sums = back_blocks(
        "back_proj", info,
        [(grad_query, wq), (grad_gate, wg), (grad_key, wk), (grad_value, wv)],
        gain1, low1, (kv_other,),
    )
    pieces, sent = ring_scatter(*blocks[:6])
    kv_blocks = weight_own_y(
        "kv_own", info, low1_own, [grad_key, grad_value], kv_got, sent
    )

    grad_x, gain1_grad = norm_back(
        "norm_back1", info, blocks[6], sums, pieces, gain1, layer_in, mean1, inv1, grad_middle,
        False, (kv_blocks[0],),
    )
    keys, vals = HEADS * KEY, HEADS * VAL
    kv_sent = send_blocks(kv_blocks[:3], False)
    kv_half = phase_sum("kv_mid", info, X_AT, kv_blocks[3], kv_sent)
    gains = sum_core_x(jnp.concatenate([gain1_grad, gain2_grad], axis=0), (mix_x, feed_grad))
    mix_half = weight_mid("mix_mid", mix_x, gains)
    feed_grad = feed_grad.astype(F32)
    grad_wo, grad_wg, grad_wq, gains = weight_sum(
        "mix_sum", exchange(mix_half, axis_groups(False)), [vals, vals, keys, PART]
    )
    grad_wk, grad_wv = last_sum(
        "kv_sum", kv_half[3], send_blocks(kv_half[:3], True), (keys, vals)
    )
    output = (middle + fed.astype(F32)).astype(BF16)
    return (
        output,
        grad_x,
        gains[0],
        grad_wq,
        grad_wk,
        grad_wv,
        grad_wg,
        grad_wo.T,
        gains[1],
        feed_grad[:, vals:],
        feed_grad[:, :vals].T,
    )


def solution(mesh):
    rows = P("seq", "head")
    cols = P(None, "head")
    tall = P("head", None)
    return jax.shard_map(
        shards,
        mesh=mesh,
        in_specs=(rows, P(), cols, cols, cols, cols, tall, P(), cols, tall, P(), rows),
        out_specs=(
            rows, rows, P("head"), rows, rows, rows, rows, P("head", "seq"), P("head"), rows,
            P("head", "seq"),
        ),
        check_vma=False,
    )
```

```python
import math

import jax
import jax.numpy as jnp
from jax import lax
from jax.experimental import pallas as pl
from jax.experimental.pallas import tpu as pltpu
from jax.sharding import PartitionSpec as P

KEY = 256
VAL = 512
SIDE = 4
CORES = 2
HEADS = 2
ROWS = 512
HALF = 256
PART = 512
MODEL = 2048
EXTRA = 16
EPSILON = 1e-05
F32 = jnp.float32
BF16 = jnp.bfloat16
VMEM_BYTES = 26 * 1024 * 1024
ORDER = (2, 1, 3, 0)


def head_shift(step):
    return [(h, (h + step) % SIDE) for h in range(SIDE)]


def seq_index(x, y, core):
    return (x * SIDE + y) * CORES + core


def seq_shift(dx, dy, swap=0):
    return [
        (seq_index(x, y, core), seq_index((x + dx) % SIDE, (y + dy) % SIDE, core ^ swap))
        for x in range(SIDE)
        for y in range(SIDE)
        for core in range(CORES)
    ]


SWAP = seq_shift(0, 0, 1)


def up(block):
    return lax.ppermute(block, "head", head_shift(1))


def down(block):
    return lax.ppermute(block, "head", head_shift(SIDE - 1))


def add_low(a, b):
    return (a.astype(F32) + b.astype(F32)).astype(BF16)


def relay(a, b, tokens):
    def body(a, b, to_a, to_b):
        to_a[...] = a[...]
        to_b[...] = b[...]

    return call(
        "relay", body, (1,), [], [(a,), (b,)], [(a.shape, a.dtype), (b.shape, b.dtype)], tokens
    )


def gated(array, tokens):
    n = len(tokens)

    def body(*refs):
        del refs

    out = pl.pallas_call(
        body,
        name="gated",
        in_specs=[pl.BlockSpec(memory_space=pl.ANY)] * (1 + n),
        out_specs=pl.BlockSpec(memory_space=pl.ANY),
        out_shape=pltpu.HBM(array.shape, array.dtype),
        input_output_aliases={0: 0},
    )(in_hbm(array), *[in_hbm(t) if is_pinned(t) else t for t in tokens])
    pin(out)
    return out


def hold(tokens):
    def body(out):
        out[...] = jnp.zeros_like(out)

    return call("hold", body, (1,), [], [], [((8, 128), F32)], tokens)[0]


def gather_direct(block):
    got = {k: lax.ppermute(block, "head", head_shift(k)) for k in (2, 1, 3)}
    return [block, got[1], got[2], got[3]]


def ring_gather(a, b, first=None):
    r1, l1 = up(a), down(b)
    r2, l2 = up(b), down(a)
    on_r, on_l = first(r1, l1) if first else (r1, l1)
    r3, l3 = up(on_r), down(on_l)
    return [a, b, r1, r2, r3, l3, l2, l1]


def ring_scatter(p2a, p2b, p1a, p1b, pma, pmb):
    t1, t2 = up(p2a), down(p2b)
    rb, la = up(p1b), down(pma)
    s1, s2 = add_low(p1a, t1), add_low(pmb, t2)
    ra, lb = up(s1), down(s2)
    return [ra, rb, la, lb], (s1, s2)


def whole(shape):
    return pl.BlockSpec(shape, lambda *_: (0,) * len(shape))


def once(shape):
    return pl.BlockSpec(
        shape, lambda *_: (0,) * len(shape), pipeline_mode=pl.Buffered(buffer_count=1)
    )


PINNED = []


def pin(*arrays):
    PINNED.extend(arrays)


def is_pinned(array):
    return any(array is other for other in PINNED)


def in_hbm(array):
    return pltpu.with_memory_space_constraint(array, pltpu.HBM)


COST_SCALE = 1.0
COSTS = {
    "kv_mid": 100,
    "scan_start_b": 100,
    "relay": 1,
    "hold": 0.1,
    "turn_low2": 1.5,
    "late": 100,
    "scan_end_b": 50,
    "norm1": 5,
    "key_value": 8,
    "query_part": 6,
    "gate": 4,
    "mix": 9,
    "cot_pass": 100,
    "feed_up": 11,
    "back_feed": 7,
    "back_mix": 6,
    "retain_back": 0.6,
    "feed_down": 2,
    "key_value_back": 100,
    "back_proj": 0.1,
    "feed_other": 5,
    "feed_own": 8,
    "mix_other": 0.180,
    "mix_own": 1,
    "kv_other": 0.90,
    "kv_own": 0.1,
    "feed_sum": 0.1,
    "mix_sum": 2,
    "kv_sum": 0.1,
    "norm_back1": 0.1,
    "norm_back2": 100,
}


def call(name, body, grid, scalars, ins, outs, tokens=(), scratch=(), keep=False):
    arrays = [in_hbm(item[0]) if is_pinned(item[0]) else item[0] for item in ins]
    in_specs = [once(i[0].shape) if len(i) == 1 else pl.BlockSpec(i[1], i[2]) for i in ins]
    out_specs = [whole(o[0]) if len(o) == 2 else pl.BlockSpec(o[2], o[3]) for o in outs]
    out_shape = [jax.ShapeDtypeStruct(o[0], o[1]) for o in outs]
    keep = range(len(outs)) if keep is True else (keep or ())
    out_shape = [
        pltpu.HBM(o.shape, o.dtype) if i in keep else o for i, o in enumerate(out_shape)
    ]
    n_in, n_tok, n_sc = len(arrays), len(tokens), len(scalars)
    tokens = [in_hbm(t) if is_pinned(t) else t for t in tokens]
    in_specs += [pl.BlockSpec(memory_space=pl.ANY)] * n_tok

    def run(*refs):
        body(*refs[: n_sc + n_in], *refs[n_sc + n_in + n_tok :])

    results = pl.pallas_call(
        run,
        name=name,
        grid_spec=pltpu.PrefetchScalarGridSpec(
            num_scalar_prefetch=n_sc,
            grid=grid,
            in_specs=in_specs,
            out_specs=out_specs,
            scratch_shapes=list(scratch),
        ),
        out_shape=out_shape,
        compiler_params=pltpu.CompilerParams(
            dimension_semantics=("arbitrary",) * len(grid), vmem_limit_bytes=VMEM_BYTES
        ),
        cost_estimate=pl.CostEstimate(
            flops=int(COSTS.get(name, 0.1) * COST_SCALE * 1.1e9),
            bytes_accessed=0,
            transcendentals=0,
        ),
    )(*scalars, *arrays, *tokens)
    pin(*[results[i] for i in keep])
    return results


def dot(left, right):
    return jnp.dot(left, right, preferred_element_type=F32)


def dot_t(left, right):
    return lax.dot_general(left, right, (((1,), (1,)), ((), ())), preferred_element_type=F32)


def t_dot(left, right):
    return lax.dot_general(left, right, (((0,), (0,)), ((), ())), preferred_element_type=F32)


def rotate(rows, cosine, sine):
    half = rows.shape[-1] // 2
    first, second = rows[:, :half], rows[:, half:]
    return jnp.concatenate([first * cosine - second * sine, second * cosine + first * sine], axis=1)


def sigmoid(v):
    return 0.5 + 0.5 * jnp.tanh(0.5 * v)


def head_col(info, k):
    return pl.multiple_of(lax.rem(info[0] + SIDE - k, SIDE) * PART, PART)


CHUNK = 16


def norm_rows(info, load, gain, low, mean_ref, inv_ref, own=None):
    for half in range(2):

        def step(i, _):
            at = pl.multiple_of(i * CHUNK, CHUNK)
            out = pl.ds(pl.multiple_of(half * HALF + i * CHUNK, CHUNK), CHUNK)
            parts = [load(k, half, at) for k in range(SIDE)]
            if own is not None:
                own[out, :] = parts[0]
            mean = sum(jnp.sum(p, axis=1, keepdims=True) for p in parts) / MODEL
            parts = [p - mean for p in parts]
            var = sum(jnp.sum(p * p, axis=1, keepdims=True) for p in parts) / MODEL
            inv = lax.rsqrt(var + EPSILON)
            mean_ref[out, :] = mean
            inv_ref[out, :] = inv
            for k in range(SIDE):
                cols = pl.ds(head_col(info, k), PART)
                low[out, cols] = (parts[k] * inv * gain[:, cols]).astype(BF16)
            return 0

        lax.fori_loop(0, HALF // CHUNK, step, 0, unroll=8)


def chunk_of(part, half, at):
    return part[pl.ds(pl.multiple_of(half * HALF + at, CHUNK), CHUNK), :].astype(F32)


def norm1(info, parts, gain, cotangent):
    def body(info, *refs):
        x = refs[:8]
        gain, cot, low, mean, inv, cot_out, rows = refs[8:]
        cot_out[...] = cot[...]
        for k in range(SIDE):
            rows[k, :HALF] = x[2 * k][...]
            rows[k, HALF:] = x[2 * k + 1][...]
        norm_rows(
            info,
            lambda k, half, at: x[2 * k + half][pl.ds(at, CHUNK), :].astype(F32),
            gain,
            low,
            mean,
            inv,
        )

    return call(
        "norm1",
        body,
        (1,),
        [info],
        [(p,) for p in parts] + [(gain,), (cotangent,)],
        [
            ((ROWS, MODEL), BF16),
            ((ROWS, 1), F32),
            ((ROWS, 1), F32),
            ((ROWS, PART), BF16),
            ((SIDE, ROWS, PART), BF16),
        ],
        keep=(4,),
    )


def key_value(info, low, wk, wv, cosine, sine, departure):
    def body(info, low, wk, wv, cosine, sine, departure, key, value, own, give):
        head = pl.program_id(0)
        k = rotate(dot(low[...], wk[...]), cosine[...], sine[...]).astype(BF16)
        key[...] = k
        v = dot(low[...], wv[...]).astype(BF16)
        value[...] = v
        state = t_dot((k.astype(F32) * departure[0]).astype(BF16), v)

        @pl.when(head == info[1])
        def _():
            own[...] = state

        @pl.when(head != info[1])
        def _():
            give[...] = state.astype(BF16)

    by_head = lambda h, *_: (0, h)
    return call(
        "key_value",
        body,
        (HEADS,),
        [info],
        [
            (low,),
            (wk, (MODEL, KEY), by_head),
            (wv, (MODEL, VAL), by_head),
            (cosine,),
            (sine,),
            (departure, (1, ROWS, 1), lambda h, *_: (h, 0, 0)),
        ],
        [
            ((ROWS, HEADS * KEY), BF16, (ROWS, KEY), by_head),
            ((ROWS, HEADS * VAL), BF16, (ROWS, VAL), by_head),
            ((KEY, VAL), F32),
            ((KEY, VAL), BF16),
        ],
        keep=(0, 1),
    )


def query_part(low, wq, key, value, decay, cosine, sine, tokens):
    def body(low, wq, key, value, decay, cosine, sine, query, weighted, within):
        q = rotate(dot(low[...], wq[...]), cosine[...], sine[...]).astype(BF16)
        query[...] = q
        w = (dot_t(q, key[...]) * decay[0]).astype(BF16)
        weighted[0] = w
        within[...] = dot(w, value[...])

    by_head = lambda h, *_: (0, h)
    cube = lambda h, *_: (h, 0, 0)
    return call(
        "query_part",
        body,
        (HEADS,),
        [],
        [
            (low,),
            (wq, (MODEL, KEY), by_head),
            (key, (ROWS, KEY), by_head),
            (value, (ROWS, VAL), by_head),
            (decay, (1, ROWS, ROWS), cube),
            (cosine,),
            (sine,),
        ],
        [
            ((ROWS, HEADS * KEY), BF16, (ROWS, KEY), by_head),
            ((HEADS, ROWS, ROWS), BF16, (1, ROWS, ROWS), cube),
            ((ROWS, HEADS * VAL), F32, (ROWS, VAL), by_head),
        ],
        tokens,
        keep=(0, 1),
    )


def matmul_cols(name, left, right, out_type, tokens=(), block=512):
    def body(left, right, out):
        out[...] = dot(left[...], right[...]).astype(out_type)

    depth, cols = right.shape
    by_col = lambda i, *_: (0, i)
    return call(
        name,
        body,
        (cols // block,),
        [],
        [(left,), (right, (depth, block), by_col)],
        [((left.shape[0], cols), out_type, (left.shape[0], block), by_col)],
        tokens,
        keep=True,
    )[0]


def block_outs(extra):
    tall = ((HALF + extra, PART), BF16)
    return [tall, ((HALF, PART), BF16)] * 3 + [((ROWS, PART), F32)]


def put_blocks(step, make, outs):
    for i in range(2):
        block = make(i)
        for s in range(2):
            k = 2 * s + i

            @pl.when(step == s)
            def _():
                if k == SIDE - 1:
                    outs[6][...] = block
                else:
                    outs[2 * k][:HALF, :] = block[:HALF].astype(BF16)
                    outs[2 * k + 1][...] = block[HALF:].astype(BF16)


def pick(mine, sibling, info, head):
    return jnp.where(info[1] == head, mine[...], sibling[...])


def mix(info, within, gate, query, mine, sibling, arrival, wo, tokens):
    def body(info, within, gate, query, mine, sibling, arrival, wo, mixed, grouped, ginv, *outs):
        for half in range(2):
            rows = slice(half * HALF, (half + 1) * HALF)
            for head in range(HEADS):
                cols = slice(head * VAL, (head + 1) * VAL)
                state = pick(mine, sibling, info, head)
                cross = dot(query[rows, head * KEY : (head + 1) * KEY], state)
                kept = within[rows, cols] + arrival[head, rows] * cross
                kept = kept - jnp.mean(kept, axis=1, keepdims=True)
                inv = lax.rsqrt(jnp.mean(kept * kept, axis=1, keepdims=True) + float(KEY))
                group = kept * inv
                g = gate[rows, cols].astype(F32)
                ginv[head, rows] = inv
                grouped[rows, cols] = group.astype(BF16)
                mixed[rows, cols] = (group * (g * sigmoid(g))).astype(BF16)
            for i in range(SIDE):
                at = pl.ds(pl.multiple_of(info[2 + i] * PART, PART), PART)
                block = dot(mixed[rows], wo[:, at])
                if i == SIDE - 1:
                    outs[6][rows] = block
                else:
                    outs[2 * i + half][...] = block.astype(BF16)

    cols = HEADS * VAL
    return call(
        "mix",
        body,
        (1,),
        [info],
        [(within,), (gate,), (query,), (mine,), (sibling,), (arrival,), (wo,)],
        [((ROWS, cols), BF16), ((ROWS, cols), BF16), ((HEADS, ROWS, 1), F32)] + block_outs(0),
        tokens,
        keep=(0, 1),
    )


def sum_branch(p0, pieces, tokens):
    def body(p0, ra, rb, la, lb, a, b):
        a[...] = (p0[:HALF] + ra[...].astype(F32) + la[...].astype(F32)).astype(BF16)
        b[...] = (p0[HALF:] + rb[...].astype(F32) + lb[...].astype(F32)).astype(BF16)

    return call(
        "sum_branch",
        body,
        (1,),
        [],
        [(p0,)] + [(p,) for p in pieces],
        [((HALF, PART), BF16), ((HALF, PART), BF16)],
        tokens,
    )


def feed_up(info, x_rows, b_parts, gain, w1, grad_hidden, tokens):
    block = 512

    def body(info, *refs):
        x, b = refs[0], refs[1:9]
        gain, w1, grad_hidden, ffn_in, mean, inv, own, hidden, grad_pre = refs[9:]

        @pl.when(pl.program_id(0) == 0)
        def _():
            def load(k, half, at):
                branch = b[2 * k + half][pl.ds(at, CHUNK), :].astype(F32)
                return chunk_of(x.at[k], half, at) + branch

            norm_rows(info, load, gain, ffn_in, mean, inv, own)

        pre = dot(ffn_in[...], w1[...])
        cdf = 0.5 * (1.0 + lax.erf(pre * (2.0**-0.5)))
        hidden[...] = (pre * cdf).astype(BF16)
        pdf = jnp.exp(-0.5 * pre * pre) * ((2.0 * math.pi) ** -0.5)
        grad_pre[...] = ((cdf + pre * pdf) * grad_hidden[...].astype(F32)).astype(BF16)

    by_col = lambda i, *_: (0, i)
    cols = w1.shape[1]
    tall = ((ROWS, cols), BF16, (ROWS, block), by_col)
    return call(
        "feed_up",
        body,
        (cols // block,),
        [info],
        [(x_rows,)]
        + [(p,) for p in b_parts]
        + [
            (gain,),
            (w1, (MODEL, block), by_col),
            (grad_hidden, (ROWS, block), by_col),
        ],
        [
            ((ROWS, MODEL), BF16),
            ((ROWS, 1), F32),
            ((ROWS, 1), F32),
            ((ROWS, PART), F32),
            tall,
            tall,
        ],
        tokens,
        keep=(1, 2, 3),
    )


def back_blocks(name, info, pairs, gain, low, tokens=()):
    n = len(pairs)

    def body(info, *refs):
        grads, weights = refs[:n], refs[n : 3 * n]
        gains, lows = refs[3 * n : 3 * n + 2], refs[3 * n + 2 : 3 * n + 4]
        outs, sums, acc = refs[3 * n + 4 : 3 * n + 11], refs[3 * n + 11], refs[3 * n + 12]
        step = pl.program_id(0)
        lane = lax.broadcasted_iota(jnp.int32, (ROWS, 128), 1)

        @pl.when(step == 0)
        def _():
            acc[...] = jnp.zeros_like(acc)

        def make(i):
            total = dot_t(grads[0][...], weights[2 * 0 + i][...])
            for j in range(1, n):
                total = total + dot_t(grads[j][...], weights[2 * j + i][...])
            first = jnp.sum(total * gains[i][...], axis=1, keepdims=True) / MODEL
            second = jnp.sum(total * lows[i][...].astype(F32), axis=1, keepdims=True) / MODEL
            acc[...] += jnp.where(lane == 0, first, jnp.where(lane == 1, second, 0.0))
            return total

        put_blocks(step, make, outs)

        @pl.when(step == 1)
        def _():
            turned = acc[...].T[:EXTRA]
            sums[...] = turned
            for k in range(SIDE - 1):
                outs[2 * k][HALF:, :] = turned.astype(BF16)

    def by_row(j):
        return lambda i, info: (info[2 + j + 2 * i], 0)

    def by_col(j):
        return lambda i, info: (0, info[2 + j + 2 * i])

    return call(
        name,
        body,
        (2,),
        [info],
        [(g,) for g, _ in pairs]
        + [(in_hbm(w), (PART, w.shape[1]), by_row(j)) for _, w in pairs for j in range(2)]
        + [(gain, (1, PART), by_col(j)) for j in range(2)]
        + [(low, (ROWS, PART), by_col(j)) for j in range(2)],
        block_outs(EXTRA) + [((EXTRA, PART), F32)],
        tokens,
        [pltpu.VMEM((ROWS, 128), F32)],
        keep=(6,),
    )


def norm_back(
    name, info, p0, sums, pieces, gain, rows, mean, inv, residual, low_out, tokens
):
    def body(
        info, p0, sums, ra, rb, la, lb, gain, rows, mean, inv, residual, grad, gain_grad, *low
    ):
        scale = gain[:, pl.ds(head_col(info, 0), PART)]
        total = sums[...] + ra[HALF:].astype(F32) + la[HALF:].astype(F32)
        total = jnp.concatenate([total, jnp.zeros((128 - EXTRA, PART), F32)], axis=0).T
        acc = jnp.zeros((1, PART), F32)
        for half, (one, two) in enumerate(((ra, la), (rb, lb))):
            for quarter in range(2):
                at = slice(quarter * 128, (quarter + 1) * 128)
                out = slice(half * HALF + quarter * 128, half * HALF + (quarter + 1) * 128)
                g = p0[out] + one[at].astype(F32) + two[at].astype(F32)
                normed = (rows[out].astype(F32) - mean[out]) * inv[out]
                acc = acc + jnp.sum(g * normed, axis=0, keepdims=True)
                back = inv[out] * (g * scale - total[out, 0:1] - normed * total[out, 1:2])
                new = residual[out].astype(F32) + back
                grad[out] = new
                if low_out:
                    low[half][at] = new.astype(BF16)
        gain_grad[...] = acc

    outs = [((ROWS, PART), F32), ((1, PART), F32)]
    if low_out:
        outs += [((HALF, PART), BF16)] * 2
    return call(
        name,
        body,
        (1,),
        [info],
        [(p0,), (sums,)]
        + [(p,) for p in pieces]
        + [(gain,), (rows,), (mean,), (inv,), (residual,)],
        outs,
        tokens,
        keep=(0,) if low_out else (),
    )


def back_mix(info, parts, wo, gate, grouped, ginv, query, arrival, tokens):
    def body(info, *refs):
        parts = refs[:8]
        wo, gate, grouped, ginv, query, arrival, branch, grad_gate, kept, own, give = refs[8:]
        head = pl.program_id(0)

        @pl.when(head == 0)
        def _():
            for k in range(SIDE):
                cols = pl.ds(head_col(info, k), PART)
                branch[:HALF, cols] = parts[2 * k][...]
                branch[HALF:, cols] = parts[2 * k + 1][...]

        for half in range(2):
            rows = slice(half * HALF, (half + 1) * HALF)
            m = dot_t(branch[rows], wo[...])
            g = gate[rows].astype(F32)
            gate_s = sigmoid(g)
            group = grouped[rows].astype(F32)
            slope = gate_s * (1.0 + g * (1.0 - gate_s))
            grad_gate[rows] = (m * group * slope).astype(BF16)
            e = m * (g * gate_s)
            e = ginv[0, rows] * (
                e
                - jnp.mean(e, axis=1, keepdims=True)
                - group * jnp.mean(e * group, axis=1, keepdims=True)
            )
            kept[rows] = e.astype(BF16)
        moved = (query[...].astype(F32) * arrival[0]).astype(BF16)
        state = t_dot(moved, kept[...])

        @pl.when(head == info[1])
        def _():
            own[...] = state

        @pl.when(head != info[1])
        def _():
            give[...] = state.astype(BF16)

    by_head = lambda h, *_: (0, h)
    cube = lambda h, *_: (h, 0, 0)
    cols = HEADS * VAL
    return call(
        "back_mix",
        body,
        (HEADS,),
        [info],
        [(p,) for p in parts]
        + [
            (wo, (VAL, MODEL), lambda h, *_: (h, 0)),
            (gate, (ROWS, VAL), by_head),
            (grouped, (ROWS, VAL), by_head),
            (ginv, (1, ROWS, 1), cube),
            (query, (ROWS, KEY), by_head),
            (arrival, (1, ROWS, 1), cube),
        ],
        [
            ((ROWS, MODEL), BF16),
            ((ROWS, cols), BF16, (ROWS, VAL), by_head),
            ((ROWS, cols), BF16, (ROWS, VAL), by_head),
            ((KEY, VAL), F32),
            ((KEY, VAL), BF16),
        ],
        tokens,
        keep=(1, 2),
    )


def retain_back(info, kept, value, decay, key, query, weighted, mine, sibling, arrival, cosine, sine, tokens):
    def body(
        info, kept, value, decay, key, query, weighted, mine, sibling, arrival, cosine, sine,
        grad_query, near_key, near_value,
    ):
        head = pl.program_id(0)
        e = kept[...]
        s = (dot_t(e, value[...]) * decay[0]).astype(BF16)
        state = pick(mine, sibling, info, head)
        gq = dot(s, key[...]) + arrival[0] * dot_t(e, state)
        grad_query[...] = rotate(gq, cosine[...], -sine[...]).astype(BF16)
        near_key[...] = t_dot(s, query[...])
        near_value[...] = t_dot(weighted[0], e)

    by_head = lambda h, *_: (0, h)
    cube = lambda h, *_: (h, 0, 0)
    keys, vals = HEADS * KEY, HEADS * VAL
    return call(
        "retain_back",
        body,
        (HEADS,),
        [info],
        [
            (kept, (ROWS, VAL), by_head),
            (value, (ROWS, VAL), by_head),
            (decay, (1, ROWS, ROWS), cube),
            (key, (ROWS, KEY), by_head),
            (query, (ROWS, KEY), by_head),
            (weighted, (1, ROWS, ROWS), cube),
            (mine,),
            (sibling,),
            (arrival, (1, ROWS, 1), cube),
            (cosine,),
            (sine,),
        ],
        [
            ((ROWS, keys), BF16, (ROWS, KEY), by_head),
            ((ROWS, keys), F32, (ROWS, KEY), by_head),
            ((ROWS, vals), F32, (ROWS, VAL), by_head),
        ],
        tokens,
        keep=True,
    )


def key_value_back(info, mine, sibling, key, value, departure, near_key, near_value, cosine, sine, tokens):
    def body(
        info, mine, sibling, key, value, departure, near_key, near_value, cosine, sine,
        grad_key, grad_value,
    ):
        state = pick(mine, sibling, info, pl.program_id(0))
        gk = near_key[...] + departure[0] * dot_t(value[...], state)
        grad_key[...] = rotate(gk, cosine[...], -sine[...]).astype(BF16)
        gv = near_value[...] + departure[0] * dot(key[...], state)
        grad_value[...] = gv.astype(BF16)

    by_head = lambda h, *_: (0, h)
    keys, vals = HEADS * KEY, HEADS * VAL
    return call(
        "key_value_back",
        body,
        (HEADS,),
        [info],
        [
            (mine,),
            (sibling,),
            (key, (ROWS, KEY), by_head),
            (value, (ROWS, VAL), by_head),
            (departure, (1, ROWS, 1), lambda h, *_: (h, 0, 0)),
            (near_key, (ROWS, KEY), by_head),
            (near_value, (ROWS, VAL), by_head),
            (cosine,),
            (sine,),
        ],
        [
            ((ROWS, keys), BF16, (ROWS, KEY), by_head),
            ((ROWS, vals), BF16, (ROWS, VAL), by_head),
        ],
        tokens,
        keep=True,
    )


def turn(name, info, low, tokens=(), keep=False):
    xs = 2

    def body(info, low, own, other, scratch):
        scratch[...] = low[...].T
        for x in range(xs):
            for y in range(SIDE):
                base = (x * SIDE + y) * CORES * 64
                mine = pl.ds(pl.multiple_of(base + info[1] * 64, 64), 64)
                far = pl.ds(pl.multiple_of(base + (1 - info[1]) * 64, 64), 64)
                own[x, y] = scratch[mine, :]
                other[x, y] = scratch[far, :]

    out = ((SIDE, SIDE, 64, ROWS), BF16, (xs, SIDE, 64, ROWS), lambda i, *_: (i, 0, 0, 0))
    own, other = call(
        name,
        body,
        (SIDE // xs,),
        [info],
        [(low, (ROWS, xs * PART), lambda i, *_: (0, i))],
        [out, out],
        tokens,
        [pltpu.VMEM((xs * PART, ROWS), BF16)],
        keep=keep,
    )
    flat = own.reshape(-1, ROWS), other.reshape(-1, ROWS)
    if keep:
        pin(*flat)
    return flat


def cot_pass(info, parts, w2, tokens):
    xs = 2

    def body(info, a, b, c, d, w2, own, other, out, whole_rows, scratch):
        step = pl.program_id(0)

        @pl.when(step == 0)
        def _():
            for k, part in enumerate((a, b, c, d)):
                whole_rows[:, pl.ds(head_col(info, k), PART)] = part[...]

        out[...] = dot_t(whole_rows[...], w2[...]).astype(BF16)
        cols = pl.ds(pl.multiple_of(step * xs * PART, PART), xs * PART)
        scratch[...] = whole_rows[:, cols].T
        for x in range(xs):
            for y in range(SIDE):
                base = (x * SIDE + y) * CORES * 64
                mine = pl.ds(pl.multiple_of(base + info[1] * 64, 64), 64)
                far = pl.ds(pl.multiple_of(base + (1 - info[1]) * 64, 64), 64)
                own[x, y] = scratch[mine, :]
                other[x, y] = scratch[far, :]

    turned = ((SIDE, SIDE, 64, ROWS), BF16, (xs, SIDE, 64, ROWS), lambda i, *_: (i, 0, 0, 0))
    cols = w2.shape[0]
    own, other, out = call(
        "cot_pass",
        body,
        (2,),
        [info],
        [(p,) for p in parts] + [(w2, (cols // 2, MODEL), lambda i, *_: (i, 0))],
        [turned, turned, ((ROWS, cols), BF16, (ROWS, cols // 2), lambda i, *_: (0, i))],
        tokens,
        [pltpu.VMEM((ROWS, MODEL), BF16), pltpu.VMEM((xs * PART, ROWS), BF16)],
    )
    return own.reshape(-1, ROWS), other.reshape(-1, ROWS), out


def widths(groups):
    return [sum(r.shape[1] for r in rights) for _, rights in groups]


def weight_half(name, groups, arrived=None, tokens=()):
    n_left = len(groups)
    rights = [r for _, rs in groups for r in rs]
    counts = [len(rs) for _, rs in groups]
    n = len(rights)
    width = sum(widths(groups))

    def body(*refs):
        lefts, rest = refs[:n_left], refs[n_left : n_left + n]
        out = refs[-1]
        at = 0
        which = 0
        for left, count in zip(lefts, counts):
            for r in rest[which : which + count]:
                cols = slice(at, at + r.shape[1])
                total = dot(left[...], r[...])
                if arrived is not None:
                    total = total + refs[n_left + n][:, cols].astype(F32)
                out[:, cols] = total.astype(BF16)
                at += r.shape[1]
            which += count

    block = lambda i, *_: (i, 0)
    return call(
        name,
        body,
        (2,),
        [],
        [(left, (ROWS, ROWS), block) for left, _ in groups]
        + [(r,) for r in rights]
        + ([(arrived, (ROWS, width), block)] if arrived is not None else []),
        [((2 * ROWS, width), BF16, (ROWS, width), block)],
        tokens,
        keep=True,
    )[0]


def axis_groups(along_x):
    if along_x:
        return [
            [seq_index(x, y, c) for x in range(SIDE)] for y in range(SIDE) for c in range(CORES)
        ]
    return [[seq_index(x, y, c) for y in range(SIDE)] for x in range(SIDE) for c in range(CORES)]


def exchange(total, groups):
    blocks = total
    if total.ndim == 2:
        blocks = total.reshape(len(groups[0]), -1, total.shape[-1])
    blocks = lax.all_to_all(blocks, "seq", 0, 0, axis_index_groups=groups, tiled=True)
    pin(blocks)
    return blocks


def weight_mid(name, blocks, gains, tokens=()):
    count, rows, width = blocks.shape
    part = rows // SIDE
    gains = jnp.pad(gains, ((0, EXTRA - gains.shape[0]), (0, 0)))

    def body(blocks, gains, out):
        total = blocks[0].astype(F32)
        for k in range(1, count):
            total = total + blocks[k].astype(F32)
        for y in range(SIDE):
            out[y, :, :width] = total[y * part : (y + 1) * part].astype(BF16)
            out[y, :EXTRA, width:] = gains[...].astype(BF16)
            out[y, EXTRA:, width:] = jnp.zeros((part - EXTRA, PART), BF16)

    return call(
        name,
        body,
        (1,),
        [],
        [(blocks,), (gains,)],
        [((SIDE, part, width + PART), BF16)],
        tokens,
        keep=True,
    )[0]


def weight_sum(name, blocks, parts, tokens=()):
    def body(blocks, *outs):
        at = 0
        for out, part in zip(outs, parts):
            cols = slice(at, at + part)
            rows = slice(0, out.shape[0])
            total = blocks[0, rows, cols].astype(F32)
            for k in range(1, blocks.shape[0]):
                total = total + blocks[k, rows, cols].astype(F32)
            out[...] = total
            at += part

    return call(
        name,
        body,
        (1,),
        [],
        [(blocks,)],
        [((64, part), F32) for part in parts[:-1]] + [((EXTRA, parts[-1]), F32)],
        tokens,
    )

def weight_own_y(name, info, left, rights, arrived, tokens=()):
    n = len(rights)
    width = sum(r.shape[1] for r in rights)
    left = left.reshape(SIDE, SIDE, 64, ROWS)
    arrived = arrived.reshape(SIDE, SIDE, 64, width)
    pin(left)

    def body(info, *refs):
        lefts, rights, got, outs = refs[:2], refs[2 : 2 + n], refs[2 + n : 4 + n], refs[4 + n :]
        step = pl.program_id(0)
        for i in range(2):
            at = 0
            for r in rights:
                cols = slice(at, at + r.shape[1])
                total = dot(lefts[i][...].reshape(HALF, ROWS), r[...])
                total = total + got[i][:, :, :, cols].reshape(HALF, r.shape[1]).astype(F32)
                for s in range(2):

                    @pl.when(step == s)
                    def _():
                        out = outs[2 * s + i]
                        out[:, cols] = total.astype(out.dtype)

                at += r.shape[1]

    def block(j):
        def at(i, info):
            return (0, lax.rem(info[Y_AT] + ORDER_OF(2 * i + j), SIDE), 0, 0)

        return at

    return call(
        name,
        body,
        (2,),
        [info],
        [(left, (SIDE, 1, 64, ROWS), block(j)) for j in range(2)]
        + [(r,) for r in rights]
        + [(arrived, (SIDE, 1, 64, width), block(j)) for j in range(2)],
        [((HALF, width), BF16)] * 3 + [((HALF, width), F32)],
        tokens,
    )


def ORDER_OF(i):
    return jnp.where(i == 0, 2, jnp.where(i == 1, 1, jnp.where(i == 2, 3, 0)))


def phase_sum(name, info, where, base, received, tokens=()):
    width = base.shape[1]

    def body(info, base, a, b, c, *refs):
        outs, scratch = refs[:SIDE], refs[SIDE]
        scratch[...] = base[...] + a[...].astype(F32) + b[...].astype(F32) + c[...].astype(F32)
        for i, k in enumerate(ORDER):
            at = pl.multiple_of(lax.rem(info[where] + k, SIDE) * 64, 64)
            outs[i][...] = scratch[pl.ds(at, 64), :].astype(outs[i].dtype)

    return call(
        name,
        body,
        (1,),
        [info],
        [(base,)] + [(r,) for r in received],
        [((64, width), BF16)] * 3 + [((64, width), F32)],
        tokens,
        [pltpu.VMEM((HALF, width), F32)],
    )


def plain_mid(name, blocks, tokens=()):
    def body(blocks, out):
        total = blocks[0].astype(F32)
        for k in range(1, blocks.shape[0]):
            total = total + blocks[k].astype(F32)
        out[...] = total.astype(BF16)

    shape = blocks.shape[1:]
    return call(
        name, body, (1,), [], [(blocks,)], [(shape, BF16)], tokens, keep=True
    )[0]


def last_sum(name, base, received, parts, tokens=()):
    def body(base, a, b, c, *outs):
        at = 0
        for out in outs:
            cols = slice(at, at + out.shape[1])
            out[...] = base[:, cols] + sum(r[:, cols].astype(F32) for r in (a, b, c))
            at += out.shape[1]

    return call(
        name,
        body,
        (1,),
        [],
        [(base,)] + [(r,) for r in received],
        [((64, w), F32) for w in parts],
        tokens,
    )


def shift_of(along_x):
    return (lambda k: seq_shift(k, 0)) if along_x else (lambda k: seq_shift(0, k))


def send_blocks(blocks, along_x):
    shift = shift_of(along_x)
    return [lax.ppermute(b, "seq", shift(k)) for b, k in zip(blocks, ORDER[:3])]


X_AT, Y_AT = 6, 7


def scan_weights(log_decay, place, reverse):
    x, y, _ = place
    rel = jnp.arange(SIDE)
    origin = (y - rel) & 3
    target = (y + rel) & 3
    hops = jnp.arange(1, SIDE)
    if reverse:
        row = origin
        before, counts = SIDE * (SIDE - hops - 1), x + (SIDE - hops) < SIDE
        gap = origin[None, :] - target[:, None]
        carry = SIDE - 1 - target
    else:
        row = SIDE - 1 - origin
        before, counts = SIDE * (hops - 1), x >= hops
        gap = target[:, None] - origin[None, :]
        carry = target
    gap = gap.reshape(-1)
    power = jnp.concatenate([row, before, jnp.maximum(gap - 1, 0), carry]).astype(F32)
    keep = jnp.concatenate([row >= 0, counts, gap > 0, carry >= 0]).astype(F32)
    power = jnp.concatenate([jnp.full((1,), 0.5, F32), power, jnp.zeros((4,), F32)])
    keep = jnp.concatenate([jnp.ones((1,), F32), keep, jnp.zeros((4,), F32)])
    return keep * jnp.exp(2.0 * log_decay * power)


W_ROW, W_BEFORE, W_ANSWER, W_CARRY = 1, 5, 8, 24
QUARTER = KEY // SIDE


def state_scan(info, weights, own, give, reverse, tag, fills):
    far = 1 if reverse else 0

    def start_body(info, w, own, got, p2, p1, p3, p0, scratch):
        a, b = own[...], got[...].astype(F32)
        scratch[...] = jnp.where(info[1] == far, w[0] * a + b, a + w[0] * b).astype(BF16)
        for k, out in zip(ORDER, (p2, p1, p3, p0)):
            at = pl.multiple_of(lax.rem(info[Y_AT] + k, SIDE) * QUARTER, QUARTER)
            out[...] = scratch[pl.ds(at, QUARTER), :]

    piece = ((QUARTER, VAL), BF16)
    got = lax.ppermute(give, "seq", SWAP)
    sent = call(
        "scan_start" + tag, start_body, (1,), [info, weights], [(own,), (got,)], [piece] * 4,
        fills[0](), scratch=[pltpu.VMEM((KEY, VAL), BF16)],
    )
    at2, at1, at3 = send_blocks(sent[:3], False)
    pieces = [sent[3], at1, at2, at3]

    def row_body(w, p0, p1, p2, p3, total):
        total[...] = sum(
            w[W_ROW + j] * p[...].astype(F32) for j, p in enumerate((p0, p1, p2, p3))
        ).astype(BF16)

    row = call(
        "scan_row" + tag, row_body, (1,), [weights], [(p,) for p in pieces], [piece],
        fills[1](sent[0]),
    )[0]
    at2, at1, at3 = send_blocks([row] * 3, True)

    def answer_body(w, p0, p1, p2, p3, b1, b2, b3, *outs):
        p = [r[...].astype(F32) for r in (p0, p1, p2, p3)]
        before = sum(w[W_BEFORE + j] * r[...].astype(F32) for j, r in enumerate((b1, b2, b3)))
        for k, out in zip(ORDER, outs):
            total = w[W_CARRY + k] * before
            for j in range(SIDE):
                total = total + w[W_ANSWER + SIDE * k + j] * p[j]
            out[...] = total.astype(BF16)

    answers = call(
        "scan_answer" + tag, answer_body, (1,), [weights],
        [(p,) for p in pieces] + [(at1,), (at2,), (at3,)], [piece] * 4, fills[2](row),
    )
    at2, at1, at3 = send_blocks(answers[:3], False)

    def end_body(info, w, b0, b1, b2, b3, own, got, mine, theirs, scratch):
        for k, b in enumerate((b0, b1, b2, b3)):
            at = pl.multiple_of(lax.rem(info[Y_AT] + SIDE - k, SIDE) * QUARTER, QUARTER)
            scratch[pl.ds(at, QUARTER), :] = b[...].astype(F32)
        chip = scratch[...]
        is_far = info[1] == far
        later = w[0] * chip + jnp.where(is_far, own[...], got[...].astype(F32))
        mine[...] = jnp.where(is_far, chip, later).astype(BF16)
        theirs[...] = jnp.where(is_far, later, chip).astype(BF16)

    state = ((KEY, VAL), BF16)
    mine, theirs = call(
        "scan_end" + tag, end_body, (1,), [info, weights],
        [(answers[3],), (at1,), (at2,), (at3,), (own,), (got,)], [state, state],
        fills[3](answers[0]), scratch=[pltpu.VMEM((KEY, VAL), F32)],
    )
    return mine, lax.ppermute(theirs, "seq", SWAP)


def sum_core_x(values, tokens):
    def body(a, b, out):
        out[...] = a[...] + b[...]

    got = lax.ppermute(values, "seq", SWAP)
    values = call(
        "gain_pair", body, (1,), [], [(values,), (got,)], [(values.shape, F32)], tokens
    )[0]
    return values + sum(lax.ppermute(values, "seq", seq_shift(k, 0)) for k in (1, 2, 3))


def shards(layer_in, gain1, wq, wk, wv, wg, wo, gain2, w1, w2, starts, cotangent):
    seq_rank = lax.axis_index("seq")
    head_rank = lax.axis_index("head")
    x, y, core = seq_rank >> 3, (seq_rank >> 1) & 3, seq_rank & 1
    place = (x, y, core)
    PINNED.clear()
    info = jnp.stack(
        [head_rank, core] + [(head_rank + k) & 3 for k in ORDER] + [x, y]
    ).astype(jnp.int32)
    gain1, gain2 = gain1[None], gain2[None]

    offsets = jnp.arange(ROWS, dtype=jnp.int32)
    positions = seq_rank * ROWS + offsets
    member = positions[:, None] >= starts[None, :]
    doc_ids = jnp.sum(member.astype(jnp.int32), axis=-1) - 1
    last_start = jnp.max(jnp.where(member, starts[None, :], 0), axis=-1)
    relative = (positions - last_start).astype(F32)
    prior_doc = jnp.sum((seq_rank * ROWS - 1 >= starts).astype(jnp.int32)) - 1
    half_dim = KEY // 2
    frequency = jnp.exp(-math.log(10000.0) * jnp.arange(half_dim, dtype=F32) / half_dim)
    angles = relative[:, None] * frequency[None, :]
    cosine, sine = jnp.cos(angles), jnp.sin(angles)
    head_ids = (head_rank * HEADS + jnp.arange(HEADS, dtype=jnp.int32)).astype(F32)
    log_decay = jnp.log1p(-jnp.exp2(-5.0 - head_ids))
    gap_grid = offsets[:, None] - offsets[None, :]
    keep = (gap_grid >= 0) & (doc_ids[:, None] == doc_ids[None, :])
    gap_float = jnp.where(gap_grid >= 0, gap_grid, 0).astype(F32)
    decay = jnp.where(keep[None], jnp.exp(gap_float[None] * log_decay[:, None, None]), 0.0)
    step_float = offsets.astype(F32)
    arrival = jnp.exp((step_float[None, :] + 1.0) * log_decay[:, None]) * (
        doc_ids == prior_doc
    ).astype(F32)
    departure = jnp.exp((ROWS - 1.0 - step_float)[None, :] * log_decay[:, None]) * (
        doc_ids == doc_ids[ROWS - 1]
    ).astype(F32)
    arrival, departure = arrival[:, :, None], departure[:, :, None]
    pin(decay)
    own_head = (head_rank * HEADS + core).astype(F32)
    rank_log = ROWS * jnp.log1p(-jnp.exp2(-5.0 - own_head))
    ahead = scan_weights(rank_log, place, False)
    behind = scan_weights(rank_log, place, True)

    tables = (arrival, departure, ahead, behind, info)
    x_parts = ring_gather(
        layer_in[:HALF], layer_in[HALF:], lambda r, l: relay(r, l, tables)
    )
    low1, mean1, inv1, cot_again, x_rows = norm1(info, x_parts, gain1, cotangent)
    cot_parts = gather_direct(cot_again)
    key, value, own, give = key_value(info, low1, wk, wv, cosine, sine, departure)
    made = {}

    def fill_query():
        made["q"] = query_part(low1, wq, key, value, decay, cosine, sine, (give,))
        return (made["q"][0],)

    def fill_gate(token):
        made["gate"] = matmul_cols("gate", low1, wg, BF16, (token, *cot_parts[1:]))
        return (made["gate"],)

    mine, sibling = state_scan(
        info, ahead, own, give, False, "_a", (fill_query, fill_gate, lambda token: (), lambda token: ())
    )
    query, weighted, within = made["q"]
    gate = made["gate"]
    mixed, grouped, ginv, *blocks = mix(
        info, within, gate, query, mine, sibling, arrival, wo, ()
    )
    pieces, sent = ring_scatter(*blocks[:6])
    cot_own, cot_other, grad_hidden = cot_pass(info, cot_parts, w2, sent)
    low1_own, low1_other = turn("turn_low1", info, low1, (cot_own,), True)
    b_parts = ring_gather(*sum_branch(blocks[6], pieces, (grad_hidden, low1_own)))

    low2, mean2, inv2, middle, hidden, grad_pre = feed_up(
        info, x_rows, b_parts, gain2, w1, grad_hidden, (cot_own,)
    )
    low2_own, low2_other = turn("turn_low2", info, low2)
    feed_other = weight_half(
        "feed_other", [(cot_other, [hidden]), (low2_other, [grad_pre])], None, (low2_own,)
    )
    *blocks, sums = back_blocks(
        "back_feed", info, [(grad_pre, w1)], gain2, low2, (feed_other,)
    )
    pieces, sent = ring_scatter(*blocks[:6])
    feed_got = lax.ppermute(feed_other, "seq", SWAP)
    feed_total = weight_half(
        "feed_own", [(cot_own, [hidden]), (low2_own, [grad_pre])], feed_got
    )
    grad_middle, gain2_grad, half_a, half_b = norm_back(
        "norm_back2", info, blocks[6], sums, pieces, gain2, middle, mean2, inv2, cotangent, True,
        (feed_total,),
    )
    g_parts = ring_gather(half_a, half_b)
    feed_blocks = exchange(feed_total, axis_groups(True))

    branch, grad_gate, kept, own, give = back_mix(
        info, g_parts, wo, gate, grouped, ginv, query, arrival, (feed_total,)
    )

    branch_own, branch_other = turn("turn_branch", info, branch, (give,), True)
    grad_query, near_key, near_value = retain_back(
        info, kept, value, decay, key, query, weighted, mine, sibling, arrival, cosine, sine,
        (branch_own,),
    )
    mix_other = weight_half(
        "mix_other",
        [(branch_other, [mixed]), (low1_other, [grad_gate, grad_query])],
        None,
        (grad_query,),
    )
    mix_got = lax.ppermute(mix_other, "seq", SWAP)

    def fill_own(token):
        made["own"] = weight_half(
            "mix_own",
            [(branch_own, [mixed]), (low1_own, [grad_gate, grad_query])],
            mix_got,
            (token,),
        )
        return (made["own"],)

    feed = matmul_cols("feed_down", hidden, w2, BF16, (mix_other,), 1024)
    fed = lax.psum_scatter(feed, "head", scatter_dimension=1, tiled=True)
    pin(fed)

    far_mine, far_sibling = state_scan(
        info, behind, own, give, True, "_b",
        (lambda: (feed, feed_blocks), fill_own, lambda token: (), lambda token: (fed,)),
    )
    mix_x = exchange(gated(made["own"], (far_mine,)), axis_groups(True))
    feed_mid = plain_mid("feed_mid", feed_blocks, (far_mine,))
    feed_grad = lax.psum_scatter(
        feed_mid, "seq", scatter_dimension=0, axis_index_groups=axis_groups(False), tiled=True
    )
    pin(feed_grad)
    grad_key, grad_value = key_value_back(
        info, far_mine, far_sibling, key, value, departure, near_key, near_value, cosine, sine,
        (feed_mid,),
    )
    kv_other = weight_half(
        "kv_other", [(low1_other, [grad_key, grad_value])]
    )
    kv_got = lax.ppermute(kv_other, "seq", SWAP)
    *blocks, sums = back_blocks(
        "back_proj", info,
        [(grad_query, wq), (grad_gate, wg), (grad_key, wk), (grad_value, wv)],
        gain1, low1, (kv_other,),
    )
    pieces, sent = ring_scatter(*blocks[:6])
    kv_blocks = weight_own_y(
        "kv_own", info, low1_own, [grad_key, grad_value], kv_got, sent
    )

    grad_x, gain1_grad = norm_back(
        "norm_back1", info, blocks[6], sums, pieces, gain1, layer_in, mean1, inv1, grad_middle,
        False, (kv_blocks[0],),
    )
    keys, vals = HEADS * KEY, HEADS * VAL
    kv_sent = send_blocks(kv_blocks[:3], False)
    kv_half = phase_sum("kv_mid", info, X_AT, kv_blocks[3], kv_sent)
    gains = sum_core_x(jnp.concatenate([gain1_grad, gain2_grad], axis=0), (mix_x, feed_grad))
    mix_half = weight_mid("mix_mid", mix_x, gains)
    feed_grad = feed_grad.astype(F32)
    grad_wo, grad_wg, grad_wq, gains = weight_sum(
        "mix_sum", exchange(mix_half, axis_groups(False)), [vals, vals, keys, PART]
    )
    grad_wk, grad_wv = last_sum(
        "kv_sum", kv_half[3], send_blocks(kv_half[:3], True), (keys, vals)
    )
    output = (middle + fed.astype(F32)).astype(BF16)
    return (
        output,
        grad_x,
        gains[0],
        grad_wq,
        grad_wk,
        grad_wv,
        grad_wg,
        grad_wo.T,
        gains[1],
        feed_grad[:, vals:],
        feed_grad[:, :vals].T,
    )


def solution(mesh):
    rows = P("seq", "head")
    cols = P(None, "head")
    tall = P("head", None)
    return jax.shard_map(
        shards,
        mesh=mesh,
        in_specs=(rows, P(), cols, cols, cols, cols, tall, P(), cols, tall, P(), rows),
        out_specs=(
            rows, rows, P("head"), rows, rows, rows, rows, P("head", "seq"), P("head"), rows,
            P("head", "seq"),
        ),
        check_vma=False,
    )
```
